32 devices in a mesh: wide: 8 (over z, core), narrow: 2 (over y), act: 2 (over x).
Axes of the slice: x: 2, y: 2, z: 4, core: 2. Of those that a mesh axis runs over, the one named last changes fastest.
Arguments:
- value_now: float32 [16, 16, 128, 128], P('wide', 'narrow'), may hold values from -8 to 8, as said below
- cost_first: float32 [8, 16], replicated, may hold values from -6 to 332, as said below
- cost_second: float32 [8, 16], replicated, may hold values from -6 to 6
- cost_third: float32 [8, 128], replicated, may hold values from -6 to 6
- cost_fourth: float32 [8, 128], replicated, may hold values from -6 to 6
- trans_weights: float32 [8, 4, 65], replicated, may hold values from 0.0001 to 1
- trans_offsets: int32 [8, 4], replicated, may hold values from -32 to 32
- action_order: int32 [8], replicated, may hold values from 0 to 7, each once
Outputs:
- new_value: float32 [16, 16, 128, 128], P('wide', 'narrow')
- choice_prob: bfloat16 [8, 16, 16, 128, 128], P('act', 'wide', 'narrow')
The draws below stay inside these ranges and needn't reach their ends.
Inputs may be any that keep to these rules, and one draw needn't show every extreme that they name: `value_now`: A value function of order one with rough and broad variation. `cost_first`: flow utility terms of order one in most entries.
All inputs are finite; a program needn't handle non-finite values.
Results may differ from the reference program's by a relative error of at most 0.001.
Values sent between devices are 32-bit elements; how exact they have to be, the bound alone decides.
No kernel may reach another device: no remote copies, remote signals or barrier semaphores. Data moves between devices by JAX's collectives and lax.ppermute only.
A program may use at most 64 MiB of HBM per device.

```python
import math
import jax
import jax.numpy as jnp
from jax import lax

ACTIONS = 8
HALF = 32
BAND = 65
N2 = 128
N3 = 128
N0 = 16
N1 = 16


def draw_value_now(key, part):
    shape = (N0, N1, N2, N3)
    field = 0.5 * jnp.clip(jax.random.normal(jax.random.fold_in(key, 1), shape, jnp.float32), -6.0, 6.0)
    lengths = (N0, N1, N2, N3)
    for axis_id in range(4):
        amplitude = jax.random.uniform(jax.random.fold_in(key, 10 + axis_id), (), jnp.float32, 0.5, 1.0)
        frequency = jax.random.randint(jax.random.fold_in(key, 20 + axis_id), (), 1, 4).astype(jnp.float32)
        phase_shift = jax.random.uniform(jax.random.fold_in(key, 30 + axis_id), (), jnp.float32, -math.pi, math.pi)
        coords = jnp.arange(lengths[axis_id], dtype=jnp.float32)
        profile = amplitude * jnp.cos(2.0 * math.pi * frequency * coords / lengths[axis_id] + phase_shift)
        view_shape = [1, 1, 1, 1]
        view_shape[axis_id] = lengths[axis_id]
        field = field + profile.reshape(view_shape)
    return field


def draw_cost_first(key, part):
    drawn = jnp.clip(jax.random.normal(jax.random.fold_in(key, 2), (ACTIONS, N0), jnp.float32), -6.0, 6.0)
    return drawn


def place_ends(array, stream_key, smallest, top_value):
    longest = array.shape.index(max(array.shape))
    spots = []
    for shift in (0, 1):
        where = [jax.random.randint(jax.random.fold_in(stream_key, axis), (), 0, length) for axis, length in enumerate(array.shape)]
        where[longest] = (where[longest] + shift) % array.shape[longest]
        spots.append(tuple(where))
    return array.at[spots[0]].set(smallest).at[spots[1]].set(top_value)


def noise(rng, dims, width, most, held_as=jnp.bfloat16):
    entries = jax.random.normal(rng, dims, jnp.float32) * width
    return jnp.minimum(jnp.maximum(entries, -most), most).astype(held_as)


def setup_inputs(seed: int = 0) -> dict:
    arg_keys = jax.random.split(jax.random.key(seed), 9)
    value_now = draw_value_now(jax.random.fold_in(arg_keys[8], 71), 0)
    cost_first = draw_cost_first(jax.random.fold_in(arg_keys[8], 71), 0)
    cost_second = noise(arg_keys[2], (ACTIONS, N1), 1.0, 6.0, jnp.float32)
    cost_third = noise(arg_keys[3], (ACTIONS, N2), 1.0, 6.0, jnp.float32)
    cost_fourth = noise(arg_keys[4], (ACTIONS, N3), 1.0, 6.0, jnp.float32)
    trans_weights = jnp.clip(jnp.exp(jax.random.uniform(arg_keys[5], (ACTIONS, 4, BAND), jnp.float32, math.log(0.0001), math.log(1.0))), 0.0001, 1.0)
    trans_offsets = place_ends(jax.random.randint(arg_keys[6], (ACTIONS, 4), -HALF, HALF + 1), jax.random.fold_in(arg_keys[6], 1), -HALF, HALF).astype(jnp.int32)
    action_order = jax.random.permutation(arg_keys[7], ACTIONS).astype(jnp.int32)
    return {"value_now": value_now, "cost_first": cost_first, "cost_second": cost_second, "cost_third": cost_third, "cost_fourth": cost_fourth, "trans_weights": trans_weights, "trans_offsets": trans_offsets, "action_order": action_order}


DISCOUNT = 0.95
HIGHEST = lax.Precision.HIGHEST


def transition(weights, offset, length):
    band_len = weights.shape[0]
    half_band = (band_len - 1) // 2
    normed = weights / jnp.sum(weights)
    row_ids = jnp.arange(length, dtype=jnp.int32)
    tap_ids = jnp.arange(band_len, dtype=jnp.int32)
    target = jnp.clip(row_ids[:, None] + offset + tap_ids[None, :] - half_band, 0, length - 1)
    matched = (target[:, :, None] == row_ids[None, None, :]).astype(normed.dtype)
    return jnp.einsum("ijk,j->ik", matched, normed, precision=HIGHEST)


def expect(value_now, weights, offsets):
    lengths = value_now.shape
    field = value_now
    for axis_id in range(4):
        matrix = transition(weights[axis_id], offsets[axis_id], lengths[axis_id])
        field = jnp.moveaxis(jnp.tensordot(matrix, field, axes=([1], [axis_id]), precision=HIGHEST), 0, axis_id)
    return field


def reference(value_now, cost_first, cost_second, cost_third, cost_fourth, trans_weights, trans_offsets, action_order):
    def one_action(action_id):
        expected = expect(value_now, trans_weights[action_id], trans_offsets[action_id])
        utility = (cost_first[action_id][:, None, None, None] + cost_second[action_id][None, :, None, None]
                   + cost_third[action_id][None, None, :, None] + cost_fourth[action_id][None, None, None, :])
        return utility + DISCOUNT * expected

    scores = lax.map(one_action, jnp.arange(ACTIONS, dtype=jnp.int32))
    top_score = jnp.max(scores, axis=0)
    total = jnp.sum(jnp.exp(scores - top_score), axis=0)
    new_value = top_score + jnp.log(total)

    def one_prob(action_id):
        return jnp.exp(scores[action_id] - new_value).astype(jnp.bfloat16)

    choice_prob = lax.map(one_prob, action_order)
    return new_value, choice_prob
```

```python
import functools

import jax
import jax.numpy as jnp
from jax import lax
from jax.experimental import pallas as pl
from jax.experimental.pallas import tpu as pltpu
from jax.sharding import PartitionSpec as P

DISCOUNT = 0.95
HIGHEST = lax.Precision.HIGHEST
F32 = jnp.float32
BF16 = jnp.bfloat16
LANES = 128
SUBLANES = 8
CHUNK_ROWS = 8
VMEM_LIMIT = 48 * 1024 * 1024


def merged(value, axis, join):
    pieces = lax.all_gather(value, axis)
    head = pieces[0]
    tail = pieces[1:]
    subtotal, _ = lax.scan(lambda subtotal, slab: (join(subtotal, slab), None), head, tail)
    return subtotal


def transition(weights, offset, length):
    band_len = weights.shape[0]
    half_band = (band_len - 1) // 2
    normed = weights / jnp.sum(weights)
    row_ids = jnp.arange(length, dtype=jnp.int32)
    tap_ids = jnp.arange(band_len, dtype=jnp.int32)
    target = jnp.clip(row_ids[:, None] + offset + tap_ids[None, :] - half_band, 0, length - 1)
    matched = (target[:, :, None] == row_ids[None, None, :]).astype(normed.dtype)
    return jnp.einsum("ijk,j->ik", matched, normed, precision=HIGHEST)


def exchange_body(
    value_now,
    cost_first,
    cost_second,
    cost_third,
    cost_fourth,
    trans_weights,
    trans_offsets,
    action_order,
):
    size_act = lax.axis_size("act")
    per_group = action_order.shape[0] // size_act
    group_id = lax.axis_index("act")
    my_actions = lax.dynamic_slice_in_dim(action_order, group_id * per_group, per_group)
    rows_first, rows_second, len_third, len_fourth = value_now.shape
    len_first = rows_first * lax.axis_size("wide")
    len_second = rows_second * lax.axis_size("narrow")
    my_weights = jnp.take(trans_weights, my_actions, axis=0)
    my_offsets = jnp.take(trans_offsets, my_actions, axis=0)

    def build(axis_id, length):
        return jax.vmap(lambda weight_row, offset_one: transition(weight_row, offset_one, length))(
            my_weights[:, axis_id], my_offsets[:, axis_id]
        )

    mat_first = build(0, len_first)
    mat_second = build(1, len_second)
    mat_third = build(2, len_third)
    mat_fourth = build(3, len_fourth)
    spread = lax.all_to_all(value_now, "narrow", split_axis=2, concat_axis=1, tiled=True)
    field = jnp.einsum("gij,ajcd->gaicd", mat_second, spread, precision=HIGHEST)
    field = jnp.einsum("gij,gabcj->gabci", mat_fourth, field, precision=HIGHEST)
    field = lax.all_to_all(field, "narrow", split_axis=2, concat_axis=3, tiled=True)
    field = lax.all_to_all(field, "wide", split_axis=3, concat_axis=1, tiled=True)
    field = jnp.einsum("gij,gjbcd->gibcd", mat_first, field, precision=HIGHEST)
    field = lax.all_to_all(field, "wide", split_axis=1, concat_axis=3, tiled=True)
    expected = jnp.einsum("gij,gabjd->gabid", mat_third, field, precision=HIGHEST)
    start_first = lax.axis_index("wide") * rows_first
    start_second = lax.axis_index("narrow") * rows_second
    util_first = lax.dynamic_slice_in_dim(
        jnp.take(cost_first, my_actions, axis=0), start_first, rows_first, 1
    )
    util_second = lax.dynamic_slice_in_dim(
        jnp.take(cost_second, my_actions, axis=0), start_second, rows_second, 1
    )
    util_third = jnp.take(cost_third, my_actions, axis=0)
    util_fourth = jnp.take(cost_fourth, my_actions, axis=0)
    utility = (
        util_first[:, :, None, None, None]
        + util_second[:, None, :, None, None]
        + util_third[:, None, None, :, None]
        + util_fourth[:, None, None, None, :]
    )
    scores = utility + DISCOUNT * expected
    local_max = jnp.max(scores, axis=0)
    local_sum = jnp.sum(jnp.exp(scores - local_max), axis=0)
    log_total = merged(local_max + jnp.log(local_sum), "act", jnp.logaddexp)
    choice_prob = jnp.exp(scores - log_total).astype(jnp.bfloat16)
    return (log_total, choice_prob)


def halves(x):
    high = x.astype(BF16)
    return high, (x - high.astype(F32)).astype(BF16)


def dot32(a, b):
    return jnp.dot(a, b, preferred_element_type=F32, precision=HIGHEST)


def banded(weights, offset, length, taps):
    half_band = (taps - 1) // 2
    width = weights.shape[1]
    normed = weights / jnp.sum(weights, axis=1, keepdims=True)
    rows = jnp.broadcast_to(normed, (length, width))
    rows = pltpu.roll(rows, lax.rem(offset + (width - half_band), width), 1)
    rows = pltpu.roll(rows, 0, 1, stride=1, stride_axis=0)
    lane = lax.broadcasted_iota(jnp.int32, (length, width), 1)
    under = lane >= width - 2 * half_band
    over = (lane >= length) & (lane < length + 2 * half_band)
    under_sum = jnp.sum(jnp.where(under, rows, 0.0), axis=1, keepdims=True)
    over_sum = jnp.sum(jnp.where(over, rows, 0.0), axis=1, keepdims=True)
    span = -(-length // LANES) * LANES
    kept = lane[:, :span]
    body = jnp.where(kept < length, rows[:, :span], 0.0)
    body = body + jnp.where(kept == 0, under_sum, 0.0)
    return body + jnp.where(kept == length - 1, over_sum, 0.0)


def prepare_kernel(
    lengths, taps, groups, offs, weights, pick0, spread0, pick1, spread1, order2, kron_hi, kron_lo, left2, right3
):
    actions = offs.shape[0]
    per_group = actions // groups
    picked0 = pick0.shape[0]
    own0 = picked0 // 2
    rows1 = pick1.shape[0]
    for action in range(actions):
        mats = [
            banded(weights[action, axis : axis + 1, :], offs[action, axis], lengths[axis], taps)
            for axis in range(4)
        ]
        group, slot = divmod(action, per_group)
        wide0 = dot32(dot32(pick0[...], mats[0]), spread0[...])
        wide1 = dot32(dot32(pick1[...], mats[1]), spread1[...])
        for part in range(2):
            for row in range(own0):
                start = (((group * 2 + part) * per_group + slot) * own0 + row) * rows1
                index = part * own0 + row
                high, low = halves(wide0[index : index + 1, :] * wide1)
                kron_hi[start : start + rows1, :] = high.astype(F32)
                kron_lo[start : start + rows1, :] = low.astype(F32)
        high, low = halves(mats[3].T)
        row_pair = jnp.concatenate([high, low], axis=1)
        right3[action] = jnp.concatenate([row_pair, row_pair], axis=0)
        if group == 0:
            high, low = halves(dot32(mats[2], order2[...]))
            left2[action] = jnp.concatenate(
                [jnp.concatenate([high, high], axis=1), jnp.concatenate([low, low], axis=1)], axis=0
            )


def short_dims_kernel(n_pieces, groups, kron_hi, kron_lo, right3, *refs):
    pieces, outs = refs[:n_pieces], refs[n_pieces:]
    rows = pieces[0].shape[1]
    depth = pieces[0].shape[2]
    actions = right3.shape[0]
    per_group = actions // groups
    per_out = outs[0].shape[1]
    q_hi, q_lo = kron_hi[...].astype(BF16), kron_lo[...].astype(BF16)
    mixed = []
    for row in range(0, rows, 2):
        cols = [
            jnp.concatenate([piece[:, row + extra, :] for piece in pieces], axis=0)
            for extra in range(2)
        ]
        x_hi, x_lo = halves(jnp.concatenate(cols, axis=1))
        out = (
            jnp.dot(q_hi, x_hi, preferred_element_type=F32)
            + jnp.dot(q_hi, x_lo, preferred_element_type=F32)
            + jnp.dot(q_lo, x_hi, preferred_element_type=F32)
        )
        mixed += [out[:, :depth], out[:, depth:]]
    for action in range(actions):
        group, slot = divmod(action, per_group)
        blocks = []
        for part in range(2):
            start = ((group * 2 + part) * per_group + slot) * per_out
            blocks += [mixed[row][start : start + per_out] for row in range(rows)]
        t_hi, t_lo = halves(jnp.concatenate(blocks, axis=0))
        both = jnp.dot(
            jnp.concatenate([t_hi, t_lo], axis=1), right3[action], preferred_element_type=F32
        )
        done = both[:, :depth] + both[:, depth:]
        for part in range(2):
            for row in range(rows):
                start = (part * rows + row) * per_out
                outs[group * 2 + part][slot, :, row, :] = done[start : start + per_out]


def third_dim_kernel(n_pieces, scalars0, scalars1, left2, util23, *refs):
    pieces, scores, local = refs[:n_pieces], refs[n_pieces], refs[n_pieces + 1]
    per_group, rows1 = pieces[0].shape[0], pieces[0].shape[1]
    length = util23.shape[1]
    depth = util23.shape[2]
    first = pl.program_id(0)
    for second in range(0, rows1, 2):
        for slot in range(per_group):
            cols = [
                jnp.concatenate([piece[slot, second + extra] for piece in pieces], axis=0)
                for extra in range(2)
            ]
            g_hi, g_lo = halves(jnp.concatenate(cols, axis=1))
            both = jnp.dot(
                left2[slot], jnp.concatenate([g_hi, g_lo], axis=0), preferred_element_type=F32
            )
            expected = both[:length] + both[length:]
            for extra in range(2):
                flat = scalars0[slot, first] + scalars1[slot, second + extra]
                scores[slot, 0, second + extra] = (util23[slot] + flat) + DISCOUNT * expected[
                    :, extra * depth : (extra + 1) * depth
                ]
        for extra in range(2):
            found = [scores[slot, 0, second + extra] for slot in range(per_group)]
            top = functools.reduce(jnp.maximum, found)
            total = functools.reduce(jnp.add, [jnp.exp(one - top) for one in found])
            local[0, second + extra] = top + jnp.log(total)


def choice_kernel(scores, mine, other, new_value, choice_prob):
    a, b = mine[...], other[...]
    top, low = jnp.maximum(a, b), jnp.minimum(a, b)
    total = top + jnp.log(1.0 + jnp.exp(low - top))
    new_value[...] = total
    for slot in range(scores.shape[0]):
        choice_prob[slot] = jnp.exp(scores[slot] - total).astype(choice_prob.dtype)


def whole_block():
    return pl.BlockSpec(memory_space=pltpu.VMEM)


def params():
    return pltpu.CompilerParams(vmem_limit_bytes=VMEM_LIMIT)


def gather_body(
    value_now,
    cost_first,
    cost_second,
    cost_third,
    cost_fourth,
    trans_weights,
    trans_offsets,
    action_order,
):
    n_act, n_narrow, n_wide = (lax.axis_size(name) for name in ("act", "narrow", "wide"))
    n_outer = n_wide // 2
    act, narrow, wide = (lax.axis_index(name) for name in ("act", "narrow", "wide"))
    outer, core = wide // 2, wide % 2
    actions, _, taps = trans_weights.shape
    per_group = actions // n_act
    rows0, rows1, len2, len3 = value_now.shape
    len0, len1 = rows0 * n_wide, rows1 * n_narrow
    lengths = (len0, len1, len2, len3)
    quarter = len2 // (2 * n_act)
    chunk = CHUNK_ROWS
    n_chunks = quarter // chunk

    core_flip = [(i, i ^ 1) for i in range(n_wide)]
    own_part = 2 * act + core
    mine = lax.dynamic_slice_in_dim(value_now, own_part * quarter, quarter, 2)
    handed = lax.dynamic_slice_in_dim(value_now, (own_part + 1 - 2 * core) * quarter, quarter, 2)
    taken = lax.ppermute(handed, "wide", core_flip)
    block = jnp.concatenate([mine, taken], axis=0)
    block = block.reshape(2 * rows0, rows1, n_chunks, chunk, len3)

    order = jnp.roll(action_order, -act * per_group)
    half_band = (taps - 1) // 2
    width = -(-(max(lengths) + 4 * half_band) // LANES) * LANES
    weights = jnp.pad(jnp.take(trans_weights, order, axis=0), ((0, 0), (0, 0), (0, width - taps)))
    offsets = jnp.take(trans_offsets, order, axis=0)

    def one_hot(ids, size):
        return (ids[:, None] == jnp.arange(size, dtype=jnp.int32)[None, :]).astype(F32)

    def padded(length):
        return -(-length // LANES) * LANES

    part_ids = jnp.arange(2 * rows0, dtype=jnp.int32)
    pick0 = (outer * 2 + (part_ids // rows0 + core) % 2) * rows0 + part_ids % rows0
    pick1 = narrow * rows1 + jnp.arange(rows1, dtype=jnp.int32)
    cols = jnp.arange(len0 * len1, dtype=jnp.int32)
    col1 = cols % rows1
    col0 = (cols // rows1) % (2 * rows0)
    piece = cols // (rows1 * 2 * rows0)
    ahead, behind = piece // n_outer, piece % n_outer
    from_outer = (outer - behind + n_outer) % n_outer
    from_core = (col0 // rows0 + core) % 2
    spread0 = one_hot((from_outer * 2 + from_core) * rows0 + col0 % rows0, padded(len0)).T
    spread1 = one_hot(((narrow - ahead + n_narrow) % n_narrow) * rows1 + col1, padded(len1)).T
    slots = jnp.arange(len2, dtype=jnp.int32)
    kind = slots // quarter
    part_act = (act + kind // 2) % n_act
    part_core = (core + kind % 2) % 2
    order2 = one_hot((2 * part_act + part_core) * quarter + slots % quarter, len2).T

    q_rows = actions * 2 * rows0 * rows1
    kron_hi, kron_lo, left2, right3 = pl.pallas_call(
        functools.partial(prepare_kernel, lengths, taps, n_act),
        out_shape=(
            jax.ShapeDtypeStruct((q_rows, len0 * len1), F32),
            jax.ShapeDtypeStruct((q_rows, len0 * len1), F32),
            jax.ShapeDtypeStruct((per_group, 2 * len2, 2 * len2), BF16),
            jax.ShapeDtypeStruct((actions, 2 * len3, 2 * len3), BF16),
        ),
        in_specs=[pl.BlockSpec(memory_space=pltpu.SMEM)] + [whole_block()] * 6,
        compiler_params=params(),
        cost_estimate=pl.CostEstimate(flops=10**9, bytes_accessed=4 * 10**6, transcendentals=0),
        name="prepare",
    )(offsets, weights, one_hot(pick0, len0), spread0, one_hot(pick1, len1), spread1, order2)

    act_flip = [(i, (i + 1) % n_act) for i in range(n_act)]
    cross = [
        (w * n_act + a, (w ^ 1) * n_act + (a + 1) % n_act) for w in range(n_wide) for a in range(n_act)
    ]
    per_out = rows0 * rows1
    out_piece = jax.ShapeDtypeStruct((per_group, per_out, chunk, len3), F32)
    gathered = [[], [], [], []]
    for index in range(n_chunks):
        held = [block[:, :, index]]
        for step in range(1, n_outer):
            hops = [(i, (i + 2 * step) % n_wide) for i in range(n_wide)]
            held.append(lax.ppermute(held[0], "wide", hops))
        pieces = list(held)
        for step in range(1, n_narrow):
            hops = [(i, (i + step) % n_narrow) for i in range(n_narrow)]
            pieces += [lax.ppermute(one, "narrow", hops) for one in held]
        pieces = [one.reshape(2 * rows0 * rows1, chunk, len3) for one in pieces]
        keep, for_core, for_act, for_cross = pl.pallas_call(
            functools.partial(short_dims_kernel, len(pieces), n_act),
            out_shape=(out_piece,) * 4,
            in_specs=[whole_block()] * (3 + len(pieces)),
            out_specs=(whole_block(),) * 4,
            compiler_params=params(),
            cost_estimate=pl.CostEstimate(flops=10**9, bytes_accessed=3 * 10**6, transcendentals=0),
            name="short_dims",
        )(kron_hi, kron_lo, right3, *pieces)
        gathered[0].append(keep)
        gathered[1].append(lax.ppermute(for_core, "wide", core_flip))
        gathered[2].append(lax.ppermute(for_act, "act", act_flip))
        gathered[3].append(lax.ppermute(for_cross, ("wide", "act"), cross))
    parts = [one for kind_parts in gathered for one in kind_parts]

    my_actions = order[:per_group]
    util_first = lax.dynamic_slice_in_dim(
        jnp.take(cost_first, my_actions, axis=0), wide * rows0, rows0, 1
    )
    util_second = lax.dynamic_slice_in_dim(
        jnp.take(cost_second, my_actions, axis=0), narrow * rows1, rows1, 1
    )
    util23 = (
        jnp.take(cost_third, my_actions, axis=0)[:, :, None]
        + jnp.take(cost_fourth, my_actions, axis=0)[:, None, :]
    )
    smem = pl.BlockSpec(memory_space=pltpu.SMEM)
    scores_shape = (per_group, rows0, rows1, len2, len3)
    score_spec = pl.BlockSpec((per_group, 1, rows1, len2, len3), lambda i: (0, i, 0, 0, 0))
    state_spec = pl.BlockSpec((1, rows1, len2, len3), lambda i: (i, 0, 0, 0))
    scores, local = pl.pallas_call(
        functools.partial(third_dim_kernel, len(parts)),
        grid=(rows0,),
        out_shape=(
            jax.ShapeDtypeStruct(scores_shape, F32),
            jax.ShapeDtypeStruct(value_now.shape, F32),
        ),
        in_specs=[smem, smem, whole_block(), whole_block()]
        + [pl.BlockSpec((per_group, rows1, chunk, len3), lambda i: (0, i, 0, 0))] * len(parts),
        out_specs=(score_spec, state_spec),
        compiler_params=params(),
        cost_estimate=pl.CostEstimate(flops=2 * 10**9, bytes_accessed=10**7, transcendentals=10**6),
        name="third_dim",
    )(util_first, util_second, left2, util23, *parts)

    other = lax.ppermute(local, "act", act_flip)
    return tuple(
        pl.pallas_call(
            choice_kernel,
            grid=(rows0,),
            out_shape=(
                jax.ShapeDtypeStruct(value_now.shape, F32),
                jax.ShapeDtypeStruct(scores_shape, BF16),
            ),
            in_specs=[score_spec, state_spec, state_spec],
            out_specs=(state_spec, score_spec),
            compiler_params=params(),
            cost_estimate=pl.CostEstimate(flops=10**7, bytes_accessed=10**7, transcendentals=10**6),
            name="choice",
        )(scores, local, other)
    )


def gather_fits(mesh, value_shape, actions, offset_reach):
    n_wide, n_narrow, n_act = (mesh.shape[name] for name in ("wide", "narrow", "act"))
    len0, len1, len2, len3 = value_shape
    if n_act != 2 or n_wide % 2 or actions % n_act:
        return False
    if len2 % (2 * n_act * CHUNK_ROWS) or len2 % LANES or len3 != LANES or len2 != LANES:
        return False
    if (len1 // n_narrow) % SUBLANES or len0 % n_wide or len1 % n_narrow:
        return False
    raw = len0 * len1 * len2 * len3 // (2 * n_act)
    exchanged = 2 * (actions // n_act) * len0 * len1 * len2 * len3 // (n_wide * n_narrow)
    return raw <= exchanged


def solution(mesh):
    def run(value_now, *rest):
        actions = rest[-1].shape[0]
        small = gather_fits(mesh, value_now.shape, actions, rest[4].shape[-1])
        return jax.shard_map(
            gather_body if small else exchange_body,
            mesh=mesh,
            in_specs=(P("wide", "narrow", None, None), P(), P(), P(), P(), P(), P(), P()),
            out_specs=(P("wide", "narrow", None, None), P("act", "wide", "narrow", None, None)),
            check_vma=False,
        )(value_now, *rest)

    return run
```

```python
import functools

import jax
import jax.numpy as jnp
from jax import lax
from jax.experimental import pallas as pl
from jax.experimental.pallas import tpu as pltpu
from jax.sharding import PartitionSpec as P

DISCOUNT = 0.95
HIGHEST = lax.Precision.HIGHEST
F32 = jnp.float32
BF16 = jnp.bfloat16
LANES = 128
SUBLANES = 8
CHUNK_ROWS = 8
MIB = 1024 * 1024


def merged(value, axis, join):
    pieces = lax.all_gather(value, axis)
    head = pieces[0]
    tail = pieces[1:]
    subtotal, _ = lax.scan(lambda subtotal, slab: (join(subtotal, slab), None), head, tail)
    return subtotal


def transition(weights, offset, length):
    band_len = weights.shape[0]
    half_band = (band_len - 1) // 2
    normed = weights / jnp.sum(weights)
    row_ids = jnp.arange(length, dtype=jnp.int32)
    tap_ids = jnp.arange(band_len, dtype=jnp.int32)
    target = jnp.clip(row_ids[:, None] + offset + tap_ids[None, :] - half_band, 0, length - 1)
    matched = (target[:, :, None] == row_ids[None, None, :]).astype(normed.dtype)
    return jnp.einsum("ijk,j->ik", matched, normed, precision=HIGHEST)


def exchange_body(
    value_now,
    cost_first,
    cost_second,
    cost_third,
    cost_fourth,
    trans_weights,
    trans_offsets,
    action_order,
):
    size_act = lax.axis_size("act")
    per_group = action_order.shape[0] // size_act
    group_id = lax.axis_index("act")
    my_actions = lax.dynamic_slice_in_dim(action_order, group_id * per_group, per_group)
    rows_first, rows_second, len_third, len_fourth = value_now.shape
    len_first = rows_first * lax.axis_size("wide")
    len_second = rows_second * lax.axis_size("narrow")
    my_weights = jnp.take(trans_weights, my_actions, axis=0)
    my_offsets = jnp.take(trans_offsets, my_actions, axis=0)

    def build(axis_id, length):
        return jax.vmap(lambda weight_row, offset_one: transition(weight_row, offset_one, length))(
            my_weights[:, axis_id], my_offsets[:, axis_id]
        )

    mat_first = build(0, len_first)
    mat_second = build(1, len_second)
    mat_third = build(2, len_third)
    mat_fourth = build(3, len_fourth)
    spread = lax.all_to_all(value_now, "narrow", split_axis=2, concat_axis=1, tiled=True)
    field = jnp.einsum("gij,ajcd->gaicd", mat_second, spread, precision=HIGHEST)
    field = jnp.einsum("gij,gabcj->gabci", mat_fourth, field, precision=HIGHEST)
    field = lax.all_to_all(field, "narrow", split_axis=2, concat_axis=3, tiled=True)
    field = lax.all_to_all(field, "wide", split_axis=3, concat_axis=1, tiled=True)
    field = jnp.einsum("gij,gjbcd->gibcd", mat_first, field, precision=HIGHEST)
    field = lax.all_to_all(field, "wide", split_axis=1, concat_axis=3, tiled=True)
    expected = jnp.einsum("gij,gabjd->gabid", mat_third, field, precision=HIGHEST)
    start_first = lax.axis_index("wide") * rows_first
    start_second = lax.axis_index("narrow") * rows_second
    util_first = lax.dynamic_slice_in_dim(
        jnp.take(cost_first, my_actions, axis=0), start_first, rows_first, 1
    )
    util_second = lax.dynamic_slice_in_dim(
        jnp.take(cost_second, my_actions, axis=0), start_second, rows_second, 1
    )
    util_third = jnp.take(cost_third, my_actions, axis=0)
    util_fourth = jnp.take(cost_fourth, my_actions, axis=0)
    utility = (
        util_first[:, :, None, None, None]
        + util_second[:, None, :, None, None]
        + util_third[:, None, None, :, None]
        + util_fourth[:, None, None, None, :]
    )
    scores = utility + DISCOUNT * expected
    local_max = jnp.max(scores, axis=0)
    local_sum = jnp.sum(jnp.exp(scores - local_max), axis=0)
    log_total = merged(local_max + jnp.log(local_sum), "act", jnp.logaddexp)
    choice_prob = jnp.exp(scores - log_total).astype(jnp.bfloat16)
    return (log_total, choice_prob)


def halves(x):
    high = x.astype(BF16)
    return high, (x - high.astype(F32)).astype(BF16)


def dot32(a, b):
    return jnp.dot(a, b, preferred_element_type=F32, precision=HIGHEST)


def banded(weights, offset, length, taps):
    half_band = (taps - 1) // 2
    width = weights.shape[1]
    normed = weights / jnp.sum(weights, axis=1, keepdims=True)
    rows = jnp.broadcast_to(normed, (length, width))
    rows = pltpu.roll(rows, lax.rem(offset + (width - half_band), width), 1)
    rows = pltpu.roll(rows, 0, 1, stride=1, stride_axis=0)
    lane = lax.broadcasted_iota(jnp.int32, (length, width), 1)
    under = lane >= width - 2 * half_band
    over = (lane >= length) & (lane < length + 2 * half_band)
    under_sum = jnp.sum(jnp.where(under, rows, 0.0), axis=1, keepdims=True)
    over_sum = jnp.sum(jnp.where(over, rows, 0.0), axis=1, keepdims=True)
    span = -(-length // LANES) * LANES
    kept = lane[:, :span]
    body = jnp.where(kept < length, rows[:, :span], 0.0)
    body = body + jnp.where(kept == 0, under_sum, 0.0)
    return body + jnp.where(kept == length - 1, over_sum, 0.0)


def prepare_kernel(
    lengths, taps, groups, offs, weights, pick0, spread0, pick1, spread1, order2, kron_hi, kron_lo, left2, right3
):
    actions = offs.shape[0]
    per_group = actions // groups
    picked0 = pick0.shape[0]
    own0 = picked0 // 2
    rows1 = pick1.shape[0]
    for action in range(actions):
        mats = [
            banded(weights[action, axis : axis + 1, :], offs[action, axis], lengths[axis], taps)
            for axis in range(4)
        ]
        group, slot = divmod(action, per_group)
        wide0 = dot32(dot32(pick0[...], mats[0]), spread0[...])
        wide1 = dot32(dot32(pick1[...], mats[1]), spread1[...])
        for part in range(2):
            for row in range(own0):
                start = (((group * 2 + part) * per_group + slot) * own0 + row) * rows1
                index = part * own0 + row
                high, low = halves(wide0[index : index + 1, :] * wide1)
                kron_hi[start : start + rows1, :] = high.astype(F32)
                kron_lo[start : start + rows1, :] = low.astype(F32)
        high, low = halves(mats[3].T)
        row_pair = jnp.concatenate([high, low], axis=1)
        right3[action] = jnp.concatenate([row_pair, row_pair], axis=0)
        if group == 0:
            high, low = halves(dot32(mats[2], order2[...]))
            left2[action] = jnp.concatenate(
                [jnp.concatenate([high, high], axis=1), jnp.concatenate([low, low], axis=1)], axis=0
            )


def short_dims_kernel(n_pieces, groups, kron_hi, kron_lo, right3, *refs):
    pieces, outs = refs[:n_pieces], refs[n_pieces:]
    rows = pieces[0].shape[1]
    depth = pieces[0].shape[2]
    actions = right3.shape[0]
    per_group = actions // groups
    per_out = outs[0].shape[1]
    q_hi, q_lo = kron_hi[...].astype(BF16), kron_lo[...].astype(BF16)
    mixed = []
    for row in range(0, rows, 2):
        cols = [
            jnp.concatenate([piece[:, row + extra, :] for piece in pieces], axis=0)
            for extra in range(2)
        ]
        x_hi, x_lo = halves(jnp.concatenate(cols, axis=1))
        out = (
            jnp.dot(q_hi, x_hi, preferred_element_type=F32)
            + jnp.dot(q_hi, x_lo, preferred_element_type=F32)
            + jnp.dot(q_lo, x_hi, preferred_element_type=F32)
        )
        mixed += [out[:, :depth], out[:, depth:]]
    for action in range(actions):
        group, slot = divmod(action, per_group)
        blocks = []
        for part in range(2):
            start = ((group * 2 + part) * per_group + slot) * per_out
            blocks += [mixed[row][start : start + per_out] for row in range(rows)]
        t_hi, t_lo = halves(jnp.concatenate(blocks, axis=0))
        both = jnp.dot(
            jnp.concatenate([t_hi, t_lo], axis=1), right3[action], preferred_element_type=F32
        )
        done = both[:, :depth] + both[:, depth:]
        for part in range(2):
            for row in range(rows):
                start = (part * rows + row) * per_out
                outs[group * 2 + part][slot, :, row, :] = done[start : start + per_out]


def third_dim_kernel(n_pieces, scalars0, scalars1, left2, util23, *refs):
    pieces, scores, local = refs[:n_pieces], refs[n_pieces], refs[n_pieces + 1]
    per_group, rows1 = pieces[0].shape[0], pieces[0].shape[1]
    length = util23.shape[1]
    depth = util23.shape[2]
    first = pl.program_id(0)
    for second in range(0, rows1, 2):
        for slot in range(per_group):
            cols = [
                jnp.concatenate([piece[slot, second + extra] for piece in pieces], axis=0)
                for extra in range(2)
            ]
            g_hi, g_lo = halves(jnp.concatenate(cols, axis=1))
            both = jnp.dot(
                left2[slot], jnp.concatenate([g_hi, g_lo], axis=0), preferred_element_type=F32
            )
            expected = both[:length] + both[length:]
            for extra in range(2):
                flat = scalars0[slot, first] + scalars1[slot, second + extra]
                scores[slot, 0, second + extra] = (util23[slot] + flat) + DISCOUNT * expected[
                    :, extra * depth : (extra + 1) * depth
                ]
        for extra in range(2):
            found = [scores[slot, 0, second + extra] for slot in range(per_group)]
            top = functools.reduce(jnp.maximum, found)
            total = functools.reduce(jnp.add, [jnp.exp(one - top) for one in found])
            local[0, second + extra] = top + jnp.log(total)


def choice_kernel(scores, mine, other, new_value, choice_prob):
    a, b = mine[...], other[...]
    top, low = jnp.maximum(a, b), jnp.minimum(a, b)
    total = top + jnp.log(1.0 + jnp.exp(low - top))
    new_value[...] = total
    for slot in range(scores.shape[0]):
        choice_prob[slot] = jnp.exp(scores[slot] - total).astype(choice_prob.dtype)


def whole_block():
    return pl.BlockSpec(memory_space=pltpu.VMEM)


def params(mebibytes):
    return pltpu.CompilerParams(vmem_limit_bytes=mebibytes * MIB)


def gather_body(
    value_now,
    cost_first,
    cost_second,
    cost_third,
    cost_fourth,
    trans_weights,
    trans_offsets,
    action_order,
):
    n_act, n_narrow, n_wide = (lax.axis_size(name) for name in ("act", "narrow", "wide"))
    n_outer = n_wide // 2
    act, narrow, wide = (lax.axis_index(name) for name in ("act", "narrow", "wide"))
    outer, core = wide // 2, wide % 2
    actions, _, taps = trans_weights.shape
    per_group = actions // n_act
    rows0, rows1, len2, len3 = value_now.shape
    len0, len1 = rows0 * n_wide, rows1 * n_narrow
    lengths = (len0, len1, len2, len3)
    quarter = len2 // (2 * n_act)
    chunk = CHUNK_ROWS
    n_chunks = quarter // chunk

    core_flip = [(i, i ^ 1) for i in range(n_wide)]
    own_part = 2 * act + core
    mine = lax.dynamic_slice_in_dim(value_now, own_part * quarter, quarter, 2)
    handed = lax.dynamic_slice_in_dim(value_now, (own_part + 1 - 2 * core) * quarter, quarter, 2)
    taken = lax.ppermute(handed, "wide", core_flip)
    block = jnp.concatenate([mine, taken], axis=0)
    block = block.reshape(2 * rows0, rows1, n_chunks, chunk, len3)

    order = jnp.roll(action_order, -act * per_group)
    half_band = (taps - 1) // 2
    width = -(-(max(lengths) + 4 * half_band) // LANES) * LANES
    weights = jnp.pad(jnp.take(trans_weights, order, axis=0), ((0, 0), (0, 0), (0, width - taps)))
    offsets = jnp.take(trans_offsets, order, axis=0)

    def one_hot(ids, size):
        return (ids[:, None] == jnp.arange(size, dtype=jnp.int32)[None, :]).astype(F32)

    def padded(length):
        return -(-length // LANES) * LANES

    part_ids = jnp.arange(2 * rows0, dtype=jnp.int32)
    pick0 = (outer * 2 + (part_ids // rows0 + core) % 2) * rows0 + part_ids % rows0
    pick1 = narrow * rows1 + jnp.arange(rows1, dtype=jnp.int32)
    cols = jnp.arange(len0 * len1, dtype=jnp.int32)
    col1 = cols % rows1
    col0 = (cols // rows1) % (2 * rows0)
    piece = cols // (rows1 * 2 * rows0)
    ahead, behind = piece // n_outer, piece % n_outer
    from_core = (col0 // rows0 + core) % 2
    spread0 = one_hot((behind * 2 + from_core) * rows0 + col0 % rows0, padded(len0)).T
    spread1 = one_hot(((narrow - ahead + n_narrow) % n_narrow) * rows1 + col1, padded(len1)).T
    slots = jnp.arange(len2, dtype=jnp.int32)
    kind = slots // quarter
    part_act = (act + kind // 2) % n_act
    part_core = (core + kind % 2) % 2
    order2 = one_hot((2 * part_act + part_core) * quarter + slots % quarter, len2).T

    q_rows = actions * 2 * rows0 * rows1
    kron_hi, kron_lo, left2, right3 = pl.pallas_call(
        functools.partial(prepare_kernel, lengths, taps, n_act),
        out_shape=(
            jax.ShapeDtypeStruct((q_rows, len0 * len1), F32),
            jax.ShapeDtypeStruct((q_rows, len0 * len1), F32),
            jax.ShapeDtypeStruct((per_group, 2 * len2, 2 * len2), BF16),
            jax.ShapeDtypeStruct((actions, 2 * len3, 2 * len3), BF16),
        ),
        in_specs=[pl.BlockSpec(memory_space=pltpu.SMEM)] + [whole_block()] * 6,
        compiler_params=params(16),
        cost_estimate=pl.CostEstimate(flops=10**9, bytes_accessed=4 * 10**6, transcendentals=0),
        name="prepare",
    )(offsets, weights, one_hot(pick0, len0), spread0, one_hot(pick1, len1), spread1, order2)

    act_flip = [(i, (i + 1) % n_act) for i in range(n_act)]
    same_core = [[2 * i + parity for i in range(n_outer)] for parity in range(2)]
    cross = [
        (w * n_act + a, (w ^ 1) * n_act + (a + 1) % n_act) for w in range(n_wide) for a in range(n_act)
    ]
    per_out = rows0 * rows1
    out_piece = jax.ShapeDtypeStruct((per_group, per_out, chunk, len3), F32)
    gathered = [[], [], [], []]
    chunks = [block[:, :, index] for index in range(n_chunks)]
    for index in range(n_chunks):
        held = lax.all_gather(chunks[index], "wide", axis_index_groups=same_core)
        if index + 1 < n_chunks:
            chunks[index + 1], held = lax.optimization_barrier((chunks[index + 1], held))
        pieces = [held]
        for step in range(1, n_narrow):
            hops = [(i, (i + step) % n_narrow) for i in range(n_narrow)]
            pieces.append(lax.ppermute(held, "narrow", hops))
        pieces = [one.reshape(len0 * rows1, chunk, len3) for one in pieces]
        keep, for_core, for_act, for_cross = pl.pallas_call(
            functools.partial(short_dims_kernel, len(pieces), n_act),
            out_shape=(out_piece,) * 4,
            in_specs=[whole_block()] * (3 + len(pieces)),
            out_specs=(whole_block(),) * 4,
            compiler_params=params(12),
            cost_estimate=pl.CostEstimate(flops=10**9, bytes_accessed=3 * 10**6, transcendentals=0),
            name="short_dims",
        )(kron_hi, kron_lo, right3, *pieces)
        gathered[0].append(keep)
        gathered[1].append(lax.ppermute(for_core, "wide", core_flip))
        gathered[2].append(lax.ppermute(for_act, "act", act_flip))
        gathered[3].append(lax.ppermute(for_cross, ("wide", "act"), cross))
    parts = [one for kind_parts in gathered for one in kind_parts]

    my_actions = order[:per_group]
    util_first = lax.dynamic_slice_in_dim(
        jnp.take(cost_first, my_actions, axis=0), wide * rows0, rows0, 1
    )
    util_second = lax.dynamic_slice_in_dim(
        jnp.take(cost_second, my_actions, axis=0), narrow * rows1, rows1, 1
    )
    util23 = (
        jnp.take(cost_third, my_actions, axis=0)[:, :, None]
        + jnp.take(cost_fourth, my_actions, axis=0)[:, None, :]
    )
    smem = pl.BlockSpec(memory_space=pltpu.SMEM)
    scores_shape = (per_group, rows0, rows1, len2, len3)
    score_spec = pl.BlockSpec((per_group, 1, rows1, len2, len3), lambda i: (0, i, 0, 0, 0))
    state_spec = pl.BlockSpec((1, rows1, len2, len3), lambda i: (i, 0, 0, 0))
    scores, local = pl.pallas_call(
        functools.partial(third_dim_kernel, len(parts)),
        grid=(rows0,),
        out_shape=(
            jax.ShapeDtypeStruct(scores_shape, F32),
            jax.ShapeDtypeStruct(value_now.shape, F32),
        ),
        in_specs=[smem, smem, whole_block(), whole_block()]
        + [pl.BlockSpec((per_group, rows1, chunk, len3), lambda i: (0, i, 0, 0))] * len(parts),
        out_specs=(score_spec, state_spec),
        compiler_params=params(20),
        cost_estimate=pl.CostEstimate(flops=2 * 10**9, bytes_accessed=10**7, transcendentals=10**6),
        name="third_dim",
    )(util_first, util_second, left2, util23, *parts)

    other = lax.ppermute(local, "act", act_flip)
    return tuple(
        pl.pallas_call(
            choice_kernel,
            grid=(rows0,),
            out_shape=(
                jax.ShapeDtypeStruct(value_now.shape, F32),
                jax.ShapeDtypeStruct(scores_shape, BF16),
            ),
            in_specs=[score_spec, state_spec, state_spec],
            out_specs=(state_spec, score_spec),
            compiler_params=params(16),
            cost_estimate=pl.CostEstimate(flops=10**7, bytes_accessed=10**7, transcendentals=10**6),
            name="choice",
        )(scores, local, other)
    )


def gather_fits(mesh, value_shape, actions, offset_reach):
    n_wide, n_narrow, n_act = (mesh.shape[name] for name in ("wide", "narrow", "act"))
    len0, len1, len2, len3 = value_shape
    if n_act != 2 or n_wide % 2 or actions % n_act:
        return False
    if len2 % (2 * n_act * CHUNK_ROWS) or len2 % LANES or len3 != LANES or len2 != LANES:
        return False
    if (len1 // n_narrow) % SUBLANES or len0 % n_wide or len1 % n_narrow:
        return False
    raw = len0 * len1 * len2 * len3 // (2 * n_act)
    exchanged = 2 * (actions // n_act) * len0 * len1 * len2 * len3 // (n_wide * n_narrow)
    return raw <= exchanged


def solution(mesh):
    def run(value_now, *rest):
        actions = rest[-1].shape[0]
        small = gather_fits(mesh, value_now.shape, actions, rest[4].shape[-1])
        return jax.shard_map(
            gather_body if small else exchange_body,
            mesh=mesh,
            in_specs=(P("wide", "narrow", None, None), P(), P(), P(), P(), P(), P(), P()),
            out_specs=(P("wide", "narrow", None, None), P("act", "wide", "narrow", None, None)),
            check_vma=False,
        )(value_now, *rest)

    return run
```

```python
import functools

import jax
import jax.numpy as jnp
from jax import lax
from jax.experimental import pallas as pl
from jax.experimental.pallas import tpu as pltpu
from jax.sharding import PartitionSpec as P

DISCOUNT = 0.95
HIGHEST = lax.Precision.HIGHEST
F32 = jnp.float32
BF16 = jnp.bfloat16
LANES = 128
SUBLANES = 8
CHUNK_ROWS = 8
MIB = 1024 * 1024


def merged(value, axis, join):
    pieces = lax.all_gather(value, axis)
    head = pieces[0]
    tail = pieces[1:]
    subtotal, _ = lax.scan(lambda subtotal, slab: (join(subtotal, slab), None), head, tail)
    return subtotal


def transition(weights, offset, length):
    band_len = weights.shape[0]
    half_band = (band_len - 1) // 2
    normed = weights / jnp.sum(weights)
    row_ids = jnp.arange(length, dtype=jnp.int32)
    tap_ids = jnp.arange(band_len, dtype=jnp.int32)
    target = jnp.clip(row_ids[:, None] + offset + tap_ids[None, :] - half_band, 0, length - 1)
    matched = (target[:, :, None] == row_ids[None, None, :]).astype(normed.dtype)
    return jnp.einsum("ijk,j->ik", matched, normed, precision=HIGHEST)


def exchange_body(
    value_now,
    cost_first,
    cost_second,
    cost_third,
    cost_fourth,
    trans_weights,
    trans_offsets,
    action_order,
):
    size_act = lax.axis_size("act")
    per_group = action_order.shape[0] // size_act
    group_id = lax.axis_index("act")
    my_actions = lax.dynamic_slice_in_dim(action_order, group_id * per_group, per_group)
    rows_first, rows_second, len_third, len_fourth = value_now.shape
    len_first = rows_first * lax.axis_size("wide")
    len_second = rows_second * lax.axis_size("narrow")
    my_weights = jnp.take(trans_weights, my_actions, axis=0)
    my_offsets = jnp.take(trans_offsets, my_actions, axis=0)

    def build(axis_id, length):
        return jax.vmap(lambda weight_row, offset_one: transition(weight_row, offset_one, length))(
            my_weights[:, axis_id], my_offsets[:, axis_id]
        )

    mat_first = build(0, len_first)
    mat_second = build(1, len_second)
    mat_third = build(2, len_third)
    mat_fourth = build(3, len_fourth)
    spread = lax.all_to_all(value_now, "narrow", split_axis=2, concat_axis=1, tiled=True)
    field = jnp.einsum("gij,ajcd->gaicd", mat_second, spread, precision=HIGHEST)
    field = jnp.einsum("gij,gabcj->gabci", mat_fourth, field, precision=HIGHEST)
    field = lax.all_to_all(field, "narrow", split_axis=2, concat_axis=3, tiled=True)
    field = lax.all_to_all(field, "wide", split_axis=3, concat_axis=1, tiled=True)
    field = jnp.einsum("gij,gjbcd->gibcd", mat_first, field, precision=HIGHEST)
    field = lax.all_to_all(field, "wide", split_axis=1, concat_axis=3, tiled=True)
    expected = jnp.einsum("gij,gabjd->gabid", mat_third, field, precision=HIGHEST)
    start_first = lax.axis_index("wide") * rows_first
    start_second = lax.axis_index("narrow") * rows_second
    util_first = lax.dynamic_slice_in_dim(
        jnp.take(cost_first, my_actions, axis=0), start_first, rows_first, 1
    )
    util_second = lax.dynamic_slice_in_dim(
        jnp.take(cost_second, my_actions, axis=0), start_second, rows_second, 1
    )
    util_third = jnp.take(cost_third, my_actions, axis=0)
    util_fourth = jnp.take(cost_fourth, my_actions, axis=0)
    utility = (
        util_first[:, :, None, None, None]
        + util_second[:, None, :, None, None]
        + util_third[:, None, None, :, None]
        + util_fourth[:, None, None, None, :]
    )
    scores = utility + DISCOUNT * expected
    local_max = jnp.max(scores, axis=0)
    local_sum = jnp.sum(jnp.exp(scores - local_max), axis=0)
    log_total = merged(local_max + jnp.log(local_sum), "act", jnp.logaddexp)
    choice_prob = jnp.exp(scores - log_total).astype(jnp.bfloat16)
    return (log_total, choice_prob)


def halves(x):
    high = x.astype(BF16)
    return high, (x - high.astype(F32)).astype(BF16)


def dot32(a, b):
    return jnp.dot(a, b, preferred_element_type=F32, precision=HIGHEST)


def banded(weights, offset, length, taps):
    half_band = (taps - 1) // 2
    width = weights.shape[1]
    normed = weights / jnp.sum(weights, axis=1, keepdims=True)
    rows = jnp.broadcast_to(normed, (length, width))
    rows = pltpu.roll(rows, lax.rem(offset + (width - half_band), width), 1)
    rows = pltpu.roll(rows, 0, 1, stride=1, stride_axis=0)
    lane = lax.broadcasted_iota(jnp.int32, (length, width), 1)
    under = lane >= width - 2 * half_band
    over = (lane >= length) & (lane < length + 2 * half_band)
    under_sum = jnp.sum(jnp.where(under, rows, 0.0), axis=1, keepdims=True)
    over_sum = jnp.sum(jnp.where(over, rows, 0.0), axis=1, keepdims=True)
    span = -(-length // LANES) * LANES
    kept = lane[:, :span]
    body = jnp.where(kept < length, rows[:, :span], 0.0)
    body = body + jnp.where(kept == 0, under_sum, 0.0)
    return body + jnp.where(kept == length - 1, over_sum, 0.0)


def prepare_kernel(
    lengths, taps, sizes, rows0, rows1, place, order, offs, weights, third, fourth,
    kron_hi, kron_lo, left2, right3, util23, wide0, wide1,
):
    n_act, n_narrow, n_outer = sizes
    len0, len1, len2, len3 = lengths
    act, narrow, outer, core = (place[i] for i in range(4))
    actions = offs.shape[0]
    per_group = actions // n_act
    columns = len0 * len1

    def wrapped(index, size):
        return lax.rem(index + size, size)

    lane = lax.broadcasted_iota(jnp.int32, (1, columns), 1)
    ids0 = jnp.zeros((1, columns), jnp.int32)
    ids1 = jnp.zeros((1, columns), jnp.int32)
    for block in range(columns // rows1):
        ahead, rest = divmod(block, n_outer * 2 * rows0)
        behind, rest = divmod(rest, 2 * rows0)
        part, row = divmod(rest, rows0)
        start = block * rows1
        inside = (lane >= start) & (lane < start + rows1)
        from_outer = outer ^ behind
        first = (from_outer * 2 + wrapped(core + part, 2)) * rows0 + row
        second = wrapped(narrow - ahead, n_narrow) * rows1 - start
        ids0 = jnp.where(inside, first, ids0)
        ids1 = jnp.where(inside, second + lane, ids1)
    spread0 = (lax.broadcasted_iota(jnp.int32, (LANES, columns), 0) == ids0).astype(F32)
    spread1 = (lax.broadcasted_iota(jnp.int32, (LANES, columns), 0) == ids1).astype(F32)

    quarter = len2 // (2 * n_act)
    lane2 = lax.broadcasted_iota(jnp.int32, (1, len2), 1)
    ids2 = jnp.zeros((1, len2), jnp.int32)
    for kind in range(2 * n_act):
        part = 2 * wrapped(act + kind // 2, n_act) + wrapped(core + kind % 2, 2)
        inside = (lane2 >= kind * quarter) & (lane2 < (kind + 1) * quarter)
        ids2 = jnp.where(inside, (part - kind) * quarter + lane2, ids2)
    order2 = (lax.broadcasted_iota(jnp.int32, (len2, len2), 0) == ids2).astype(F32)

    for action in range(actions):
        group, slot = divmod(action, per_group)
        which = order[wrapped(act + group, n_act) * per_group + slot]
        rows = weights[which]
        mats = [
            banded(rows[axis : axis + 1, :], offs[which, axis], lengths[axis], taps)
            for axis in range(4)
        ]
        wide0[...] = dot32(mats[0], spread0)
        wide1[...] = dot32(mats[1], spread1)
        second = wide1[pl.ds(pl.multiple_of(narrow * rows1, SUBLANES), rows1), :]
        for part in range(2):
            base = (outer * 2 + wrapped(core + part, 2)) * rows0
            blocks = [wide0[pl.ds(base + row, 1), :] * second for row in range(rows0)]
            start = ((group * 2 + part) * per_group + slot) * rows0 * rows1
            high, low = halves(jnp.concatenate(blocks, axis=0))
            kron_hi[start : start + rows0 * rows1, :] = high
            kron_lo[start : start + rows0 * rows1, :] = low
        high, low = halves(mats[3].T)
        row_pair = jnp.concatenate([high, low], axis=1)
        right3[action] = jnp.concatenate([row_pair, row_pair], axis=0)
        if group == 0:
            high, low = halves(dot32(mats[2], order2))
            left2[slot] = jnp.concatenate(
                [jnp.concatenate([high, high], axis=1), jnp.concatenate([low, low], axis=1)], axis=0
            )
            column = jnp.broadcast_to(third[pl.ds(which, 1), :], (len3, len2)).T
            util23[slot] = column + fourth[pl.ds(which, 1), :]


def short_dims_kernel(n_pieces, groups, kron_hi, kron_lo, right3, *refs):
    pieces, outs = refs[:n_pieces], refs[n_pieces:]
    rows = pieces[0].shape[1]
    depth = pieces[0].shape[2]
    actions = right3.shape[0]
    per_group = actions // groups
    per_out = outs[0].shape[1]
    q_hi, q_lo = kron_hi[...], kron_lo[...]
    mixed = []
    for row in range(0, rows, 2):
        cols = [
            jnp.concatenate([piece[:, row + extra, :] for piece in pieces], axis=0)
            for extra in range(2)
        ]
        x_hi, x_lo = halves(jnp.concatenate(cols, axis=1))
        out = (
            jnp.dot(q_hi, x_hi, preferred_element_type=F32)
            + jnp.dot(q_hi, x_lo, preferred_element_type=F32)
            + jnp.dot(q_lo, x_hi, preferred_element_type=F32)
        )
        mixed += [out[:, :depth], out[:, depth:]]
    for action in range(actions):
        group, slot = divmod(action, per_group)
        blocks = []
        for part in range(2):
            start = ((group * 2 + part) * per_group + slot) * per_out
            blocks += [mixed[row][start : start + per_out] for row in range(rows)]
        t_hi, t_lo = halves(jnp.concatenate(blocks, axis=0))
        both = jnp.dot(
            jnp.concatenate([t_hi, t_lo], axis=1), right3[action], preferred_element_type=F32
        )
        done = both[:, :depth] + both[:, depth:]
        for part in range(2):
            for row in range(rows):
                start = (part * rows + row) * per_out
                outs[group * 2 + part][slot, :, row, :] = done[start : start + per_out]


def third_dim_kernel(n_pieces, rows0, place, order, costs0, costs1, left2, util23, *refs):
    pieces, scores, local = refs[:n_pieces], refs[n_pieces], refs[n_pieces + 1]
    per_group, rows1 = pieces[0].shape[0], pieces[0].shape[1]
    length = util23.shape[1]
    depth = util23.shape[2]
    which = [order[place[0] * per_group + slot] for slot in range(per_group)]
    first = (place[2] * 2 + place[3]) * rows0 + pl.program_id(0)
    start1 = place[1] * rows1
    for second in range(0, rows1, 2):
        for slot in range(per_group):
            cols = [
                jnp.concatenate([piece[slot, second + extra] for piece in pieces], axis=0)
                for extra in range(2)
            ]
            g_hi, g_lo = halves(jnp.concatenate(cols, axis=1))
            both = jnp.dot(
                left2[slot], jnp.concatenate([g_hi, g_lo], axis=0), preferred_element_type=F32
            )
            expected = both[:length] + both[length:]
            for extra in range(2):
                flat = costs0[which[slot], first] + costs1[which[slot], start1 + second + extra]
                scores[slot, 0, second + extra] = (util23[slot] + flat) + DISCOUNT * expected[
                    :, extra * depth : (extra + 1) * depth
                ]
        for extra in range(2):
            found = [scores[slot, 0, second + extra] for slot in range(per_group)]
            top = functools.reduce(jnp.maximum, found)
            total = functools.reduce(jnp.add, [jnp.exp(one - top) for one in found])
            local[0, second + extra] = top + jnp.log(total)


def choice_kernel(scores, mine, other, new_value, choice_prob):
    a, b = mine[...], other[...]
    top, low = jnp.maximum(a, b), jnp.minimum(a, b)
    total = top + jnp.log(1.0 + jnp.exp(low - top))
    new_value[...] = total
    for slot in range(scores.shape[0]):
        choice_prob[slot] = jnp.exp(scores[slot] - total).astype(choice_prob.dtype)


def after(value, *done):
    return lax.optimization_barrier((value, *done))[0]


def whole_block():
    return pl.BlockSpec(memory_space=pltpu.VMEM)


def params(mebibytes):
    return pltpu.CompilerParams(vmem_limit_bytes=mebibytes * MIB)


def gather_body(
    value_now,
    cost_first,
    cost_second,
    cost_third,
    cost_fourth,
    trans_weights,
    trans_offsets,
    action_order,
):
    n_act, n_narrow, n_wide = (lax.axis_size(name) for name in ("act", "narrow", "wide"))
    n_outer = n_wide // 2
    act, narrow, wide = (lax.axis_index(name) for name in ("act", "narrow", "wide"))
    outer, core = wide // 2, wide % 2
    actions, _, taps = trans_weights.shape
    per_group = actions // n_act
    rows0, rows1, len2, len3 = value_now.shape
    len0, len1 = rows0 * n_wide, rows1 * n_narrow
    lengths = (len0, len1, len2, len3)
    quarter = len2 // (2 * n_act)
    chunk = CHUNK_ROWS
    n_chunks = quarter // chunk

    core_flip = [(i, i ^ 1) for i in range(n_wide)]
    own_part = 2 * act + core
    mine = lax.dynamic_slice_in_dim(value_now, own_part * quarter, quarter, 2)
    handed = lax.dynamic_slice_in_dim(value_now, (own_part + 1 - 2 * core) * quarter, quarter, 2)
    taken = lax.ppermute(handed, "wide", core_flip)
    block = jnp.concatenate([mine, taken], axis=0)
    block = block.reshape(2 * rows0, rows1, n_chunks, chunk, len3)

    half_band = (taps - 1) // 2
    width = -(-(max(lengths) + 4 * half_band) // LANES) * LANES
    weights = jnp.pad(trans_weights, ((0, 0), (0, 0), (0, width - taps)))
    place = jnp.stack([act, narrow, outer, core]).astype(jnp.int32)
    smem = pl.BlockSpec(memory_space=pltpu.SMEM)
    q_rows = actions * 2 * rows0 * rows1
    kron_hi, kron_lo, left2, right3, util23 = pl.pallas_call(
        functools.partial(prepare_kernel, lengths, taps, (n_act, n_narrow, n_outer), rows0, rows1),
        out_shape=(
            jax.ShapeDtypeStruct((q_rows, len0 * len1), BF16),
            jax.ShapeDtypeStruct((q_rows, len0 * len1), BF16),
            jax.ShapeDtypeStruct((per_group, 2 * len2, 2 * len2), BF16),
            jax.ShapeDtypeStruct((actions, 2 * len3, 2 * len3), BF16),
            jax.ShapeDtypeStruct((per_group, len2, len3), F32),
        ),
        in_specs=[smem] * 3 + [whole_block()] * 3,
        out_specs=(whole_block(),) * 5,
        scratch_shapes=[pltpu.VMEM((len0, len0 * len1), F32), pltpu.VMEM((len1, len0 * len1), F32)],
        compiler_params=params(16),
        cost_estimate=pl.CostEstimate(flops=10**9, bytes_accessed=4 * 10**6, transcendentals=0),
        name="prepare",
    )(place, action_order, trans_offsets, weights, cost_third, cost_fourth)

    act_flip = [(i, (i + 1) % n_act) for i in range(n_act)]
    cross = [
        (w * n_act + a, (w ^ 1) * n_act + (a + 1) % n_act) for w in range(n_wide) for a in range(n_act)
    ]
    per_out = rows0 * rows1
    out_piece = jax.ShapeDtypeStruct((per_group, per_out, chunk, len3), F32)
    def across(bit):
        return [(i, i ^ (2 * bit)) for i in range(n_wide)]

    bits = [1 << bit for bit in range(n_outer.bit_length() - 1)]
    chunks = [block[:, :, index] for index in range(n_chunks)]
    held = [chunks[0]] + [lax.ppermute(chunks[0], "wide", across(far)) for far in range(1, n_outer)]
    held = [jnp.concatenate(held, axis=0)]
    pairs = [None] * n_chunks
    early = jnp.stack(chunks[1:2])
    late = after(jnp.stack(chunks[2:]), held[0])
    for first, group in ((1, early), (2, late)):
        near = lax.ppermute(group, "wide", across(1))
        for index in range(group.shape[0]):
            pairs[first + index] = jnp.concatenate([group[index], near[index]], axis=0)
    pieces, gathered = [], [[], [], [], []]
    for index in range(n_chunks):
        if index:
            grown = after(pairs[index], held[index - 1], *(pieces[index - 2] if index > 1 else ()))
            for bit in bits[1:]:
                grown = jnp.concatenate([grown, lax.ppermute(grown, "wide", across(bit))], axis=0)
            held.append(grown)
        if index > 1:
            held[index] = after(held[index], *(kind_parts[index - 2] for kind_parts in gathered))
        pieces.append([held[index]])
        for step in range(1, n_narrow):
            hops = [(i, (i + step) % n_narrow) for i in range(n_narrow)]
            pieces[index].append(lax.ppermute(held[index], "narrow", hops))
        operands = [one.reshape(len0 * rows1, chunk, len3) for one in pieces[index]]
        keep, for_core, for_act, for_cross = pl.pallas_call(
            functools.partial(short_dims_kernel, len(operands), n_act),
            out_shape=(out_piece,) * 4,
            in_specs=[whole_block()] * (3 + len(operands)),
            out_specs=(whole_block(),) * 4,
            compiler_params=params(12),
            cost_estimate=pl.CostEstimate(flops=10**9, bytes_accessed=3 * 10**6, transcendentals=0),
            name="short_dims",
        )(kron_hi, kron_lo, right3, *operands)
        gathered[0].append(keep)
        gathered[1].append(lax.ppermute(for_core, "wide", core_flip))
        gathered[2].append(lax.ppermute(for_act, "act", act_flip))
        gathered[3].append(lax.ppermute(for_cross, ("wide", "act"), cross))
    parts = [one for kind_parts in gathered for one in kind_parts]

    scores_shape = (per_group, rows0, rows1, len2, len3)
    score_spec = pl.BlockSpec((per_group, 1, rows1, len2, len3), lambda i: (0, i, 0, 0, 0))
    state_spec = pl.BlockSpec((1, rows1, len2, len3), lambda i: (i, 0, 0, 0))
    scores, local = pl.pallas_call(
        functools.partial(third_dim_kernel, len(parts), rows0),
        grid=(rows0,),
        out_shape=(
            jax.ShapeDtypeStruct(scores_shape, F32),
            jax.ShapeDtypeStruct(value_now.shape, F32),
        ),
        in_specs=[smem] * 4 + [whole_block()] * 2
        + [pl.BlockSpec((per_group, rows1, chunk, len3), lambda i: (0, i, 0, 0))] * len(parts),
        out_specs=(score_spec, state_spec),
        compiler_params=params(20),
        cost_estimate=pl.CostEstimate(flops=2 * 10**9, bytes_accessed=10**7, transcendentals=10**6),
        name="third_dim",
    )(place, action_order, cost_first, cost_second, left2, util23, *parts)

    other = lax.ppermute(local, "act", act_flip)
    return tuple(
        pl.pallas_call(
            choice_kernel,
            grid=(rows0,),
            out_shape=(
                jax.ShapeDtypeStruct(value_now.shape, F32),
                jax.ShapeDtypeStruct(scores_shape, BF16),
            ),
            in_specs=[score_spec, state_spec, state_spec],
            out_specs=(state_spec, score_spec),
            compiler_params=params(16),
            cost_estimate=pl.CostEstimate(flops=10**7, bytes_accessed=10**7, transcendentals=10**6),
            name="choice",
        )(scores, local, other)
    )


def gather_fits(mesh, value_shape, actions, offset_reach):
    n_wide, n_narrow, n_act = (mesh.shape[name] for name in ("wide", "narrow", "act"))
    len0, len1, len2, len3 = value_shape
    if n_act != 2 or n_wide < 4 or n_wide & (n_wide - 1) or actions % n_act:
        return False
    if len2 % (2 * n_act * CHUNK_ROWS) or len2 < 6 * n_act * CHUNK_ROWS or len2 % LANES or len3 != LANES or len2 != LANES:
        return False
    if (len1 // n_narrow) % SUBLANES or len0 * len1 // (n_wide * n_narrow) % 16 or len0 % n_wide:
        return False
    if max(len0, len1) > LANES or len1 % n_narrow:
        return False
    raw = len0 * len1 * len2 * len3 // (2 * n_act)
    exchanged = 2 * (actions // n_act) * len0 * len1 * len2 * len3 // (n_wide * n_narrow)
    return raw <= exchanged


def solution(mesh):
    def run(value_now, *rest):
        actions = rest[-1].shape[0]
        small = gather_fits(mesh, value_now.shape, actions, rest[4].shape[-1])
        return jax.shard_map(
            gather_body if small else exchange_body,
            mesh=mesh,
            in_specs=(P("wide", "narrow", None, None), P(), P(), P(), P(), P(), P(), P()),
            out_specs=(P("wide", "narrow", None, None), P("act", "wide", "narrow", None, None)),
            check_vma=False,
        )(value_now, *rest)

    return run
```

```python
import functools

import jax
import jax.numpy as jnp
from jax import lax
from jax.experimental import pallas as pl
from jax.experimental.pallas import tpu as pltpu
from jax.sharding import PartitionSpec as P

DISCOUNT = 0.95
HIGHEST = lax.Precision.HIGHEST
F32 = jnp.float32
BF16 = jnp.bfloat16
LANES = 128
SUBLANES = 8
CHUNK_ROWS = 16
MIB = 1024 * 1024


def merged(value, axis, join):
    pieces = lax.all_gather(value, axis)
    head = pieces[0]
    tail = pieces[1:]
    subtotal, _ = lax.scan(lambda subtotal, slab: (join(subtotal, slab), None), head, tail)
    return subtotal


def transition(weights, offset, length):
    band_len = weights.shape[0]
    half_band = (band_len - 1) // 2
    normed = weights / jnp.sum(weights)
    row_ids = jnp.arange(length, dtype=jnp.int32)
    tap_ids = jnp.arange(band_len, dtype=jnp.int32)
    target = jnp.clip(row_ids[:, None] + offset + tap_ids[None, :] - half_band, 0, length - 1)
    matched = (target[:, :, None] == row_ids[None, None, :]).astype(normed.dtype)
    return jnp.einsum("ijk,j->ik", matched, normed, precision=HIGHEST)


def exchange_body(
    value_now,
    cost_first,
    cost_second,
    cost_third,
    cost_fourth,
    trans_weights,
    trans_offsets,
    action_order,
):
    size_act = lax.axis_size("act")
    per_group = action_order.shape[0] // size_act
    group_id = lax.axis_index("act")
    my_actions = lax.dynamic_slice_in_dim(action_order, group_id * per_group, per_group)
    rows_first, rows_second, len_third, len_fourth = value_now.shape
    len_first = rows_first * lax.axis_size("wide")
    len_second = rows_second * lax.axis_size("narrow")
    my_weights = jnp.take(trans_weights, my_actions, axis=0)
    my_offsets = jnp.take(trans_offsets, my_actions, axis=0)

    def build(axis_id, length):
        return jax.vmap(lambda weight_row, offset_one: transition(weight_row, offset_one, length))(
            my_weights[:, axis_id], my_offsets[:, axis_id]
        )

    mat_first = build(0, len_first)
    mat_second = build(1, len_second)
    mat_third = build(2, len_third)
    mat_fourth = build(3, len_fourth)
    spread = lax.all_to_all(value_now, "narrow", split_axis=2, concat_axis=1, tiled=True)
    field = jnp.einsum("gij,ajcd->gaicd", mat_second, spread, precision=HIGHEST)
    field = jnp.einsum("gij,gabcj->gabci", mat_fourth, field, precision=HIGHEST)
    field = lax.all_to_all(field, "narrow", split_axis=2, concat_axis=3, tiled=True)
    field = lax.all_to_all(field, "wide", split_axis=3, concat_axis=1, tiled=True)
    field = jnp.einsum("gij,gjbcd->gibcd", mat_first, field, precision=HIGHEST)
    field = lax.all_to_all(field, "wide", split_axis=1, concat_axis=3, tiled=True)
    expected = jnp.einsum("gij,gabjd->gabid", mat_third, field, precision=HIGHEST)
    start_first = lax.axis_index("wide") * rows_first
    start_second = lax.axis_index("narrow") * rows_second
    util_first = lax.dynamic_slice_in_dim(
        jnp.take(cost_first, my_actions, axis=0), start_first, rows_first, 1
    )
    util_second = lax.dynamic_slice_in_dim(
        jnp.take(cost_second, my_actions, axis=0), start_second, rows_second, 1
    )
    util_third = jnp.take(cost_third, my_actions, axis=0)
    util_fourth = jnp.take(cost_fourth, my_actions, axis=0)
    utility = (
        util_first[:, :, None, None, None]
        + util_second[:, None, :, None, None]
        + util_third[:, None, None, :, None]
        + util_fourth[:, None, None, None, :]
    )
    scores = utility + DISCOUNT * expected
    local_max = jnp.max(scores, axis=0)
    local_sum = jnp.sum(jnp.exp(scores - local_max), axis=0)
    log_total = merged(local_max + jnp.log(local_sum), "act", jnp.logaddexp)
    choice_prob = jnp.exp(scores - log_total).astype(jnp.bfloat16)
    return (log_total, choice_prob)


def halves(x):
    high = x.astype(BF16)
    return high, (x - high.astype(F32)).astype(BF16)


def dot32(a, b):
    return jnp.dot(a, b, preferred_element_type=F32, precision=HIGHEST)


def banded(weights, offset, length, taps):
    half_band = (taps - 1) // 2
    width = weights.shape[1]
    normed = weights / jnp.sum(weights, axis=1, keepdims=True)
    rows = jnp.broadcast_to(normed, (length, width))
    rows = pltpu.roll(rows, lax.rem(offset + (width - half_band), width), 1)
    rows = pltpu.roll(rows, 0, 1, stride=1, stride_axis=0)
    lane = lax.broadcasted_iota(jnp.int32, (length, width), 1)
    under = lane >= width - 2 * half_band
    over = (lane >= length) & (lane < length + 2 * half_band)
    under_sum = jnp.sum(jnp.where(under, rows, 0.0), axis=1, keepdims=True)
    over_sum = jnp.sum(jnp.where(over, rows, 0.0), axis=1, keepdims=True)
    span = -(-length // LANES) * LANES
    kept = lane[:, :span]
    body = jnp.where(kept < length, rows[:, :span], 0.0)
    body = body + jnp.where(kept == 0, under_sum, 0.0)
    return body + jnp.where(kept == length - 1, over_sum, 0.0)


def prepare_kernel(
    lengths, taps, sizes, rows0, rows1, arrivals, place, order, offs, weights, third, fourth,
    kron_hi, kron_lo, left2, right3, util23, wide0, wide1,
):
    n_act, n_narrow, n_outer = sizes
    len0, len1, len2, len3 = lengths
    act, narrow, outer, core = (place[i] for i in range(4))
    actions = offs.shape[0]
    per_group = actions // n_act
    columns = len0 * len1

    def wrapped(index, size):
        return lax.rem(index + size, size)

    lane = lax.broadcasted_iota(jnp.int32, (1, columns), 1)
    ids0 = jnp.zeros((1, columns), jnp.int32)
    ids1 = jnp.zeros((1, columns), jnp.int32)
    for block, (far, part, ahead) in enumerate(arrivals):
        from_outer, from_core = outer ^ far, wrapped(core + part, 2)
        for row in range(rows0):
            start = (block * rows0 + row) * rows1
            inside = (lane >= start) & (lane < start + rows1)
            first = (from_outer * 2 + from_core) * rows0 + row
            second = wrapped(narrow - ahead, n_narrow) * rows1 - start
            ids0 = jnp.where(inside, first, ids0)
            ids1 = jnp.where(inside, second + lane, ids1)
    spread0 = (lax.broadcasted_iota(jnp.int32, (LANES, columns), 0) == ids0).astype(F32)
    spread1 = (lax.broadcasted_iota(jnp.int32, (LANES, columns), 0) == ids1).astype(F32)

    share = len2 // n_act
    lane2 = lax.broadcasted_iota(jnp.int32, (1, len2), 1)
    ids2 = jnp.zeros((1, len2), jnp.int32)
    for group in range(n_act):
        inside = (lane2 >= group * share) & (lane2 < (group + 1) * share)
        ids2 = jnp.where(inside, (wrapped(act + group, n_act) - group) * share + lane2, ids2)
    order2 = (lax.broadcasted_iota(jnp.int32, (len2, len2), 0) == ids2).astype(F32)

    for action in range(actions):
        group, slot = divmod(action, per_group)
        which = order[wrapped(act + group, n_act) * per_group + slot]
        rows = weights[which]
        mats = [
            banded(rows[axis : axis + 1, :], offs[which, axis], lengths[axis], taps)
            for axis in range(4)
        ]
        wide0[...] = dot32(mats[0], spread0)
        wide1[...] = dot32(mats[1], spread1)
        second = wide1[pl.ds(pl.multiple_of(narrow * rows1, SUBLANES), rows1), :]
        base = (outer * 2 + core) * rows0
        blocks = [wide0[pl.ds(base + row, 1), :] * second for row in range(rows0)]
        start = action * rows0 * rows1
        high, low = halves(jnp.concatenate(blocks, axis=0))
        kron_hi[start : start + rows0 * rows1, :] = high
        kron_lo[start : start + rows0 * rows1, :] = low
        high, low = halves(mats[3].T)
        row_pair = jnp.concatenate([high, low], axis=1)
        right3[action] = jnp.concatenate([row_pair, row_pair], axis=0)
        if group == 0:
            high, low = halves(dot32(mats[2], order2))
            left2[slot] = jnp.concatenate(
                [jnp.concatenate([high, high], axis=1), jnp.concatenate([low, low], axis=1)], axis=0
            )
            column = jnp.broadcast_to(third[pl.ds(which, 1), :], (len3, len2)).T
            util23[slot] = column + fourth[pl.ds(which, 1), :]


def short_dims_kernel(starts, groups, kron_hi, kron_lo, right3, *refs):
    pieces, outs = refs[: len(starts)], refs[len(starts) :]
    rows, depth = outs[0].shape[2:]
    actions = right3.shape[0]
    per_group = actions // groups
    per_out = outs[0].shape[1]
    q_hi, q_lo = kron_hi[...], kron_lo[...]
    mixed = []
    for row in range(0, rows, 2):
        cols = [
            jnp.concatenate(
                [piece[:, start + row + extra, :] for start, piece in zip(starts, pieces)], axis=0
            )
            for extra in range(2)
        ]
        x_hi, x_lo = halves(jnp.concatenate(cols, axis=1))
        out = (
            jnp.dot(q_hi, x_hi, preferred_element_type=F32)
            + jnp.dot(q_hi, x_lo, preferred_element_type=F32)
            + jnp.dot(q_lo, x_hi, preferred_element_type=F32)
        )
        mixed += [out[:, :depth], out[:, depth:]]
    for action in range(actions):
        group, slot = divmod(action, per_group)
        start = action * per_out
        block = jnp.concatenate([one[start : start + per_out] for one in mixed], axis=0)
        t_hi, t_lo = halves(block)
        both = jnp.dot(
            jnp.concatenate([t_hi, t_lo], axis=1), right3[action], preferred_element_type=F32
        )
        done = both[:, :depth] + both[:, depth:]
        for row in range(rows):
            outs[group][slot, :, row, :] = done[row * per_out : (row + 1) * per_out]


def third_dim_kernel(n_pieces, rows0, place, order, costs0, costs1, left2, util23, *refs):
    pieces, scores, local = refs[:n_pieces], refs[n_pieces], refs[n_pieces + 1]
    per_group, rows1 = pieces[0].shape[0], pieces[0].shape[1]
    length = util23.shape[1]
    depth = util23.shape[2]
    which = [order[place[0] * per_group + slot] for slot in range(per_group)]
    first = (place[2] * 2 + place[3]) * rows0 + pl.program_id(0)
    start1 = place[1] * rows1
    for second in range(0, rows1, 2):
        for slot in range(per_group):
            cols = [
                jnp.concatenate([piece[slot, second + extra] for piece in pieces], axis=0)
                for extra in range(2)
            ]
            g_hi, g_lo = halves(jnp.concatenate(cols, axis=1))
            both = jnp.dot(
                left2[slot], jnp.concatenate([g_hi, g_lo], axis=0), preferred_element_type=F32
            )
            expected = both[:length] + both[length:]
            for extra in range(2):
                flat = costs0[which[slot], first] + costs1[which[slot], start1 + second + extra]
                scores[slot, 0, second + extra] = (util23[slot] + flat) + DISCOUNT * expected[
                    :, extra * depth : (extra + 1) * depth
                ]
        for extra in range(2):
            found = [scores[slot, 0, second + extra] for slot in range(per_group)]
            top = functools.reduce(jnp.maximum, found)
            total = functools.reduce(jnp.add, [jnp.exp(one - top) for one in found])
            local[0, second + extra] = top + jnp.log(total)


def choice_kernel(scores, mine, other, new_value, choice_prob):
    a, b = mine[...], other[...]
    top, low = jnp.maximum(a, b), jnp.minimum(a, b)
    total = top + jnp.log(1.0 + jnp.exp(low - top))
    new_value[...] = total
    for slot in range(scores.shape[0]):
        choice_prob[slot] = jnp.exp(scores[slot] - total).astype(choice_prob.dtype)


def after(value, *done):
    return lax.optimization_barrier((value, *done))[0]


def whole_block():
    return pl.BlockSpec(memory_space=pltpu.VMEM)


def params(mebibytes):
    return pltpu.CompilerParams(vmem_limit_bytes=mebibytes * MIB)


def gather_body(
    value_now,
    cost_first,
    cost_second,
    cost_third,
    cost_fourth,
    trans_weights,
    trans_offsets,
    action_order,
):
    n_act, n_narrow, n_wide = (lax.axis_size(name) for name in ("act", "narrow", "wide"))
    n_outer = n_wide // 2
    act, narrow, wide = (lax.axis_index(name) for name in ("act", "narrow", "wide"))
    outer, core = wide // 2, wide % 2
    actions, _, taps = trans_weights.shape
    per_group = actions // n_act
    rows0, rows1, len2, len3 = value_now.shape
    len0, len1 = rows0 * n_wide, rows1 * n_narrow
    lengths = (len0, len1, len2, len3)
    share = len2 // n_act
    chunk = CHUNK_ROWS
    n_chunks = share // chunk
    core_flip = [(i, i ^ 1) for i in range(n_wide)]
    act_flip = [(i, (i + 1) % n_act) for i in range(n_act)]
    narrow_hops = [
        [(i, (i + step) % n_narrow) for i in range(n_narrow)] for step in range(1, n_narrow)
    ]

    def across(bit):
        return [(i, i ^ (2 * bit)) for i in range(n_wide)]

    def part(index):
        return lax.dynamic_slice_in_dim(value_now, act * share + index * chunk, chunk, 2)

    near = [(0, other, ahead) for ahead in range(n_narrow) for other in range(2)]
    arrivals = near + [
        (far, other, ahead)
        for ahead in range(n_narrow)
        for other in range(2)
        for far in range(1, n_outer)
    ]

    half_band = (taps - 1) // 2
    width = -(-(max(lengths) + 4 * half_band) // LANES) * LANES
    weights = jnp.pad(trans_weights, ((0, 0), (0, 0), (0, width - taps)))
    place = jnp.stack([act, narrow, outer, core]).astype(jnp.int32)
    smem = pl.BlockSpec(memory_space=pltpu.SMEM)
    q_rows = actions * rows0 * rows1
    kron_hi, kron_lo, left2, right3, util23 = pl.pallas_call(
        functools.partial(
            prepare_kernel, lengths, taps, (n_act, n_narrow, n_outer), rows0, rows1, arrivals
        ),
        out_shape=(
            jax.ShapeDtypeStruct((q_rows, len0 * len1), BF16),
            jax.ShapeDtypeStruct((q_rows, len0 * len1), BF16),
            jax.ShapeDtypeStruct((per_group, 2 * len2, 2 * len2), BF16),
            jax.ShapeDtypeStruct((actions, 2 * len3, 2 * len3), BF16),
            jax.ShapeDtypeStruct((per_group, len2, len3), F32),
        ),
        in_specs=[smem] * 3 + [whole_block()] * 3,
        out_specs=(whole_block(),) * 5,
        scratch_shapes=[pltpu.VMEM((len0, len0 * len1), F32), pltpu.VMEM((len1, len0 * len1), F32)],
        compiler_params=params(16),
        cost_estimate=pl.CostEstimate(flops=10**9, bytes_accessed=4 * 10**6, transcendentals=0),
        name="prepare",
    )(place, action_order, trans_offsets, weights, cost_third, cost_fourth)

    chunks = [part(index) for index in range(n_chunks)]
    half = lax.dynamic_slice_in_dim(value_now, act * share, share, 2)
    direct = [lax.ppermute(chunks[0], "wide", across(far)) for far in range(1, n_outer)]
    around = [lax.ppermute(half, "narrow", hops) for hops in narrow_hops]
    second = lax.ppermute(chunks[1], "wide", across(1))
    direct, around, second, *_ = lax.optimization_barrier((direct, around, second, kron_hi, right3))

    out_piece = jax.ShapeDtypeStruct((per_group, rows0 * rows1, chunk, len3), F32)
    bits = [1 << bit for bit in range(1, n_outer.bit_length() - 1)]
    twins = [None, second]
    fars = [jnp.concatenate(direct, axis=0)]
    nears = []
    kept, sent = [], []
    def doubled(index):
        grown = jnp.concatenate([chunks[index], twins[index]], axis=0)
        grown = after(grown, fars[index - 1], *kept[: index - 1])
        parts = [twins[index]]
        for bit in bits:
            parts.append(lax.ppermute(grown, "wide", across(bit)))
            if bit != bits[-1]:
                grown = jnp.concatenate([grown, parts[-1]], axis=0)
        return jnp.concatenate(parts, axis=0)

    for index in range(n_chunks):
        far = fars[index]
        if index == 1:
            far = after(far, *twins[2:])
        if index > 1:
            far = after(far, sent[index - 2], kept[index - 1] if index == 2 else ())
        crossed = lax.ppermute(far, "wide", core_flip)
        if index == 0:
            chunks[1], half_late, late, *around_late = lax.optimization_barrier(
                (chunks[1], half, jnp.stack(chunks[2:]), *around, crossed)
            )[: 3 + len(around)]
            twins += list(lax.ppermute(late, "wide", across(1)))
            for one, source in zip([half] + around, [half_late] + around_late):
                nears += [one, lax.ppermute(source, "wide", core_flip)]
            nears = [one.reshape(rows0 * rows1, share, len3) for one in nears]
        moved = [lax.ppermute(far, "narrow", hops) for hops in narrow_hops]
        if index + 1 < n_chunks:
            fars.append(doubled(index + 1))
        if index > 1:
            moved = [after(one, kept[index - 1], fars[-1]) for one in moved]
        pieces = [far, crossed]
        for one in moved:
            pieces += [one, lax.ppermute(one, "wide", core_flip)]
        pieces = [one.reshape(-1, chunk, len3) for one in pieces]
        starts = [index * chunk] * len(nears) + [0] * len(pieces)
        keep, for_act = pl.pallas_call(
            functools.partial(short_dims_kernel, starts, n_act),
            out_shape=(out_piece,) * 2,
            in_specs=[whole_block()] * (3 + len(starts)),
            out_specs=(whole_block(),) * 2,
            compiler_params=params(12),
            cost_estimate=pl.CostEstimate(flops=10**9, bytes_accessed=3 * 10**6, transcendentals=0),
            name="short_dims",
        )(kron_hi, kron_lo, right3, *nears, *pieces)
        kept.append(keep)
        sent.append(lax.ppermute(for_act, "act", act_flip))
    parts = kept + sent

    scores_shape = (per_group, rows0, rows1, len2, len3)
    score_spec = pl.BlockSpec((per_group, 1, rows1, len2, len3), lambda i: (0, i, 0, 0, 0))
    state_spec = pl.BlockSpec((1, rows1, len2, len3), lambda i: (i, 0, 0, 0))
    scores, local = pl.pallas_call(
        functools.partial(third_dim_kernel, len(parts), rows0),
        grid=(rows0,),
        out_shape=(
            jax.ShapeDtypeStruct(scores_shape, F32),
            jax.ShapeDtypeStruct(value_now.shape, F32),
        ),
        in_specs=[smem] * 4 + [whole_block()] * 2
        + [pl.BlockSpec((per_group, rows1, chunk, len3), lambda i: (0, i, 0, 0))] * len(parts),
        out_specs=(score_spec, state_spec),
        compiler_params=params(20),
        cost_estimate=pl.CostEstimate(flops=2 * 10**9, bytes_accessed=10**7, transcendentals=10**6),
        name="third_dim",
    )(place, action_order, cost_first, cost_second, left2, util23, *parts)

    other = lax.ppermute(local, "act", act_flip)
    return tuple(
        pl.pallas_call(
            choice_kernel,
            grid=(rows0,),
            out_shape=(
                jax.ShapeDtypeStruct(value_now.shape, F32),
                jax.ShapeDtypeStruct(scores_shape, BF16),
            ),
            in_specs=[score_spec, state_spec, state_spec],
            out_specs=(state_spec, score_spec),
            compiler_params=params(16),
            cost_estimate=pl.CostEstimate(flops=10**7, bytes_accessed=10**7, transcendentals=10**6),
            name="choice",
        )(scores, local, other)
    )


def gather_fits(mesh, value_shape, actions, offset_reach):
    n_wide, n_narrow, n_act = (mesh.shape[name] for name in ("wide", "narrow", "act"))
    len0, len1, len2, len3 = value_shape
    if n_act != 2 or n_wide < 4 or n_wide & (n_wide - 1) or actions % n_act:
        return False
    if len2 % (n_act * CHUNK_ROWS) or len2 < 3 * n_act * CHUNK_ROWS:
        return False
    if len2 != LANES or len3 != LANES:
        return False
    if (len1 // n_narrow) % SUBLANES or len0 * len1 // (n_wide * n_narrow) % 16 or len0 % n_wide:
        return False
    if max(len0, len1) > LANES or len1 % n_narrow:
        return False
    raw = len0 * len1 * len2 * len3 // (2 * n_act)
    exchanged = 2 * (actions // n_act) * len0 * len1 * len2 * len3 // (n_wide * n_narrow)
    return raw <= exchanged


def solution(mesh):
    def run(value_now, *rest):
        actions = rest[-1].shape[0]
        small = gather_fits(mesh, value_now.shape, actions, rest[4].shape[-1])
        return jax.shard_map(
            gather_body if small else exchange_body,
            mesh=mesh,
            in_specs=(P("wide", "narrow", None, None), P(), P(), P(), P(), P(), P(), P()),
            out_specs=(P("wide", "narrow", None, None), P("act", "wide", "narrow", None, None)),
            check_vma=False,
        )(value_now, *rest)

    return run
```

```python
import functools

import jax
import jax.numpy as jnp
from jax import lax
from jax.experimental import pallas as pl
from jax.experimental.pallas import tpu as pltpu
from jax.sharding import PartitionSpec as P

DISCOUNT = 0.95
HIGHEST = lax.Precision.HIGHEST
F32 = jnp.float32
BF16 = jnp.bfloat16
LANES = 128
SUBLANES = 8
CHUNK_ROWS = 16
MIB = 1024 * 1024


def merged(value, axis, join):
    pieces = lax.all_gather(value, axis)
    head = pieces[0]
    tail = pieces[1:]
    subtotal, _ = lax.scan(lambda subtotal, slab: (join(subtotal, slab), None), head, tail)
    return subtotal


def transition(weights, offset, length):
    band_len = weights.shape[0]
    half_band = (band_len - 1) // 2
    normed = weights / jnp.sum(weights)
    row_ids = jnp.arange(length, dtype=jnp.int32)
    tap_ids = jnp.arange(band_len, dtype=jnp.int32)
    target = jnp.clip(row_ids[:, None] + offset + tap_ids[None, :] - half_band, 0, length - 1)
    matched = (target[:, :, None] == row_ids[None, None, :]).astype(normed.dtype)
    return jnp.einsum("ijk,j->ik", matched, normed, precision=HIGHEST)


def exchange_body(
    value_now,
    cost_first,
    cost_second,
    cost_third,
    cost_fourth,
    trans_weights,
    trans_offsets,
    action_order,
):
    size_act = lax.axis_size("act")
    per_group = action_order.shape[0] // size_act
    group_id = lax.axis_index("act")
    my_actions = lax.dynamic_slice_in_dim(action_order, group_id * per_group, per_group)
    rows_first, rows_second, len_third, len_fourth = value_now.shape
    len_first = rows_first * lax.axis_size("wide")
    len_second = rows_second * lax.axis_size("narrow")
    my_weights = jnp.take(trans_weights, my_actions, axis=0)
    my_offsets = jnp.take(trans_offsets, my_actions, axis=0)

    def build(axis_id, length):
        return jax.vmap(lambda weight_row, offset_one: transition(weight_row, offset_one, length))(
            my_weights[:, axis_id], my_offsets[:, axis_id]
        )

    mat_first = build(0, len_first)
    mat_second = build(1, len_second)
    mat_third = build(2, len_third)
    mat_fourth = build(3, len_fourth)
    spread = lax.all_to_all(value_now, "narrow", split_axis=2, concat_axis=1, tiled=True)
    field = jnp.einsum("gij,ajcd->gaicd", mat_second, spread, precision=HIGHEST)
    field = jnp.einsum("gij,gabcj->gabci", mat_fourth, field, precision=HIGHEST)
    field = lax.all_to_all(field, "narrow", split_axis=2, concat_axis=3, tiled=True)
    field = lax.all_to_all(field, "wide", split_axis=3, concat_axis=1, tiled=True)
    field = jnp.einsum("gij,gjbcd->gibcd", mat_first, field, precision=HIGHEST)
    field = lax.all_to_all(field, "wide", split_axis=1, concat_axis=3, tiled=True)
    expected = jnp.einsum("gij,gabjd->gabid", mat_third, field, precision=HIGHEST)
    start_first = lax.axis_index("wide") * rows_first
    start_second = lax.axis_index("narrow") * rows_second
    util_first = lax.dynamic_slice_in_dim(
        jnp.take(cost_first, my_actions, axis=0), start_first, rows_first, 1
    )
    util_second = lax.dynamic_slice_in_dim(
        jnp.take(cost_second, my_actions, axis=0), start_second, rows_second, 1
    )
    util_third = jnp.take(cost_third, my_actions, axis=0)
    util_fourth = jnp.take(cost_fourth, my_actions, axis=0)
    utility = (
        util_first[:, :, None, None, None]
        + util_second[:, None, :, None, None]
        + util_third[:, None, None, :, None]
        + util_fourth[:, None, None, None, :]
    )
    scores = utility + DISCOUNT * expected
    local_max = jnp.max(scores, axis=0)
    local_sum = jnp.sum(jnp.exp(scores - local_max), axis=0)
    log_total = merged(local_max + jnp.log(local_sum), "act", jnp.logaddexp)
    choice_prob = jnp.exp(scores - log_total).astype(jnp.bfloat16)
    return (log_total, choice_prob)


def halves(x):
    high = x.astype(BF16)
    return high, (x - high.astype(F32)).astype(BF16)


def dot32(a, b):
    return jnp.dot(a, b, preferred_element_type=F32, precision=HIGHEST)


def banded(weights, offset, length, taps):
    half_band = (taps - 1) // 2
    width = weights.shape[1]
    normed = weights / jnp.sum(weights, axis=1, keepdims=True)
    rows = jnp.broadcast_to(normed, (length, width))
    rows = pltpu.roll(rows, lax.rem(offset + (width - half_band), width), 1)
    rows = pltpu.roll(rows, 0, 1, stride=1, stride_axis=0)
    lane = lax.broadcasted_iota(jnp.int32, (length, width), 1)
    under = lane >= width - 2 * half_band
    over = (lane >= length) & (lane < length + 2 * half_band)
    under_sum = jnp.sum(jnp.where(under, rows, 0.0), axis=1, keepdims=True)
    over_sum = jnp.sum(jnp.where(over, rows, 0.0), axis=1, keepdims=True)
    span = -(-length // LANES) * LANES
    kept = lane[:, :span]
    body = jnp.where(kept < length, rows[:, :span], 0.0)
    body = body + jnp.where(kept == 0, under_sum, 0.0)
    return body + jnp.where(kept == length - 1, over_sum, 0.0)


def prepare_kernel(
    lengths, taps, sizes, rows0, rows1, arrivals, place, order, offs, weights, third, fourth,
    kron_hi, kron_lo, left2, right3, util23, wide0, wide1,
):
    n_act, n_narrow, n_outer = sizes
    len0, len1, len2, len3 = lengths
    act, narrow, outer, core = (place[i] for i in range(4))
    actions = offs.shape[0]
    per_group = actions // n_act
    columns = len0 * len1

    def wrapped(index, size):
        return lax.rem(index + size, size)

    lane = lax.broadcasted_iota(jnp.int32, (1, columns), 1)
    ids0 = jnp.zeros((1, columns), jnp.int32)
    ids1 = jnp.zeros((1, columns), jnp.int32)
    for block, (far, part, ahead) in enumerate(arrivals):
        from_outer, from_core = outer ^ far, wrapped(core + part, 2)
        for row in range(rows0):
            start = (block * rows0 + row) * rows1
            inside = (lane >= start) & (lane < start + rows1)
            first = (from_outer * 2 + from_core) * rows0 + row
            second = wrapped(narrow - ahead, n_narrow) * rows1 - start
            ids0 = jnp.where(inside, first, ids0)
            ids1 = jnp.where(inside, second + lane, ids1)
    spread0 = (lax.broadcasted_iota(jnp.int32, (LANES, columns), 0) == ids0).astype(F32)
    spread1 = (lax.broadcasted_iota(jnp.int32, (LANES, columns), 0) == ids1).astype(F32)

    share = len2 // n_act
    lane2 = lax.broadcasted_iota(jnp.int32, (1, len2), 1)
    ids2 = jnp.zeros((1, len2), jnp.int32)
    for group in range(n_act):
        inside = (lane2 >= group * share) & (lane2 < (group + 1) * share)
        ids2 = jnp.where(inside, (wrapped(act + group, n_act) - group) * share + lane2, ids2)
    order2 = (lax.broadcasted_iota(jnp.int32, (len2, len2), 0) == ids2).astype(F32)

    for action in range(actions):
        group, slot = divmod(action, per_group)
        which = order[wrapped(act + group, n_act) * per_group + slot]
        rows = weights[which]
        mats = [
            banded(rows[axis : axis + 1, :], offs[which, axis], lengths[axis], taps)
            for axis in range(4)
        ]
        wide0[...] = dot32(mats[0], spread0)
        wide1[...] = dot32(mats[1], spread1)
        second = wide1[pl.ds(pl.multiple_of(narrow * rows1, SUBLANES), rows1), :]
        base = (outer * 2 + core) * rows0
        blocks = [wide0[pl.ds(base + row, 1), :] * second for row in range(rows0)]
        start = action * rows0 * rows1
        high, low = halves(jnp.concatenate(blocks, axis=0))
        kron_hi[start : start + rows0 * rows1, :] = high
        kron_lo[start : start + rows0 * rows1, :] = low
        high, low = halves(mats[3].T)
        row_pair = jnp.concatenate([high, low], axis=1)
        right3[action] = jnp.concatenate([row_pair, row_pair], axis=0)
        if group == 0:
            high, low = halves(dot32(mats[2], order2))
            left2[slot] = jnp.concatenate(
                [jnp.concatenate([high, high], axis=1), jnp.concatenate([low, low], axis=1)], axis=0
            )
            column = jnp.broadcast_to(third[pl.ds(which, 1), :], (len3, len2)).T
            util23[slot] = column + fourth[pl.ds(which, 1), :]


def short_dims_kernel(starts, groups, kron_hi, kron_lo, right3, *refs):
    pieces, outs = refs[: len(starts)], refs[len(starts) :]
    rows, depth = outs[0].shape[2:]
    actions = right3.shape[0]
    per_group = actions // groups
    per_out = outs[0].shape[1]
    q_hi, q_lo = kron_hi[...], kron_lo[...]
    mixed = []
    for row in range(0, rows, 2):
        cols = [
            jnp.concatenate(
                [piece[:, start + row + extra, :] for start, piece in zip(starts, pieces)], axis=0
            )
            for extra in range(2)
        ]
        x_hi, x_lo = halves(jnp.concatenate(cols, axis=1))
        out = (
            jnp.dot(q_hi, x_hi, preferred_element_type=F32)
            + jnp.dot(q_hi, x_lo, preferred_element_type=F32)
            + jnp.dot(q_lo, x_hi, preferred_element_type=F32)
        )
        mixed += [out[:, :depth], out[:, depth:]]
    for action in range(actions):
        group, slot = divmod(action, per_group)
        start = action * per_out
        block = jnp.concatenate([one[start : start + per_out] for one in mixed], axis=0)
        t_hi, t_lo = halves(block)
        both = jnp.dot(
            jnp.concatenate([t_hi, t_lo], axis=1), right3[action], preferred_element_type=F32
        )
        done = both[:, :depth] + both[:, depth:]
        for row in range(rows):
            outs[group][slot, :, row, :] = done[row * per_out : (row + 1) * per_out]


def third_dim_kernel(n_pieces, rows0, place, order, costs0, costs1, left2, util23, *refs):
    pieces, scores, local = refs[:n_pieces], refs[n_pieces], refs[n_pieces + 1]
    per_group, rows1 = pieces[0].shape[0], pieces[0].shape[1]
    length = util23.shape[1]
    depth = util23.shape[2]
    which = [order[place[0] * per_group + slot] for slot in range(per_group)]
    first = (place[2] * 2 + place[3]) * rows0 + pl.program_id(0)
    start1 = place[1] * rows1
    for second in range(0, rows1, 2):
        for slot in range(per_group):
            cols = [
                jnp.concatenate([piece[slot, second + extra] for piece in pieces], axis=0)
                for extra in range(2)
            ]
            g_hi, g_lo = halves(jnp.concatenate(cols, axis=1))
            both = jnp.dot(
                left2[slot], jnp.concatenate([g_hi, g_lo], axis=0), preferred_element_type=F32
            )
            expected = both[:length] + both[length:]
            for extra in range(2):
                flat = costs0[which[slot], first] + costs1[which[slot], start1 + second + extra]
                scores[slot, 0, second + extra] = (util23[slot] + flat) + DISCOUNT * expected[
                    :, extra * depth : (extra + 1) * depth
                ]
        for extra in range(2):
            found = [scores[slot, 0, second + extra] for slot in range(per_group)]
            top = functools.reduce(jnp.maximum, found)
            total = functools.reduce(jnp.add, [jnp.exp(one - top) for one in found])
            local[0, second + extra] = top + jnp.log(total)


def choice_kernel(scores, mine, other, new_value, choice_prob):
    a, b = mine[...], other[...]
    top, low = jnp.maximum(a, b), jnp.minimum(a, b)
    total = top + jnp.log(1.0 + jnp.exp(low - top))
    new_value[...] = total
    for slot in range(scores.shape[0]):
        choice_prob[slot] = jnp.exp(scores[slot] - total).astype(choice_prob.dtype)


def after(value, *done):
    return lax.optimization_barrier((value, *done))[0] if done else value


def whole_block():
    return pl.BlockSpec(memory_space=pltpu.VMEM)


def params(mebibytes):
    return pltpu.CompilerParams(vmem_limit_bytes=mebibytes * MIB)


def gather_body(
    value_now,
    cost_first,
    cost_second,
    cost_third,
    cost_fourth,
    trans_weights,
    trans_offsets,
    action_order,
):
    n_act, n_narrow, n_wide = (lax.axis_size(name) for name in ("act", "narrow", "wide"))
    n_outer = n_wide // 2
    act, narrow, wide = (lax.axis_index(name) for name in ("act", "narrow", "wide"))
    outer, core = wide // 2, wide % 2
    actions, _, taps = trans_weights.shape
    per_group = actions // n_act
    rows0, rows1, len2, len3 = value_now.shape
    len0, len1 = rows0 * n_wide, rows1 * n_narrow
    lengths = (len0, len1, len2, len3)
    share = len2 // n_act
    chunk = CHUNK_ROWS
    n_chunks = share // chunk
    core_flip = [(i, i ^ 1) for i in range(n_wide)]
    act_flip = [(i, (i + 1) % n_act) for i in range(n_act)]
    narrow_hops = [
        [(i, (i + step) % n_narrow) for i in range(n_narrow)] for step in range(1, n_narrow)
    ]

    def across(bit):
        return [(i, i ^ (2 * bit)) for i in range(n_wide)]

    def part(index):
        return lax.dynamic_slice_in_dim(value_now, act * share + index * chunk, chunk, 2)

    near = [(0, other, ahead) for ahead in range(n_narrow) for other in range(2)]
    arrivals = near + [
        (far, other, ahead)
        for ahead in range(n_narrow)
        for other in range(2)
        for far in range(1, n_outer)
    ]

    half_band = (taps - 1) // 2
    width = -(-(max(lengths) + 4 * half_band) // LANES) * LANES
    weights = jnp.pad(trans_weights, ((0, 0), (0, 0), (0, width - taps)))
    place = jnp.stack([act, narrow, outer, core]).astype(jnp.int32)
    smem = pl.BlockSpec(memory_space=pltpu.SMEM)
    q_rows = actions * rows0 * rows1
    kron_hi, kron_lo, left2, right3, util23 = pl.pallas_call(
        functools.partial(
            prepare_kernel, lengths, taps, (n_act, n_narrow, n_outer), rows0, rows1, arrivals
        ),
        out_shape=(
            jax.ShapeDtypeStruct((q_rows, len0 * len1), BF16),
            jax.ShapeDtypeStruct((q_rows, len0 * len1), BF16),
            jax.ShapeDtypeStruct((per_group, 2 * len2, 2 * len2), BF16),
            jax.ShapeDtypeStruct((actions, 2 * len3, 2 * len3), BF16),
            jax.ShapeDtypeStruct((per_group, len2, len3), F32),
        ),
        in_specs=[smem] * 3 + [whole_block()] * 3,
        out_specs=(whole_block(),) * 5,
        scratch_shapes=[pltpu.VMEM((len0, len0 * len1), F32), pltpu.VMEM((len1, len0 * len1), F32)],
        compiler_params=params(16),
        cost_estimate=pl.CostEstimate(flops=10**9, bytes_accessed=4 * 10**6, transcendentals=0),
        name="prepare",
    )(place, action_order, trans_offsets, weights, cost_third, cost_fourth)

    chunks = [part(index) for index in range(n_chunks)]
    half = lax.dynamic_slice_in_dim(value_now, act * share, share, 2)
    direct = [lax.ppermute(chunks[0], "wide", across(far)) for far in range(1, n_outer)]
    around = [lax.ppermute(half, "narrow", hops) for hops in narrow_hops]
    second = lax.ppermute(chunks[1], "wide", across(1))
    direct, around, second, *_ = lax.optimization_barrier((direct, around, second, kron_hi, right3))

    out_piece = jax.ShapeDtypeStruct((per_group, rows0 * rows1, chunk, len3), F32)
    bits = [1 << bit for bit in range(1, n_outer.bit_length() - 1)]
    twins = [None, second]
    fars = [jnp.concatenate(direct, axis=0)]
    nears = []
    kept, sent = [], []
    def doubled(index):
        grown = jnp.concatenate([chunks[index], twins[index]], axis=0)
        grown = after(grown, fars[index - 1])
        parts = [twins[index]]
        for bit in bits:
            parts.append(lax.ppermute(grown, "wide", across(bit)))
            if bit != bits[-1]:
                grown = jnp.concatenate([grown, parts[-1]], axis=0)
        return jnp.concatenate(parts, axis=0)

    far, moved = fars[0], []
    for index in range(n_chunks):
        crossed = lax.ppermute(far, "wide", core_flip)
        if index == 0:
            late = after(jnp.stack(chunks[2:]), far)
            twins += list(lax.ppermute(late, "wide", across(1)))
            sources = lax.optimization_barrier((half, *around, crossed))[:-1]
            for one, source in zip([half] + around, sources):
                nears += [one, lax.ppermute(source, "wide", core_flip)]
            nears = [one.reshape(rows0 * rows1, share, len3) for one in nears]
        moved = [lax.ppermute(after(far, *moved), "narrow", hops) for hops in narrow_hops]
        pieces = [far, crossed]
        for one in moved:
            pieces += [one, lax.ppermute(one, "wide", core_flip)]
        pieces = [one.reshape(-1, chunk, len3) for one in pieces]
        starts = [index * chunk] * len(nears) + [0] * len(pieces)
        keep, for_act = pl.pallas_call(
            functools.partial(short_dims_kernel, starts, n_act),
            out_shape=(out_piece,) * 2,
            in_specs=[whole_block()] * (3 + len(starts)),
            out_specs=(whole_block(),) * 2,
            compiler_params=params(12),
            cost_estimate=pl.CostEstimate(flops=10**9, bytes_accessed=3 * 10**6, transcendentals=0),
            name="short_dims",
        )(kron_hi, kron_lo, right3, *nears, *pieces)
        kept.append(keep)
        if index + 1 < n_chunks:
            far = doubled(index + 1)
            fars.append(far)
            if index == 0:
                far = after(far, *twins[2:])
        sent.append(lax.ppermute(after(for_act, *sent[-1:], *fars[index + 1 :]), "act", act_flip))
    parts = kept + sent

    scores_shape = (per_group, rows0, rows1, len2, len3)
    score_spec = pl.BlockSpec((per_group, 1, rows1, len2, len3), lambda i: (0, i, 0, 0, 0))
    state_spec = pl.BlockSpec((1, rows1, len2, len3), lambda i: (i, 0, 0, 0))
    scores, local = pl.pallas_call(
        functools.partial(third_dim_kernel, len(parts), rows0),
        grid=(rows0,),
        out_shape=(
            jax.ShapeDtypeStruct(scores_shape, F32),
            jax.ShapeDtypeStruct(value_now.shape, F32),
        ),
        in_specs=[smem] * 4 + [whole_block()] * 2
        + [pl.BlockSpec((per_group, rows1, chunk, len3), lambda i: (0, i, 0, 0))] * len(parts),
        out_specs=(score_spec, state_spec),
        compiler_params=params(20),
        cost_estimate=pl.CostEstimate(flops=2 * 10**9, bytes_accessed=10**7, transcendentals=10**6),
        name="third_dim",
    )(place, action_order, cost_first, cost_second, left2, util23, *parts)

    other = lax.ppermute(local, "act", act_flip)
    return tuple(
        pl.pallas_call(
            choice_kernel,
            grid=(rows0,),
            out_shape=(
                jax.ShapeDtypeStruct(value_now.shape, F32),
                jax.ShapeDtypeStruct(scores_shape, BF16),
            ),
            in_specs=[score_spec, state_spec, state_spec],
            out_specs=(state_spec, score_spec),
            compiler_params=params(16),
            cost_estimate=pl.CostEstimate(flops=10**7, bytes_accessed=10**7, transcendentals=10**6),
            name="choice",
        )(scores, local, other)
    )


def gather_fits(mesh, value_shape, actions, offset_reach):
    n_wide, n_narrow, n_act = (mesh.shape[name] for name in ("wide", "narrow", "act"))
    len0, len1, len2, len3 = value_shape
    if n_act != 2 or n_wide < 4 or n_wide & (n_wide - 1) or actions % n_act:
        return False
    if len2 % (n_act * CHUNK_ROWS) or len2 < 3 * n_act * CHUNK_ROWS:
        return False
    if len2 != LANES or len3 != LANES:
        return False
    if (len1 // n_narrow) % SUBLANES or len0 * len1 // (n_wide * n_narrow) % 16 or len0 % n_wide:
        return False
    if max(len0, len1) > LANES or len1 % n_narrow:
        return False
    raw = len0 * len1 * len2 * len3 // (2 * n_act)
    exchanged = 2 * (actions // n_act) * len0 * len1 * len2 * len3 // (n_wide * n_narrow)
    return raw <= exchanged


def solution(mesh):
    def run(value_now, *rest):
        actions = rest[-1].shape[0]
        small = gather_fits(mesh, value_now.shape, actions, rest[4].shape[-1])
        return jax.shard_map(
            gather_body if small else exchange_body,
            mesh=mesh,
            in_specs=(P("wide", "narrow", None, None), P(), P(), P(), P(), P(), P(), P()),
            out_specs=(P("wide", "narrow", None, None), P("act", "wide", "narrow", None, None)),
            check_vma=False,
        )(value_now, *rest)

    return run
```

```python
import functools

import jax
import jax.numpy as jnp
from jax import lax
from jax.experimental import pallas as pl
from jax.experimental.pallas import tpu as pltpu
from jax.sharding import PartitionSpec as P

DISCOUNT = 0.95
HIGHEST = lax.Precision.HIGHEST
F32 = jnp.float32
BF16 = jnp.bfloat16
LANES = 128
SUBLANES = 8
PLACE = 4
CHUNK_ROWS = 16
MIB = 1024 * 1024


def merged(value, axis, join):
    pieces = lax.all_gather(value, axis)
    head = pieces[0]
    tail = pieces[1:]
    subtotal, _ = lax.scan(lambda subtotal, slab: (join(subtotal, slab), None), head, tail)
    return subtotal


def transition(weights, offset, length):
    band_len = weights.shape[0]
    half_band = (band_len - 1) // 2
    normed = weights / jnp.sum(weights)
    row_ids = jnp.arange(length, dtype=jnp.int32)
    tap_ids = jnp.arange(band_len, dtype=jnp.int32)
    target = jnp.clip(row_ids[:, None] + offset + tap_ids[None, :] - half_band, 0, length - 1)
    matched = (target[:, :, None] == row_ids[None, None, :]).astype(normed.dtype)
    return jnp.einsum("ijk,j->ik", matched, normed, precision=HIGHEST)


def exchange_body(
    value_now,
    cost_first,
    cost_second,
    cost_third,
    cost_fourth,
    trans_weights,
    trans_offsets,
    action_order,
):
    size_act = lax.axis_size("act")
    per_group = action_order.shape[0] // size_act
    group_id = lax.axis_index("act")
    my_actions = lax.dynamic_slice_in_dim(action_order, group_id * per_group, per_group)
    rows_first, rows_second, len_third, len_fourth = value_now.shape
    len_first = rows_first * lax.axis_size("wide")
    len_second = rows_second * lax.axis_size("narrow")
    my_weights = jnp.take(trans_weights, my_actions, axis=0)
    my_offsets = jnp.take(trans_offsets, my_actions, axis=0)

    def build(axis_id, length):
        return jax.vmap(lambda weight_row, offset_one: transition(weight_row, offset_one, length))(
            my_weights[:, axis_id], my_offsets[:, axis_id]
        )

    mat_first = build(0, len_first)
    mat_second = build(1, len_second)
    mat_third = build(2, len_third)
    mat_fourth = build(3, len_fourth)
    spread = lax.all_to_all(value_now, "narrow", split_axis=2, concat_axis=1, tiled=True)
    field = jnp.einsum("gij,ajcd->gaicd", mat_second, spread, precision=HIGHEST)
    field = jnp.einsum("gij,gabcj->gabci", mat_fourth, field, precision=HIGHEST)
    field = lax.all_to_all(field, "narrow", split_axis=2, concat_axis=3, tiled=True)
    field = lax.all_to_all(field, "wide", split_axis=3, concat_axis=1, tiled=True)
    field = jnp.einsum("gij,gjbcd->gibcd", mat_first, field, precision=HIGHEST)
    field = lax.all_to_all(field, "wide", split_axis=1, concat_axis=3, tiled=True)
    expected = jnp.einsum("gij,gabjd->gabid", mat_third, field, precision=HIGHEST)
    start_first = lax.axis_index("wide") * rows_first
    start_second = lax.axis_index("narrow") * rows_second
    util_first = lax.dynamic_slice_in_dim(
        jnp.take(cost_first, my_actions, axis=0), start_first, rows_first, 1
    )
    util_second = lax.dynamic_slice_in_dim(
        jnp.take(cost_second, my_actions, axis=0), start_second, rows_second, 1
    )
    util_third = jnp.take(cost_third, my_actions, axis=0)
    util_fourth = jnp.take(cost_fourth, my_actions, axis=0)
    utility = (
        util_first[:, :, None, None, None]
        + util_second[:, None, :, None, None]
        + util_third[:, None, None, :, None]
        + util_fourth[:, None, None, None, :]
    )
    scores = utility + DISCOUNT * expected
    local_max = jnp.max(scores, axis=0)
    local_sum = jnp.sum(jnp.exp(scores - local_max), axis=0)
    log_total = merged(local_max + jnp.log(local_sum), "act", jnp.logaddexp)
    choice_prob = jnp.exp(scores - log_total).astype(jnp.bfloat16)
    return (log_total, choice_prob)


def halves(x):
    high = x.astype(BF16)
    return high, (x - high.astype(F32)).astype(BF16)


def dot32(a, b):
    return jnp.dot(a, b, preferred_element_type=F32, precision=HIGHEST)


def banded(weights, offset, length, taps):
    half_band = (taps - 1) // 2
    width = weights.shape[1]
    normed = weights / jnp.sum(weights, axis=1, keepdims=True)
    tile = jnp.broadcast_to(normed, (SUBLANES, width))
    tile = pltpu.roll(tile, lax.rem(offset + (width - half_band), width), 1)
    rows = jnp.concatenate([tile] * (length // SUBLANES), axis=0)
    rows = pltpu.roll(rows, 0, 1, stride=1, stride_axis=0)
    lane = lax.broadcasted_iota(jnp.int32, (length, width), 1)
    under = lane >= width - 2 * half_band
    over = (lane >= length) & (lane < length + 2 * half_band)
    under_sum = jnp.sum(jnp.where(under, rows, 0.0), axis=1, keepdims=True)
    over_sum = jnp.sum(jnp.where(over, rows, 0.0), axis=1, keepdims=True)
    span = -(-length // LANES) * LANES
    kept = lane[:, :span]
    body = jnp.where(kept < length, rows[:, :span], 0.0)
    body = body + jnp.where(kept == 0, under_sum, 0.0)
    return body + jnp.where(kept == length - 1, over_sum, 0.0)


def prepare_kernel(
    lengths, taps, sizes, rows0, rows1, arrivals, meta, weights, kron_hi, kron_lo, right3, wide0, wide1
):
    n_act, n_narrow, n_outer = sizes
    len0, len1, len2, len3 = lengths
    act, narrow, outer, core = (meta[i] for i in range(PLACE))
    actions = weights.shape[0]
    per_group = actions // n_act
    columns = len0 * len1

    def wrapped(index, size):
        return lax.rem(index + size, size)

    lane = lax.broadcasted_iota(jnp.int32, (1, columns), 1)
    ids0 = jnp.zeros((1, columns), jnp.int32)
    ids1 = jnp.zeros((1, columns), jnp.int32)
    for block, (far, part, ahead) in enumerate(arrivals):
        from_outer, from_core = outer ^ far, wrapped(core + part, 2)
        for row in range(rows0):
            start = (block * rows0 + row) * rows1
            inside = (lane >= start) & (lane < start + rows1)
            first = (from_outer * 2 + from_core) * rows0 + row
            second = wrapped(narrow - ahead, n_narrow) * rows1 - start
            ids0 = jnp.where(inside, first, ids0)
            ids1 = jnp.where(inside, second + lane, ids1)
    spread0 = (lax.broadcasted_iota(jnp.int32, (LANES, columns), 0) == ids0).astype(F32)
    spread1 = (lax.broadcasted_iota(jnp.int32, (LANES, columns), 0) == ids1).astype(F32)

    for action in range(actions):
        group, slot = divmod(action, per_group)
        which = meta[PLACE + wrapped(act + group, n_act) * per_group + slot]
        rows = weights[which]
        mats = [
            banded(
                rows[axis : axis + 1, :],
                meta[PLACE + (1 + axis) * actions + which],
                lengths[axis],
                taps,
            )
            for axis in (0, 1, 3)
        ]
        wide0[...] = dot32(mats[0], spread0)
        wide1[...] = dot32(mats[1], spread1)
        second = wide1[pl.ds(pl.multiple_of(narrow * rows1, SUBLANES), rows1), :]
        base = (outer * 2 + core) * rows0
        blocks = [wide0[pl.ds(base + row, 1), :] * second for row in range(rows0)]
        start = action * rows0 * rows1
        high, low = halves(jnp.concatenate(blocks, axis=0))
        kron_hi[start : start + rows0 * rows1, :] = high
        kron_lo[start : start + rows0 * rows1, :] = low
        high, low = halves(mats[2].T)
        row_pair = jnp.concatenate([high, low], axis=1)
        right3[action] = jnp.concatenate([row_pair, row_pair], axis=0)


def prepare_third_kernel(taps, n_act, meta, weights, third, fourth, left2, util23):
    act, actions, per_group = meta[0], weights.shape[0], left2.shape[0]
    len2, len3 = util23.shape[1:]
    share = len2 // n_act
    lane2 = lax.broadcasted_iota(jnp.int32, (1, len2), 1)
    ids2 = jnp.zeros((1, len2), jnp.int32)
    for group in range(n_act):
        inside = (lane2 >= group * share) & (lane2 < (group + 1) * share)
        ids2 = jnp.where(inside, (lax.rem(act + group, n_act) - group) * share + lane2, ids2)
    order2 = (lax.broadcasted_iota(jnp.int32, (len2, len2), 0) == ids2).astype(F32)

    for slot in range(per_group):
        which = meta[PLACE + act * per_group + slot]
        offset = meta[PLACE + 3 * actions + which]
        matrix = banded(weights[which][2:3, :], offset, len2, taps)
        high, low = halves(dot32(matrix, order2))
        left2[slot] = jnp.concatenate(
            [jnp.concatenate([high, high], axis=1), jnp.concatenate([low, low], axis=1)], axis=0
        )
        column = jnp.broadcast_to(third[pl.ds(which, 1), :], (len3, len2)).T
        util23[slot] = column + fourth[pl.ds(which, 1), :]


def short_dims_kernel(starts, groups, kron_hi, kron_lo, right3, *refs):
    pieces, keep, outs = refs[: len(starts)], refs[len(starts)], refs[len(starts) + 1 :]
    rows, depth = keep.shape[2:]
    actions = right3.shape[0]
    per_group = actions // groups
    per_out = keep.shape[1]
    per_piece = per_out // len(outs)
    q_hi, q_lo = kron_hi[...], kron_lo[...]
    mixed = []
    for row in range(0, rows, 2):
        cols = [
            jnp.concatenate(
                [piece[:, start + row + extra, :] for start, piece in zip(starts, pieces)], axis=0
            )
            for extra in range(2)
        ]
        x_hi, x_lo = halves(jnp.concatenate(cols, axis=1))
        out = (
            jnp.dot(q_hi, x_hi, preferred_element_type=F32)
            + jnp.dot(q_hi, x_lo, preferred_element_type=F32)
            + jnp.dot(q_lo, x_hi, preferred_element_type=F32)
        )
        mixed += [out[:, :depth], out[:, depth:]]
    for action in range(actions):
        group, slot = divmod(action, per_group)
        start = action * per_out
        block = jnp.concatenate([one[start : start + per_out] for one in mixed], axis=0)
        t_hi, t_lo = halves(block)
        both = jnp.dot(
            jnp.concatenate([t_hi, t_lo], axis=1), right3[action], preferred_element_type=F32
        )
        done = both[:, :depth] + both[:, depth:]
        for row in range(rows):
            start = row * per_out
            if group == 0:
                keep[slot, :, row, :] = done[start : start + per_out]
                continue
            for index, out in enumerate(outs):
                first = start + index * per_piece
                out[slot, :, row, :] = done[first : first + per_piece]


def third_dim_kernel(n_pieces, rows0, row, meta, costs0, costs1, left2, util23, *refs):
    pieces, scores, local = refs[:n_pieces], refs[n_pieces], refs[n_pieces + 1]
    per_group, rows1 = scores.shape[:2]
    length = util23.shape[1]
    depth = util23.shape[2]
    which = [meta[PLACE + meta[0] * per_group + slot] for slot in range(per_group)]
    first = (meta[2] * 2 + meta[3]) * rows0 + row
    start1 = meta[1] * rows1
    for second in range(0, rows1, 2):
        for slot in range(per_group):
            cols = [
                jnp.concatenate([piece[slot, second + extra] for piece in pieces], axis=0)
                for extra in range(2)
            ]
            g_hi, g_lo = halves(jnp.concatenate(cols, axis=1))
            both = jnp.dot(
                left2[slot], jnp.concatenate([g_hi, g_lo], axis=0), preferred_element_type=F32
            )
            expected = both[:length] + both[length:]
            for extra in range(2):
                flat = costs0[which[slot], first] + costs1[which[slot], start1 + second + extra]
                scores[slot, second + extra] = (util23[slot] + flat) + DISCOUNT * expected[
                    :, extra * depth : (extra + 1) * depth
                ]
        for extra in range(2):
            found = [scores[slot, second + extra] for slot in range(per_group)]
            top = functools.reduce(jnp.maximum, found)
            total = functools.reduce(jnp.add, [jnp.exp(one - top) for one in found])
            local[second + extra] = top + jnp.log(total)


def choice_kernel(scores, mine, other, *refs):
    new_value, choice_prob = refs[-2:]
    a, b = mine[...], other[...]
    top, low = jnp.maximum(a, b), jnp.minimum(a, b)
    total = top + jnp.log(1.0 + jnp.exp(low - top))
    new_value[0] = total
    for slot in range(scores.shape[0]):
        choice_prob[slot, 0] = jnp.exp(scores[slot] - total).astype(choice_prob.dtype)


def after(value, *done):
    return lax.optimization_barrier((value, *done))[0] if done else value


def whole_block():
    return pl.BlockSpec(memory_space=pltpu.VMEM)


def params(mebibytes):
    return pltpu.CompilerParams(vmem_limit_bytes=mebibytes * MIB)


def gather_body(
    value_now,
    cost_first,
    cost_second,
    cost_third,
    cost_fourth,
    trans_weights,
    trans_offsets,
    action_order,
):
    n_act, n_narrow, n_wide = (lax.axis_size(name) for name in ("act", "narrow", "wide"))
    n_outer = n_wide // 2
    act, narrow, wide = (lax.axis_index(name) for name in ("act", "narrow", "wide"))
    outer, core = wide // 2, wide % 2
    actions, _, taps = trans_weights.shape
    per_group = actions // n_act
    rows0, rows1, len2, len3 = value_now.shape
    len0, len1 = rows0 * n_wide, rows1 * n_narrow
    lengths = (len0, len1, len2, len3)
    share = len2 // n_act
    sizes = chunk_sizes(share)
    n_chunks = len(sizes)
    begins = [sum(sizes[:index]) for index in range(n_chunks)]
    core_flip = [(i, i ^ 1) for i in range(n_wide)]
    act_flip = [(i, (i + 1) % n_act) for i in range(n_act)]
    narrow_hops = [
        [(i, (i + step) % n_narrow) for i in range(n_narrow)] for step in range(1, n_narrow)
    ]

    def across(bit):
        return [(i, i ^ (2 * bit)) for i in range(n_wide)]

    def part(begin, size):
        return lax.dynamic_slice_in_dim(value_now, act * share + begin, size, 2)

    near = [(0, other, ahead) for ahead in range(n_narrow) for other in range(2)]
    arrivals = near + [
        (far, other, ahead)
        for ahead in range(n_narrow)
        for other in range(2)
        for far in range(1, n_outer)
    ]

    half_band = (taps - 1) // 2
    width = -(-(max(lengths) + 4 * half_band) // LANES) * LANES
    weights = jnp.pad(trans_weights, ((0, 0), (0, 0), (0, width - taps)))
    place = jnp.stack([act, narrow, outer, core]).astype(jnp.int32)
    meta = jnp.concatenate([place, action_order, trans_offsets.T.reshape(-1)])
    smem = pl.BlockSpec(memory_space=pltpu.SMEM)
    q_rows = actions * rows0 * rows1
    kron_hi, kron_lo, right3 = pl.pallas_call(
        functools.partial(
            prepare_kernel, lengths, taps, (n_act, n_narrow, n_outer), rows0, rows1, arrivals
        ),
        out_shape=(
            jax.ShapeDtypeStruct((q_rows, len0 * len1), BF16),
            jax.ShapeDtypeStruct((q_rows, len0 * len1), BF16),
            jax.ShapeDtypeStruct((actions, 2 * len3, 2 * len3), BF16),
        ),
        in_specs=[smem, whole_block()],
        out_specs=(whole_block(),) * 3,
        scratch_shapes=[pltpu.VMEM((len0, len0 * len1), F32), pltpu.VMEM((len1, len0 * len1), F32)],
        compiler_params=params(16),
        cost_estimate=pl.CostEstimate(flops=10**9, bytes_accessed=4 * 10**6, transcendentals=0),
        name="prepare",
    )(meta, weights)
    left2, util23 = pl.pallas_call(
        functools.partial(prepare_third_kernel, taps, n_act),
        out_shape=(
            jax.ShapeDtypeStruct((per_group, 2 * len2, 2 * len2), BF16),
            jax.ShapeDtypeStruct((per_group, len2, len3), F32),
        ),
        in_specs=[smem] + [whole_block()] * 3,
        out_specs=(whole_block(),) * 2,
        compiler_params=params(12),
        cost_estimate=pl.CostEstimate(flops=10**9, bytes_accessed=4 * 10**6, transcendentals=0),
        name="prepare_third",
    )(meta, weights, cost_third, cost_fourth)

    chunks = [part(begin, size) for begin, size in zip(begins, sizes)]
    half = part(0, share)
    direct = [lax.ppermute(chunks[0], "wide", across(far)) for far in range(1, n_outer)]
    around = [lax.ppermute(half, "narrow", hops) for hops in narrow_hops]
    second = lax.ppermute(chunks[1], "wide", across(1))
    direct, second, *_ = lax.optimization_barrier((direct, second, kron_hi, right3))

    bits = [1 << bit for bit in range(1, n_outer.bit_length() - 1)]
    twins = [None, second]
    fars = [jnp.concatenate(direct, axis=0)]
    nears = []
    kept, sent = [], []

    def doubled(index):
        grown = jnp.concatenate([chunks[index], twins[index]], axis=0)
        grown = after(grown, fars[index - 1])
        parts = [twins[index]]
        for bit in bits:
            parts.append(lax.ppermute(grown, "wide", across(bit)))
            if bit != bits[-1]:
                grown = jnp.concatenate([grown, parts[-1]], axis=0)
        return jnp.concatenate(parts, axis=0)

    far, moved = fars[0], []
    for index, size in enumerate(sizes):
        crossed = lax.ppermute(far, "wide", core_flip)
        if index == 0:
            late = lax.ppermute(after(part(begins[2], share - begins[2]), far), "wide", across(1))
            for begin, rows in zip(begins[2:], sizes[2:]):
                twins.append(late[:, :, begin - begins[2] : begin - begins[2] + rows])
        moved = [lax.ppermute(after(far, *moved), "narrow", hops) for hops in narrow_hops]
        if index == 0:
            for one, done in [(half, crossed)] + [(one, moved[0]) for one in around]:
                nears += [one, lax.ppermute(after(one, done), "wide", core_flip)]
            nears = [one.reshape(rows0 * rows1, share, len3) for one in nears]
        if index < n_chunks - 1:
            fars.append(doubled(index + 1))
        pieces = [far, crossed]
        for one in moved:
            ready = sent[0] if index == 1 else fars[index + 1 :]
            pieces += [one, lax.ppermute(after(one, *ready), "wide", core_flip)]
        pieces = [one.reshape(-1, size, len3) for one in pieces]
        starts = [begins[index]] * len(nears) + [0] * len(pieces)
        cuts = rows0 if index == n_chunks - 1 else 1
        cut_rows = [rows0 * rows1] + [rows0 * rows1 // cuts] * cuts
        keep, *for_act = pl.pallas_call(
            functools.partial(short_dims_kernel, starts, n_act),
            out_shape=tuple(
                jax.ShapeDtypeStruct((per_group, rows, size, len3), F32) for rows in cut_rows
            ),
            in_specs=[whole_block()] * (3 + len(starts)),
            out_specs=(whole_block(),) * len(cut_rows),
            compiler_params=params(12),
            cost_estimate=pl.CostEstimate(flops=10**9, bytes_accessed=3 * 10**6, transcendentals=0),
            name="short_dims",
        )(kron_hi, kron_lo, right3, *nears, *pieces)
        kept.append(keep)
        if index + 1 < n_chunks:
            far = after(fars[index + 1], late) if index == 0 else fars[index + 1]
        before = [one for ones in sent[-1:] for one in ones]
        sent.append([lax.ppermute(after(one, *before), "act", act_flip) for one in for_act])

    parts = [(keep, True) for keep in kept] + [(ones[0], len(ones) == 1) for ones in sent]
    by_row = []
    for row in range(rows0):
        arrays = [one for one, _ in parts[:-1]] + [sent[-1][row]]
        specs = [
            pl.BlockSpec(
                (per_group, rows1) + one.shape[2:],
                lambda i, block=row if uncut else 0: (0, block, 0, 0),
            )
            for one, (_, uncut) in zip(arrays, parts)
        ]
        scores, local = pl.pallas_call(
            functools.partial(third_dim_kernel, len(parts), rows0, row),
            grid=(1,),
            out_shape=(
                jax.ShapeDtypeStruct((per_group, rows1, len2, len3), F32),
                jax.ShapeDtypeStruct((rows1, len2, len3), F32),
            ),
            in_specs=[smem] * 3 + [whole_block()] * 2 + specs,
            out_specs=(whole_block(),) * 2,
            compiler_params=params(20),
            cost_estimate=pl.CostEstimate(
                flops=10**9, bytes_accessed=5 * 10**6, transcendentals=10**6
            ),
            name="third_dim",
        )(meta, cost_first, cost_second, left2, util23, *arrays)
        by_row.append((scores, local, lax.ppermute(local, "act", act_flip)))

    results = ()
    for row, operands in enumerate(by_row):
        results = pl.pallas_call(
            choice_kernel,
            grid=(1,),
            out_shape=(
                jax.ShapeDtypeStruct(value_now.shape, F32),
                jax.ShapeDtypeStruct((per_group,) + value_now.shape, BF16),
            ),
            in_specs=[whole_block()] * 3 + [pl.BlockSpec(memory_space=pl.ANY)] * len(results),
            out_specs=(
                pl.BlockSpec((1, rows1, len2, len3), lambda i, row=row: (row, 0, 0, 0)),
                pl.BlockSpec(
                    (per_group, 1, rows1, len2, len3), lambda i, row=row: (0, row, 0, 0, 0)
                ),
            ),
            input_output_aliases={3: 0, 4: 1} if results else {},
            compiler_params=params(16),
            cost_estimate=pl.CostEstimate(
                flops=10**7, bytes_accessed=5 * 10**6, transcendentals=10**6
            ),
            name="choice",
        )(*operands, *results)
    return tuple(results)


def chunk_sizes(share):
    edge = CHUNK_ROWS // 2
    return [edge] + [CHUNK_ROWS] * ((share - 2 * edge) // CHUNK_ROWS) + [edge]


def gather_fits(mesh, value_shape, actions, offset_reach):
    n_wide, n_narrow, n_act = (mesh.shape[name] for name in ("wide", "narrow", "act"))
    len0, len1, len2, len3 = value_shape
    if n_act != 2 or n_wide < 4 or n_wide & (n_wide - 1) or actions % n_act:
        return False
    if len2 % (n_act * CHUNK_ROWS) or len2 < 4 * n_act * CHUNK_ROWS:
        return False
    if len2 != LANES or len3 != LANES:
        return False
    if (len1 // n_narrow) % SUBLANES or len0 * len1 // (n_wide * n_narrow) % 16 or len0 % n_wide:
        return False
    if max(len0, len1) > LANES or len1 % n_narrow:
        return False
    raw = len0 * len1 * len2 * len3 // (2 * n_act)
    exchanged = 2 * (actions // n_act) * len0 * len1 * len2 * len3 // (n_wide * n_narrow)
    return raw <= exchanged


def solution(mesh):
    def run(value_now, *rest):
        actions = rest[-1].shape[0]
        small = gather_fits(mesh, value_now.shape, actions, rest[4].shape[-1])
        return jax.shard_map(
            gather_body if small else exchange_body,
            mesh=mesh,
            in_specs=(P("wide", "narrow", None, None), P(), P(), P(), P(), P(), P(), P()),
            out_specs=(P("wide", "narrow", None, None), P("act", "wide", "narrow", None, None)),
            check_vma=False,
        )(value_now, *rest)

    return run
```

```python
import functools

import jax
import jax.numpy as jnp
from jax import lax
from jax.experimental import pallas as pl
from jax.experimental.pallas import tpu as pltpu
from jax.sharding import PartitionSpec as P

DISCOUNT = 0.95
HIGHEST = lax.Precision.HIGHEST
F32 = jnp.float32
BF16 = jnp.bfloat16
LANES = 128
SUBLANES = 8
PLACE = 4
CHUNK_ROWS = 16
MIB = 1024 * 1024


def merged(value, axis, join):
    pieces = lax.all_gather(value, axis)
    head = pieces[0]
    tail = pieces[1:]
    subtotal, _ = lax.scan(lambda subtotal, slab: (join(subtotal, slab), None), head, tail)
    return subtotal


def transition(weights, offset, length):
    band_len = weights.shape[0]
    half_band = (band_len - 1) // 2
    normed = weights / jnp.sum(weights)
    row_ids = jnp.arange(length, dtype=jnp.int32)
    tap_ids = jnp.arange(band_len, dtype=jnp.int32)
    target = jnp.clip(row_ids[:, None] + offset + tap_ids[None, :] - half_band, 0, length - 1)
    matched = (target[:, :, None] == row_ids[None, None, :]).astype(normed.dtype)
    return jnp.einsum("ijk,j->ik", matched, normed, precision=HIGHEST)


def exchange_body(
    value_now,
    cost_first,
    cost_second,
    cost_third,
    cost_fourth,
    trans_weights,
    trans_offsets,
    action_order,
):
    size_act = lax.axis_size("act")
    per_group = action_order.shape[0] // size_act
    group_id = lax.axis_index("act")
    my_actions = lax.dynamic_slice_in_dim(action_order, group_id * per_group, per_group)
    rows_first, rows_second, len_third, len_fourth = value_now.shape
    len_first = rows_first * lax.axis_size("wide")
    len_second = rows_second * lax.axis_size("narrow")
    my_weights = jnp.take(trans_weights, my_actions, axis=0)
    my_offsets = jnp.take(trans_offsets, my_actions, axis=0)

    def build(axis_id, length):
        return jax.vmap(lambda weight_row, offset_one: transition(weight_row, offset_one, length))(
            my_weights[:, axis_id], my_offsets[:, axis_id]
        )

    mat_first = build(0, len_first)
    mat_second = build(1, len_second)
    mat_third = build(2, len_third)
    mat_fourth = build(3, len_fourth)
    spread = lax.all_to_all(value_now, "narrow", split_axis=2, concat_axis=1, tiled=True)
    field = jnp.einsum("gij,ajcd->gaicd", mat_second, spread, precision=HIGHEST)
    field = jnp.einsum("gij,gabcj->gabci", mat_fourth, field, precision=HIGHEST)
    field = lax.all_to_all(field, "narrow", split_axis=2, concat_axis=3, tiled=True)
    field = lax.all_to_all(field, "wide", split_axis=3, concat_axis=1, tiled=True)
    field = jnp.einsum("gij,gjbcd->gibcd", mat_first, field, precision=HIGHEST)
    field = lax.all_to_all(field, "wide", split_axis=1, concat_axis=3, tiled=True)
    expected = jnp.einsum("gij,gabjd->gabid", mat_third, field, precision=HIGHEST)
    start_first = lax.axis_index("wide") * rows_first
    start_second = lax.axis_index("narrow") * rows_second
    util_first = lax.dynamic_slice_in_dim(
        jnp.take(cost_first, my_actions, axis=0), start_first, rows_first, 1
    )
    util_second = lax.dynamic_slice_in_dim(
        jnp.take(cost_second, my_actions, axis=0), start_second, rows_second, 1
    )
    util_third = jnp.take(cost_third, my_actions, axis=0)
    util_fourth = jnp.take(cost_fourth, my_actions, axis=0)
    utility = (
        util_first[:, :, None, None, None]
        + util_second[:, None, :, None, None]
        + util_third[:, None, None, :, None]
        + util_fourth[:, None, None, None, :]
    )
    scores = utility + DISCOUNT * expected
    local_max = jnp.max(scores, axis=0)
    local_sum = jnp.sum(jnp.exp(scores - local_max), axis=0)
    log_total = merged(local_max + jnp.log(local_sum), "act", jnp.logaddexp)
    choice_prob = jnp.exp(scores - log_total).astype(jnp.bfloat16)
    return (log_total, choice_prob)


def halves(x):
    high = x.astype(BF16)
    return high, (x - high.astype(F32)).astype(BF16)


def dot32(a, b):
    return jnp.dot(a, b, preferred_element_type=F32, precision=HIGHEST)


def banded(weights, offset, length, taps):
    half_band = (taps - 1) // 2
    width = weights.shape[1]
    normed = weights / jnp.sum(weights, axis=1, keepdims=True)
    tile = jnp.broadcast_to(normed, (SUBLANES, width))
    tile = pltpu.roll(tile, lax.rem(offset + (width - half_band), width), 1)
    rows = jnp.concatenate([tile] * (length // SUBLANES), axis=0)
    rows = pltpu.roll(rows, 0, 1, stride=1, stride_axis=0)
    lane = lax.broadcasted_iota(jnp.int32, (length, width), 1)
    under = lane >= width - 2 * half_band
    over = (lane >= length) & (lane < length + 2 * half_band)
    under_sum = jnp.sum(jnp.where(under, rows, 0.0), axis=1, keepdims=True)
    over_sum = jnp.sum(jnp.where(over, rows, 0.0), axis=1, keepdims=True)
    span = -(-length // LANES) * LANES
    kept = lane[:, :span]
    body = jnp.where(kept < length, rows[:, :span], 0.0)
    body = body + jnp.where(kept == 0, under_sum, 0.0)
    return body + jnp.where(kept == length - 1, over_sum, 0.0)


def prepare_kernel(
    lengths, taps, sizes, rows0, rows1, arrivals, meta, weights, kron_hi, kron_lo, right3, wide0, wide1
):
    n_act, n_narrow, n_outer = sizes
    len0, len1, len2, len3 = lengths
    act, narrow, outer, core = (meta[i] for i in range(PLACE))
    actions = weights.shape[0]
    per_group = actions // n_act
    columns = len0 * len1

    def wrapped(index, size):
        return lax.rem(index + size, size)

    lane = lax.broadcasted_iota(jnp.int32, (1, columns), 1)
    ids0 = jnp.zeros((1, columns), jnp.int32)
    ids1 = jnp.zeros((1, columns), jnp.int32)
    for block, (far, part, ahead) in enumerate(arrivals):
        from_outer, from_core = outer ^ far, wrapped(core + part, 2)
        for row in range(rows0):
            start = (block * rows0 + row) * rows1
            inside = (lane >= start) & (lane < start + rows1)
            first = (from_outer * 2 + from_core) * rows0 + row
            second = wrapped(narrow - ahead, n_narrow) * rows1 - start
            ids0 = jnp.where(inside, first, ids0)
            ids1 = jnp.where(inside, second + lane, ids1)
    spread0 = (lax.broadcasted_iota(jnp.int32, (LANES, columns), 0) == ids0).astype(F32)
    spread1 = (lax.broadcasted_iota(jnp.int32, (LANES, columns), 0) == ids1).astype(F32)

    for action in range(actions):
        group, slot = divmod(action, per_group)
        which = meta[PLACE + wrapped(act + group, n_act) * per_group + slot]
        rows = weights[which]
        mats = [
            banded(
                rows[axis : axis + 1, :],
                meta[PLACE + (1 + axis) * actions + which],
                lengths[axis],
                taps,
            )
            for axis in (0, 1, 3)
        ]
        wide0[...] = dot32(mats[0], spread0)
        wide1[...] = dot32(mats[1], spread1)
        second = wide1[pl.ds(pl.multiple_of(narrow * rows1, SUBLANES), rows1), :]
        base = (outer * 2 + core) * rows0
        blocks = [wide0[pl.ds(base + row, 1), :] * second for row in range(rows0)]
        start = action * rows0 * rows1
        high, low = halves(jnp.concatenate(blocks, axis=0))
        kron_hi[start : start + rows0 * rows1, :] = high
        kron_lo[start : start + rows0 * rows1, :] = low
        high, low = halves(mats[2].T)
        row_pair = jnp.concatenate([high, low], axis=1)
        right3[action] = jnp.concatenate([row_pair, row_pair], axis=0)


def prepare_third_kernel(taps, n_act, meta, weights, third, fourth, left2, util23):
    act, actions, per_group = meta[0], weights.shape[0], left2.shape[0]
    len2, len3 = util23.shape[1:]
    share = len2 // n_act
    lane2 = lax.broadcasted_iota(jnp.int32, (1, len2), 1)
    ids2 = jnp.zeros((1, len2), jnp.int32)
    for group in range(n_act):
        inside = (lane2 >= group * share) & (lane2 < (group + 1) * share)
        ids2 = jnp.where(inside, (lax.rem(act + group, n_act) - group) * share + lane2, ids2)
    order2 = (lax.broadcasted_iota(jnp.int32, (len2, len2), 0) == ids2).astype(F32)

    for slot in range(per_group):
        which = meta[PLACE + act * per_group + slot]
        offset = meta[PLACE + 3 * actions + which]
        matrix = banded(weights[which][2:3, :], offset, len2, taps)
        high, low = halves(dot32(matrix, order2))
        left2[slot] = jnp.concatenate(
            [jnp.concatenate([high, high], axis=1), jnp.concatenate([low, low], axis=1)], axis=0
        )
        column = jnp.broadcast_to(third[pl.ds(which, 1), :], (len3, len2)).T
        util23[slot] = column + fourth[pl.ds(which, 1), :]


def short_dims_kernel(starts, groups, kron_hi, kron_lo, right3, *refs):
    pieces, keep, outs = refs[: len(starts)], refs[len(starts)], refs[len(starts) + 1 :]
    rows, depth = keep.shape[2:]
    actions = right3.shape[0]
    per_group = actions // groups
    per_out = keep.shape[1]
    per_piece = per_out // len(outs)
    q_hi, q_lo = kron_hi[...], kron_lo[...]
    mixed = []
    for row in range(0, rows, 2):
        cols = [
            jnp.concatenate(
                [piece[:, start + row + extra, :] for start, piece in zip(starts, pieces)], axis=0
            )
            for extra in range(2)
        ]
        x_hi, x_lo = halves(jnp.concatenate(cols, axis=1))
        out = (
            jnp.dot(q_hi, x_hi, preferred_element_type=F32)
            + jnp.dot(q_hi, x_lo, preferred_element_type=F32)
            + jnp.dot(q_lo, x_hi, preferred_element_type=F32)
        )
        mixed += [out[:, :depth], out[:, depth:]]
    for action in range(actions):
        group, slot = divmod(action, per_group)
        start = action * per_out
        block = jnp.concatenate([one[start : start + per_out] for one in mixed], axis=0)
        t_hi, t_lo = halves(block)
        both = jnp.dot(
            jnp.concatenate([t_hi, t_lo], axis=1), right3[action], preferred_element_type=F32
        )
        done = both[:, :depth] + both[:, depth:]
        for row in range(rows):
            start = row * per_out
            if group == 0:
                keep[slot, :, row, :] = done[start : start + per_out]
                continue
            for index, out in enumerate(outs):
                first = start + index * per_piece
                out[slot, :, row, :] = done[first : first + per_piece]


def third_dim_kernel(n_pieces, rows0, row, meta, costs0, costs1, left2, util23, *refs):
    pieces, scores, local = refs[:n_pieces], refs[n_pieces], refs[n_pieces + 1]
    per_group, rows1 = scores.shape[:2]
    length = util23.shape[1]
    depth = util23.shape[2]
    which = [meta[PLACE + meta[0] * per_group + slot] for slot in range(per_group)]
    first = (meta[2] * 2 + meta[3]) * rows0 + row
    start1 = meta[1] * rows1
    for second in range(0, rows1, 2):
        for slot in range(per_group):
            cols = [
                jnp.concatenate([piece[slot, second + extra] for piece in pieces], axis=0)
                for extra in range(2)
            ]
            g_hi, g_lo = halves(jnp.concatenate(cols, axis=1))
            both = jnp.dot(
                left2[slot], jnp.concatenate([g_hi, g_lo], axis=0), preferred_element_type=F32
            )
            expected = both[:length] + both[length:]
            for extra in range(2):
                flat = costs0[which[slot], first] + costs1[which[slot], start1 + second + extra]
                scores[slot, second + extra] = (util23[slot] + flat) + DISCOUNT * expected[
                    :, extra * depth : (extra + 1) * depth
                ]
        for extra in range(2):
            found = [scores[slot, second + extra] for slot in range(per_group)]
            top = functools.reduce(jnp.maximum, found)
            total = functools.reduce(jnp.add, [jnp.exp(one - top) for one in found])
            local[second + extra] = top + jnp.log(total)


def choice_kernel(scores, mine, other, *refs):
    new_value, choice_prob = refs[-2:]
    a, b = mine[...], other[...]
    top, low = jnp.maximum(a, b), jnp.minimum(a, b)
    total = top + jnp.log(1.0 + jnp.exp(low - top))
    new_value[0] = total
    for slot in range(scores.shape[0]):
        choice_prob[slot, 0] = jnp.exp(scores[slot] - total).astype(choice_prob.dtype)


def after(value, *done):
    return lax.optimization_barrier((value, *done))[0] if done else value


def whole_block():
    return pl.BlockSpec(memory_space=pltpu.VMEM)


def params(mebibytes):
    return pltpu.CompilerParams(vmem_limit_bytes=mebibytes * MIB)


def gather_body(
    value_now,
    cost_first,
    cost_second,
    cost_third,
    cost_fourth,
    trans_weights,
    trans_offsets,
    action_order,
):
    n_act, n_narrow, n_wide = (lax.axis_size(name) for name in ("act", "narrow", "wide"))
    n_outer = n_wide // 2
    act, narrow, wide = (lax.axis_index(name) for name in ("act", "narrow", "wide"))
    outer, core = wide // 2, wide % 2
    actions, _, taps = trans_weights.shape
    per_group = actions // n_act
    rows0, rows1, len2, len3 = value_now.shape
    len0, len1 = rows0 * n_wide, rows1 * n_narrow
    lengths = (len0, len1, len2, len3)
    share = len2 // n_act
    sizes = chunk_sizes(share)
    n_chunks = len(sizes)
    begins = [sum(sizes[:index]) for index in range(n_chunks)]
    core_flip = [(i, i ^ 1) for i in range(n_wide)]
    act_flip = [(i, (i + 1) % n_act) for i in range(n_act)]
    narrow_hops = [
        [(i, (i + step) % n_narrow) for i in range(n_narrow)] for step in range(1, n_narrow)
    ]

    def across(bit):
        return [(i, i ^ (2 * bit)) for i in range(n_wide)]

    def part(begin, size):
        return lax.dynamic_slice_in_dim(value_now, act * share + begin, size, 2)

    near = [(0, other, ahead) for ahead in range(n_narrow) for other in range(2)]
    arrivals = near + [
        (far, other, ahead)
        for ahead in range(n_narrow)
        for other in range(2)
        for far in range(1, n_outer)
    ]

    half_band = (taps - 1) // 2
    width = -(-(max(lengths) + 4 * half_band) // LANES) * LANES
    weights = jnp.pad(trans_weights, ((0, 0), (0, 0), (0, width - taps)))
    place = jnp.stack([act, narrow, outer, core]).astype(jnp.int32)
    meta = jnp.concatenate([place, action_order, trans_offsets.T.reshape(-1)])
    smem = pl.BlockSpec(memory_space=pltpu.SMEM)
    q_rows = actions * rows0 * rows1
    kron_hi, kron_lo, right3 = pl.pallas_call(
        functools.partial(
            prepare_kernel, lengths, taps, (n_act, n_narrow, n_outer), rows0, rows1, arrivals
        ),
        out_shape=(
            jax.ShapeDtypeStruct((q_rows, len0 * len1), BF16),
            jax.ShapeDtypeStruct((q_rows, len0 * len1), BF16),
            jax.ShapeDtypeStruct((actions, 2 * len3, 2 * len3), BF16),
        ),
        in_specs=[smem, whole_block()],
        out_specs=(whole_block(),) * 3,
        scratch_shapes=[pltpu.VMEM((len0, len0 * len1), F32), pltpu.VMEM((len1, len0 * len1), F32)],
        compiler_params=params(16),
        cost_estimate=pl.CostEstimate(flops=10**9, bytes_accessed=4 * 10**6, transcendentals=0),
        name="prepare",
    )(meta, weights)
    left2, util23 = pl.pallas_call(
        functools.partial(prepare_third_kernel, taps, n_act),
        out_shape=(
            jax.ShapeDtypeStruct((per_group, 2 * len2, 2 * len2), BF16),
            jax.ShapeDtypeStruct((per_group, len2, len3), F32),
        ),
        in_specs=[smem] + [whole_block()] * 3,
        out_specs=(whole_block(),) * 2,
        compiler_params=params(12),
        cost_estimate=pl.CostEstimate(flops=10**9, bytes_accessed=4 * 10**6, transcendentals=0),
        name="prepare_third",
    )(meta, weights, cost_third, cost_fourth)

    chunks = [part(begin, size) for begin, size in zip(begins, sizes)]
    half = part(0, share)
    direct = [lax.ppermute(chunks[0], "wide", across(far)) for far in range(1, n_outer)]
    around = [lax.ppermute(half, "narrow", hops) for hops in narrow_hops]
    soon = lax.ppermute(part(begins[1], sizes[1] + sizes[2]), "wide", across(1))
    direct, *_ = lax.optimization_barrier((direct, kron_hi, right3))

    bits = [1 << bit for bit in range(1, n_outer.bit_length() - 1)]
    twins = [None, soon[:, :, : sizes[1]], soon[:, :, sizes[1] :]]
    fars = [jnp.concatenate(direct, axis=0)]
    nears = []
    kept, sent = [], []

    def doubled(index):
        grown = jnp.concatenate([chunks[index], twins[index]], axis=0)
        grown = after(grown, fars[index - 1])
        parts = [twins[index]]
        for bit in bits:
            parts.append(lax.ppermute(grown, "wide", across(bit)))
            if bit != bits[-1]:
                grown = jnp.concatenate([grown, parts[-1]], axis=0)
        return jnp.concatenate(parts, axis=0)

    far, moved = fars[0], []
    for index, size in enumerate(sizes):
        crossed = lax.ppermute(far, "wide", core_flip)
        if index == 0:
            late = lax.ppermute(after(part(begins[3], share - begins[3]), far), "wide", across(1))
            for begin, rows in zip(begins[3:], sizes[3:]):
                twins.append(late[:, :, begin - begins[3] : begin - begins[3] + rows])
        moved = [lax.ppermute(after(far, *moved), "narrow", hops) for hops in narrow_hops]
        if index == 0:
            sources = lax.optimization_barrier((half, *around, crossed))[:-1]
            for one, source in zip([half] + around, sources):
                nears += [one, lax.ppermute(source, "wide", core_flip)]
            nears = [one.reshape(rows0 * rows1, share, len3) for one in nears]
        if index + 1 < n_chunks:
            fars.append(doubled(index + 1))
        pieces = [far, crossed]
        for one in moved:
            source = after(one, fars[1]) if index == 0 else one
            pieces += [one, lax.ppermute(source, "wide", core_flip)]
        pieces = [one.reshape(-1, size, len3) for one in pieces]
        starts = [begins[index]] * len(nears) + [0] * len(pieces)
        cuts = rows0 if index == n_chunks - 1 else 1
        cut_rows = [rows0 * rows1] + [rows0 * rows1 // cuts] * cuts
        keep, *for_act = pl.pallas_call(
            functools.partial(short_dims_kernel, starts, n_act),
            out_shape=tuple(
                jax.ShapeDtypeStruct((per_group, rows, size, len3), F32) for rows in cut_rows
            ),
            in_specs=[whole_block()] * (3 + len(starts)),
            out_specs=(whole_block(),) * len(cut_rows),
            compiler_params=params(12),
            cost_estimate=pl.CostEstimate(flops=10**6, bytes_accessed=10**4, transcendentals=0),
            name="short_dims",
        )(kron_hi, kron_lo, right3, *nears, *pieces)
        kept.append(keep)
        if index + 1 < n_chunks:
            far = after(fars[index + 1], late) if index == 0 else fars[index + 1]
        before = [one for ones in sent[-1:] for one in ones] + fars[index + 1 :]
        sent.append([lax.ppermute(after(one, *before), "act", act_flip) for one in for_act])

    parts = [(keep, True) for keep in kept] + [(ones[0], len(ones) == 1) for ones in sent]
    by_row = []
    for row in range(rows0):
        arrays = [one for one, _ in parts[:-1]] + [sent[-1][row]]
        specs = [
            pl.BlockSpec(
                (per_group, rows1) + one.shape[2:],
                lambda i, block=row if uncut else 0: (0, block, 0, 0),
            )
            for one, (_, uncut) in zip(arrays, parts)
        ]
        scores, local = pl.pallas_call(
            functools.partial(third_dim_kernel, len(parts), rows0, row),
            grid=(1,),
            out_shape=(
                jax.ShapeDtypeStruct((per_group, rows1, len2, len3), F32),
                jax.ShapeDtypeStruct((rows1, len2, len3), F32),
            ),
            in_specs=[smem] * 3 + [whole_block()] * 2 + specs,
            out_specs=(whole_block(),) * 2,
            compiler_params=params(20),
            cost_estimate=pl.CostEstimate(
                flops=10**9, bytes_accessed=5 * 10**6, transcendentals=10**6
            ),
            name="third_dim",
        )(meta, cost_first, cost_second, left2, util23, *arrays)
        by_row.append((scores, local, lax.ppermute(local, "act", act_flip)))

    results = ()
    for row, operands in enumerate(by_row):
        results = pl.pallas_call(
            choice_kernel,
            grid=(1,),
            out_shape=(
                jax.ShapeDtypeStruct(value_now.shape, F32),
                jax.ShapeDtypeStruct((per_group,) + value_now.shape, BF16),
            ),
            in_specs=[whole_block()] * 3 + [pl.BlockSpec(memory_space=pl.ANY)] * len(results),
            out_specs=(
                pl.BlockSpec((1, rows1, len2, len3), lambda i, row=row: (row, 0, 0, 0)),
                pl.BlockSpec(
                    (per_group, 1, rows1, len2, len3), lambda i, row=row: (0, row, 0, 0, 0)
                ),
            ),
            input_output_aliases={3: 0, 4: 1} if results else {},
            compiler_params=params(16),
            cost_estimate=pl.CostEstimate(
                flops=10**7, bytes_accessed=5 * 10**6, transcendentals=10**6
            ),
            name="choice",
        )(*operands, *results)
    return tuple(results)


def chunk_sizes(share):
    return [CHUNK_ROWS] * (share // CHUNK_ROWS)


def gather_fits(mesh, value_shape, actions, offset_reach):
    n_wide, n_narrow, n_act = (mesh.shape[name] for name in ("wide", "narrow", "act"))
    len0, len1, len2, len3 = value_shape
    if n_act != 2 or n_wide < 4 or n_wide & (n_wide - 1) or actions % n_act:
        return False
    if len2 % (n_act * CHUNK_ROWS) or len2 < 4 * n_act * CHUNK_ROWS:
        return False
    if len2 != LANES or len3 != LANES:
        return False
    if (len1 // n_narrow) % SUBLANES or len0 * len1 // (n_wide * n_narrow) % 16 or len0 % n_wide:
        return False
    if max(len0, len1) > LANES or len1 % n_narrow:
        return False
    raw = len0 * len1 * len2 * len3 // (2 * n_act)
    exchanged = 2 * (actions // n_act) * len0 * len1 * len2 * len3 // (n_wide * n_narrow)
    return raw <= exchanged


def solution(mesh):
    def run(value_now, *rest):
        actions = rest[-1].shape[0]
        small = gather_fits(mesh, value_now.shape, actions, rest[4].shape[-1])
        return jax.shard_map(
            gather_body if small else exchange_body,
            mesh=mesh,
            in_specs=(P("wide", "narrow", None, None), P(), P(), P(), P(), P(), P(), P()),
            out_specs=(P("wide", "narrow", None, None), P("act", "wide", "narrow", None, None)),
            check_vma=False,
        )(value_now, *rest)

    return run
```

```python
import functools

import jax
import jax.numpy as jnp
from jax import lax
from jax.experimental import pallas as pl
from jax.experimental.pallas import tpu as pltpu
from jax.sharding import PartitionSpec as P

DISCOUNT = 0.95
HIGHEST = lax.Precision.HIGHEST
F32 = jnp.float32
BF16 = jnp.bfloat16
LANES = 128
SUBLANES = 8
PLACE = 4
CHUNK_ROWS = 16
MIB = 1024 * 1024


def merged(value, axis, join):
    pieces = lax.all_gather(value, axis)
    head = pieces[0]
    tail = pieces[1:]
    subtotal, _ = lax.scan(lambda subtotal, slab: (join(subtotal, slab), None), head, tail)
    return subtotal


def transition(weights, offset, length):
    band_len = weights.shape[0]
    half_band = (band_len - 1) // 2
    normed = weights / jnp.sum(weights)
    row_ids = jnp.arange(length, dtype=jnp.int32)
    tap_ids = jnp.arange(band_len, dtype=jnp.int32)
    target = jnp.clip(row_ids[:, None] + offset + tap_ids[None, :] - half_band, 0, length - 1)
    matched = (target[:, :, None] == row_ids[None, None, :]).astype(normed.dtype)
    return jnp.einsum("ijk,j->ik", matched, normed, precision=HIGHEST)


def exchange_body(
    value_now,
    cost_first,
    cost_second,
    cost_third,
    cost_fourth,
    trans_weights,
    trans_offsets,
    action_order,
):
    size_act = lax.axis_size("act")
    per_group = action_order.shape[0] // size_act
    group_id = lax.axis_index("act")
    my_actions = lax.dynamic_slice_in_dim(action_order, group_id * per_group, per_group)
    rows_first, rows_second, len_third, len_fourth = value_now.shape
    len_first = rows_first * lax.axis_size("wide")
    len_second = rows_second * lax.axis_size("narrow")
    my_weights = jnp.take(trans_weights, my_actions, axis=0)
    my_offsets = jnp.take(trans_offsets, my_actions, axis=0)

    def build(axis_id, length):
        return jax.vmap(lambda weight_row, offset_one: transition(weight_row, offset_one, length))(
            my_weights[:, axis_id], my_offsets[:, axis_id]
        )

    mat_first = build(0, len_first)
    mat_second = build(1, len_second)
    mat_third = build(2, len_third)
    mat_fourth = build(3, len_fourth)
    spread = lax.all_to_all(value_now, "narrow", split_axis=2, concat_axis=1, tiled=True)
    field = jnp.einsum("gij,ajcd->gaicd", mat_second, spread, precision=HIGHEST)
    field = jnp.einsum("gij,gabcj->gabci", mat_fourth, field, precision=HIGHEST)
    field = lax.all_to_all(field, "narrow", split_axis=2, concat_axis=3, tiled=True)
    field = lax.all_to_all(field, "wide", split_axis=3, concat_axis=1, tiled=True)
    field = jnp.einsum("gij,gjbcd->gibcd", mat_first, field, precision=HIGHEST)
    field = lax.all_to_all(field, "wide", split_axis=1, concat_axis=3, tiled=True)
    expected = jnp.einsum("gij,gabjd->gabid", mat_third, field, precision=HIGHEST)
    start_first = lax.axis_index("wide") * rows_first
    start_second = lax.axis_index("narrow") * rows_second
    util_first = lax.dynamic_slice_in_dim(
        jnp.take(cost_first, my_actions, axis=0), start_first, rows_first, 1
    )
    util_second = lax.dynamic_slice_in_dim(
        jnp.take(cost_second, my_actions, axis=0), start_second, rows_second, 1
    )
    util_third = jnp.take(cost_third, my_actions, axis=0)
    util_fourth = jnp.take(cost_fourth, my_actions, axis=0)
    utility = (
        util_first[:, :, None, None, None]
        + util_second[:, None, :, None, None]
        + util_third[:, None, None, :, None]
        + util_fourth[:, None, None, None, :]
    )
    scores = utility + DISCOUNT * expected
    local_max = jnp.max(scores, axis=0)
    local_sum = jnp.sum(jnp.exp(scores - local_max), axis=0)
    log_total = merged(local_max + jnp.log(local_sum), "act", jnp.logaddexp)
    choice_prob = jnp.exp(scores - log_total).astype(jnp.bfloat16)
    return (log_total, choice_prob)


def halves(x):
    high = x.astype(BF16)
    return high, (x - high.astype(F32)).astype(BF16)


def dot32(a, b):
    return jnp.dot(a, b, preferred_element_type=F32, precision=HIGHEST)


def banded(weights, offset, length, taps):
    half_band = (taps - 1) // 2
    width = weights.shape[1]
    normed = weights / jnp.sum(weights, axis=1, keepdims=True)
    tile = jnp.broadcast_to(normed, (SUBLANES, width))
    tile = pltpu.roll(tile, lax.rem(offset + (width - half_band), width), 1)
    rows = jnp.concatenate([tile] * (length // SUBLANES), axis=0)
    rows = pltpu.roll(rows, 0, 1, stride=1, stride_axis=0)
    lane = lax.broadcasted_iota(jnp.int32, (length, width), 1)
    under = lane >= width - 2 * half_band
    over = (lane >= length) & (lane < length + 2 * half_band)
    under_sum = jnp.sum(jnp.where(under, rows, 0.0), axis=1, keepdims=True)
    over_sum = jnp.sum(jnp.where(over, rows, 0.0), axis=1, keepdims=True)
    span = -(-length // LANES) * LANES
    kept = lane[:, :span]
    body = jnp.where(kept < length, rows[:, :span], 0.0)
    body = body + jnp.where(kept == 0, under_sum, 0.0)
    return body + jnp.where(kept == length - 1, over_sum, 0.0)


def prepare_kernel(
    lengths, taps, sizes, rows0, rows1, arrivals, meta, weights, kron_hi, kron_lo, right3, wide0, wide1
):
    n_act, n_narrow, n_outer = sizes
    len0, len1, len2, len3 = lengths
    act, narrow, outer, core = (meta[i] for i in range(PLACE))
    actions = weights.shape[0]
    per_group = actions // n_act
    columns = len0 * len1

    def wrapped(index, size):
        return lax.rem(index + size, size)

    lane = lax.broadcasted_iota(jnp.int32, (1, columns), 1)
    ids0 = jnp.zeros((1, columns), jnp.int32)
    ids1 = jnp.zeros((1, columns), jnp.int32)
    for block, (far, part, ahead) in enumerate(arrivals):
        from_outer, from_core = outer ^ far, wrapped(core + part, 2)
        for row in range(rows0):
            start = (block * rows0 + row) * rows1
            inside = (lane >= start) & (lane < start + rows1)
            first = (from_outer * 2 + from_core) * rows0 + row
            second = wrapped(narrow - ahead, n_narrow) * rows1 - start
            ids0 = jnp.where(inside, first, ids0)
            ids1 = jnp.where(inside, second + lane, ids1)
    spread0 = (lax.broadcasted_iota(jnp.int32, (LANES, columns), 0) == ids0).astype(F32)
    spread1 = (lax.broadcasted_iota(jnp.int32, (LANES, columns), 0) == ids1).astype(F32)

    for action in range(actions):
        group, slot = divmod(action, per_group)
        which = meta[PLACE + wrapped(act + group, n_act) * per_group + slot]
        rows = weights[which]
        mats = [
            banded(
                rows[axis : axis + 1, :],
                meta[PLACE + (1 + axis) * actions + which],
                lengths[axis],
                taps,
            )
            for axis in (0, 1, 3)
        ]
        wide0[...] = dot32(mats[0], spread0)
        wide1[...] = dot32(mats[1], spread1)
        second = wide1[pl.ds(pl.multiple_of(narrow * rows1, SUBLANES), rows1), :]
        base = (outer * 2 + core) * rows0
        blocks = [wide0[pl.ds(base + row, 1), :] * second for row in range(rows0)]
        start = action * rows0 * rows1
        high, low = halves(jnp.concatenate(blocks, axis=0))
        kron_hi[start : start + rows0 * rows1, :] = high
        kron_lo[start : start + rows0 * rows1, :] = low
        high, low = halves(mats[2].T)
        row_pair = jnp.concatenate([high, low], axis=1)
        right3[action] = jnp.concatenate([row_pair, row_pair], axis=0)


def prepare_third_kernel(taps, n_act, meta, weights, third, fourth, left2, util23):
    act, actions, per_group = meta[0], weights.shape[0], left2.shape[0]
    len2, len3 = util23.shape[1:]
    share = len2 // n_act
    lane2 = lax.broadcasted_iota(jnp.int32, (1, len2), 1)
    ids2 = jnp.zeros((1, len2), jnp.int32)
    for group in range(n_act):
        inside = (lane2 >= group * share) & (lane2 < (group + 1) * share)
        ids2 = jnp.where(inside, (lax.rem(act + group, n_act) - group) * share + lane2, ids2)
    order2 = (lax.broadcasted_iota(jnp.int32, (len2, len2), 0) == ids2).astype(F32)

    for slot in range(per_group):
        which = meta[PLACE + act * per_group + slot]
        offset = meta[PLACE + 3 * actions + which]
        matrix = banded(weights[which][2:3, :], offset, len2, taps)
        high, low = halves(dot32(matrix, order2))
        left2[slot] = jnp.concatenate(
            [jnp.concatenate([high, high], axis=1), jnp.concatenate([low, low], axis=1)], axis=0
        )
        column = jnp.broadcast_to(third[pl.ds(which, 1), :], (len3, len2)).T
        util23[slot] = column + fourth[pl.ds(which, 1), :]


def short_dims_kernel(starts, groups, kron_hi, kron_lo, right3, *refs):
    pieces, keep, outs = refs[: len(starts)], refs[len(starts)], refs[len(starts) + 1 :]
    rows, depth = keep.shape[2:]
    actions = right3.shape[0]
    per_group = actions // groups
    per_out = keep.shape[1]
    per_piece = per_out // len(outs)
    q_hi, q_lo = kron_hi[...], kron_lo[...]
    mixed = []
    for row in range(0, rows, 2):
        cols = [
            jnp.concatenate(
                [piece[:, start + row + extra, :] for start, piece in zip(starts, pieces)], axis=0
            )
            for extra in range(2)
        ]
        x_hi, x_lo = halves(jnp.concatenate(cols, axis=1))
        out = (
            jnp.dot(q_hi, x_hi, preferred_element_type=F32)
            + jnp.dot(q_hi, x_lo, preferred_element_type=F32)
            + jnp.dot(q_lo, x_hi, preferred_element_type=F32)
        )
        mixed += [out[:, :depth], out[:, depth:]]
    for action in range(actions):
        group, slot = divmod(action, per_group)
        start = action * per_out
        block = jnp.concatenate([one[start : start + per_out] for one in mixed], axis=0)
        t_hi, t_lo = halves(block)
        both = jnp.dot(
            jnp.concatenate([t_hi, t_lo], axis=1), right3[action], preferred_element_type=F32
        )
        done = both[:, :depth] + both[:, depth:]
        for row in range(rows):
            start = row * per_out
            if group == 0:
                keep[slot, :, row, :] = done[start : start + per_out]
                continue
            for index, out in enumerate(outs):
                first = start + index * per_piece
                out[slot, :, row, :] = done[first : first + per_piece]


def third_dim_kernel(n_pieces, rows0, row, meta, costs0, costs1, left2, util23, *refs):
    pieces, scores, local = refs[:n_pieces], refs[n_pieces], refs[n_pieces + 1]
    per_group, rows1 = scores.shape[:2]
    length = util23.shape[1]
    depth = util23.shape[2]
    which = [meta[PLACE + meta[0] * per_group + slot] for slot in range(per_group)]
    first = (meta[2] * 2 + meta[3]) * rows0 + row
    start1 = meta[1] * rows1
    for second in range(0, rows1, 2):
        for slot in range(per_group):
            cols = [
                jnp.concatenate([piece[slot, second + extra] for piece in pieces], axis=0)
                for extra in range(2)
            ]
            g_hi, g_lo = halves(jnp.concatenate(cols, axis=1))
            both = jnp.dot(
                left2[slot], jnp.concatenate([g_hi, g_lo], axis=0), preferred_element_type=F32
            )
            expected = both[:length] + both[length:]
            for extra in range(2):
                flat = costs0[which[slot], first] + costs1[which[slot], start1 + second + extra]
                scores[slot, second + extra] = (util23[slot] + flat) + DISCOUNT * expected[
                    :, extra * depth : (extra + 1) * depth
                ]
        for extra in range(2):
            found = [scores[slot, second + extra] for slot in range(per_group)]
            top = functools.reduce(jnp.maximum, found)
            total = functools.reduce(jnp.add, [jnp.exp(one - top) for one in found])
            local[second + extra] = top + jnp.log(total)


def choice_kernel(scores, mine, other, *refs):
    new_value, choice_prob = refs[-2:]
    a, b = mine[...], other[...]
    top, low = jnp.maximum(a, b), jnp.minimum(a, b)
    total = top + jnp.log(1.0 + jnp.exp(low - top))
    new_value[0] = total
    for slot in range(scores.shape[0]):
        choice_prob[slot, 0] = jnp.exp(scores[slot] - total).astype(choice_prob.dtype)


def after(value, *done):
    return lax.optimization_barrier((value, *done))[0] if done else value


def whole_block():
    return pl.BlockSpec(memory_space=pltpu.VMEM)


def params(mebibytes):
    return pltpu.CompilerParams(vmem_limit_bytes=mebibytes * MIB)


def gather_body(
    value_now,
    cost_first,
    cost_second,
    cost_third,
    cost_fourth,
    trans_weights,
    trans_offsets,
    action_order,
):
    n_act, n_narrow, n_wide = (lax.axis_size(name) for name in ("act", "narrow", "wide"))
    n_outer = n_wide // 2
    act, narrow, wide = (lax.axis_index(name) for name in ("act", "narrow", "wide"))
    outer, core = wide // 2, wide % 2
    actions, _, taps = trans_weights.shape
    per_group = actions // n_act
    rows0, rows1, len2, len3 = value_now.shape
    len0, len1 = rows0 * n_wide, rows1 * n_narrow
    lengths = (len0, len1, len2, len3)
    share = len2 // n_act
    sizes = chunk_sizes(share)
    n_chunks = len(sizes)
    begins = [sum(sizes[:index]) for index in range(n_chunks)]
    core_flip = [(i, i ^ 1) for i in range(n_wide)]
    act_flip = [(i, (i + 1) % n_act) for i in range(n_act)]
    narrow_hops = [
        [(i, (i + step) % n_narrow) for i in range(n_narrow)] for step in range(1, n_narrow)
    ]

    def across(bit):
        return [(i, i ^ (2 * bit)) for i in range(n_wide)]

    def part(begin, size):
        return lax.dynamic_slice_in_dim(value_now, act * share + begin, size, 2)

    near = [(0, other, ahead) for ahead in range(n_narrow) for other in range(2)]
    arrivals = near + [
        (far, other, ahead)
        for ahead in range(n_narrow)
        for other in range(2)
        for far in range(1, n_outer)
    ]

    half_band = (taps - 1) // 2
    width = -(-(max(lengths) + 4 * half_band) // LANES) * LANES
    weights = jnp.pad(trans_weights, ((0, 0), (0, 0), (0, width - taps)))
    place = jnp.stack([act, narrow, outer, core]).astype(jnp.int32)
    meta = jnp.concatenate([place, action_order, trans_offsets.T.reshape(-1)])
    smem = pl.BlockSpec(memory_space=pltpu.SMEM)
    q_rows = actions * rows0 * rows1
    kron_hi, kron_lo, right3 = pl.pallas_call(
        functools.partial(
            prepare_kernel, lengths, taps, (n_act, n_narrow, n_outer), rows0, rows1, arrivals
        ),
        out_shape=(
            jax.ShapeDtypeStruct((q_rows, len0 * len1), BF16),
            jax.ShapeDtypeStruct((q_rows, len0 * len1), BF16),
            jax.ShapeDtypeStruct((actions, 2 * len3, 2 * len3), BF16),
        ),
        in_specs=[smem, whole_block()],
        out_specs=(whole_block(),) * 3,
        scratch_shapes=[pltpu.VMEM((len0, len0 * len1), F32), pltpu.VMEM((len1, len0 * len1), F32)],
        compiler_params=params(16),
        cost_estimate=pl.CostEstimate(flops=10**9, bytes_accessed=4 * 10**6, transcendentals=0),
        name="prepare",
    )(meta, weights)
    left2, util23 = pl.pallas_call(
        functools.partial(prepare_third_kernel, taps, n_act),
        out_shape=(
            jax.ShapeDtypeStruct((per_group, 2 * len2, 2 * len2), BF16),
            jax.ShapeDtypeStruct((per_group, len2, len3), F32),
        ),
        in_specs=[smem] + [whole_block()] * 3,
        out_specs=(whole_block(),) * 2,
        compiler_params=params(12),
        cost_estimate=pl.CostEstimate(flops=10**9, bytes_accessed=4 * 10**6, transcendentals=0),
        name="prepare_third",
    )(meta, weights, cost_third, cost_fourth)

    chunks = [part(begin, size) for begin, size in zip(begins, sizes)]
    half = part(0, share)
    direct = [lax.ppermute(chunks[0], "wide", across(far)) for far in range(1, n_outer)]
    around = [lax.ppermute(half, "narrow", hops) for hops in narrow_hops]
    soon = lax.ppermute(chunks[1], "wide", across(1))
    direct, *_ = lax.optimization_barrier((direct, kron_hi, right3))

    bits = [1 << bit for bit in range(1, n_outer.bit_length() - 1)]
    twins = [None, soon]
    fars = [jnp.concatenate(direct, axis=0)]
    nears = []
    kept, sent = [], []

    is_line = n_outer == 4
    inner = (outer == 1) | (outer == 2)
    inner_swap = [(2 * a + c, 2 * b + c) for a, b in ((1, 2), (2, 1)) for c in range(2)]
    outward = [(2 * a + c, 2 * b + c) for a, b in ((1, 0), (2, 3)) for c in range(2)]
    swapped = [None] * n_chunks

    def swap_inner(index):
        grown = jnp.concatenate([chunks[index], twins[index]], axis=0)
        grown = after(grown, *([swapped[index - 1]] if index > 1 else fars))
        swapped[index] = lax.ppermute(grown, "wide", inner_swap)

    def line(index, done):
        inward = swapped[index]
        if index + 1 < n_chunks:
            swap_inner(index + 1)
        passed = lax.ppermute(after(inward, fars[index - 1], *done), "wide", outward)
        parts = [
            twins[index],
            jnp.where(inner, inward[rows0:], passed[:rows0]),
            jnp.where(inner, inward[:rows0], passed[rows0:]),
        ]
        return jnp.concatenate(parts, axis=0)

    def doubled(index):
        grown = jnp.concatenate([chunks[index], twins[index]], axis=0)
        grown = after(grown, fars[index - 1])
        parts = [twins[index]]
        for bit in bits:
            parts.append(lax.ppermute(grown, "wide", across(bit)))
            if bit != bits[-1]:
                grown = jnp.concatenate([grown, parts[-1]], axis=0)
        return jnp.concatenate(parts, axis=0)

    far, moved = fars[0], around
    for index, size in enumerate(sizes):
        crossed = lax.ppermute(far, "wide", core_flip)
        if index == 0:
            late = lax.ppermute(after(part(begins[2], share - begins[2]), far), "wide", across(1))
            for begin, rows in zip(begins[2:], sizes[2:]):
                twins.append(late[:, :, begin - begins[2] : begin - begins[2] + rows])
        moved = [lax.ppermute(after(far, *moved), "narrow", hops) for hops in narrow_hops]
        if index == 0:
            sources = lax.optimization_barrier((half, *around, crossed))[:-1]
            for one, source in zip([half] + around, sources):
                nears += [one, lax.ppermute(source, "wide", core_flip)]
            nears = [one.reshape(rows0 * rows1, share, len3) for one in nears]
        if index == 0 and is_line:
            swap_inner(1)
        if index + 1 < n_chunks:
            done = moved if index == 0 else ()
            fars.append(line(index + 1, done) if is_line else doubled(index + 1))
        pieces = [far, crossed]
        for one in moved:
            ahead = fars[index + 1 :] + [one for one in swapped[index + 2 : index + 3] if is_line]
            pieces += [one, lax.ppermute(after(one, *ahead), "wide", core_flip)]
        pieces = [one.reshape(-1, size, len3) for one in pieces]
        starts = [begins[index]] * len(nears) + [0] * len(pieces)
        cuts = rows0 if index == n_chunks - 1 else 1
        cut_rows = [rows0 * rows1] + [rows0 * rows1 // cuts] * cuts
        keep, *for_act = pl.pallas_call(
            functools.partial(short_dims_kernel, starts, n_act),
            out_shape=tuple(
                jax.ShapeDtypeStruct((per_group, rows, size, len3), F32) for rows in cut_rows
            ),
            in_specs=[whole_block()] * (3 + len(starts)),
            out_specs=(whole_block(),) * len(cut_rows),
            compiler_params=params(12),
            cost_estimate=pl.CostEstimate(flops=10**6, bytes_accessed=10**4, transcendentals=0),
            name="short_dims",
        )(kron_hi, kron_lo, right3, *nears, *pieces)
        kept.append(keep)
        if index + 1 < n_chunks:
            far = fars[index + 1]
        before = [one for ones in sent[-1:] for one in ones]
        sent.append([lax.ppermute(after(one, *before), "act", act_flip) for one in for_act])

    parts = [(keep, True) for keep in kept] + [(ones[0], len(ones) == 1) for ones in sent]
    by_row = []
    for row in range(rows0):
        arrays = [one for one, _ in parts[:-1]] + [sent[-1][row]]
        specs = [
            pl.BlockSpec(
                (per_group, rows1) + one.shape[2:],
                lambda i, block=row if uncut else 0: (0, block, 0, 0),
            )
            for one, (_, uncut) in zip(arrays, parts)
        ]
        scores, local = pl.pallas_call(
            functools.partial(third_dim_kernel, len(parts), rows0, row),
            grid=(1,),
            out_shape=(
                jax.ShapeDtypeStruct((per_group, rows1, len2, len3), F32),
                jax.ShapeDtypeStruct((rows1, len2, len3), F32),
            ),
            in_specs=[smem] * 3 + [whole_block()] * 2 + specs,
            out_specs=(whole_block(),) * 2,
            compiler_params=params(20),
            cost_estimate=pl.CostEstimate(
                flops=10**9, bytes_accessed=5 * 10**6, transcendentals=10**6
            ),
            name="third_dim",
        )(meta, cost_first, cost_second, left2, util23, *arrays)
        by_row.append((scores, local, lax.ppermute(local, "act", act_flip)))

    results = ()
    for row, operands in enumerate(by_row):
        results = pl.pallas_call(
            choice_kernel,
            grid=(1,),
            out_shape=(
                jax.ShapeDtypeStruct(value_now.shape, F32),
                jax.ShapeDtypeStruct((per_group,) + value_now.shape, BF16),
            ),
            in_specs=[whole_block()] * 3 + [pl.BlockSpec(memory_space=pl.ANY)] * len(results),
            out_specs=(
                pl.BlockSpec((1, rows1, len2, len3), lambda i, row=row: (row, 0, 0, 0)),
                pl.BlockSpec(
                    (per_group, 1, rows1, len2, len3), lambda i, row=row: (0, row, 0, 0, 0)
                ),
            ),
            input_output_aliases={3: 0, 4: 1} if results else {},
            compiler_params=params(16),
            cost_estimate=pl.CostEstimate(
                flops=10**7, bytes_accessed=5 * 10**6, transcendentals=10**6
            ),
            name="choice",
        )(*operands, *results)
    return tuple(results)


def chunk_sizes(share):
    return [CHUNK_ROWS] * (share // CHUNK_ROWS)


def gather_fits(mesh, value_shape, actions, offset_reach):
    n_wide, n_narrow, n_act = (mesh.shape[name] for name in ("wide", "narrow", "act"))
    len0, len1, len2, len3 = value_shape
    if n_act != 2 or n_wide < 4 or n_wide & (n_wide - 1) or actions % n_act:
        return False
    if len2 % (n_act * CHUNK_ROWS) or len2 < 4 * n_act * CHUNK_ROWS:
        return False
    if len2 != LANES or len3 != LANES:
        return False
    if (len1 // n_narrow) % SUBLANES or len0 * len1 // (n_wide * n_narrow) % 16 or len0 % n_wide:
        return False
    if max(len0, len1) > LANES or len1 % n_narrow:
        return False
    raw = len0 * len1 * len2 * len3 // (2 * n_act)
    exchanged = 2 * (actions // n_act) * len0 * len1 * len2 * len3 // (n_wide * n_narrow)
    return raw <= exchanged


def solution(mesh):
    def run(value_now, *rest):
        actions = rest[-1].shape[0]
        small = gather_fits(mesh, value_now.shape, actions, rest[4].shape[-1])
        return jax.shard_map(
            gather_body if small else exchange_body,
            mesh=mesh,
            in_specs=(P("wide", "narrow", None, None), P(), P(), P(), P(), P(), P(), P()),
            out_specs=(P("wide", "narrow", None, None), P("act", "wide", "narrow", None, None)),
            check_vma=False,
        )(value_now, *rest)

    return run
```

```python
import functools

import jax
import jax.numpy as jnp
from jax import lax
from jax.experimental import pallas as pl
from jax.experimental.pallas import tpu as pltpu
from jax.sharding import PartitionSpec as P

DISCOUNT = 0.95
HIGHEST = lax.Precision.HIGHEST
F32 = jnp.float32
BF16 = jnp.bfloat16
LANES = 128
SUBLANES = 8
PLACE = 4
CHUNK_ROWS = 16
MIB = 1024 * 1024


def merged(value, axis, join):
    pieces = lax.all_gather(value, axis)
    head = pieces[0]
    tail = pieces[1:]
    subtotal, _ = lax.scan(lambda subtotal, slab: (join(subtotal, slab), None), head, tail)
    return subtotal


def transition(weights, offset, length):
    band_len = weights.shape[0]
    half_band = (band_len - 1) // 2
    normed = weights / jnp.sum(weights)
    row_ids = jnp.arange(length, dtype=jnp.int32)
    tap_ids = jnp.arange(band_len, dtype=jnp.int32)
    target = jnp.clip(row_ids[:, None] + offset + tap_ids[None, :] - half_band, 0, length - 1)
    matched = (target[:, :, None] == row_ids[None, None, :]).astype(normed.dtype)
    return jnp.einsum("ijk,j->ik", matched, normed, precision=HIGHEST)


def exchange_body(
    value_now,
    cost_first,
    cost_second,
    cost_third,
    cost_fourth,
    trans_weights,
    trans_offsets,
    action_order,
):
    size_act = lax.axis_size("act")
    per_group = action_order.shape[0] // size_act
    group_id = lax.axis_index("act")
    my_actions = lax.dynamic_slice_in_dim(action_order, group_id * per_group, per_group)
    rows_first, rows_second, len_third, len_fourth = value_now.shape
    len_first = rows_first * lax.axis_size("wide")
    len_second = rows_second * lax.axis_size("narrow")
    my_weights = jnp.take(trans_weights, my_actions, axis=0)
    my_offsets = jnp.take(trans_offsets, my_actions, axis=0)

    def build(axis_id, length):
        return jax.vmap(lambda weight_row, offset_one: transition(weight_row, offset_one, length))(
            my_weights[:, axis_id], my_offsets[:, axis_id]
        )

    mat_first = build(0, len_first)
    mat_second = build(1, len_second)
    mat_third = build(2, len_third)
    mat_fourth = build(3, len_fourth)
    spread = lax.all_to_all(value_now, "narrow", split_axis=2, concat_axis=1, tiled=True)
    field = jnp.einsum("gij,ajcd->gaicd", mat_second, spread, precision=HIGHEST)
    field = jnp.einsum("gij,gabcj->gabci", mat_fourth, field, precision=HIGHEST)
    field = lax.all_to_all(field, "narrow", split_axis=2, concat_axis=3, tiled=True)
    field = lax.all_to_all(field, "wide", split_axis=3, concat_axis=1, tiled=True)
    field = jnp.einsum("gij,gjbcd->gibcd", mat_first, field, precision=HIGHEST)
    field = lax.all_to_all(field, "wide", split_axis=1, concat_axis=3, tiled=True)
    expected = jnp.einsum("gij,gabjd->gabid", mat_third, field, precision=HIGHEST)
    start_first = lax.axis_index("wide") * rows_first
    start_second = lax.axis_index("narrow") * rows_second
    util_first = lax.dynamic_slice_in_dim(
        jnp.take(cost_first, my_actions, axis=0), start_first, rows_first, 1
    )
    util_second = lax.dynamic_slice_in_dim(
        jnp.take(cost_second, my_actions, axis=0), start_second, rows_second, 1
    )
    util_third = jnp.take(cost_third, my_actions, axis=0)
    util_fourth = jnp.take(cost_fourth, my_actions, axis=0)
    utility = (
        util_first[:, :, None, None, None]
        + util_second[:, None, :, None, None]
        + util_third[:, None, None, :, None]
        + util_fourth[:, None, None, None, :]
    )
    scores = utility + DISCOUNT * expected
    local_max = jnp.max(scores, axis=0)
    local_sum = jnp.sum(jnp.exp(scores - local_max), axis=0)
    log_total = merged(local_max + jnp.log(local_sum), "act", jnp.logaddexp)
    choice_prob = jnp.exp(scores - log_total).astype(jnp.bfloat16)
    return (log_total, choice_prob)


def halves(x):
    high = x.astype(BF16)
    return high, (x - high.astype(F32)).astype(BF16)


def dot32(a, b):
    return jnp.dot(a, b, preferred_element_type=F32, precision=HIGHEST)


def banded(weights, offset, length, taps):
    half_band = (taps - 1) // 2
    width = weights.shape[1]
    normed = weights / jnp.sum(weights, axis=1, keepdims=True)
    tile = jnp.broadcast_to(normed, (SUBLANES, width))
    tile = pltpu.roll(tile, lax.rem(offset + (width - half_band), width), 1)
    rows = jnp.concatenate([tile] * (length // SUBLANES), axis=0)
    rows = pltpu.roll(rows, 0, 1, stride=1, stride_axis=0)
    lane = lax.broadcasted_iota(jnp.int32, (length, width), 1)
    under = lane >= width - 2 * half_band
    over = (lane >= length) & (lane < length + 2 * half_band)
    under_sum = jnp.sum(jnp.where(under, rows, 0.0), axis=1, keepdims=True)
    over_sum = jnp.sum(jnp.where(over, rows, 0.0), axis=1, keepdims=True)
    span = -(-length // LANES) * LANES
    kept = lane[:, :span]
    body = jnp.where(kept < length, rows[:, :span], 0.0)
    body = body + jnp.where(kept == 0, under_sum, 0.0)
    return body + jnp.where(kept == length - 1, over_sum, 0.0)


def prepare_kernel(
    lengths, taps, sizes, rows0, rows1, arrivals, meta, weights,
    kron_hi, kron_lo, side_hi, side_lo, right3, wide0, wide1,
):
    n_act, n_narrow, n_outer = sizes
    len0, len1, len2, len3 = lengths
    act, narrow, outer, core = (meta[i] for i in range(PLACE))
    actions = weights.shape[0]
    per_group = actions // n_act
    columns = len0 * len1

    def wrapped(index, size):
        return lax.rem(index + size, size)

    lane = lax.broadcasted_iota(jnp.int32, (1, columns), 1)
    ids0 = jnp.zeros((1, columns), jnp.int32)
    ids1 = jnp.zeros((1, columns), jnp.int32)
    for block, (far, part, ahead) in enumerate(arrivals):
        from_outer, from_core = outer ^ far, wrapped(core + part, 2)
        for row in range(rows0):
            start = (block * rows0 + row) * rows1
            inside = (lane >= start) & (lane < start + rows1)
            first = (from_outer * 2 + from_core) * rows0 + row
            second = wrapped(narrow - ahead, n_narrow) * rows1 - start
            ids0 = jnp.where(inside, first, ids0)
            ids1 = jnp.where(inside, second + lane, ids1)
    spread0 = (lax.broadcasted_iota(jnp.int32, (LANES, columns), 0) == ids0).astype(F32)
    spread1 = (lax.broadcasted_iota(jnp.int32, (LANES, columns), 0) == ids1).astype(F32)

    for action in range(actions):
        group, slot = divmod(action, per_group)
        which = meta[PLACE + wrapped(act + group, n_act) * per_group + slot]
        rows = weights[which]
        mats = [
            banded(
                rows[axis : axis + 1, :],
                meta[PLACE + (1 + axis) * actions + which],
                lengths[axis],
                taps,
            )
            for axis in (0, 1, 3)
        ]
        wide0[...] = dot32(mats[0], spread0)
        wide1[...] = dot32(mats[1], spread1)
        base = (outer * 2 + core) * rows0
        for ahead in range(n_narrow if group == 0 else 1):
            begin = wrapped(narrow + ahead, n_narrow) * rows1
            second = wide1[pl.ds(pl.multiple_of(begin, SUBLANES), rows1), :]
            blocks = [wide0[pl.ds(base + row, 1), :] * second for row in range(rows0)]
            high, low = halves(jnp.concatenate(blocks, axis=0))
            if ahead == 0:
                start = action * rows0 * rows1
                kron_hi[start : start + rows0 * rows1, :] = high
                kron_lo[start : start + rows0 * rows1, :] = low
            if group == 0:
                start = (slot * n_narrow + ahead) * rows0 * rows1
                side_hi[start : start + rows0 * rows1, :] = high
                side_lo[start : start + rows0 * rows1, :] = low
        high, low = halves(mats[2].T)
        row_pair = jnp.concatenate([high, low], axis=1)
        right3[action] = jnp.concatenate([row_pair, row_pair], axis=0)


def prepare_third_kernel(taps, segments, meta, weights, third, fourth, left2, util23):
    act, actions, per_group = meta[0], weights.shape[0], left2.shape[0]
    len2, len3 = util23.shape[1:]
    lane2 = lax.broadcasted_iota(jnp.int32, (1, len2), 1)
    ids2 = jnp.zeros((1, len2), jnp.int32)
    filled = 0
    for begin, size, axis, ahead, count in segments:
        source = begin + lax.rem(meta[axis] + ahead, count) * size
        inside = (lane2 >= filled) & (lane2 < filled + size)
        ids2 = jnp.where(inside, source - filled + lane2, ids2)
        filled += size
    order2 = (lax.broadcasted_iota(jnp.int32, (len2, len2), 0) == ids2).astype(F32)

    for slot in range(per_group):
        which = meta[PLACE + act * per_group + slot]
        offset = meta[PLACE + 3 * actions + which]
        matrix = banded(weights[which][2:3, :], offset, len2, taps)
        high, low = halves(dot32(matrix, order2))
        left2[slot] = jnp.concatenate(
            [jnp.concatenate([high, high], axis=1), jnp.concatenate([low, low], axis=1)], axis=0
        )
        column = jnp.broadcast_to(third[pl.ds(which, 1), :], (len3, len2)).T
        util23[slot] = column + fourth[pl.ds(which, 1), :]


def short_dims_kernel(views, routes, kron_hi, kron_lo, right3, *refs):
    n_inputs = 1 + max(view[0] for view in views)
    inputs, outs = refs[:n_inputs], refs[n_inputs:]
    rows, depth = outs[0].shape[2:]
    per_action = kron_hi.shape[0] // len(routes)
    q_hi, q_lo = kron_hi[...], kron_lo[...]
    mixed = []
    for row in range(0, rows, 2):
        cols = [
            jnp.concatenate(
                [
                    inputs[which][lead : lead + count, start + row + extra, :]
                    for which, lead, count, start in views
                ],
                axis=0,
            )
            for extra in range(2)
        ]
        x_hi, x_lo = halves(jnp.concatenate(cols, axis=1))
        out = (
            jnp.dot(q_hi, x_hi, preferred_element_type=F32)
            + jnp.dot(q_hi, x_lo, preferred_element_type=F32)
            + jnp.dot(q_lo, x_hi, preferred_element_type=F32)
        )
        mixed += [out[:, :depth], out[:, depth:]]
    for action, route in enumerate(routes):
        start = action * per_action
        block = jnp.concatenate([one[start : start + per_action] for one in mixed], axis=0)
        t_hi, t_lo = halves(block)
        both = jnp.dot(
            jnp.concatenate([t_hi, t_lo], axis=1), right3[action], preferred_element_type=F32
        )
        done = both[:, :depth] + both[:, depth:]
        for row in range(rows):
            first = row * per_action
            for which, slot in route:
                count = outs[which].shape[1]
                outs[which][slot, :, row, :] = done[first : first + count]
                first += count


def third_dim_kernel(n_pieces, rows0, row, meta, costs0, costs1, left2, util23, *refs):
    pieces, scores, local = refs[:n_pieces], refs[n_pieces], refs[n_pieces + 1]
    per_group, rows1 = scores.shape[:2]
    length = util23.shape[1]
    depth = util23.shape[2]
    which = [meta[PLACE + meta[0] * per_group + slot] for slot in range(per_group)]
    first = (meta[2] * 2 + meta[3]) * rows0 + row
    start1 = meta[1] * rows1
    for second in range(0, rows1, 2):
        for slot in range(per_group):
            cols = [
                jnp.concatenate([piece[slot, second + extra] for piece in pieces], axis=0)
                for extra in range(2)
            ]
            g_hi, g_lo = halves(jnp.concatenate(cols, axis=1))
            both = jnp.dot(
                left2[slot], jnp.concatenate([g_hi, g_lo], axis=0), preferred_element_type=F32
            )
            expected = both[:length] + both[length:]
            for extra in range(2):
                flat = costs0[which[slot], first] + costs1[which[slot], start1 + second + extra]
                scores[slot, second + extra] = (util23[slot] + flat) + DISCOUNT * expected[
                    :, extra * depth : (extra + 1) * depth
                ]
        for extra in range(2):
            found = [scores[slot, second + extra] for slot in range(per_group)]
            top = functools.reduce(jnp.maximum, found)
            total = functools.reduce(jnp.add, [jnp.exp(one - top) for one in found])
            local[second + extra] = top + jnp.log(total)


def choice_kernel(scores, mine, other, *refs):
    new_value, choice_prob = refs[-2:]
    a, b = mine[...], other[...]
    top, low = jnp.maximum(a, b), jnp.minimum(a, b)
    total = top + jnp.log(1.0 + jnp.exp(low - top))
    new_value[0] = total
    for slot in range(scores.shape[0]):
        choice_prob[slot, 0] = jnp.exp(scores[slot] - total).astype(choice_prob.dtype)


def after(value, *done):
    return lax.optimization_barrier((value, *done))[0] if done else value


def whole_block():
    return pl.BlockSpec(memory_space=pltpu.VMEM)


def params(mebibytes):
    return pltpu.CompilerParams(vmem_limit_bytes=mebibytes * MIB)


def gather_body(
    value_now,
    cost_first,
    cost_second,
    cost_third,
    cost_fourth,
    trans_weights,
    trans_offsets,
    action_order,
):
    n_act, n_narrow, n_wide = (lax.axis_size(name) for name in ("act", "narrow", "wide"))
    n_outer = n_wide // 2
    act, narrow, wide = (lax.axis_index(name) for name in ("act", "narrow", "wide"))
    outer, core = wide // 2, wide % 2
    actions, _, taps = trans_weights.shape
    per_group = actions // n_act
    rows0, rows1, len2, len3 = value_now.shape
    len0, len1 = rows0 * n_wide, rows1 * n_narrow
    lengths = (len0, len1, len2, len3)
    chunk = CHUNK_ROWS
    share = (len2 - n_narrow * chunk) // n_act
    n_chunks = share // chunk
    core_flip = [(i, i ^ 1) for i in range(n_wide)]
    act_flip = [(i, (i + 1) % n_act) for i in range(n_act)]
    narrow_flip = [(i, (i + 1) % n_narrow) for i in range(n_narrow)]

    def across(bit):
        return [(i, i ^ (2 * bit)) for i in range(n_wide)]

    def part(begin, size):
        return lax.dynamic_slice_in_dim(value_now, begin, size, 2)

    near = [(0, other, ahead) for ahead in range(n_narrow) for other in range(2)]
    arrivals = near + [
        (far, other, ahead)
        for ahead in range(n_narrow)
        for other in range(2)
        for far in range(1, n_outer)
    ]

    half_band = (taps - 1) // 2
    width = -(-(max(lengths) + 4 * half_band) // LANES) * LANES
    weights = jnp.pad(trans_weights, ((0, 0), (0, 0), (0, width - taps)))
    place = jnp.stack([act, narrow, outer, core]).astype(jnp.int32)
    meta = jnp.concatenate([place, action_order, trans_offsets.T.reshape(-1)])
    smem = pl.BlockSpec(memory_space=pltpu.SMEM)
    q_rows = actions * rows0 * rows1
    kron_hi, kron_lo, side_hi, side_lo, right3 = pl.pallas_call(
        functools.partial(
            prepare_kernel, lengths, taps, (n_act, n_narrow, n_outer), rows0, rows1, arrivals
        ),
        out_shape=(
            jax.ShapeDtypeStruct((q_rows, len0 * len1), BF16),
            jax.ShapeDtypeStruct((q_rows, len0 * len1), BF16),
            jax.ShapeDtypeStruct((q_rows * n_narrow // n_act, len0 * len1), BF16),
            jax.ShapeDtypeStruct((q_rows * n_narrow // n_act, len0 * len1), BF16),
            jax.ShapeDtypeStruct((actions, 2 * len3, 2 * len3), BF16),
        ),
        in_specs=[smem, whole_block()],
        out_specs=(whole_block(),) * 5,
        scratch_shapes=[pltpu.VMEM((len0, len0 * len1), F32), pltpu.VMEM((len1, len0 * len1), F32)],
        compiler_params=params(16),
        cost_estimate=pl.CostEstimate(flops=10**9, bytes_accessed=4 * 10**6, transcendentals=0),
        name="prepare",
    )(meta, weights)
    segments = [(0, share, 0, ahead, n_act) for ahead in range(n_act)]
    segments += [(n_act * share, chunk, 1, ahead, n_narrow) for ahead in range(n_narrow)]
    left2, util23 = pl.pallas_call(
        functools.partial(prepare_third_kernel, taps, segments),
        out_shape=(
            jax.ShapeDtypeStruct((per_group, 2 * len2, 2 * len2), BF16),
            jax.ShapeDtypeStruct((per_group, len2, len3), F32),
        ),
        in_specs=[smem] + [whole_block()] * 3,
        out_specs=(whole_block(),) * 2,
        compiler_params=params(12),
        cost_estimate=pl.CostEstimate(flops=10**9, bytes_accessed=4 * 10**6, transcendentals=0),
        name="prepare_third",
    )(meta, weights, cost_third, cost_fourth)

    chunks = [part(act * share + index * chunk, chunk) for index in range(n_chunks)]
    side_begin = n_act * share
    to_narrow = jnp.concatenate(
        [part(act * share, share), part(side_begin + (n_narrow - 1 - narrow) * chunk, chunk)], axis=2
    )
    own_side = part(side_begin + narrow * chunk, chunk)
    mine = jnp.concatenate([part(act * share, share), own_side], axis=2)
    direct = [lax.ppermute(chunks[0], "wide", across(far)) for far in range(1, n_outer)]
    around = lax.ppermute(to_narrow, "narrow", narrow_flip)
    twin = lax.ppermute(chunks[1], "wide", across(1))
    direct, *_ = lax.optimization_barrier((direct, kron_hi, right3))
    side = jnp.concatenate([own_side, around[:, :, share:]], axis=0)

    bits = [1 << bit for bit in range(1, n_outer.bit_length() - 1)]
    is_line = n_outer == 4
    inner = (outer == 1) | (outer == 2)
    inner_swap = [(2 * a + c, 2 * b + c) for a, b in ((1, 2), (2, 1)) for c in range(2)]
    outward = [(2 * a + c, 2 * b + c) for a, b in ((1, 0), (2, 3)) for c in range(2)]

    def spread_first(own, twin, *done):
        grown = after(jnp.concatenate([own, twin], axis=0), *done)
        return lax.ppermute(grown, "wide", inner_swap if is_line else across(bits[0]))

    def spread_rest(own, twin, came, *done):
        size = own.shape[0]
        if is_line:
            passed = lax.ppermute(after(came, *done), "wide", outward)
            return [
                twin,
                jnp.where(inner, came[size:], passed[:size]),
                jnp.where(inner, came[:size], passed[size:]),
            ]
        blocks = [own, twin] + [came[i : i + size] for i in range(0, came.shape[0], size)]
        for bit in bits[1:]:
            more = lax.ppermute(jnp.concatenate(blocks, axis=0), "wide", across(bit))
            blocks += [more[i : i + size] for i in range(0, more.shape[0], size)]
        return blocks[1:]

    far0 = jnp.concatenate(direct, axis=0)
    came1 = spread_first(chunks[1], twin, far0)
    crossed = [lax.ppermute(far0, "wide", core_flip)]
    moved = [lax.ppermute(after(far0, around), "narrow", narrow_flip)]
    twins = lax.ppermute(
        jnp.concatenate([after(one, far0) for one in chunks[2:]] + [side], axis=0), "wide", across(1)
    )
    twins = [twins[i * rows0 : (i + 1) * rows0] for i in range(n_chunks - 2)] + [
        twins[(n_chunks - 2) * rows0 :]
    ]
    nears = [mine, lax.ppermute(mine, "wide", core_flip)]
    nears += [around, lax.ppermute(around, "wide", core_flip)]
    nears = [one.reshape(rows0 * rows1, share + chunk, len3) for one in nears]
    def contract(kron, views, routes, out_rows, inputs):
        return pl.pallas_call(
            functools.partial(short_dims_kernel, views, routes),
            out_shape=tuple(
                jax.ShapeDtypeStruct((per_group, rows, chunk, len3), F32) for rows in out_rows
            ),
            in_specs=[whole_block()] * (3 + len(inputs)),
            out_specs=(whole_block(),) * len(out_rows),
            compiler_params=params(12),
            cost_estimate=pl.CostEstimate(flops=10**6, bytes_accessed=10**4, transcendentals=0),
            name="short_dims",
        )(*kron, right3, *inputs)

    block_rows = rows0 * rows1
    far_rows = (n_outer - 1) * block_rows
    owns, twins = chunks + [side], [None, twin] + twins
    came, fars = [None, came1], [far0]
    kept, sent = [], []
    for index in range(n_chunks):
        far = fars[index]
        if index:
            far = after(far, *(came[index + 1 :] if index > 1 else ()))
            crossed.append(lax.ppermute(far, "wide", core_flip))
            moved.append(lax.ppermute(after(far, moved[-1]), "narrow", narrow_flip))
        done = [fars[index]] + (kept[:1] if index == 1 else moved[max(index - 1, 0) : max(index, 1)])
        blocks = spread_rest(owns[index + 1], twins[index + 1], came[index + 1], *done)
        fars.append(jnp.concatenate(blocks, axis=0))
        if index == 0:
            ready = [came1, crossed[0], *nears]
        else:
            ready = fars[-1:] + kept[-1:] if index == n_chunks - 1 else sent[index - 1]
        handed = lax.ppermute(after(moved[index], *ready), "wide", core_flip)
        if index + 2 <= n_chunks:
            done = [came[index + 1]] + (kept[index - 1 : index] if index else [handed])
            came.append(spread_first(owns[index + 2], twins[index + 2], *done))
        pieces = [far, crossed[index], moved[index], handed]
        inputs = nears + [one.reshape(far_rows, chunk, len3) for one in pieces]
        views = [(i, 0, block_rows, index * chunk) for i in range(len(nears))]
        views += [(len(nears) + i, 0, far_rows, 0) for i in range(len(pieces))]
        cuts = rows0 if index == n_chunks - 1 else 1
        routes = [[(0, slot)] for slot in range(per_group)]
        routes += [[(1 + cut, slot) for cut in range(cuts)] for slot in range(per_group)]
        out_rows = [block_rows] + [block_rows // cuts] * cuts
        keep, *for_act = contract((kron_hi, kron_lo), views, routes, out_rows, inputs)
        kept.append(keep)
        sent.append([])
        for one in for_act:
            before = [one for ones in sent for one in ones][-1:]
            sent[-1].append(lax.ppermute(after(one, *before), "act", act_flip))

    sides = []
    for ahead in range(n_narrow):
        own = [one[ahead * rows0 : (ahead + 1) * rows0] for one in blocks]
        own = jnp.concatenate(own, axis=0)
        sides += [own, lax.ppermute(after(own, moved[-1], kept[-2]), "wide", core_flip)]
    inputs = nears + [one.reshape(far_rows, chunk, len3) for one in sides]
    views = [(i, 0, block_rows, share) for i in range(len(nears))]
    views += [(len(nears) + i, 0, far_rows, 0) for i in range(len(sides))]
    routes = [[(out, slot) for out in range(1 + rows0)] for slot in range(per_group)]
    out_rows = [block_rows] + [block_rows // rows0] * rows0
    side_keep, *side_give = contract((side_hi, side_lo), views, routes, out_rows, inputs)
    side_got = [lax.ppermute(one, "narrow", narrow_flip) for one in side_give]

    parts = [(keep, None) for keep in kept] + [(ones[0], None) for ones in sent[:-1]]
    parts += [(sent[-1][0], sent[-1]), (side_keep, None), (side_got[0], side_got)]
    by_row = []
    for row in range(rows0):
        arrays = [cut[row] if cut else one for one, cut in parts]
        specs = [
            pl.BlockSpec(
                (per_group, rows1) + one.shape[2:],
                lambda i, block=0 if cut else row: (0, block, 0, 0),
            )
            for one, (_, cut) in zip(arrays, parts)
        ]
        scores, local = pl.pallas_call(
            functools.partial(third_dim_kernel, len(parts), rows0, row),
            grid=(1,),
            out_shape=(
                jax.ShapeDtypeStruct((per_group, rows1, len2, len3), F32),
                jax.ShapeDtypeStruct((rows1, len2, len3), F32),
            ),
            in_specs=[smem] * 3 + [whole_block()] * 2 + specs,
            out_specs=(whole_block(),) * 2,
            compiler_params=params(20),
            cost_estimate=pl.CostEstimate(
                flops=10**9, bytes_accessed=5 * 10**6, transcendentals=10**6
            ),
            name="third_dim",
        )(meta, cost_first, cost_second, left2, util23, *arrays)
        by_row.append((scores, local, lax.ppermute(local, "act", act_flip)))

    results = ()
    for row, operands in enumerate(by_row):
        results = pl.pallas_call(
            choice_kernel,
            grid=(1,),
            out_shape=(
                jax.ShapeDtypeStruct(value_now.shape, F32),
                jax.ShapeDtypeStruct((per_group,) + value_now.shape, BF16),
            ),
            in_specs=[whole_block()] * 3 + [pl.BlockSpec(memory_space=pl.ANY)] * len(results),
            out_specs=(
                pl.BlockSpec((1, rows1, len2, len3), lambda i, row=row: (row, 0, 0, 0)),
                pl.BlockSpec(
                    (per_group, 1, rows1, len2, len3), lambda i, row=row: (0, row, 0, 0, 0)
                ),
            ),
            input_output_aliases={3: 0, 4: 1} if results else {},
            compiler_params=params(16),
            cost_estimate=pl.CostEstimate(
                flops=10**7, bytes_accessed=5 * 10**6, transcendentals=10**6
            ),
            name="choice",
        )(*operands, *results)
    return tuple(results)


def gather_fits(mesh, value_shape, actions, offset_reach):
    n_wide, n_narrow, n_act = (mesh.shape[name] for name in ("wide", "narrow", "act"))
    len0, len1, len2, len3 = value_shape
    if n_act != 2 or n_wide < 4 or n_wide & (n_wide - 1) or actions % n_act:
        return False
    if n_narrow != 2 or len2 % (n_act * CHUNK_ROWS) or len2 < 4 * n_act * CHUNK_ROWS:
        return False
    if len2 != LANES or len3 != LANES:
        return False
    if (len1 // n_narrow) % SUBLANES or len0 * len1 // (n_wide * n_narrow) % 16 or len0 % n_wide:
        return False
    if max(len0, len1) > LANES or len1 % n_narrow:
        return False
    raw = len0 * len1 * len2 * len3 // (2 * n_act)
    exchanged = 2 * (actions // n_act) * len0 * len1 * len2 * len3 // (n_wide * n_narrow)
    return raw <= exchanged


def solution(mesh):
    def run(value_now, *rest):
        actions = rest[-1].shape[0]
        small = gather_fits(mesh, value_now.shape, actions, rest[4].shape[-1])
        return jax.shard_map(
            gather_body if small else exchange_body,
            mesh=mesh,
            in_specs=(P("wide", "narrow", None, None), P(), P(), P(), P(), P(), P(), P()),
            out_specs=(P("wide", "narrow", None, None), P("act", "wide", "narrow", None, None)),
            check_vma=False,
        )(value_now, *rest)

    return run
```

```python
import functools

import jax
import jax.numpy as jnp
from jax import lax
from jax.experimental import pallas as pl
from jax.experimental.pallas import tpu as pltpu
from jax.sharding import PartitionSpec as P

DISCOUNT = 0.95
HIGHEST = lax.Precision.HIGHEST
F32 = jnp.float32
BF16 = jnp.bfloat16
LANES = 128
SUBLANES = 8
PLACE = 4
CHUNK_ROWS = 16
MIB = 1024 * 1024


def merged(value, axis, join):
    pieces = lax.all_gather(value, axis)
    head = pieces[0]
    tail = pieces[1:]
    subtotal, _ = lax.scan(lambda subtotal, slab: (join(subtotal, slab), None), head, tail)
    return subtotal


def transition(weights, offset, length):
    band_len = weights.shape[0]
    half_band = (band_len - 1) // 2
    normed = weights / jnp.sum(weights)
    row_ids = jnp.arange(length, dtype=jnp.int32)
    tap_ids = jnp.arange(band_len, dtype=jnp.int32)
    target = jnp.clip(row_ids[:, None] + offset + tap_ids[None, :] - half_band, 0, length - 1)
    matched = (target[:, :, None] == row_ids[None, None, :]).astype(normed.dtype)
    return jnp.einsum("ijk,j->ik", matched, normed, precision=HIGHEST)


def exchange_body(
    value_now,
    cost_first,
    cost_second,
    cost_third,
    cost_fourth,
    trans_weights,
    trans_offsets,
    action_order,
):
    size_act = lax.axis_size("act")
    per_group = action_order.shape[0] // size_act
    group_id = lax.axis_index("act")
    my_actions = lax.dynamic_slice_in_dim(action_order, group_id * per_group, per_group)
    rows_first, rows_second, len_third, len_fourth = value_now.shape
    len_first = rows_first * lax.axis_size("wide")
    len_second = rows_second * lax.axis_size("narrow")
    my_weights = jnp.take(trans_weights, my_actions, axis=0)
    my_offsets = jnp.take(trans_offsets, my_actions, axis=0)

    def build(axis_id, length):
        return jax.vmap(lambda weight_row, offset_one: transition(weight_row, offset_one, length))(
            my_weights[:, axis_id], my_offsets[:, axis_id]
        )

    mat_first = build(0, len_first)
    mat_second = build(1, len_second)
    mat_third = build(2, len_third)
    mat_fourth = build(3, len_fourth)
    spread = lax.all_to_all(value_now, "narrow", split_axis=2, concat_axis=1, tiled=True)
    field = jnp.einsum("gij,ajcd->gaicd", mat_second, spread, precision=HIGHEST)
    field = jnp.einsum("gij,gabcj->gabci", mat_fourth, field, precision=HIGHEST)
    field = lax.all_to_all(field, "narrow", split_axis=2, concat_axis=3, tiled=True)
    field = lax.all_to_all(field, "wide", split_axis=3, concat_axis=1, tiled=True)
    field = jnp.einsum("gij,gjbcd->gibcd", mat_first, field, precision=HIGHEST)
    field = lax.all_to_all(field, "wide", split_axis=1, concat_axis=3, tiled=True)
    expected = jnp.einsum("gij,gabjd->gabid", mat_third, field, precision=HIGHEST)
    start_first = lax.axis_index("wide") * rows_first
    start_second = lax.axis_index("narrow") * rows_second
    util_first = lax.dynamic_slice_in_dim(
        jnp.take(cost_first, my_actions, axis=0), start_first, rows_first, 1
    )
    util_second = lax.dynamic_slice_in_dim(
        jnp.take(cost_second, my_actions, axis=0), start_second, rows_second, 1
    )
    util_third = jnp.take(cost_third, my_actions, axis=0)
    util_fourth = jnp.take(cost_fourth, my_actions, axis=0)
    utility = (
        util_first[:, :, None, None, None]
        + util_second[:, None, :, None, None]
        + util_third[:, None, None, :, None]
        + util_fourth[:, None, None, None, :]
    )
    scores = utility + DISCOUNT * expected
    local_max = jnp.max(scores, axis=0)
    local_sum = jnp.sum(jnp.exp(scores - local_max), axis=0)
    log_total = merged(local_max + jnp.log(local_sum), "act", jnp.logaddexp)
    choice_prob = jnp.exp(scores - log_total).astype(jnp.bfloat16)
    return (log_total, choice_prob)


def halves(x):
    high = x.astype(BF16)
    return high, (x - high.astype(F32)).astype(BF16)


def dot32(a, b):
    return jnp.dot(a, b, preferred_element_type=F32, precision=HIGHEST)


def banded(weights, offset, length, taps):
    half_band = (taps - 1) // 2
    width = weights.shape[1]
    normed = weights / jnp.sum(weights, axis=1, keepdims=True)
    tile = jnp.broadcast_to(normed, (SUBLANES, width))
    tile = pltpu.roll(tile, lax.rem(offset + (width - half_band), width), 1)
    rows = jnp.concatenate([tile] * (length // SUBLANES), axis=0)
    rows = pltpu.roll(rows, 0, 1, stride=1, stride_axis=0)
    lane = lax.broadcasted_iota(jnp.int32, (length, width), 1)
    under = lane >= width - 2 * half_band
    over = (lane >= length) & (lane < length + 2 * half_band)
    under_sum = jnp.sum(jnp.where(under, rows, 0.0), axis=1, keepdims=True)
    over_sum = jnp.sum(jnp.where(over, rows, 0.0), axis=1, keepdims=True)
    span = -(-length // LANES) * LANES
    kept = lane[:, :span]
    body = jnp.where(kept < length, rows[:, :span], 0.0)
    body = body + jnp.where(kept == 0, under_sum, 0.0)
    return body + jnp.where(kept == length - 1, over_sum, 0.0)


def prepare_kernel(
    lengths, taps, sizes, rows0, rows1, arrivals, meta, weights,
    kron_hi, kron_lo, side_hi, side_lo, right3, wide0, wide1,
):
    n_act, n_narrow, n_outer = sizes
    len0, len1, len2, len3 = lengths
    act, narrow, outer, core = (meta[i] for i in range(PLACE))
    actions = weights.shape[0]
    per_group = actions // n_act
    columns = len0 * len1

    def wrapped(index, size):
        return lax.rem(index + size, size)

    lane = lax.broadcasted_iota(jnp.int32, (1, columns), 1)
    ids0 = jnp.zeros((1, columns), jnp.int32)
    ids1 = jnp.zeros((1, columns), jnp.int32)
    for block, (far, part, ahead) in enumerate(arrivals):
        from_outer, from_core = outer ^ far, wrapped(core + part, 2)
        for row in range(rows0):
            start = (block * rows0 + row) * rows1
            inside = (lane >= start) & (lane < start + rows1)
            first = (from_outer * 2 + from_core) * rows0 + row
            second = wrapped(narrow - ahead, n_narrow) * rows1 - start
            ids0 = jnp.where(inside, first, ids0)
            ids1 = jnp.where(inside, second + lane, ids1)
    spread0 = (lax.broadcasted_iota(jnp.int32, (LANES, columns), 0) == ids0).astype(F32)
    spread1 = (lax.broadcasted_iota(jnp.int32, (LANES, columns), 0) == ids1).astype(F32)

    for action in range(actions):
        group, slot = divmod(action, per_group)
        which = meta[PLACE + wrapped(act + group, n_act) * per_group + slot]
        rows = weights[which]
        mats = [
            banded(
                rows[axis : axis + 1, :],
                meta[PLACE + (1 + axis) * actions + which],
                lengths[axis],
                taps,
            )
            for axis in (0, 1, 3)
        ]
        wide0[...] = dot32(mats[0], spread0)
        wide1[...] = dot32(mats[1], spread1)
        base = (outer * 2 + core) * rows0
        for ahead in range(n_narrow if group == 0 else 1):
            begin = wrapped(narrow + ahead, n_narrow) * rows1
            second = wide1[pl.ds(pl.multiple_of(begin, SUBLANES), rows1), :]
            blocks = [wide0[pl.ds(base + row, 1), :] * second for row in range(rows0)]
            high, low = halves(jnp.concatenate(blocks, axis=0))
            if ahead == 0:
                start = action * rows0 * rows1
                kron_hi[start : start + rows0 * rows1, :] = high
                kron_lo[start : start + rows0 * rows1, :] = low
            if group == 0:
                start = (slot * n_narrow + ahead) * rows0 * rows1
                side_hi[start : start + rows0 * rows1, :] = high
                side_lo[start : start + rows0 * rows1, :] = low
        high, low = halves(mats[2].T)
        row_pair = jnp.concatenate([high, low], axis=1)
        right3[action] = jnp.concatenate([row_pair, row_pair], axis=0)


def prepare_third_kernel(taps, segments, meta, weights, third, fourth, left2, util23):
    act, actions, per_group = meta[0], weights.shape[0], left2.shape[0]
    len2, len3 = util23.shape[1:]
    lane2 = lax.broadcasted_iota(jnp.int32, (1, len2), 1)
    ids2 = jnp.zeros((1, len2), jnp.int32)
    filled = 0
    for begin, size, axis, ahead, count in segments:
        source = begin + lax.rem(meta[axis] + ahead, count) * size
        inside = (lane2 >= filled) & (lane2 < filled + size)
        ids2 = jnp.where(inside, source - filled + lane2, ids2)
        filled += size
    order2 = (lax.broadcasted_iota(jnp.int32, (len2, len2), 0) == ids2).astype(F32)

    for slot in range(per_group):
        which = meta[PLACE + act * per_group + slot]
        offset = meta[PLACE + 3 * actions + which]
        matrix = banded(weights[which][2:3, :], offset, len2, taps)
        high, low = halves(dot32(matrix, order2))
        left2[slot] = jnp.concatenate(
            [jnp.concatenate([high, high], axis=1), jnp.concatenate([low, low], axis=1)], axis=0
        )
        column = jnp.broadcast_to(third[pl.ds(which, 1), :], (len3, len2)).T
        util23[slot] = column + fourth[pl.ds(which, 1), :]


def short_dims_kernel(views, routes, kron_hi, kron_lo, right3, *refs):
    n_inputs = 1 + max(view[0] for view in views)
    inputs, outs = refs[:n_inputs], refs[n_inputs:]
    rows, depth = outs[0].shape[2:]
    per_action = kron_hi.shape[0] // len(routes)
    q_hi, q_lo = kron_hi[...], kron_lo[...]
    mixed = []
    for row in range(0, rows, 2):
        cols = [
            jnp.concatenate(
                [
                    inputs[which][lead : lead + count, start + row + extra, :]
                    for which, lead, count, start in views
                ],
                axis=0,
            )
            for extra in range(2)
        ]
        x_hi, x_lo = halves(jnp.concatenate(cols, axis=1))
        out = (
            jnp.dot(q_hi, x_hi, preferred_element_type=F32)
            + jnp.dot(q_hi, x_lo, preferred_element_type=F32)
            + jnp.dot(q_lo, x_hi, preferred_element_type=F32)
        )
        mixed += [out[:, :depth], out[:, depth:]]
    for action, route in enumerate(routes):
        start = action * per_action
        block = jnp.concatenate([one[start : start + per_action] for one in mixed], axis=0)
        t_hi, t_lo = halves(block)
        both = jnp.dot(
            jnp.concatenate([t_hi, t_lo], axis=1), right3[action], preferred_element_type=F32
        )
        done = both[:, :depth] + both[:, depth:]
        for row in range(rows):
            first = row * per_action
            for which, slot in route:
                count = outs[which].shape[1]
                outs[which][slot, :, row, :] = done[first : first + count]
                first += count


def third_dim_kernel(n_pieces, rows0, row, meta, costs0, costs1, left2, util23, *refs):
    pieces, scores, local = refs[:n_pieces], refs[n_pieces], refs[n_pieces + 1]
    per_group, rows1 = scores.shape[:2]
    length = util23.shape[1]
    depth = util23.shape[2]
    which = [meta[PLACE + meta[0] * per_group + slot] for slot in range(per_group)]
    first = (meta[2] * 2 + meta[3]) * rows0 + row
    start1 = meta[1] * rows1
    for second in range(0, rows1, 2):
        for slot in range(per_group):
            cols = [
                jnp.concatenate([piece[slot, second + extra] for piece in pieces], axis=0)
                for extra in range(2)
            ]
            g_hi, g_lo = halves(jnp.concatenate(cols, axis=1))
            both = jnp.dot(
                left2[slot], jnp.concatenate([g_hi, g_lo], axis=0), preferred_element_type=F32
            )
            expected = both[:length] + both[length:]
            for extra in range(2):
                flat = costs0[which[slot], first] + costs1[which[slot], start1 + second + extra]
                scores[slot, second + extra] = (util23[slot] + flat) + DISCOUNT * expected[
                    :, extra * depth : (extra + 1) * depth
                ]
        for extra in range(2):
            found = [scores[slot, second + extra] for slot in range(per_group)]
            top = functools.reduce(jnp.maximum, found)
            total = functools.reduce(jnp.add, [jnp.exp(one - top) for one in found])
            local[second + extra] = top + jnp.log(total)


def choice_kernel(scores, mine, other, *refs):
    new_value, choice_prob = refs[-2:]
    a, b = mine[...], other[...]
    top, low = jnp.maximum(a, b), jnp.minimum(a, b)
    total = top + jnp.log(1.0 + jnp.exp(low - top))
    new_value[0] = total
    for slot in range(scores.shape[0]):
        choice_prob[slot, 0] = jnp.exp(scores[slot] - total).astype(choice_prob.dtype)


def after(value, *done):
    return lax.optimization_barrier((value, *done))[0] if done else value


def whole_block():
    return pl.BlockSpec(memory_space=pltpu.VMEM)


def params(mebibytes):
    return pltpu.CompilerParams(vmem_limit_bytes=mebibytes * MIB)


def gather_body(
    value_now,
    cost_first,
    cost_second,
    cost_third,
    cost_fourth,
    trans_weights,
    trans_offsets,
    action_order,
):
    n_act, n_narrow, n_wide = (lax.axis_size(name) for name in ("act", "narrow", "wide"))
    n_outer = n_wide // 2
    act, narrow, wide = (lax.axis_index(name) for name in ("act", "narrow", "wide"))
    outer, core = wide // 2, wide % 2
    actions, _, taps = trans_weights.shape
    per_group = actions // n_act
    rows0, rows1, len2, len3 = value_now.shape
    len0, len1 = rows0 * n_wide, rows1 * n_narrow
    lengths = (len0, len1, len2, len3)
    chunk = CHUNK_ROWS
    share = (len2 - n_narrow * chunk) // n_act
    n_chunks = share // chunk
    core_flip = [(i, i ^ 1) for i in range(n_wide)]
    act_flip = [(i, (i + 1) % n_act) for i in range(n_act)]
    narrow_flip = [(i, (i + 1) % n_narrow) for i in range(n_narrow)]

    def across(bit):
        return [(i, i ^ (2 * bit)) for i in range(n_wide)]

    def part(begin, size):
        return lax.dynamic_slice_in_dim(value_now, begin, size, 2)

    near = [(0, other, ahead) for ahead in range(n_narrow) for other in range(2)]
    arrivals = near + [
        (far, other, ahead)
        for ahead in range(n_narrow)
        for other in range(2)
        for far in range(1, n_outer)
    ]

    half_band = (taps - 1) // 2
    width = -(-(max(lengths) + 4 * half_band) // LANES) * LANES
    weights = jnp.pad(trans_weights, ((0, 0), (0, 0), (0, width - taps)))
    place = jnp.stack([act, narrow, outer, core]).astype(jnp.int32)
    meta = jnp.concatenate([place, action_order, trans_offsets.T.reshape(-1)])
    smem = pl.BlockSpec(memory_space=pltpu.SMEM)
    q_rows = actions * rows0 * rows1
    kron_hi, kron_lo, side_hi, side_lo, right3 = pl.pallas_call(
        functools.partial(
            prepare_kernel, lengths, taps, (n_act, n_narrow, n_outer), rows0, rows1, arrivals
        ),
        out_shape=(
            jax.ShapeDtypeStruct((q_rows, len0 * len1), BF16),
            jax.ShapeDtypeStruct((q_rows, len0 * len1), BF16),
            jax.ShapeDtypeStruct((q_rows * n_narrow // n_act, len0 * len1), BF16),
            jax.ShapeDtypeStruct((q_rows * n_narrow // n_act, len0 * len1), BF16),
            jax.ShapeDtypeStruct((actions, 2 * len3, 2 * len3), BF16),
        ),
        in_specs=[smem, whole_block()],
        out_specs=(whole_block(),) * 5,
        scratch_shapes=[pltpu.VMEM((len0, len0 * len1), F32), pltpu.VMEM((len1, len0 * len1), F32)],
        compiler_params=params(16),
        cost_estimate=pl.CostEstimate(flops=10**9, bytes_accessed=4 * 10**6, transcendentals=0),
        name="prepare",
    )(meta, weights)
    segments = [(0, share, 0, ahead, n_act) for ahead in range(n_act)]
    segments += [(n_act * share, chunk, 1, ahead, n_narrow) for ahead in range(n_narrow)]
    left2, util23 = pl.pallas_call(
        functools.partial(prepare_third_kernel, taps, segments),
        out_shape=(
            jax.ShapeDtypeStruct((per_group, 2 * len2, 2 * len2), BF16),
            jax.ShapeDtypeStruct((per_group, len2, len3), F32),
        ),
        in_specs=[smem] + [whole_block()] * 3,
        out_specs=(whole_block(),) * 2,
        compiler_params=params(12),
        cost_estimate=pl.CostEstimate(flops=10**9, bytes_accessed=4 * 10**6, transcendentals=0),
        name="prepare_third",
    )(meta, weights, cost_third, cost_fourth)

    side_begin = n_act * share
    inner = (outer == 1) | (outer == 2)
    value_now, inner, place, act_begin, own_begin, other_begin = lax.optimization_barrier(
        (
            value_now,
            inner,
            place,
            act * share,
            side_begin + narrow * chunk,
            side_begin + (n_narrow - 1 - narrow) * chunk,
        )
    )
    chunks = [part(act_begin + index * chunk, chunk) for index in range(n_chunks)]
    to_narrow = jnp.concatenate([part(act_begin, share), part(other_begin, chunk)], axis=2)
    own_side = part(own_begin, chunk)
    mine = jnp.concatenate([part(act_begin, share), own_side], axis=2)
    direct = [lax.ppermute(chunks[0], "wide", across(far)) for far in range(1, n_outer)]
    around = lax.ppermute(to_narrow, "narrow", narrow_flip)
    soon = lax.ppermute(part(act_begin + chunk, share - chunk), "wide", across(1))
    direct, *_ = lax.optimization_barrier((direct, kron_hi, right3))
    side = jnp.concatenate([own_side, around[:, :, share:]], axis=0)

    bits = [1 << bit for bit in range(1, n_outer.bit_length() - 1)]

    def doubled(own, twin, *done):
        size = own.shape[0]
        blocks = [own, twin]
        for bit in bits:
            grown = after(jnp.concatenate(blocks, axis=0), *done)
            more = lax.ppermute(grown, "wide", across(bit))
            blocks += [more[i : i + size] for i in range(0, more.shape[0], size)]
        return blocks[1:]

    inner_swap = [(2 * a + c, 2 * b + c) for a, b in ((1, 2), (2, 1)) for c in range(2)]
    outward = [(2 * a + c, 2 * b + c) for a, b in ((1, 0), (2, 3)) for c in range(2)]

    def by_line(own, twin, *done):
        size = own.shape[0]
        grown = after(jnp.concatenate([own, twin], axis=0), *done)
        came = lax.ppermute(grown, "wide", inner_swap)
        passed = lax.ppermute(after(came, moved[-1]), "wide", outward)
        return [
            twin,
            jnp.where(inner, came[size:], passed[:size]),
            jnp.where(inner, came[:size], passed[size:]),
        ]

    far0 = jnp.concatenate(direct, axis=0)
    crossed = [lax.ppermute(far0, "wide", core_flip)]
    moved = [lax.ppermute(after(far0, around), "narrow", narrow_flip)]
    late = lax.ppermute(after(side, far0), "wide", across(1))
    owns = chunks + [side]
    twins = [None] + [soon[:, :, i : i + chunk] for i in range(0, share - chunk, chunk)] + [late]
    nears = [mine, lax.ppermute(after(mine, crossed[0]), "wide", core_flip)]
    nears += [around, lax.ppermute(after(around, crossed[0]), "wide", core_flip)]
    nears = [one.reshape(rows0 * rows1, share + chunk, len3) for one in nears]

    def contract(kron, views, routes, out_rows, inputs):
        return pl.pallas_call(
            functools.partial(short_dims_kernel, views, routes),
            out_shape=tuple(
                jax.ShapeDtypeStruct((per_group, rows, chunk, len3), F32) for rows in out_rows
            ),
            in_specs=[whole_block()] * (3 + len(inputs)),
            out_specs=(whole_block(),) * len(out_rows),
            compiler_params=params(12),
            cost_estimate=pl.CostEstimate(flops=10**6, bytes_accessed=10**4, transcendentals=0),
            name="short_dims",
        )(*kron, right3, *inputs)

    block_rows = rows0 * rows1
    far_rows = (n_outer - 1) * block_rows
    def halved(one):
        return [one[i : i + rows0] for i in range(0, n_narrow * rows0, rows0)]

    side_early = [lax.ppermute(half, "wide", core_flip) for half in halved(late)]
    fars = [far0]
    kept, sent = [], []
    for index in range(n_chunks):
        far = fars[index]
        if index:
            if index == 1:
                far = after(far, late)
            crossed.append(lax.ppermute(far, "wide", core_flip))
            moved.append(lax.ppermute(after(far, moved[-1]), "narrow", narrow_flip))
        spread = by_line if index + 1 == n_chunks and n_outer == 4 else doubled
        done = [fars[index]] + ([], moved[:1], kept[:1] + moved[1:2])[min(index, 2)]
        blocks = spread(owns[index + 1], twins[index + 1], *done)
        fars.append(jnp.concatenate(blocks, axis=0))
        ready = side_early if index == 1 else ()
        handed = lax.ppermute(after(moved[index], *ready), "wide", core_flip)
        pieces = [far, crossed[index], moved[index], handed]
        inputs = nears + [one.reshape(far_rows, chunk, len3) for one in pieces]
        views = [(i, 0, block_rows, index * chunk) for i in range(len(nears))]
        views += [(len(nears) + i, 0, far_rows, 0) for i in range(len(pieces))]
        cuts = rows0 if index == n_chunks - 1 else 1
        routes = [[(0, slot)] for slot in range(per_group)]
        routes += [[(1 + cut, slot) for cut in range(cuts)] for slot in range(per_group)]
        out_rows = [block_rows] + [block_rows // cuts] * cuts
        keep, *for_act = contract((kron_hi, kron_lo), views, routes, out_rows, inputs)
        kept.append(keep)
        sent.append([])
        for one in for_act:
            before = [one for ones in sent for one in ones][-1:]
            sent[-1].append(lax.ppermute(after(one, *before), "act", act_flip))

    turned = side_early + [
        lax.ppermute(half, "wide", core_flip) for one in blocks[1:] for half in halved(one)
    ]
    inputs = nears + [one.reshape(-1, chunk, len3) for one in blocks + turned]
    views = [(i, 0, block_rows, share) for i in range(len(nears))]
    for ahead in range(n_narrow):
        views += [(len(nears) + i, ahead * block_rows, block_rows, 0) for i in range(len(blocks))]
        first = len(nears) + len(blocks) + ahead
        views += [(first + n_narrow * i, 0, block_rows, 0) for i in range(len(blocks))]
    routes = [[(out, slot) for out in range(1 + rows0)] for slot in range(per_group)]
    out_rows = [block_rows] + [block_rows // rows0] * rows0
    side_kron = (after(side_hi, sent[-1][0]), side_lo)
    side_keep, *side_give = contract(side_kron, views, routes, out_rows, inputs)
    side_got = [lax.ppermute(one, "narrow", narrow_flip) for one in side_give]

    parts = [(keep, None) for keep in kept] + [(ones[0], None) for ones in sent[:-1]]
    parts += [(sent[-1][0], sent[-1]), (side_keep, None), (side_got[0], side_got)]
    by_row = []
    for row in range(rows0):
        arrays = [cut[row] if cut else one for one, cut in parts]
        specs = [
            pl.BlockSpec(
                (per_group, rows1) + one.shape[2:],
                lambda i, block=0 if cut else row: (0, block, 0, 0),
            )
            for one, (_, cut) in zip(arrays, parts)
        ]
        scores, local = pl.pallas_call(
            functools.partial(third_dim_kernel, len(parts), rows0, row),
            grid=(1,),
            out_shape=(
                jax.ShapeDtypeStruct((per_group, rows1, len2, len3), F32),
                jax.ShapeDtypeStruct((rows1, len2, len3), F32),
            ),
            in_specs=[smem] * 3 + [whole_block()] * 2 + specs,
            out_specs=(whole_block(),) * 2,
            compiler_params=params(20),
            cost_estimate=pl.CostEstimate(
                flops=10**9, bytes_accessed=5 * 10**6, transcendentals=10**6
            ),
            name="third_dim",
        )(meta, cost_first, cost_second, left2, util23, *arrays)
        by_row.append((scores, local, lax.ppermute(local, "act", act_flip)))

    results = ()
    for row, operands in enumerate(by_row):
        results = pl.pallas_call(
            choice_kernel,
            grid=(1,),
            out_shape=(
                jax.ShapeDtypeStruct(value_now.shape, F32),
                jax.ShapeDtypeStruct((per_group,) + value_now.shape, BF16),
            ),
            in_specs=[whole_block()] * 3 + [pl.BlockSpec(memory_space=pl.ANY)] * len(results),
            out_specs=(
                pl.BlockSpec((1, rows1, len2, len3), lambda i, row=row: (row, 0, 0, 0)),
                pl.BlockSpec(
                    (per_group, 1, rows1, len2, len3), lambda i, row=row: (0, row, 0, 0, 0)
                ),
            ),
            input_output_aliases={3: 0, 4: 1} if results else {},
            compiler_params=params(16),
            cost_estimate=pl.CostEstimate(
                flops=10**7, bytes_accessed=5 * 10**6, transcendentals=10**6
            ),
            name="choice",
        )(*operands, *results)
    return tuple(results)


def gather_fits(mesh, value_shape, actions, offset_reach):
    n_wide, n_narrow, n_act = (mesh.shape[name] for name in ("wide", "narrow", "act"))
    len0, len1, len2, len3 = value_shape
    if n_act != 2 or n_wide < 4 or n_wide & (n_wide - 1) or actions % n_act:
        return False
    if n_narrow != 2 or len2 % (n_act * CHUNK_ROWS) or len2 < 4 * n_act * CHUNK_ROWS:
        return False
    if len2 != LANES or len3 != LANES:
        return False
    if (len1 // n_narrow) % SUBLANES or len0 * len1 // (n_wide * n_narrow) % 16 or len0 % n_wide:
        return False
    if max(len0, len1) > LANES or len1 % n_narrow:
        return False
    raw = len0 * len1 * len2 * len3 // (2 * n_act)
    exchanged = 2 * (actions // n_act) * len0 * len1 * len2 * len3 // (n_wide * n_narrow)
    return raw <= exchanged


def solution(mesh):
    def run(value_now, *rest):
        actions = rest[-1].shape[0]
        small = gather_fits(mesh, value_now.shape, actions, rest[4].shape[-1])
        return jax.shard_map(
            gather_body if small else exchange_body,
            mesh=mesh,
            in_specs=(P("wide", "narrow", None, None), P(), P(), P(), P(), P(), P(), P()),
            out_specs=(P("wide", "narrow", None, None), P("act", "wide", "narrow", None, None)),
            check_vma=False,
        )(value_now, *rest)

    return run
```

```python
import functools

import jax
import jax.numpy as jnp
from jax import lax
from jax.experimental import pallas as pl
from jax.experimental.pallas import tpu as pltpu
from jax.sharding import PartitionSpec as P

DISCOUNT = 0.95
HIGHEST = lax.Precision.HIGHEST
F32 = jnp.float32
BF16 = jnp.bfloat16
LANES = 128
SUBLANES = 8
PLACE = 4
CHUNK_ROWS = 16
MIB = 1024 * 1024


def merged(value, axis, join):
    pieces = lax.all_gather(value, axis)
    head = pieces[0]
    tail = pieces[1:]
    subtotal, _ = lax.scan(lambda subtotal, slab: (join(subtotal, slab), None), head, tail)
    return subtotal


def transition(weights, offset, length):
    band_len = weights.shape[0]
    half_band = (band_len - 1) // 2
    normed = weights / jnp.sum(weights)
    row_ids = jnp.arange(length, dtype=jnp.int32)
    tap_ids = jnp.arange(band_len, dtype=jnp.int32)
    target = jnp.clip(row_ids[:, None] + offset + tap_ids[None, :] - half_band, 0, length - 1)
    matched = (target[:, :, None] == row_ids[None, None, :]).astype(normed.dtype)
    return jnp.einsum("ijk,j->ik", matched, normed, precision=HIGHEST)


def exchange_body(
    value_now,
    cost_first,
    cost_second,
    cost_third,
    cost_fourth,
    trans_weights,
    trans_offsets,
    action_order,
):
    size_act = lax.axis_size("act")
    per_group = action_order.shape[0] // size_act
    group_id = lax.axis_index("act")
    my_actions = lax.dynamic_slice_in_dim(action_order, group_id * per_group, per_group)
    rows_first, rows_second, len_third, len_fourth = value_now.shape
    len_first = rows_first * lax.axis_size("wide")
    len_second = rows_second * lax.axis_size("narrow")
    my_weights = jnp.take(trans_weights, my_actions, axis=0)
    my_offsets = jnp.take(trans_offsets, my_actions, axis=0)

    def build(axis_id, length):
        return jax.vmap(lambda weight_row, offset_one: transition(weight_row, offset_one, length))(
            my_weights[:, axis_id], my_offsets[:, axis_id]
        )

    mat_first = build(0, len_first)
    mat_second = build(1, len_second)
    mat_third = build(2, len_third)
    mat_fourth = build(3, len_fourth)
    spread = lax.all_to_all(value_now, "narrow", split_axis=2, concat_axis=1, tiled=True)
    field = jnp.einsum("gij,ajcd->gaicd", mat_second, spread, precision=HIGHEST)
    field = jnp.einsum("gij,gabcj->gabci", mat_fourth, field, precision=HIGHEST)
    field = lax.all_to_all(field, "narrow", split_axis=2, concat_axis=3, tiled=True)
    field = lax.all_to_all(field, "wide", split_axis=3, concat_axis=1, tiled=True)
    field = jnp.einsum("gij,gjbcd->gibcd", mat_first, field, precision=HIGHEST)
    field = lax.all_to_all(field, "wide", split_axis=1, concat_axis=3, tiled=True)
    expected = jnp.einsum("gij,gabjd->gabid", mat_third, field, precision=HIGHEST)
    start_first = lax.axis_index("wide") * rows_first
    start_second = lax.axis_index("narrow") * rows_second
    util_first = lax.dynamic_slice_in_dim(
        jnp.take(cost_first, my_actions, axis=0), start_first, rows_first, 1
    )
    util_second = lax.dynamic_slice_in_dim(
        jnp.take(cost_second, my_actions, axis=0), start_second, rows_second, 1
    )
    util_third = jnp.take(cost_third, my_actions, axis=0)
    util_fourth = jnp.take(cost_fourth, my_actions, axis=0)
    utility = (
        util_first[:, :, None, None, None]
        + util_second[:, None, :, None, None]
        + util_third[:, None, None, :, None]
        + util_fourth[:, None, None, None, :]
    )
    scores = utility + DISCOUNT * expected
    local_max = jnp.max(scores, axis=0)
    local_sum = jnp.sum(jnp.exp(scores - local_max), axis=0)
    log_total = merged(local_max + jnp.log(local_sum), "act", jnp.logaddexp)
    choice_prob = jnp.exp(scores - log_total).astype(jnp.bfloat16)
    return (log_total, choice_prob)


def halves(x):
    high = x.astype(BF16)
    return high, (x - high.astype(F32)).astype(BF16)


def dot32(a, b):
    return jnp.dot(a, b, preferred_element_type=F32, precision=HIGHEST)


def banded(weights, offset, length, taps):
    half_band = (taps - 1) // 2
    width = weights.shape[1]
    normed = weights / jnp.sum(weights, axis=1, keepdims=True)
    tile = jnp.broadcast_to(normed, (SUBLANES, width))
    tile = pltpu.roll(tile, lax.rem(offset + (width - half_band), width), 1)
    rows = jnp.concatenate([tile] * (length // SUBLANES), axis=0)
    rows = pltpu.roll(rows, 0, 1, stride=1, stride_axis=0)
    lane = lax.broadcasted_iota(jnp.int32, (length, width), 1)
    under = lane >= width - 2 * half_band
    over = (lane >= length) & (lane < length + 2 * half_band)
    under_sum = jnp.sum(jnp.where(under, rows, 0.0), axis=1, keepdims=True)
    over_sum = jnp.sum(jnp.where(over, rows, 0.0), axis=1, keepdims=True)
    span = -(-length // LANES) * LANES
    kept = lane[:, :span]
    body = jnp.where(kept < length, rows[:, :span], 0.0)
    body = body + jnp.where(kept == 0, under_sum, 0.0)
    return body + jnp.where(kept == length - 1, over_sum, 0.0)


def prepare_kernel(
    lengths, taps, sizes, rows0, rows1, arrivals, meta, weights,
    kron_hi, kron_lo, side_hi, side_lo, right3, wide0, wide1,
):
    n_act, n_narrow, n_outer = sizes
    len0, len1, len2, len3 = lengths
    act, narrow, outer, core = (meta[i] for i in range(PLACE))
    actions = weights.shape[0]
    per_group = actions // n_act
    columns = len0 * len1

    def wrapped(index, size):
        return lax.rem(index + size, size)

    lane = lax.broadcasted_iota(jnp.int32, (1, columns), 1)
    ids0 = jnp.zeros((1, columns), jnp.int32)
    ids1 = jnp.zeros((1, columns), jnp.int32)
    for block, (far, part, ahead) in enumerate(arrivals):
        from_outer, from_core = outer ^ far, wrapped(core + part, 2)
        for row in range(rows0):
            start = (block * rows0 + row) * rows1
            inside = (lane >= start) & (lane < start + rows1)
            first = (from_outer * 2 + from_core) * rows0 + row
            second = wrapped(narrow - ahead, n_narrow) * rows1 - start
            ids0 = jnp.where(inside, first, ids0)
            ids1 = jnp.where(inside, second + lane, ids1)
    spread0 = (lax.broadcasted_iota(jnp.int32, (LANES, columns), 0) == ids0).astype(F32)
    spread1 = (lax.broadcasted_iota(jnp.int32, (LANES, columns), 0) == ids1).astype(F32)

    for action in range(actions):
        group, slot = divmod(action, per_group)
        which = meta[PLACE + wrapped(act + group, n_act) * per_group + slot]
        rows = weights[which]
        mats = [
            banded(
                rows[axis : axis + 1, :],
                meta[PLACE + (1 + axis) * actions + which],
                lengths[axis],
                taps,
            )
            for axis in (0, 1, 3)
        ]
        wide0[...] = dot32(mats[0], spread0)
        wide1[...] = dot32(mats[1], spread1)
        base = (outer * 2 + core) * rows0
        for ahead in range(n_narrow if group == 0 else 1):
            begin = wrapped(narrow + ahead, n_narrow) * rows1
            second = wide1[pl.ds(pl.multiple_of(begin, SUBLANES), rows1), :]
            blocks = [wide0[pl.ds(base + row, 1), :] * second for row in range(rows0)]
            high, low = halves(jnp.concatenate(blocks, axis=0))
            if ahead == 0:
                start = action * rows0 * rows1
                kron_hi[start : start + rows0 * rows1, :] = high
                kron_lo[start : start + rows0 * rows1, :] = low
            if group == 0:
                start = (slot * n_narrow + ahead) * rows0 * rows1
                side_hi[start : start + rows0 * rows1, :] = high
                side_lo[start : start + rows0 * rows1, :] = low
        high, low = halves(mats[2].T)
        row_pair = jnp.concatenate([high, low], axis=1)
        right3[action] = jnp.concatenate([row_pair, row_pair], axis=0)


def prepare_third_kernel(taps, segments, meta, weights, third, fourth, left2, util23):
    act, actions, per_group = meta[0], weights.shape[0], left2.shape[0]
    len2, len3 = util23.shape[1:]
    lane2 = lax.broadcasted_iota(jnp.int32, (1, len2), 1)
    ids2 = jnp.zeros((1, len2), jnp.int32)
    filled = 0
    for begin, size, axis, ahead, count in segments:
        source = begin + lax.rem(meta[axis] + ahead, count) * size
        inside = (lane2 >= filled) & (lane2 < filled + size)
        ids2 = jnp.where(inside, source - filled + lane2, ids2)
        filled += size
    order2 = (lax.broadcasted_iota(jnp.int32, (len2, len2), 0) == ids2).astype(F32)

    for slot in range(per_group):
        which = meta[PLACE + act * per_group + slot]
        offset = meta[PLACE + 3 * actions + which]
        matrix = banded(weights[which][2:3, :], offset, len2, taps)
        high, low = halves(dot32(matrix, order2))
        left2[slot] = jnp.concatenate(
            [jnp.concatenate([high, high], axis=1), jnp.concatenate([low, low], axis=1)], axis=0
        )
        column = jnp.broadcast_to(third[pl.ds(which, 1), :], (len3, len2)).T
        util23[slot] = column + fourth[pl.ds(which, 1), :]


def short_dims_kernel(views, routes, kron_hi, kron_lo, right3, *refs):
    n_inputs = 1 + max(view[0] for view in views)
    inputs, outs = refs[:n_inputs], refs[n_inputs:]
    rows, depth = outs[0].shape[2:]
    per_action = kron_hi.shape[0] // len(routes)
    q_hi, q_lo = kron_hi[...], kron_lo[...]
    mixed = []
    for row in range(0, rows, 2):
        cols = [
            jnp.concatenate(
                [
                    inputs[which][lead : lead + count, start + row + extra, :]
                    for which, lead, count, start in views
                ],
                axis=0,
            )
            for extra in range(2)
        ]
        x_hi, x_lo = halves(jnp.concatenate(cols, axis=1))
        out = (
            jnp.dot(q_hi, x_hi, preferred_element_type=F32)
            + jnp.dot(q_hi, x_lo, preferred_element_type=F32)
            + jnp.dot(q_lo, x_hi, preferred_element_type=F32)
        )
        mixed += [out[:, :depth], out[:, depth:]]
    for action, route in enumerate(routes):
        start = action * per_action
        block = jnp.concatenate([one[start : start + per_action] for one in mixed], axis=0)
        t_hi, t_lo = halves(block)
        both = jnp.dot(
            jnp.concatenate([t_hi, t_lo], axis=1), right3[action], preferred_element_type=F32
        )
        done = both[:, :depth] + both[:, depth:]
        for row in range(rows):
            first = row * per_action
            for which, slot in route:
                count = outs[which].shape[1]
                outs[which][slot, :, row, :] = done[first : first + count]
                first += count


def third_dim_kernel(n_pieces, rows0, row, meta, costs0, costs1, left2, util23, *refs):
    pieces, scores, local = refs[:n_pieces], refs[n_pieces], refs[n_pieces + 1]
    per_group, rows1 = scores.shape[:2]
    length = util23.shape[1]
    depth = util23.shape[2]
    which = [meta[PLACE + meta[0] * per_group + slot] for slot in range(per_group)]
    first = (meta[2] * 2 + meta[3]) * rows0 + row
    start1 = meta[1] * rows1
    for second in range(0, rows1, 2):
        for slot in range(per_group):
            cols = [
                jnp.concatenate([piece[slot, second + extra] for piece in pieces], axis=0)
                for extra in range(2)
            ]
            g_hi, g_lo = halves(jnp.concatenate(cols, axis=1))
            both = jnp.dot(
                left2[slot], jnp.concatenate([g_hi, g_lo], axis=0), preferred_element_type=F32
            )
            expected = both[:length] + both[length:]
            for extra in range(2):
                flat = costs0[which[slot], first] + costs1[which[slot], start1 + second + extra]
                scores[slot, second + extra] = (util23[slot] + flat) + DISCOUNT * expected[
                    :, extra * depth : (extra + 1) * depth
                ]
        for extra in range(2):
            found = [scores[slot, second + extra] for slot in range(per_group)]
            top = functools.reduce(jnp.maximum, found)
            total = functools.reduce(jnp.add, [jnp.exp(one - top) for one in found])
            local[second + extra] = top + jnp.log(total)


def choice_kernel(scores, mine, other, *refs):
    new_value, choice_prob = refs[-2:]
    a, b = mine[...], other[...]
    top, low = jnp.maximum(a, b), jnp.minimum(a, b)
    total = top + jnp.log(1.0 + jnp.exp(low - top))
    new_value[0] = total
    for slot in range(scores.shape[0]):
        choice_prob[slot, 0] = jnp.exp(scores[slot] - total).astype(choice_prob.dtype)


def after(value, *done):
    return lax.optimization_barrier((value, *done))[0] if done else value


def whole_block():
    return pl.BlockSpec(memory_space=pltpu.VMEM)


def params(mebibytes):
    return pltpu.CompilerParams(vmem_limit_bytes=mebibytes * MIB)


def gather_body(
    value_now,
    cost_first,
    cost_second,
    cost_third,
    cost_fourth,
    trans_weights,
    trans_offsets,
    action_order,
):
    n_act, n_narrow, n_wide = (lax.axis_size(name) for name in ("act", "narrow", "wide"))
    n_outer = n_wide // 2
    act, narrow, wide = (lax.axis_index(name) for name in ("act", "narrow", "wide"))
    outer, core = wide // 2, wide % 2
    actions, _, taps = trans_weights.shape
    per_group = actions // n_act
    rows0, rows1, len2, len3 = value_now.shape
    len0, len1 = rows0 * n_wide, rows1 * n_narrow
    lengths = (len0, len1, len2, len3)
    chunk = CHUNK_ROWS
    share = (len2 - n_narrow * chunk) // n_act
    n_chunks = share // chunk
    core_flip = [(i, i ^ 1) for i in range(n_wide)]
    act_flip = [(i, (i + 1) % n_act) for i in range(n_act)]
    narrow_flip = [(i, (i + 1) % n_narrow) for i in range(n_narrow)]

    def across(bit):
        return [(i, i ^ (2 * bit)) for i in range(n_wide)]

    def part(begin, size):
        return lax.dynamic_slice_in_dim(value_now, begin, size, 2)

    near = [(0, other, ahead) for ahead in range(n_narrow) for other in range(2)]
    arrivals = near + [
        (far, other, ahead)
        for ahead in range(n_narrow)
        for other in range(2)
        for far in range(1, n_outer)
    ]

    half_band = (taps - 1) // 2
    width = -(-(max(lengths) + 4 * half_band) // LANES) * LANES
    weights = jnp.pad(trans_weights, ((0, 0), (0, 0), (0, width - taps)))
    place = jnp.stack([act, narrow, outer, core]).astype(jnp.int32)
    meta = jnp.concatenate([place, action_order, trans_offsets.T.reshape(-1)])
    smem = pl.BlockSpec(memory_space=pltpu.SMEM)
    q_rows = actions * rows0 * rows1
    kron_hi, kron_lo, side_hi, side_lo, right3 = pl.pallas_call(
        functools.partial(
            prepare_kernel, lengths, taps, (n_act, n_narrow, n_outer), rows0, rows1, arrivals
        ),
        out_shape=(
            jax.ShapeDtypeStruct((q_rows, len0 * len1), BF16),
            jax.ShapeDtypeStruct((q_rows, len0 * len1), BF16),
            jax.ShapeDtypeStruct((q_rows * n_narrow // n_act, len0 * len1), BF16),
            jax.ShapeDtypeStruct((q_rows * n_narrow // n_act, len0 * len1), BF16),
            jax.ShapeDtypeStruct((actions, 2 * len3, 2 * len3), BF16),
        ),
        in_specs=[smem, whole_block()],
        out_specs=(whole_block(),) * 5,
        scratch_shapes=[pltpu.VMEM((len0, len0 * len1), F32), pltpu.VMEM((len1, len0 * len1), F32)],
        compiler_params=params(16),
        cost_estimate=pl.CostEstimate(flops=10**9, bytes_accessed=4 * 10**6, transcendentals=0),
        name="prepare",
    )(meta, weights)
    segments = [(0, share, 0, ahead, n_act) for ahead in range(n_act)]
    segments += [(n_act * share, chunk, 1, ahead, n_narrow) for ahead in range(n_narrow)]
    left2, util23 = pl.pallas_call(
        functools.partial(prepare_third_kernel, taps, segments),
        out_shape=(
            jax.ShapeDtypeStruct((per_group, 2 * len2, 2 * len2), BF16),
            jax.ShapeDtypeStruct((per_group, len2, len3), F32),
        ),
        in_specs=[smem] + [whole_block()] * 3,
        out_specs=(whole_block(),) * 2,
        compiler_params=params(12),
        cost_estimate=pl.CostEstimate(flops=10**9, bytes_accessed=4 * 10**6, transcendentals=0),
        name="prepare_third",
    )(meta, weights, cost_third, cost_fourth)

    side_begin = n_act * share
    inner = (outer == 1) | (outer == 2)
    value_now, inner, place, act_begin, own_begin, other_begin = lax.optimization_barrier(
        (
            value_now,
            inner,
            place,
            act * share,
            side_begin + narrow * chunk,
            side_begin + (n_narrow - 1 - narrow) * chunk,
        )
    )
    chunks = [part(act_begin + index * chunk, chunk) for index in range(n_chunks)]
    to_narrow = jnp.concatenate([part(act_begin, share), part(other_begin, chunk)], axis=2)
    own_side = part(own_begin, chunk)
    mine = jnp.concatenate([part(act_begin, share), own_side], axis=2)
    direct = [lax.ppermute(chunks[0], "wide", across(far)) for far in range(1, n_outer)]
    around = lax.ppermute(to_narrow, "narrow", narrow_flip)
    soon = lax.ppermute(part(act_begin + chunk, share - chunk), "wide", across(1))
    direct, *_ = lax.optimization_barrier((direct, kron_hi, right3))
    side = jnp.concatenate([own_side, around[:, :, share:]], axis=0)

    bits = [1 << bit for bit in range(1, n_outer.bit_length() - 1)]

    def doubled(own, twin, *done):
        size = own.shape[0]
        blocks = [own, twin]
        for bit in bits:
            grown = after(jnp.concatenate(blocks, axis=0), *done)
            more = lax.ppermute(grown, "wide", across(bit))
            blocks += [more[i : i + size] for i in range(0, more.shape[0], size)]
        return blocks[1:]

    inner_swap = [(2 * a + c, 2 * b + c) for a, b in ((1, 2), (2, 1)) for c in range(2)]
    outward = [(2 * a + c, 2 * b + c) for a, b in ((1, 0), (2, 3)) for c in range(2)]

    def by_line(own, twin, *done):
        size = own.shape[0]
        grown = after(jnp.concatenate([own, twin], axis=0), *done)
        came = lax.ppermute(grown, "wide", inner_swap)
        passed = lax.ppermute(after(came, moved[-1]), "wide", outward)
        return [
            twin,
            jnp.where(inner, came[size:], passed[:size]),
            jnp.where(inner, came[:size], passed[size:]),
        ]

    far0 = jnp.concatenate(direct, axis=0)
    crossed = [lax.ppermute(far0, "wide", core_flip)]
    moved = [lax.ppermute(far0, "narrow", narrow_flip)]
    late = lax.ppermute(after(side, far0), "wide", across(1))
    owns = chunks + [side]
    twins = [None] + [soon[:, :, i : i + chunk] for i in range(0, share - chunk, chunk)] + [late]
    nears = [mine, lax.ppermute(after(mine, crossed[0]), "wide", core_flip)]
    nears += [around, lax.ppermute(after(around, crossed[0]), "wide", core_flip)]
    nears = [one.reshape(rows0 * rows1, share + chunk, len3) for one in nears]

    def contract(kron, views, routes, out_rows, inputs):
        return pl.pallas_call(
            functools.partial(short_dims_kernel, views, routes),
            out_shape=tuple(
                jax.ShapeDtypeStruct((per_group, rows, chunk, len3), F32) for rows in out_rows
            ),
            in_specs=[whole_block()] * (3 + len(inputs)),
            out_specs=(whole_block(),) * len(out_rows),
            compiler_params=params(12),
            cost_estimate=pl.CostEstimate(flops=10**6, bytes_accessed=10**4, transcendentals=0),
            name="short_dims",
        )(*kron, right3, *inputs)

    block_rows = rows0 * rows1
    far_rows = (n_outer - 1) * block_rows
    def halved(one):
        return [one[i : i + rows0] for i in range(0, n_narrow * rows0, rows0)]

    side_early = [lax.ppermute(half, "wide", core_flip) for half in halved(late)]
    fars = [far0]
    kept, sent = [], []
    for index in range(n_chunks):
        far = fars[index]
        if index:
            if index == 1:
                far = after(far, late)
            crossed.append(lax.ppermute(far, "wide", core_flip))
            moved.append(lax.ppermute(after(far, moved[-1]), "narrow", narrow_flip))
        spread = by_line if index + 1 == n_chunks and n_outer == 4 else doubled
        done = [fars[index]] + ([], moved[:1], kept[:1] + moved[1:2])[min(index, 2)]
        blocks = spread(owns[index + 1], twins[index + 1], *done)
        fars.append(jnp.concatenate(blocks, axis=0))
        ready = ([left2, util23], side_early, ())[min(index, 2)]
        handed = lax.ppermute(after(moved[index], *ready), "wide", core_flip)
        pieces = [far, crossed[index], moved[index], handed]
        inputs = nears + [one.reshape(far_rows, chunk, len3) for one in pieces]
        views = [(i, 0, block_rows, index * chunk) for i in range(len(nears))]
        views += [(len(nears) + i, 0, far_rows, 0) for i in range(len(pieces))]
        cuts = rows0 if index == n_chunks - 1 else 1
        routes = [[(0, slot)] for slot in range(per_group)]
        routes += [[(1 + cut, slot) for cut in range(cuts)] for slot in range(per_group)]
        out_rows = [block_rows] + [block_rows // cuts] * cuts
        keep, *for_act = contract((kron_hi, kron_lo), views, routes, out_rows, inputs)
        kept.append(keep)
        sent.append([])
        for one in for_act:
            before = [one for ones in sent for one in ones][-1:]
            sent[-1].append(lax.ppermute(after(one, *before), "act", act_flip))

    turned = side_early + [
        lax.ppermute(half, "wide", core_flip) for one in blocks[1:] for half in halved(one)
    ]
    inputs = nears + [one.reshape(-1, chunk, len3) for one in blocks + turned]
    views = [(i, 0, block_rows, share) for i in range(len(nears))]
    for ahead in range(n_narrow):
        views += [(len(nears) + i, ahead * block_rows, block_rows, 0) for i in range(len(blocks))]
        first = len(nears) + len(blocks) + ahead
        views += [(first + n_narrow * i, 0, block_rows, 0) for i in range(len(blocks))]
    routes = [[(out, slot) for out in range(1 + rows0)] for slot in range(per_group)]
    out_rows = [block_rows] + [block_rows // rows0] * rows0
    side_kron = (after(side_hi, sent[-1][0]), side_lo)
    side_keep, *side_give = contract(side_kron, views, routes, out_rows, inputs)
    side_got = []
    for one in side_give:
        side_got.append(lax.ppermute(after(one, *side_got[-1:]), "narrow", narrow_flip))

    parts = [(keep, None) for keep in kept] + [(ones[0], None) for ones in sent[:-1]]
    parts += [(sent[-1][0], sent[-1]), (side_keep, None), (side_got[0], side_got)]
    by_row = []
    for row in range(rows0):
        arrays = [cut[row] if cut else one for one, cut in parts]
        specs = [
            pl.BlockSpec(
                (per_group, rows1) + one.shape[2:],
                lambda i, block=0 if cut else row: (0, block, 0, 0),
            )
            for one, (_, cut) in zip(arrays, parts)
        ]
        scores, local = pl.pallas_call(
            functools.partial(third_dim_kernel, len(parts), rows0, row),
            grid=(1,),
            out_shape=(
                jax.ShapeDtypeStruct((per_group, rows1, len2, len3), F32),
                jax.ShapeDtypeStruct((rows1, len2, len3), F32),
            ),
            in_specs=[smem] * 3 + [whole_block()] * 2 + specs,
            out_specs=(whole_block(),) * 2,
            compiler_params=params(20),
            cost_estimate=pl.CostEstimate(
                flops=10**9, bytes_accessed=5 * 10**6, transcendentals=10**6
            ),
            name="third_dim",
        )(meta, cost_first, cost_second, left2, util23, *arrays)
        by_row.append((scores, local, lax.ppermute(local, "act", act_flip)))

    results = ()
    for row, operands in enumerate(by_row):
        results = pl.pallas_call(
            choice_kernel,
            grid=(1,),
            out_shape=(
                jax.ShapeDtypeStruct(value_now.shape, F32),
                jax.ShapeDtypeStruct((per_group,) + value_now.shape, BF16),
            ),
            in_specs=[whole_block()] * 3 + [pl.BlockSpec(memory_space=pl.ANY)] * len(results),
            out_specs=(
                pl.BlockSpec((1, rows1, len2, len3), lambda i, row=row: (row, 0, 0, 0)),
                pl.BlockSpec(
                    (per_group, 1, rows1, len2, len3), lambda i, row=row: (0, row, 0, 0, 0)
                ),
            ),
            input_output_aliases={3: 0, 4: 1} if results else {},
            compiler_params=params(16),
            cost_estimate=pl.CostEstimate(
                flops=10**7, bytes_accessed=5 * 10**6, transcendentals=10**6
            ),
            name="choice",
        )(*operands, *results)
    return tuple(results)


def gather_fits(mesh, value_shape, actions, offset_reach):
    n_wide, n_narrow, n_act = (mesh.shape[name] for name in ("wide", "narrow", "act"))
    len0, len1, len2, len3 = value_shape
    if n_act != 2 or n_wide < 4 or n_wide & (n_wide - 1) or actions % n_act:
        return False
    if n_narrow != 2 or len2 % (n_act * CHUNK_ROWS) or len2 < 4 * n_act * CHUNK_ROWS:
        return False
    if len2 != LANES or len3 != LANES:
        return False
    if (len1 // n_narrow) % SUBLANES or len0 * len1 // (n_wide * n_narrow) % 16 or len0 % n_wide:
        return False
    if max(len0, len1) > LANES or len1 % n_narrow:
        return False
    raw = len0 * len1 * len2 * len3 // (2 * n_act)
    exchanged = 2 * (actions // n_act) * len0 * len1 * len2 * len3 // (n_wide * n_narrow)
    return raw <= exchanged


def solution(mesh):
    def run(value_now, *rest):
        actions = rest[-1].shape[0]
        small = gather_fits(mesh, value_now.shape, actions, rest[4].shape[-1])
        return jax.shard_map(
            gather_body if small else exchange_body,
            mesh=mesh,
            in_specs=(P("wide", "narrow", None, None), P(), P(), P(), P(), P(), P(), P()),
            out_specs=(P("wide", "narrow", None, None), P("act", "wide", "narrow", None, None)),
            check_vma=False,
        )(value_now, *rest)

    return run
```

```python
import functools

import jax
import jax.numpy as jnp
from jax import lax
from jax.experimental import pallas as pl
from jax.experimental.pallas import tpu as pltpu
from jax.sharding import PartitionSpec as P

DISCOUNT = 0.95
HIGHEST = lax.Precision.HIGHEST
F32 = jnp.float32
BF16 = jnp.bfloat16
LANES = 128
SUBLANES = 8
PLACE = 4
CHUNK_ROWS = 16
MIB = 1024 * 1024


def merged(value, axis, join):
    pieces = lax.all_gather(value, axis)
    head = pieces[0]
    tail = pieces[1:]
    subtotal, _ = lax.scan(lambda subtotal, slab: (join(subtotal, slab), None), head, tail)
    return subtotal


def transition(weights, offset, length):
    band_len = weights.shape[0]
    half_band = (band_len - 1) // 2
    normed = weights / jnp.sum(weights)
    row_ids = jnp.arange(length, dtype=jnp.int32)
    tap_ids = jnp.arange(band_len, dtype=jnp.int32)
    target = jnp.clip(row_ids[:, None] + offset + tap_ids[None, :] - half_band, 0, length - 1)
    matched = (target[:, :, None] == row_ids[None, None, :]).astype(normed.dtype)
    return jnp.einsum("ijk,j->ik", matched, normed, precision=HIGHEST)


def exchange_body(
    value_now,
    cost_first,
    cost_second,
    cost_third,
    cost_fourth,
    trans_weights,
    trans_offsets,
    action_order,
):
    size_act = lax.axis_size("act")
    per_group = action_order.shape[0] // size_act
    group_id = lax.axis_index("act")
    my_actions = lax.dynamic_slice_in_dim(action_order, group_id * per_group, per_group)
    rows_first, rows_second, len_third, len_fourth = value_now.shape
    len_first = rows_first * lax.axis_size("wide")
    len_second = rows_second * lax.axis_size("narrow")
    my_weights = jnp.take(trans_weights, my_actions, axis=0)
    my_offsets = jnp.take(trans_offsets, my_actions, axis=0)

    def build(axis_id, length):
        return jax.vmap(lambda weight_row, offset_one: transition(weight_row, offset_one, length))(
            my_weights[:, axis_id], my_offsets[:, axis_id]
        )

    mat_first = build(0, len_first)
    mat_second = build(1, len_second)
    mat_third = build(2, len_third)
    mat_fourth = build(3, len_fourth)
    spread = lax.all_to_all(value_now, "narrow", split_axis=2, concat_axis=1, tiled=True)
    field = jnp.einsum("gij,ajcd->gaicd", mat_second, spread, precision=HIGHEST)
    field = jnp.einsum("gij,gabcj->gabci", mat_fourth, field, precision=HIGHEST)
    field = lax.all_to_all(field, "narrow", split_axis=2, concat_axis=3, tiled=True)
    field = lax.all_to_all(field, "wide", split_axis=3, concat_axis=1, tiled=True)
    field = jnp.einsum("gij,gjbcd->gibcd", mat_first, field, precision=HIGHEST)
    field = lax.all_to_all(field, "wide", split_axis=1, concat_axis=3, tiled=True)
    expected = jnp.einsum("gij,gabjd->gabid", mat_third, field, precision=HIGHEST)
    start_first = lax.axis_index("wide") * rows_first
    start_second = lax.axis_index("narrow") * rows_second
    util_first = lax.dynamic_slice_in_dim(
        jnp.take(cost_first, my_actions, axis=0), start_first, rows_first, 1
    )
    util_second = lax.dynamic_slice_in_dim(
        jnp.take(cost_second, my_actions, axis=0), start_second, rows_second, 1
    )
    util_third = jnp.take(cost_third, my_actions, axis=0)
    util_fourth = jnp.take(cost_fourth, my_actions, axis=0)
    utility = (
        util_first[:, :, None, None, None]
        + util_second[:, None, :, None, None]
        + util_third[:, None, None, :, None]
        + util_fourth[:, None, None, None, :]
    )
    scores = utility + DISCOUNT * expected
    local_max = jnp.max(scores, axis=0)
    local_sum = jnp.sum(jnp.exp(scores - local_max), axis=0)
    log_total = merged(local_max + jnp.log(local_sum), "act", jnp.logaddexp)
    choice_prob = jnp.exp(scores - log_total).astype(jnp.bfloat16)
    return (log_total, choice_prob)


def halves(x):
    high = x.astype(BF16)
    return high, (x - high.astype(F32)).astype(BF16)


def dot32(a, b):
    return jnp.dot(a, b, preferred_element_type=F32, precision=HIGHEST)


def banded(weights, offset, length, taps):
    half_band = (taps - 1) // 2
    width = weights.shape[1]
    normed = weights / jnp.sum(weights, axis=1, keepdims=True)
    tile = jnp.broadcast_to(normed, (SUBLANES, width))
    tile = pltpu.roll(tile, lax.rem(offset + (width - half_band), width), 1)
    rows = jnp.concatenate([tile] * (length // SUBLANES), axis=0)
    rows = pltpu.roll(rows, 0, 1, stride=1, stride_axis=0)
    lane = lax.broadcasted_iota(jnp.int32, (length, width), 1)
    under = lane >= width - 2 * half_band
    over = (lane >= length) & (lane < length + 2 * half_band)
    under_sum = jnp.sum(jnp.where(under, rows, 0.0), axis=1, keepdims=True)
    over_sum = jnp.sum(jnp.where(over, rows, 0.0), axis=1, keepdims=True)
    span = -(-length // LANES) * LANES
    kept = lane[:, :span]
    body = jnp.where(kept < length, rows[:, :span], 0.0)
    body = body + jnp.where(kept == 0, under_sum, 0.0)
    return body + jnp.where(kept == length - 1, over_sum, 0.0)


def prepare_kernel(
    lengths, taps, sizes, rows0, rows1, arrivals, meta, weights,
    kron_hi, kron_lo, side_hi, side_lo, right3, wide0, wide1,
):
    n_act, n_narrow, n_outer = sizes
    len0, len1, len2, len3 = lengths
    act, narrow, outer, core = (meta[i] for i in range(PLACE))
    actions = weights.shape[0]
    per_group = actions // n_act
    columns = len0 * len1

    def wrapped(index, size):
        return lax.rem(index + size, size)

    lane = lax.broadcasted_iota(jnp.int32, (1, columns), 1)
    ids0 = jnp.zeros((1, columns), jnp.int32)
    ids1 = jnp.zeros((1, columns), jnp.int32)
    for block, (far, part, ahead) in enumerate(arrivals):
        from_outer, from_core = outer ^ far, wrapped(core + part, 2)
        for row in range(rows0):
            start = (block * rows0 + row) * rows1
            inside = (lane >= start) & (lane < start + rows1)
            first = (from_outer * 2 + from_core) * rows0 + row
            second = wrapped(narrow - ahead, n_narrow) * rows1 - start
            ids0 = jnp.where(inside, first, ids0)
            ids1 = jnp.where(inside, second + lane, ids1)
    spread0 = (lax.broadcasted_iota(jnp.int32, (LANES, columns), 0) == ids0).astype(F32)
    spread1 = (lax.broadcasted_iota(jnp.int32, (LANES, columns), 0) == ids1).astype(F32)

    for action in range(actions):
        group, slot = divmod(action, per_group)
        which = meta[PLACE + wrapped(act + group, n_act) * per_group + slot]
        rows = weights[which]
        mats = [
            banded(
                rows[axis : axis + 1, :],
                meta[PLACE + (1 + axis) * actions + which],
                lengths[axis],
                taps,
            )
            for axis in (0, 1, 3)
        ]
        wide0[...] = dot32(mats[0], spread0)
        wide1[...] = dot32(mats[1], spread1)
        base = (outer * 2 + core) * rows0
        for ahead in range(n_narrow if group == 0 else 1):
            begin = wrapped(narrow + ahead, n_narrow) * rows1
            second = wide1[pl.ds(pl.multiple_of(begin, SUBLANES), rows1), :]
            blocks = [wide0[pl.ds(base + row, 1), :] * second for row in range(rows0)]
            high, low = halves(jnp.concatenate(blocks, axis=0))
            if ahead == 0:
                start = action * rows0 * rows1
                kron_hi[start : start + rows0 * rows1, :] = high
                kron_lo[start : start + rows0 * rows1, :] = low
            if group == 0:
                start = (slot * n_narrow + ahead) * rows0 * rows1
                side_hi[start : start + rows0 * rows1, :] = high
                side_lo[start : start + rows0 * rows1, :] = low
        high, low = halves(mats[2].T)
        row_pair = jnp.concatenate([high, low], axis=1)
        right3[action] = jnp.concatenate([row_pair, row_pair], axis=0)


def prepare_third_kernel(taps, segments, meta, weights, third, fourth, left2, util23):
    act, actions, per_group = meta[0], weights.shape[0], left2.shape[0]
    len2, len3 = util23.shape[1:]
    lane2 = lax.broadcasted_iota(jnp.int32, (1, len2), 1)
    ids2 = jnp.zeros((1, len2), jnp.int32)
    filled = 0
    for begin, size, axis, ahead, count in segments:
        source = begin + lax.rem(meta[axis] + ahead, count) * size
        inside = (lane2 >= filled) & (lane2 < filled + size)
        ids2 = jnp.where(inside, source - filled + lane2, ids2)
        filled += size
    order2 = (lax.broadcasted_iota(jnp.int32, (len2, len2), 0) == ids2).astype(F32)

    for slot in range(per_group):
        which = meta[PLACE + act * per_group + slot]
        offset = meta[PLACE + 3 * actions + which]
        matrix = banded(weights[which][2:3, :], offset, len2, taps)
        high, low = halves(dot32(matrix, order2))
        left2[slot] = jnp.concatenate(
            [jnp.concatenate([high, high], axis=1), jnp.concatenate([low, low], axis=1)], axis=0
        )
        column = jnp.broadcast_to(third[pl.ds(which, 1), :], (len3, len2)).T
        util23[slot] = column + fourth[pl.ds(which, 1), :]


def short_dims_kernel(views, routes, kron_hi, kron_lo, right3, *refs):
    n_inputs = 1 + max(view[0] for view in views)
    inputs, outs = refs[:n_inputs], refs[n_inputs:]
    rows, depth = outs[0].shape[2:]
    per_action = kron_hi.shape[0] // len(routes)
    q_hi, q_lo = kron_hi[...], kron_lo[...]
    mixed = []
    for row in range(0, rows, 2):
        cols = [
            jnp.concatenate(
                [
                    inputs[which][lead : lead + count, start + row + extra, :]
                    for which, lead, count, start in views
                ],
                axis=0,
            )
            for extra in range(2)
        ]
        x_hi, x_lo = halves(jnp.concatenate(cols, axis=1))
        out = (
            jnp.dot(q_hi, x_hi, preferred_element_type=F32)
            + jnp.dot(q_hi, x_lo, preferred_element_type=F32)
            + jnp.dot(q_lo, x_hi, preferred_element_type=F32)
        )
        mixed += [out[:, :depth], out[:, depth:]]
    for action, route in enumerate(routes):
        start = action * per_action
        block = jnp.concatenate([one[start : start + per_action] for one in mixed], axis=0)
        t_hi, t_lo = halves(block)
        both = jnp.dot(
            jnp.concatenate([t_hi, t_lo], axis=1), right3[action], preferred_element_type=F32
        )
        done = both[:, :depth] + both[:, depth:]
        for row in range(rows):
            first = row * per_action
            for which, slot in route:
                count = outs[which].shape[1]
                outs[which][slot, :, row, :] = done[first : first + count]
                first += count


def third_dim_kernel(n_pieces, rows0, row, meta, costs0, costs1, left2, util23, *refs):
    pieces, scores, local = refs[:n_pieces], refs[n_pieces], refs[n_pieces + 1]
    per_group, rows1 = scores.shape[:2]
    length = util23.shape[1]
    depth = util23.shape[2]
    which = [meta[PLACE + meta[0] * per_group + slot] for slot in range(per_group)]
    first = (meta[2] * 2 + meta[3]) * rows0 + row
    start1 = meta[1] * rows1
    for second in range(0, rows1, 2):
        for slot in range(per_group):
            cols = [
                jnp.concatenate([piece[slot, second + extra] for piece in pieces], axis=0)
                for extra in range(2)
            ]
            g_hi, g_lo = halves(jnp.concatenate(cols, axis=1))
            both = jnp.dot(
                left2[slot], jnp.concatenate([g_hi, g_lo], axis=0), preferred_element_type=F32
            )
            expected = both[:length] + both[length:]
            for extra in range(2):
                flat = costs0[which[slot], first] + costs1[which[slot], start1 + second + extra]
                scores[slot, second + extra] = (util23[slot] + flat) + DISCOUNT * expected[
                    :, extra * depth : (extra + 1) * depth
                ]
        for extra in range(2):
            found = [scores[slot, second + extra] for slot in range(per_group)]
            top = functools.reduce(jnp.maximum, found)
            total = functools.reduce(jnp.add, [jnp.exp(one - top) for one in found])
            local[second + extra] = top + jnp.log(total)


def choice_kernel(scores, mine, other, *refs):
    new_value, choice_prob = refs[-2:]
    a, b = mine[...], other[...]
    top, low = jnp.maximum(a, b), jnp.minimum(a, b)
    total = top + jnp.log(1.0 + jnp.exp(low - top))
    new_value[0] = total
    for slot in range(scores.shape[0]):
        choice_prob[slot, 0] = jnp.exp(scores[slot] - total).astype(choice_prob.dtype)


def after(value, *done):
    return lax.optimization_barrier((value, *done))[0] if done else value


def whole_block():
    return pl.BlockSpec(memory_space=pltpu.VMEM)


def params(mebibytes):
    return pltpu.CompilerParams(vmem_limit_bytes=mebibytes * MIB)


def gather_body(
    value_now,
    cost_first,
    cost_second,
    cost_third,
    cost_fourth,
    trans_weights,
    trans_offsets,
    action_order,
):
    n_act, n_narrow, n_wide = (lax.axis_size(name) for name in ("act", "narrow", "wide"))
    n_outer = n_wide // 2
    act, narrow, wide = (lax.axis_index(name) for name in ("act", "narrow", "wide"))
    outer, core = wide // 2, wide % 2
    actions, _, taps = trans_weights.shape
    per_group = actions // n_act
    rows0, rows1, len2, len3 = value_now.shape
    len0, len1 = rows0 * n_wide, rows1 * n_narrow
    lengths = (len0, len1, len2, len3)
    chunk = CHUNK_ROWS
    share = (len2 - n_narrow * chunk) // n_act
    n_chunks = share // chunk
    core_flip = [(i, i ^ 1) for i in range(n_wide)]
    act_flip = [(i, (i + 1) % n_act) for i in range(n_act)]
    narrow_flip = [(i, (i + 1) % n_narrow) for i in range(n_narrow)]

    def across(bit):
        return [(i, i ^ (2 * bit)) for i in range(n_wide)]

    def part(begin, size):
        return lax.dynamic_slice_in_dim(value_now, begin, size, 2)

    near = [(0, other, ahead) for ahead in range(n_narrow) for other in range(2)]
    arrivals = near + [
        (far, other, ahead)
        for ahead in range(n_narrow)
        for other in range(2)
        for far in range(1, n_outer)
    ]

    half_band = (taps - 1) // 2
    width = -(-(max(lengths) + 4 * half_band) // LANES) * LANES
    weights = jnp.pad(trans_weights, ((0, 0), (0, 0), (0, width - taps)))
    place = jnp.stack([act, narrow, outer, core]).astype(jnp.int32)
    meta = jnp.concatenate([place, action_order, trans_offsets.T.reshape(-1)])
    smem = pl.BlockSpec(memory_space=pltpu.SMEM)
    q_rows = actions * rows0 * rows1
    kron_hi, kron_lo, side_hi, side_lo, right3 = pl.pallas_call(
        functools.partial(
            prepare_kernel, lengths, taps, (n_act, n_narrow, n_outer), rows0, rows1, arrivals
        ),
        out_shape=(
            jax.ShapeDtypeStruct((q_rows, len0 * len1), BF16),
            jax.ShapeDtypeStruct((q_rows, len0 * len1), BF16),
            jax.ShapeDtypeStruct((q_rows * n_narrow // n_act, len0 * len1), BF16),
            jax.ShapeDtypeStruct((q_rows * n_narrow // n_act, len0 * len1), BF16),
            jax.ShapeDtypeStruct((actions, 2 * len3, 2 * len3), BF16),
        ),
        in_specs=[smem, whole_block()],
        out_specs=(whole_block(),) * 5,
        scratch_shapes=[pltpu.VMEM((len0, len0 * len1), F32), pltpu.VMEM((len1, len0 * len1), F32)],
        compiler_params=params(16),
        cost_estimate=pl.CostEstimate(flops=10**9, bytes_accessed=4 * 10**6, transcendentals=0),
        name="prepare",
    )(meta, weights)
    segments = [(0, share, 0, ahead, n_act) for ahead in range(n_act)]
    segments += [(n_act * share, chunk, 1, ahead, n_narrow) for ahead in range(n_narrow)]
    left2, util23 = pl.pallas_call(
        functools.partial(prepare_third_kernel, taps, segments),
        out_shape=(
            jax.ShapeDtypeStruct((per_group, 2 * len2, 2 * len2), BF16),
            jax.ShapeDtypeStruct((per_group, len2, len3), F32),
        ),
        in_specs=[smem] + [whole_block()] * 3,
        out_specs=(whole_block(),) * 2,
        compiler_params=params(12),
        cost_estimate=pl.CostEstimate(flops=10**9, bytes_accessed=4 * 10**6, transcendentals=0),
        name="prepare_third",
    )(meta, weights, cost_third, cost_fourth)

    side_begin = n_act * share
    inner = (outer == 1) | (outer == 2)
    value_now, inner, place, act_begin, own_begin, other_begin = lax.optimization_barrier(
        (
            value_now,
            inner,
            place,
            act * share,
            side_begin + narrow * chunk,
            side_begin + (n_narrow - 1 - narrow) * chunk,
        )
    )
    chunks = [part(act_begin + index * chunk, chunk) for index in range(n_chunks)]
    to_narrow = jnp.concatenate([part(act_begin, share), part(other_begin, chunk)], axis=2)
    own_side = part(own_begin, chunk)
    mine = jnp.concatenate([part(act_begin, share), own_side], axis=2)
    direct = [lax.ppermute(chunks[0], "wide", across(far)) for far in range(1, n_outer)]
    around = lax.ppermute(to_narrow, "narrow", narrow_flip)
    soon = lax.ppermute(chunks[1], "wide", across(1))
    direct, soon, *_ = lax.optimization_barrier((direct, soon, kron_hi, right3))
    side = jnp.concatenate([own_side, around[:, :, share:]], axis=0)

    bits = [1 << bit for bit in range(1, n_outer.bit_length() - 1)]

    def doubled(own, twin, *done):
        size = own.shape[0]
        blocks = [own, twin]
        for bit in bits:
            grown = after(jnp.concatenate(blocks, axis=0), *done)
            more = lax.ppermute(grown, "wide", across(bit))
            blocks += [more[i : i + size] for i in range(0, more.shape[0], size)]
        return blocks[1:]

    inner_swap = [(2 * a + c, 2 * b + c) for a, b in ((1, 2), (2, 1)) for c in range(2)]
    outward = [(2 * a + c, 2 * b + c) for a, b in ((1, 0), (2, 3)) for c in range(2)]

    def by_line(own, twin, *done):
        size = own.shape[0]
        grown = after(jnp.concatenate([own, twin], axis=0), *done)
        came = lax.ppermute(grown, "wide", inner_swap)
        passed = lax.ppermute(after(came, moved[-1]), "wide", outward)
        return [
            twin,
            jnp.where(inner, came[size:], passed[:size]),
            jnp.where(inner, came[:size], passed[size:]),
        ]

    far0 = jnp.concatenate(direct, axis=0)
    crossed = [lax.ppermute(far0, "wide", core_flip)]
    moved = [lax.ppermute(far0, "narrow", narrow_flip)]
    more = [lax.ppermute(after(one, far0), "wide", across(1)) for one in chunks[2:]]
    late = lax.ppermute(after(side, far0), "wide", across(1))
    owns = chunks + [side]
    twins = [None, soon] + more + [late]
    nears = [mine, lax.ppermute(after(mine, crossed[0]), "wide", core_flip)]
    nears += [around, lax.ppermute(after(around, crossed[0]), "wide", core_flip)]
    nears = [one.reshape(rows0 * rows1, share + chunk, len3) for one in nears]

    def contract(kron, views, routes, out_rows, inputs):
        return pl.pallas_call(
            functools.partial(short_dims_kernel, views, routes),
            out_shape=tuple(
                jax.ShapeDtypeStruct((per_group, rows, chunk, len3), F32) for rows in out_rows
            ),
            in_specs=[whole_block()] * (3 + len(inputs)),
            out_specs=(whole_block(),) * len(out_rows),
            compiler_params=params(12),
            cost_estimate=pl.CostEstimate(flops=10**6, bytes_accessed=10**4, transcendentals=0),
            name="short_dims",
        )(*kron, right3, *inputs)

    block_rows = rows0 * rows1
    far_rows = (n_outer - 1) * block_rows
    def halved(one):
        return [one[i : i + rows0] for i in range(0, n_narrow * rows0, rows0)]

    side_early = [lax.ppermute(half, "wide", core_flip) for half in halved(late)]
    fars = [far0]
    kept, sent = [], []
    for index in range(n_chunks):
        far = fars[index]
        if index:
            if index == 1:
                far = after(far, late)
            crossed.append(lax.ppermute(far, "wide", core_flip))
            moved.append(lax.ppermute(after(far, moved[-1]), "narrow", narrow_flip))
        spread = by_line if index + 1 == n_chunks and n_outer == 4 else doubled
        done = [fars[index]] + ([], moved[:1], kept[:1] + moved[1:2])[min(index, 2)]
        blocks = spread(owns[index + 1], twins[index + 1], *done)
        fars.append(jnp.concatenate(blocks, axis=0))
        ready = ([left2, util23], side_early, ())[min(index, 2)]
        handed = lax.ppermute(after(moved[index], *ready), "wide", core_flip)
        pieces = [far, crossed[index], moved[index], handed]
        inputs = nears + [one.reshape(far_rows, chunk, len3) for one in pieces]
        views = [(i, 0, block_rows, index * chunk) for i in range(len(nears))]
        views += [(len(nears) + i, 0, far_rows, 0) for i in range(len(pieces))]
        cuts = rows0 if index == n_chunks - 1 else 1
        routes = [[(0, slot)] for slot in range(per_group)]
        routes += [[(1 + cut, slot) for cut in range(cuts)] for slot in range(per_group)]
        out_rows = [block_rows] + [block_rows // cuts] * cuts
        keep, *for_act = contract((kron_hi, kron_lo), views, routes, out_rows, inputs)
        kept.append(keep)
        sent.append([])
        for one in for_act:
            before = [one for ones in sent for one in ones][-1:]
            sent[-1].append(lax.ppermute(after(one, *before), "act", act_flip))

    turned = side_early + [
        lax.ppermute(half, "wide", core_flip) for one in blocks[1:] for half in halved(one)
    ]
    inputs = nears + [one.reshape(-1, chunk, len3) for one in blocks + turned]
    views = [(i, 0, block_rows, share) for i in range(len(nears))]
    for ahead in range(n_narrow):
        views += [(len(nears) + i, ahead * block_rows, block_rows, 0) for i in range(len(blocks))]
        first = len(nears) + len(blocks) + ahead
        views += [(first + n_narrow * i, 0, block_rows, 0) for i in range(len(blocks))]
    routes = [[(out, slot) for out in range(1 + rows0)] for slot in range(per_group)]
    out_rows = [block_rows] + [block_rows // rows0] * rows0
    side_kron = (after(side_hi, sent[-1][0]), side_lo)
    side_keep, *side_give = contract(side_kron, views, routes, out_rows, inputs)
    side_got = []
    for one in side_give:
        side_got.append(lax.ppermute(after(one, *side_got[-1:]), "narrow", narrow_flip))

    parts = [(keep, None) for keep in kept] + [(ones[0], None) for ones in sent[:-1]]
    parts += [(sent[-1][0], sent[-1]), (side_keep, None), (side_got[0], side_got)]
    by_row = []
    for row in range(rows0):
        arrays = [cut[row] if cut else one for one, cut in parts]
        specs = [
            pl.BlockSpec(
                (per_group, rows1) + one.shape[2:],
                lambda i, block=0 if cut else row: (0, block, 0, 0),
            )
            for one, (_, cut) in zip(arrays, parts)
        ]
        scores, local = pl.pallas_call(
            functools.partial(third_dim_kernel, len(parts), rows0, row),
            grid=(1,),
            out_shape=(
                jax.ShapeDtypeStruct((per_group, rows1, len2, len3), F32),
                jax.ShapeDtypeStruct((rows1, len2, len3), F32),
            ),
            in_specs=[smem] * 3 + [whole_block()] * 2 + specs,
            out_specs=(whole_block(),) * 2,
            compiler_params=params(20),
            cost_estimate=pl.CostEstimate(
                flops=10**9, bytes_accessed=5 * 10**6, transcendentals=10**6
            ),
            name="third_dim",
        )(meta, cost_first, cost_second, left2, util23, *arrays)
        by_row.append((scores, local, lax.ppermute(local, "act", act_flip)))

    results = ()
    for row, operands in enumerate(by_row):
        results = pl.pallas_call(
            choice_kernel,
            grid=(1,),
            out_shape=(
                jax.ShapeDtypeStruct(value_now.shape, F32),
                jax.ShapeDtypeStruct((per_group,) + value_now.shape, BF16),
            ),
            in_specs=[whole_block()] * 3 + [pl.BlockSpec(memory_space=pl.ANY)] * len(results),
            out_specs=(
                pl.BlockSpec((1, rows1, len2, len3), lambda i, row=row: (row, 0, 0, 0)),
                pl.BlockSpec(
                    (per_group, 1, rows1, len2, len3), lambda i, row=row: (0, row, 0, 0, 0)
                ),
            ),
            input_output_aliases={3: 0, 4: 1} if results else {},
            compiler_params=params(16),
            cost_estimate=pl.CostEstimate(
                flops=10**7, bytes_accessed=5 * 10**6, transcendentals=10**6
            ),
            name="choice",
        )(*operands, *results)
    return tuple(results)


def gather_fits(mesh, value_shape, actions, offset_reach):
    n_wide, n_narrow, n_act = (mesh.shape[name] for name in ("wide", "narrow", "act"))
    len0, len1, len2, len3 = value_shape
    if n_act != 2 or n_wide < 4 or n_wide & (n_wide - 1) or actions % n_act:
        return False
    if n_narrow != 2 or len2 % (n_act * CHUNK_ROWS) or len2 < 4 * n_act * CHUNK_ROWS:
        return False
    if len2 != LANES or len3 != LANES:
        return False
    if (len1 // n_narrow) % SUBLANES or len0 * len1 // (n_wide * n_narrow) % 16 or len0 % n_wide:
        return False
    if max(len0, len1) > LANES or len1 % n_narrow:
        return False
    raw = len0 * len1 * len2 * len3 // (2 * n_act)
    exchanged = 2 * (actions // n_act) * len0 * len1 * len2 * len3 // (n_wide * n_narrow)
    return raw <= exchanged


def solution(mesh):
    def run(value_now, *rest):
        actions = rest[-1].shape[0]
        small = gather_fits(mesh, value_now.shape, actions, rest[4].shape[-1])
        return jax.shard_map(
            gather_body if small else exchange_body,
            mesh=mesh,
            in_specs=(P("wide", "narrow", None, None), P(), P(), P(), P(), P(), P(), P()),
            out_specs=(P("wide", "narrow", None, None), P("act", "wide", "narrow", None, None)),
            check_vma=False,
        )(value_now, *rest)

    return run
```

```python
import functools

import jax
import jax.numpy as jnp
from jax import lax
from jax.experimental import pallas as pl
from jax.experimental.pallas import tpu as pltpu
from jax.sharding import PartitionSpec as P

DISCOUNT = 0.95
HIGHEST = lax.Precision.HIGHEST
F32 = jnp.float32
BF16 = jnp.bfloat16
LANES = 128
SUBLANES = 8
PLACE = 4
CHUNK_ROWS = 16
MIB = 1024 * 1024


def merged(value, axis, join):
    pieces = lax.all_gather(value, axis)
    head = pieces[0]
    tail = pieces[1:]
    subtotal, _ = lax.scan(lambda subtotal, slab: (join(subtotal, slab), None), head, tail)
    return subtotal


def transition(weights, offset, length):
    band_len = weights.shape[0]
    half_band = (band_len - 1) // 2
    normed = weights / jnp.sum(weights)
    row_ids = jnp.arange(length, dtype=jnp.int32)
    tap_ids = jnp.arange(band_len, dtype=jnp.int32)
    target = jnp.clip(row_ids[:, None] + offset + tap_ids[None, :] - half_band, 0, length - 1)
    matched = (target[:, :, None] == row_ids[None, None, :]).astype(normed.dtype)
    return jnp.einsum("ijk,j->ik", matched, normed, precision=HIGHEST)


def exchange_body(
    value_now,
    cost_first,
    cost_second,
    cost_third,
    cost_fourth,
    trans_weights,
    trans_offsets,
    action_order,
):
    size_act = lax.axis_size("act")
    per_group = action_order.shape[0] // size_act
    group_id = lax.axis_index("act")
    my_actions = lax.dynamic_slice_in_dim(action_order, group_id * per_group, per_group)
    rows_first, rows_second, len_third, len_fourth = value_now.shape
    len_first = rows_first * lax.axis_size("wide")
    len_second = rows_second * lax.axis_size("narrow")
    my_weights = jnp.take(trans_weights, my_actions, axis=0)
    my_offsets = jnp.take(trans_offsets, my_actions, axis=0)

    def build(axis_id, length):
        return jax.vmap(lambda weight_row, offset_one: transition(weight_row, offset_one, length))(
            my_weights[:, axis_id], my_offsets[:, axis_id]
        )

    mat_first = build(0, len_first)
    mat_second = build(1, len_second)
    mat_third = build(2, len_third)
    mat_fourth = build(3, len_fourth)
    spread = lax.all_to_all(value_now, "narrow", split_axis=2, concat_axis=1, tiled=True)
    field = jnp.einsum("gij,ajcd->gaicd", mat_second, spread, precision=HIGHEST)
    field = jnp.einsum("gij,gabcj->gabci", mat_fourth, field, precision=HIGHEST)
    field = lax.all_to_all(field, "narrow", split_axis=2, concat_axis=3, tiled=True)
    field = lax.all_to_all(field, "wide", split_axis=3, concat_axis=1, tiled=True)
    field = jnp.einsum("gij,gjbcd->gibcd", mat_first, field, precision=HIGHEST)
    field = lax.all_to_all(field, "wide", split_axis=1, concat_axis=3, tiled=True)
    expected = jnp.einsum("gij,gabjd->gabid", mat_third, field, precision=HIGHEST)
    start_first = lax.axis_index("wide") * rows_first
    start_second = lax.axis_index("narrow") * rows_second
    util_first = lax.dynamic_slice_in_dim(
        jnp.take(cost_first, my_actions, axis=0), start_first, rows_first, 1
    )
    util_second = lax.dynamic_slice_in_dim(
        jnp.take(cost_second, my_actions, axis=0), start_second, rows_second, 1
    )
    util_third = jnp.take(cost_third, my_actions, axis=0)
    util_fourth = jnp.take(cost_fourth, my_actions, axis=0)
    utility = (
        util_first[:, :, None, None, None]
        + util_second[:, None, :, None, None]
        + util_third[:, None, None, :, None]
        + util_fourth[:, None, None, None, :]
    )
    scores = utility + DISCOUNT * expected
    local_max = jnp.max(scores, axis=0)
    local_sum = jnp.sum(jnp.exp(scores - local_max), axis=0)
    log_total = merged(local_max + jnp.log(local_sum), "act", jnp.logaddexp)
    choice_prob = jnp.exp(scores - log_total).astype(jnp.bfloat16)
    return (log_total, choice_prob)


def halves(x):
    high = x.astype(BF16)
    return high, (x - high.astype(F32)).astype(BF16)


def dot32(a, b):
    return jnp.dot(a, b, preferred_element_type=F32, precision=HIGHEST)


def banded(weights, offset, length, taps):
    half_band = (taps - 1) // 2
    width = weights.shape[1]
    normed = weights / jnp.sum(weights, axis=1, keepdims=True)
    tile = jnp.broadcast_to(normed, (SUBLANES, width))
    tile = pltpu.roll(tile, lax.rem(offset + (width - half_band), width), 1)
    rows = jnp.concatenate([tile] * (length // SUBLANES), axis=0)
    rows = pltpu.roll(rows, 0, 1, stride=1, stride_axis=0)
    lane = lax.broadcasted_iota(jnp.int32, (length, width), 1)
    under = lane >= width - 2 * half_band
    over = (lane >= length) & (lane < length + 2 * half_band)
    under_sum = jnp.sum(jnp.where(under, rows, 0.0), axis=1, keepdims=True)
    over_sum = jnp.sum(jnp.where(over, rows, 0.0), axis=1, keepdims=True)
    span = -(-length // LANES) * LANES
    kept = lane[:, :span]
    body = jnp.where(kept < length, rows[:, :span], 0.0)
    body = body + jnp.where(kept == 0, under_sum, 0.0)
    return body + jnp.where(kept == length - 1, over_sum, 0.0)


def prepare_kernel(
    lengths, taps, sizes, rows0, rows1, arrivals, meta, weights,
    kron_hi, kron_lo, side_hi, side_lo, right3, wide0, wide1,
):
    n_act, n_narrow, n_outer = sizes
    len0, len1, len2, len3 = lengths
    act, narrow, outer, core = (meta[i] for i in range(PLACE))
    actions = weights.shape[0]
    per_group = actions // n_act
    columns = len0 * len1

    def wrapped(index, size):
        return lax.rem(index + size, size)

    lane = lax.broadcasted_iota(jnp.int32, (1, columns), 1)
    ids0 = jnp.zeros((1, columns), jnp.int32)
    ids1 = jnp.zeros((1, columns), jnp.int32)
    for block, (far, part, ahead) in enumerate(arrivals):
        from_outer, from_core = outer ^ far, wrapped(core + part, 2)
        for row in range(rows0):
            start = (block * rows0 + row) * rows1
            inside = (lane >= start) & (lane < start + rows1)
            first = (from_outer * 2 + from_core) * rows0 + row
            second = wrapped(narrow - ahead, n_narrow) * rows1 - start
            ids0 = jnp.where(inside, first, ids0)
            ids1 = jnp.where(inside, second + lane, ids1)
    spread0 = (lax.broadcasted_iota(jnp.int32, (LANES, columns), 0) == ids0).astype(F32)
    spread1 = (lax.broadcasted_iota(jnp.int32, (LANES, columns), 0) == ids1).astype(F32)

    for action in range(actions):
        group, slot = divmod(action, per_group)
        which = meta[PLACE + wrapped(act + group, n_act) * per_group + slot]
        rows = weights[which]
        mats = [
            banded(
                rows[axis : axis + 1, :],
                meta[PLACE + (1 + axis) * actions + which],
                lengths[axis],
                taps,
            )
            for axis in (0, 1, 3)
        ]
        wide0[...] = dot32(mats[0], spread0)
        wide1[...] = dot32(mats[1], spread1)
        base = (outer * 2 + core) * rows0
        for ahead in range(n_narrow if group == 0 else 1):
            begin = wrapped(narrow + ahead, n_narrow) * rows1
            second = wide1[pl.ds(pl.multiple_of(begin, SUBLANES), rows1), :]
            blocks = [wide0[pl.ds(base + row, 1), :] * second for row in range(rows0)]
            high, low = halves(jnp.concatenate(blocks, axis=0))
            if ahead == 0:
                start = action * rows0 * rows1
                kron_hi[start : start + rows0 * rows1, :] = high
                kron_lo[start : start + rows0 * rows1, :] = low
            if group == 0:
                start = (slot * n_narrow + ahead) * rows0 * rows1
                side_hi[start : start + rows0 * rows1, :] = high
                side_lo[start : start + rows0 * rows1, :] = low
        high, low = halves(mats[2].T)
        row_pair = jnp.concatenate([high, low], axis=1)
        right3[action] = jnp.concatenate([row_pair, row_pair], axis=0)


def prepare_third_kernel(taps, segments, meta, weights, third, fourth, left2, util23):
    act, actions, per_group = meta[0], weights.shape[0], left2.shape[0]
    len2, len3 = util23.shape[1:]
    lane2 = lax.broadcasted_iota(jnp.int32, (1, len2), 1)
    ids2 = jnp.zeros((1, len2), jnp.int32)
    filled = 0
    for begin, size, axis, ahead, count in segments:
        source = begin + lax.rem(meta[axis] + ahead, count) * size
        inside = (lane2 >= filled) & (lane2 < filled + size)
        ids2 = jnp.where(inside, source - filled + lane2, ids2)
        filled += size
    order2 = (lax.broadcasted_iota(jnp.int32, (len2, len2), 0) == ids2).astype(F32)

    for slot in range(per_group):
        which = meta[PLACE + act * per_group + slot]
        offset = meta[PLACE + 3 * actions + which]
        matrix = banded(weights[which][2:3, :], offset, len2, taps)
        high, low = halves(dot32(matrix, order2))
        left2[slot] = jnp.concatenate(
            [jnp.concatenate([high, high], axis=1), jnp.concatenate([low, low], axis=1)], axis=0
        )
        column = jnp.broadcast_to(third[pl.ds(which, 1), :], (len3, len2)).T
        util23[slot] = column + fourth[pl.ds(which, 1), :]


def short_dims_kernel(views, routes, kron_hi, kron_lo, right3, *refs):
    n_inputs = 1 + max(view[0] for view in views)
    inputs, outs = refs[:n_inputs], refs[n_inputs:]
    rows, depth = outs[0].shape[2:]
    per_action = kron_hi.shape[0] // len(routes)
    q_hi, q_lo = kron_hi[...], kron_lo[...]
    mixed = []
    for row in range(0, rows, 2):
        cols = [
            jnp.concatenate(
                [
                    inputs[which][lead : lead + count, start + row + extra, :]
                    for which, lead, count, start in views
                ],
                axis=0,
            )
            for extra in range(2)
        ]
        x_hi, x_lo = halves(jnp.concatenate(cols, axis=1))
        out = (
            jnp.dot(q_hi, x_hi, preferred_element_type=F32)
            + jnp.dot(q_hi, x_lo, preferred_element_type=F32)
            + jnp.dot(q_lo, x_hi, preferred_element_type=F32)
        )
        mixed += [out[:, :depth], out[:, depth:]]
    for action, route in enumerate(routes):
        start = action * per_action
        block = jnp.concatenate([one[start : start + per_action] for one in mixed], axis=0)
        t_hi, t_lo = halves(block)
        both = jnp.dot(
            jnp.concatenate([t_hi, t_lo], axis=1), right3[action], preferred_element_type=F32
        )
        done = both[:, :depth] + both[:, depth:]
        for row in range(rows):
            first = row * per_action
            for which, slot in route:
                count = outs[which].shape[1]
                outs[which][slot, :, row, :] = done[first : first + count]
                first += count


def third_dim_kernel(n_pieces, rows0, row, meta, costs0, costs1, left2, util23, *refs):
    pieces, scores, local = refs[:n_pieces], refs[n_pieces], refs[n_pieces + 1]
    per_group, rows1 = scores.shape[:2]
    length = util23.shape[1]
    depth = util23.shape[2]
    which = [meta[PLACE + meta[0] * per_group + slot] for slot in range(per_group)]
    first = (meta[2] * 2 + meta[3]) * rows0 + row
    start1 = meta[1] * rows1
    for second in range(0, rows1, 2):
        for slot in range(per_group):
            cols = [
                jnp.concatenate([piece[slot, second + extra] for piece in pieces], axis=0)
                for extra in range(2)
            ]
            g_hi, g_lo = halves(jnp.concatenate(cols, axis=1))
            both = jnp.dot(
                left2[slot], jnp.concatenate([g_hi, g_lo], axis=0), preferred_element_type=F32
            )
            expected = both[:length] + both[length:]
            for extra in range(2):
                flat = costs0[which[slot], first] + costs1[which[slot], start1 + second + extra]
                scores[slot, second + extra] = (util23[slot] + flat) + DISCOUNT * expected[
                    :, extra * depth : (extra + 1) * depth
                ]
        for extra in range(2):
            found = [scores[slot, second + extra] for slot in range(per_group)]
            top = functools.reduce(jnp.maximum, found)
            total = functools.reduce(jnp.add, [jnp.exp(one - top) for one in found])
            local[second + extra] = top + jnp.log(total)


def choice_kernel(scores, mine, other, *refs):
    new_value, choice_prob = refs[-2:]
    a, b = mine[...], other[...]
    top, low = jnp.maximum(a, b), jnp.minimum(a, b)
    total = top + jnp.log(1.0 + jnp.exp(low - top))
    new_value[0] = total
    for slot in range(scores.shape[0]):
        choice_prob[slot, 0] = jnp.exp(scores[slot] - total).astype(choice_prob.dtype)


def after(value, *done):
    return lax.optimization_barrier((value, *done))[0] if done else value


def whole_block():
    return pl.BlockSpec(memory_space=pltpu.VMEM)


def params(mebibytes):
    return pltpu.CompilerParams(vmem_limit_bytes=mebibytes * MIB)


def gather_body(
    value_now,
    cost_first,
    cost_second,
    cost_third,
    cost_fourth,
    trans_weights,
    trans_offsets,
    action_order,
):
    n_act, n_narrow, n_wide = (lax.axis_size(name) for name in ("act", "narrow", "wide"))
    n_outer = n_wide // 2
    act, narrow, wide = (lax.axis_index(name) for name in ("act", "narrow", "wide"))
    outer, core = wide // 2, wide % 2
    actions, _, taps = trans_weights.shape
    per_group = actions // n_act
    rows0, rows1, len2, len3 = value_now.shape
    len0, len1 = rows0 * n_wide, rows1 * n_narrow
    lengths = (len0, len1, len2, len3)
    chunk = CHUNK_ROWS
    share = (len2 - n_narrow * chunk) // n_act
    n_chunks = share // chunk
    core_flip = [(i, i ^ 1) for i in range(n_wide)]
    act_flip = [(i, (i + 1) % n_act) for i in range(n_act)]
    narrow_flip = [(i, (i + 1) % n_narrow) for i in range(n_narrow)]

    def across(bit):
        return [(i, i ^ (2 * bit)) for i in range(n_wide)]

    def part(begin, size):
        return lax.dynamic_slice_in_dim(value_now, begin, size, 2)

    near = [(0, other, ahead) for ahead in range(n_narrow) for other in range(2)]
    arrivals = near + [
        (far, other, ahead)
        for ahead in range(n_narrow)
        for other in range(2)
        for far in range(1, n_outer)
    ]

    half_band = (taps - 1) // 2
    width = -(-(max(lengths) + 4 * half_band) // LANES) * LANES
    weights = jnp.pad(trans_weights, ((0, 0), (0, 0), (0, width - taps)))
    place = jnp.stack([act, narrow, outer, core]).astype(jnp.int32)
    meta = jnp.concatenate([place, action_order, trans_offsets.T.reshape(-1)])
    smem = pl.BlockSpec(memory_space=pltpu.SMEM)
    q_rows = actions * rows0 * rows1
    kron_hi, kron_lo, side_hi, side_lo, right3 = pl.pallas_call(
        functools.partial(
            prepare_kernel, lengths, taps, (n_act, n_narrow, n_outer), rows0, rows1, arrivals
        ),
        out_shape=(
            jax.ShapeDtypeStruct((q_rows, len0 * len1), BF16),
            jax.ShapeDtypeStruct((q_rows, len0 * len1), BF16),
            jax.ShapeDtypeStruct((q_rows * n_narrow // n_act, len0 * len1), BF16),
            jax.ShapeDtypeStruct((q_rows * n_narrow // n_act, len0 * len1), BF16),
            jax.ShapeDtypeStruct((actions, 2 * len3, 2 * len3), BF16),
        ),
        in_specs=[smem, whole_block()],
        out_specs=(whole_block(),) * 5,
        scratch_shapes=[pltpu.VMEM((len0, len0 * len1), F32), pltpu.VMEM((len1, len0 * len1), F32)],
        compiler_params=params(16),
        cost_estimate=pl.CostEstimate(flops=10**9, bytes_accessed=4 * 10**6, transcendentals=0),
        name="prepare",
    )(meta, weights)
    segments = [(0, share, 0, ahead, n_act) for ahead in range(n_act)]
    segments += [(n_act * share, chunk, 1, ahead, n_narrow) for ahead in range(n_narrow)]
    left2, util23 = pl.pallas_call(
        functools.partial(prepare_third_kernel, taps, segments),
        out_shape=(
            jax.ShapeDtypeStruct((per_group, 2 * len2, 2 * len2), BF16),
            jax.ShapeDtypeStruct((per_group, len2, len3), F32),
        ),
        in_specs=[smem] + [whole_block()] * 3,
        out_specs=(whole_block(),) * 2,
        compiler_params=params(12),
        cost_estimate=pl.CostEstimate(flops=10**9, bytes_accessed=4 * 10**6, transcendentals=0),
        name="prepare_third",
    )(meta, weights, cost_third, cost_fourth)

    side_begin = n_act * share
    inner = (outer == 1) | (outer == 2)
    value_now, inner, place, act_begin, own_begin, other_begin = lax.optimization_barrier(
        (
            value_now,
            inner,
            place,
            act * share,
            side_begin + narrow * chunk,
            side_begin + (n_narrow - 1 - narrow) * chunk,
        )
    )
    chunks = [part(act_begin + index * chunk, chunk) for index in range(n_chunks)]
    to_narrow = jnp.concatenate([part(act_begin, share), part(other_begin, chunk)], axis=2)
    own_side = part(own_begin, chunk)
    mine = jnp.concatenate([part(act_begin, share), own_side], axis=2)
    direct = [lax.ppermute(chunks[0], "wide", across(far)) for far in range(1, n_outer)]
    around = lax.ppermute(to_narrow, "narrow", narrow_flip)
    soon = lax.ppermute(chunks[1], "wide", across(1))
    direct, soon, *_ = lax.optimization_barrier((direct, soon, kron_hi, right3))
    side = jnp.concatenate([own_side, around[:, :, share:]], axis=0)

    bits = [1 << bit for bit in range(1, n_outer.bit_length() - 1)]

    def doubled(own, twin, *done):
        size = own.shape[0]
        blocks = [own, twin]
        for bit in bits:
            grown = after(jnp.concatenate(blocks, axis=0), *done)
            more = lax.ppermute(grown, "wide", across(bit))
            blocks += [more[i : i + size] for i in range(0, more.shape[0], size)]
        return blocks[1:]

    inner_swap = [(2 * a + c, 2 * b + c) for a, b in ((1, 2), (2, 1)) for c in range(2)]
    outward = [(2 * a + c, 2 * b + c) for a, b in ((1, 0), (2, 3)) for c in range(2)]

    def by_line(own, twin, *done):
        size = own.shape[0]
        grown = after(jnp.concatenate([own, twin], axis=0), *done)
        came = lax.ppermute(grown, "wide", inner_swap)
        passed = lax.ppermute(after(came, moved[-1]), "wide", outward)
        return [
            twin,
            jnp.where(inner, came[size:], passed[:size]),
            jnp.where(inner, came[:size], passed[size:]),
        ]

    far0 = jnp.concatenate(direct, axis=0)
    crossed = [lax.ppermute(far0, "wide", core_flip)]
    moved = [lax.ppermute(far0, "narrow", narrow_flip)]
    more = [lax.ppermute(after(one, crossed[0]), "wide", across(1)) for one in chunks[2:]]
    late = lax.ppermute(after(side, far0), "wide", across(1))
    owns = chunks + [side]
    twins = [None, soon] + more + [late]
    nears = [mine, lax.ppermute(after(mine, crossed[0]), "wide", core_flip)]
    nears += [around, lax.ppermute(after(around, crossed[0]), "wide", core_flip)]
    nears = [one.reshape(rows0 * rows1, share + chunk, len3) for one in nears]

    def contract(kron, views, routes, out_rows, inputs):
        return pl.pallas_call(
            functools.partial(short_dims_kernel, views, routes),
            out_shape=tuple(
                jax.ShapeDtypeStruct((per_group, rows, chunk, len3), F32) for rows in out_rows
            ),
            in_specs=[whole_block()] * (3 + len(inputs)),
            out_specs=(whole_block(),) * len(out_rows),
            compiler_params=params(12),
            cost_estimate=pl.CostEstimate(flops=10**6, bytes_accessed=10**4, transcendentals=0),
            name="short_dims",
        )(*kron, right3, *inputs)

    block_rows = rows0 * rows1
    far_rows = (n_outer - 1) * block_rows
    def halved(one):
        return [one[i : i + rows0] for i in range(0, n_narrow * rows0, rows0)]

    side_early = [lax.ppermute(half, "wide", core_flip) for half in halved(late)]
    fars = [far0]
    kept, sent = [], []
    for index in range(n_chunks):
        far = fars[index]
        if index:
            if index == 1:
                far = after(far, late)
            crossed.append(lax.ppermute(far, "wide", core_flip))
            moved.append(lax.ppermute(after(far, moved[-1]), "narrow", narrow_flip))
        spread = by_line if index + 1 == n_chunks and n_outer == 4 else doubled
        done = [fars[index]] + ([], moved[:1], kept[:1] + moved[1:2])[min(index, 2)]
        blocks = spread(owns[index + 1], twins[index + 1], *done)
        fars.append(jnp.concatenate(blocks, axis=0))
        ready = ([left2, util23], side_early, ())[min(index, 2)]
        handed = lax.ppermute(after(moved[index], *ready), "wide", core_flip)
        pieces = [far, crossed[index], moved[index], handed]
        inputs = nears + [one.reshape(far_rows, chunk, len3) for one in pieces]
        views = [(i, 0, block_rows, index * chunk) for i in range(len(nears))]
        views += [(len(nears) + i, 0, far_rows, 0) for i in range(len(pieces))]
        cuts = rows0 if index == n_chunks - 1 else 1
        routes = [[(0, slot)] for slot in range(per_group)]
        routes += [[(1 + cut, slot) for cut in range(cuts)] for slot in range(per_group)]
        out_rows = [block_rows] + [block_rows // cuts] * cuts
        keep, *for_act = contract((kron_hi, kron_lo), views, routes, out_rows, inputs)
        kept.append(keep)
        sent.append([])
        for one in for_act:
            before = [one for ones in sent for one in ones][-1:]
            sent[-1].append(lax.ppermute(after(one, *before), "act", act_flip))

    turned = side_early + [
        lax.ppermute(half, "wide", core_flip) for one in blocks[1:] for half in halved(one)
    ]
    inputs = nears + [one.reshape(-1, chunk, len3) for one in blocks + turned]
    views = [(i, 0, block_rows, share) for i in range(len(nears))]
    for ahead in range(n_narrow):
        views += [(len(nears) + i, ahead * block_rows, block_rows, 0) for i in range(len(blocks))]
        first = len(nears) + len(blocks) + ahead
        views += [(first + n_narrow * i, 0, block_rows, 0) for i in range(len(blocks))]
    routes = [[(out, slot) for out in range(1 + rows0)] for slot in range(per_group)]
    out_rows = [block_rows] + [block_rows // rows0] * rows0
    side_kron = (after(side_hi, sent[-1][0]), side_lo)
    side_keep, *side_give = contract(side_kron, views, routes, out_rows, inputs)
    side_got = []
    for one in side_give:
        side_got.append(lax.ppermute(after(one, *side_got[-1:]), "narrow", narrow_flip))

    parts = [(keep, None) for keep in kept] + [(ones[0], None) for ones in sent[:-1]]
    parts += [(sent[-1][0], sent[-1]), (side_keep, None), (side_got[0], side_got)]
    by_row = []
    for row in range(rows0):
        arrays = [cut[row] if cut else one for one, cut in parts]
        specs = [
            pl.BlockSpec(
                (per_group, rows1) + one.shape[2:],
                lambda i, block=0 if cut else row: (0, block, 0, 0),
            )
            for one, (_, cut) in zip(arrays, parts)
        ]
        scores, local = pl.pallas_call(
            functools.partial(third_dim_kernel, len(parts), rows0, row),
            grid=(1,),
            out_shape=(
                jax.ShapeDtypeStruct((per_group, rows1, len2, len3), F32),
                jax.ShapeDtypeStruct((rows1, len2, len3), F32),
            ),
            in_specs=[smem] * 3 + [whole_block()] * 2 + specs,
            out_specs=(whole_block(),) * 2,
            compiler_params=params(20),
            cost_estimate=pl.CostEstimate(
                flops=10**9, bytes_accessed=5 * 10**6, transcendentals=10**6
            ),
            name="third_dim",
        )(meta, cost_first, cost_second, left2, util23, *arrays)
        by_row.append((scores, local, lax.ppermute(local, "act", act_flip)))

    results = ()
    for row, operands in enumerate(by_row):
        results = pl.pallas_call(
            choice_kernel,
            grid=(1,),
            out_shape=(
                jax.ShapeDtypeStruct(value_now.shape, F32),
                jax.ShapeDtypeStruct((per_group,) + value_now.shape, BF16),
            ),
            in_specs=[whole_block()] * 3 + [pl.BlockSpec(memory_space=pl.ANY)] * len(results),
            out_specs=(
                pl.BlockSpec((1, rows1, len2, len3), lambda i, row=row: (row, 0, 0, 0)),
                pl.BlockSpec(
                    (per_group, 1, rows1, len2, len3), lambda i, row=row: (0, row, 0, 0, 0)
                ),
            ),
            input_output_aliases={3: 0, 4: 1} if results else {},
            compiler_params=params(16),
            cost_estimate=pl.CostEstimate(
                flops=10**7, bytes_accessed=5 * 10**6, transcendentals=10**6
            ),
            name="choice",
        )(*operands, *results)
    return tuple(results)


def gather_fits(mesh, value_shape, actions, offset_reach):
    n_wide, n_narrow, n_act = (mesh.shape[name] for name in ("wide", "narrow", "act"))
    len0, len1, len2, len3 = value_shape
    if n_act != 2 or n_wide < 4 or n_wide & (n_wide - 1) or actions % n_act:
        return False
    if n_narrow != 2 or len2 % (n_act * CHUNK_ROWS) or len2 < 4 * n_act * CHUNK_ROWS:
        return False
    if len2 != LANES or len3 != LANES:
        return False
    if (len1 // n_narrow) % SUBLANES or len0 * len1 // (n_wide * n_narrow) % 16 or len0 % n_wide:
        return False
    if max(len0, len1) > LANES or len1 % n_narrow:
        return False
    raw = len0 * len1 * len2 * len3 // (2 * n_act)
    exchanged = 2 * (actions // n_act) * len0 * len1 * len2 * len3 // (n_wide * n_narrow)
    return raw <= exchanged


def solution(mesh):
    def run(value_now, *rest):
        actions = rest[-1].shape[0]
        small = gather_fits(mesh, value_now.shape, actions, rest[4].shape[-1])
        return jax.shard_map(
            gather_body if small else exchange_body,
            mesh=mesh,
            in_specs=(P("wide", "narrow", None, None), P(), P(), P(), P(), P(), P(), P()),
            out_specs=(P("wide", "narrow", None, None), P("act", "wide", "narrow", None, None)),
            check_vma=False,
        )(value_now, *rest)

    return run
```

```python
import functools

import jax
import jax.numpy as jnp
from jax import lax
from jax.experimental import pallas as pl
from jax.experimental.pallas import tpu as pltpu
from jax.sharding import PartitionSpec as P

DISCOUNT = 0.95
HIGHEST = lax.Precision.HIGHEST
F32 = jnp.float32
BF16 = jnp.bfloat16
LANES = 128
SUBLANES = 8
PLACE = 4
CHUNK_ROWS = 16
MIB = 1024 * 1024


def merged(value, axis, join):
    pieces = lax.all_gather(value, axis)
    head = pieces[0]
    tail = pieces[1:]
    subtotal, _ = lax.scan(lambda subtotal, slab: (join(subtotal, slab), None), head, tail)
    return subtotal


def transition(weights, offset, length):
    band_len = weights.shape[0]
    half_band = (band_len - 1) // 2
    normed = weights / jnp.sum(weights)
    row_ids = jnp.arange(length, dtype=jnp.int32)
    tap_ids = jnp.arange(band_len, dtype=jnp.int32)
    target = jnp.clip(row_ids[:, None] + offset + tap_ids[None, :] - half_band, 0, length - 1)
    matched = (target[:, :, None] == row_ids[None, None, :]).astype(normed.dtype)
    return jnp.einsum("ijk,j->ik", matched, normed, precision=HIGHEST)


def exchange_body(
    value_now,
    cost_first,
    cost_second,
    cost_third,
    cost_fourth,
    trans_weights,
    trans_offsets,
    action_order,
):
    size_act = lax.axis_size("act")
    per_group = action_order.shape[0] // size_act
    group_id = lax.axis_index("act")
    my_actions = lax.dynamic_slice_in_dim(action_order, group_id * per_group, per_group)
    rows_first, rows_second, len_third, len_fourth = value_now.shape
    len_first = rows_first * lax.axis_size("wide")
    len_second = rows_second * lax.axis_size("narrow")
    my_weights = jnp.take(trans_weights, my_actions, axis=0)
    my_offsets = jnp.take(trans_offsets, my_actions, axis=0)

    def build(axis_id, length):
        return jax.vmap(lambda weight_row, offset_one: transition(weight_row, offset_one, length))(
            my_weights[:, axis_id], my_offsets[:, axis_id]
        )

    mat_first = build(0, len_first)
    mat_second = build(1, len_second)
    mat_third = build(2, len_third)
    mat_fourth = build(3, len_fourth)
    spread = lax.all_to_all(value_now, "narrow", split_axis=2, concat_axis=1, tiled=True)
    field = jnp.einsum("gij,ajcd->gaicd", mat_second, spread, precision=HIGHEST)
    field = jnp.einsum("gij,gabcj->gabci", mat_fourth, field, precision=HIGHEST)
    field = lax.all_to_all(field, "narrow", split_axis=2, concat_axis=3, tiled=True)
    field = lax.all_to_all(field, "wide", split_axis=3, concat_axis=1, tiled=True)
    field = jnp.einsum("gij,gjbcd->gibcd", mat_first, field, precision=HIGHEST)
    field = lax.all_to_all(field, "wide", split_axis=1, concat_axis=3, tiled=True)
    expected = jnp.einsum("gij,gabjd->gabid", mat_third, field, precision=HIGHEST)
    start_first = lax.axis_index("wide") * rows_first
    start_second = lax.axis_index("narrow") * rows_second
    util_first = lax.dynamic_slice_in_dim(
        jnp.take(cost_first, my_actions, axis=0), start_first, rows_first, 1
    )
    util_second = lax.dynamic_slice_in_dim(
        jnp.take(cost_second, my_actions, axis=0), start_second, rows_second, 1
    )
    util_third = jnp.take(cost_third, my_actions, axis=0)
    util_fourth = jnp.take(cost_fourth, my_actions, axis=0)
    utility = (
        util_first[:, :, None, None, None]
        + util_second[:, None, :, None, None]
        + util_third[:, None, None, :, None]
        + util_fourth[:, None, None, None, :]
    )
    scores = utility + DISCOUNT * expected
    local_max = jnp.max(scores, axis=0)
    local_sum = jnp.sum(jnp.exp(scores - local_max), axis=0)
    log_total = merged(local_max + jnp.log(local_sum), "act", jnp.logaddexp)
    choice_prob = jnp.exp(scores - log_total).astype(jnp.bfloat16)
    return (log_total, choice_prob)


def halves(x):
    high = x.astype(BF16)
    return high, (x - high.astype(F32)).astype(BF16)


def dot32(a, b):
    return jnp.dot(a, b, preferred_element_type=F32, precision=HIGHEST)


def banded(weights, offset, length, taps):
    half_band = (taps - 1) // 2
    width = weights.shape[1]
    normed = weights / jnp.sum(weights, axis=1, keepdims=True)
    tile = jnp.broadcast_to(normed, (SUBLANES, width))
    tile = pltpu.roll(tile, lax.rem(offset + (width - half_band), width), 1)
    rows = jnp.concatenate([tile] * (length // SUBLANES), axis=0)
    rows = pltpu.roll(rows, 0, 1, stride=1, stride_axis=0)
    lane = lax.broadcasted_iota(jnp.int32, (length, width), 1)
    under = lane >= width - 2 * half_band
    over = (lane >= length) & (lane < length + 2 * half_band)
    under_sum = jnp.sum(jnp.where(under, rows, 0.0), axis=1, keepdims=True)
    over_sum = jnp.sum(jnp.where(over, rows, 0.0), axis=1, keepdims=True)
    span = -(-length // LANES) * LANES
    kept = lane[:, :span]
    body = jnp.where(kept < length, rows[:, :span], 0.0)
    body = body + jnp.where(kept == 0, under_sum, 0.0)
    return body + jnp.where(kept == length - 1, over_sum, 0.0)


def prepare_kernel(
    lengths, taps, sizes, rows0, rows1, arrivals, meta, weights,
    kron_hi, kron_lo, side_hi, side_lo, right3, wide0, wide1,
):
    n_act, n_narrow, n_outer = sizes
    len0, len1, len2, len3 = lengths
    act, narrow, outer, core = (meta[i] for i in range(PLACE))
    actions = weights.shape[0]
    per_group = actions // n_act
    columns = len0 * len1

    def wrapped(index, size):
        return lax.rem(index + size, size)

    lane = lax.broadcasted_iota(jnp.int32, (1, columns), 1)
    ids0 = jnp.zeros((1, columns), jnp.int32)
    ids1 = jnp.zeros((1, columns), jnp.int32)
    for block, (far, part, ahead) in enumerate(arrivals):
        from_outer, from_core = outer ^ far, wrapped(core + part, 2)
        for row in range(rows0):
            start = (block * rows0 + row) * rows1
            inside = (lane >= start) & (lane < start + rows1)
            first = (from_outer * 2 + from_core) * rows0 + row
            second = wrapped(narrow - ahead, n_narrow) * rows1 - start
            ids0 = jnp.where(inside, first, ids0)
            ids1 = jnp.where(inside, second + lane, ids1)
    spread0 = (lax.broadcasted_iota(jnp.int32, (LANES, columns), 0) == ids0).astype(F32)
    spread1 = (lax.broadcasted_iota(jnp.int32, (LANES, columns), 0) == ids1).astype(F32)

    for action in range(actions):
        group, slot = divmod(action, per_group)
        which = meta[PLACE + wrapped(act + group, n_act) * per_group + slot]
        rows = weights[which]
        mats = [
            banded(
                rows[axis : axis + 1, :],
                meta[PLACE + (1 + axis) * actions + which],
                lengths[axis],
                taps,
            )
            for axis in (0, 1, 3)
        ]
        wide0[...] = dot32(mats[0], spread0)
        wide1[...] = dot32(mats[1], spread1)
        base = (outer * 2 + core) * rows0
        products = []
        for ahead in range(n_narrow if group == 0 else 1):
            begin = wrapped(narrow + ahead, n_narrow) * rows1
            second = wide1[pl.ds(pl.multiple_of(begin, SUBLANES), rows1), :]
            blocks = [wide0[pl.ds(base + row, 1), :] * second for row in range(rows0)]
            high, low = halves(jnp.concatenate(blocks, axis=0))
            if ahead == 0:
                start = action * rows0 * rows1
                kron_hi[start : start + rows0 * rows1, :] = high
                kron_lo[start : start + rows0 * rows1, :] = low
            products.append(blocks)
        for row in range(rows0 if group == 0 else 0):
            high, low = halves(jnp.concatenate([blocks[row] for blocks in products], axis=0))
            start = (row * per_group + slot) * n_narrow * rows1
            side_hi[start : start + n_narrow * rows1, :] = high
            side_lo[start : start + n_narrow * rows1, :] = low
        high, low = halves(mats[2].T)
        row_pair = jnp.concatenate([high, low], axis=1)
        right3[action] = jnp.concatenate([row_pair, row_pair], axis=0)


def prepare_third_kernel(taps, segments, meta, weights, third, fourth, left2, util23):
    act, actions, per_group = meta[0], weights.shape[0], left2.shape[0]
    len2, len3 = util23.shape[1:]
    lane2 = lax.broadcasted_iota(jnp.int32, (1, len2), 1)
    ids2 = jnp.zeros((1, len2), jnp.int32)
    filled = 0
    for begin, size, axis, ahead, count in segments:
        source = begin + lax.rem(meta[axis] + ahead, count) * size
        inside = (lane2 >= filled) & (lane2 < filled + size)
        ids2 = jnp.where(inside, source - filled + lane2, ids2)
        filled += size
    order2 = (lax.broadcasted_iota(jnp.int32, (len2, len2), 0) == ids2).astype(F32)

    for slot in range(per_group):
        which = meta[PLACE + act * per_group + slot]
        offset = meta[PLACE + 3 * actions + which]
        matrix = banded(weights[which][2:3, :], offset, len2, taps)
        high, low = halves(dot32(matrix, order2))
        left2[slot] = jnp.concatenate(
            [jnp.concatenate([high, high], axis=1), jnp.concatenate([low, low], axis=1)], axis=0
        )
        column = jnp.broadcast_to(third[pl.ds(which, 1), :], (len3, len2)).T
        util23[slot] = column + fourth[pl.ds(which, 1), :]


def short_dims_kernel(views, routes, kron_hi, kron_lo, right3, *refs):
    n_inputs = 1 + max(view[0] for view in views)
    inputs, outs = refs[:n_inputs], refs[n_inputs:]
    rows, depth = outs[0].shape[2:]
    per_action = kron_hi.shape[0] // len(routes)
    q_hi, q_lo = kron_hi[...], kron_lo[...]
    mixed = []
    for row in range(0, rows, 2):
        cols = [
            jnp.concatenate(
                [
                    inputs[which][lead : lead + count, start + row + extra, :]
                    for which, lead, count, start in views
                ],
                axis=0,
            )
            for extra in range(2)
        ]
        x_hi, x_lo = halves(jnp.concatenate(cols, axis=1))
        out = (
            jnp.dot(q_hi, x_hi, preferred_element_type=F32)
            + jnp.dot(q_hi, x_lo, preferred_element_type=F32)
            + jnp.dot(q_lo, x_hi, preferred_element_type=F32)
        )
        mixed += [out[:, :depth], out[:, depth:]]
    for action, route in enumerate(routes):
        start = action * per_action
        block = jnp.concatenate([one[start : start + per_action] for one in mixed], axis=0)
        t_hi, t_lo = halves(block)
        both = jnp.dot(
            jnp.concatenate([t_hi, t_lo], axis=1), right3[action], preferred_element_type=F32
        )
        done = both[:, :depth] + both[:, depth:]
        for row in range(rows):
            first = row * per_action
            for which, slot in route:
                count = outs[which].shape[1]
                outs[which][slot, :, row, :] = done[first : first + count]
                first += count


def third_dim_kernel(n_pieces, rows0, row, meta, costs0, costs1, left2, util23, *refs):
    pieces, scores, local = refs[:n_pieces], refs[n_pieces], refs[n_pieces + 1]
    per_group, rows1 = scores.shape[:2]
    length = util23.shape[1]
    depth = util23.shape[2]
    which = [meta[PLACE + meta[0] * per_group + slot] for slot in range(per_group)]
    first = (meta[2] * 2 + meta[3]) * rows0 + row
    start1 = meta[1] * rows1
    for second in range(0, rows1, 2):
        for slot in range(per_group):
            cols = [
                jnp.concatenate([piece[slot, second + extra] for piece in pieces], axis=0)
                for extra in range(2)
            ]
            g_hi, g_lo = halves(jnp.concatenate(cols, axis=1))
            both = jnp.dot(
                left2[slot], jnp.concatenate([g_hi, g_lo], axis=0), preferred_element_type=F32
            )
            expected = both[:length] + both[length:]
            for extra in range(2):
                flat = costs0[which[slot], first] + costs1[which[slot], start1 + second + extra]
                scores[slot, second + extra] = (util23[slot] + flat) + DISCOUNT * expected[
                    :, extra * depth : (extra + 1) * depth
                ]
        for extra in range(2):
            found = [scores[slot, second + extra] for slot in range(per_group)]
            top = functools.reduce(jnp.maximum, found)
            total = functools.reduce(jnp.add, [jnp.exp(one - top) for one in found])
            local[second + extra] = top + jnp.log(total)


def choice_kernel(scores, mine, other, *refs):
    new_value, choice_prob = refs[-2:]
    a, b = mine[...], other[...]
    top, low = jnp.maximum(a, b), jnp.minimum(a, b)
    total = top + jnp.log(1.0 + jnp.exp(low - top))
    new_value[0] = total
    for slot in range(scores.shape[0]):
        choice_prob[slot, 0] = jnp.exp(scores[slot] - total).astype(choice_prob.dtype)


def after(value, *done):
    return lax.optimization_barrier((value, *done))[0] if done else value


def whole_block():
    return pl.BlockSpec(memory_space=pltpu.VMEM)


def params(mebibytes):
    return pltpu.CompilerParams(vmem_limit_bytes=mebibytes * MIB)


def gather_body(
    value_now,
    cost_first,
    cost_second,
    cost_third,
    cost_fourth,
    trans_weights,
    trans_offsets,
    action_order,
):
    n_act, n_narrow, n_wide = (lax.axis_size(name) for name in ("act", "narrow", "wide"))
    n_outer = n_wide // 2
    act, narrow, wide = (lax.axis_index(name) for name in ("act", "narrow", "wide"))
    outer, core = wide // 2, wide % 2
    actions, _, taps = trans_weights.shape
    per_group = actions // n_act
    rows0, rows1, len2, len3 = value_now.shape
    len0, len1 = rows0 * n_wide, rows1 * n_narrow
    lengths = (len0, len1, len2, len3)
    chunk = CHUNK_ROWS
    share = (len2 - n_narrow * chunk) // n_act
    n_chunks = share // chunk
    core_flip = [(i, i ^ 1) for i in range(n_wide)]
    act_flip = [(i, (i + 1) % n_act) for i in range(n_act)]
    narrow_flip = [(i, (i + 1) % n_narrow) for i in range(n_narrow)]

    def across(bit):
        return [(i, i ^ (2 * bit)) for i in range(n_wide)]

    def part(begin, size):
        return lax.dynamic_slice_in_dim(value_now, begin, size, 2)

    near = [(0, other, ahead) for ahead in range(n_narrow) for other in range(2)]
    arrivals = near + [
        (far, other, ahead)
        for ahead in range(n_narrow)
        for other in range(2)
        for far in range(1, n_outer)
    ]

    half_band = (taps - 1) // 2
    width = -(-(max(lengths) + 4 * half_band) // LANES) * LANES
    weights = jnp.pad(trans_weights, ((0, 0), (0, 0), (0, width - taps)))
    place = jnp.stack([act, narrow, outer, core]).astype(jnp.int32)
    meta = jnp.concatenate([place, action_order, trans_offsets.T.reshape(-1)])
    smem = pl.BlockSpec(memory_space=pltpu.SMEM)
    q_rows = actions * rows0 * rows1
    kron_hi, kron_lo, side_hi, side_lo, right3 = pl.pallas_call(
        functools.partial(
            prepare_kernel, lengths, taps, (n_act, n_narrow, n_outer), rows0, rows1, arrivals
        ),
        out_shape=(
            jax.ShapeDtypeStruct((q_rows, len0 * len1), BF16),
            jax.ShapeDtypeStruct((q_rows, len0 * len1), BF16),
            jax.ShapeDtypeStruct((q_rows * n_narrow // n_act, len0 * len1), BF16),
            jax.ShapeDtypeStruct((q_rows * n_narrow // n_act, len0 * len1), BF16),
            jax.ShapeDtypeStruct((actions, 2 * len3, 2 * len3), BF16),
        ),
        in_specs=[smem, whole_block()],
        out_specs=(whole_block(),) * 5,
        scratch_shapes=[pltpu.VMEM((len0, len0 * len1), F32), pltpu.VMEM((len1, len0 * len1), F32)],
        compiler_params=params(16),
        cost_estimate=pl.CostEstimate(flops=10**9, bytes_accessed=4 * 10**6, transcendentals=0),
        name="prepare",
    )(meta, weights)
    segments = [(0, share, 0, ahead, n_act) for ahead in range(n_act)]
    segments += [(n_act * share, chunk, 1, ahead, n_narrow) for ahead in range(n_narrow)]
    left2, util23 = pl.pallas_call(
        functools.partial(prepare_third_kernel, taps, segments),
        out_shape=(
            jax.ShapeDtypeStruct((per_group, 2 * len2, 2 * len2), BF16),
            jax.ShapeDtypeStruct((per_group, len2, len3), F32),
        ),
        in_specs=[smem] + [whole_block()] * 3,
        out_specs=(whole_block(),) * 2,
        compiler_params=params(12),
        cost_estimate=pl.CostEstimate(flops=10**9, bytes_accessed=4 * 10**6, transcendentals=0),
        name="prepare_third",
    )(meta, weights, cost_third, cost_fourth)

    side_begin = n_act * share
    inner = (outer == 1) | (outer == 2)
    value_now, inner, place, act_begin, own_begin, other_begin = lax.optimization_barrier(
        (
            value_now,
            inner,
            place,
            act * share,
            side_begin + narrow * chunk,
            side_begin + (n_narrow - 1 - narrow) * chunk,
        )
    )
    chunks = [part(act_begin + index * chunk, chunk) for index in range(n_chunks)]
    to_narrow = jnp.concatenate([part(act_begin, share), part(other_begin, chunk)], axis=2)
    own_side = part(own_begin, chunk)
    mine = jnp.concatenate([part(act_begin, share), own_side], axis=2)
    direct = [lax.ppermute(chunks[0], "wide", across(far)) for far in range(1, n_outer)]
    around = lax.ppermute(to_narrow, "narrow", narrow_flip)
    soon = lax.ppermute(part(act_begin + chunk, share - chunk), "wide", across(1))
    direct, *_ = lax.optimization_barrier((direct, kron_hi, right3))
    side = jnp.concatenate([own_side, around[:, :, share:]], axis=0)

    bits = [1 << bit for bit in range(1, n_outer.bit_length() - 1)]

    def doubled(own, twin, *done):
        size = own.shape[0]
        blocks = [own, twin]
        for bit in bits:
            grown = after(jnp.concatenate(blocks, axis=0), *done)
            more = lax.ppermute(grown, "wide", across(bit))
            blocks += [more[i : i + size] for i in range(0, more.shape[0], size)]
        return blocks[1:]

    inner_swap = [(2 * a + c, 2 * b + c) for a, b in ((1, 2), (2, 1)) for c in range(2)]
    outward = [(2 * a + c, 2 * b + c) for a, b in ((1, 0), (2, 3)) for c in range(2)]

    def by_line(own, twin, *done):
        size = own.shape[0]
        grown = after(jnp.concatenate([own, twin], axis=0), *done)
        came = lax.ppermute(grown, "wide", inner_swap)
        passed = lax.ppermute(after(came, moved[-1]), "wide", outward)
        return [
            twin,
            jnp.where(inner, came[size:], passed[:size]),
            jnp.where(inner, came[:size], passed[size:]),
        ]

    far0 = jnp.concatenate(direct, axis=0)
    crossed = [lax.ppermute(far0, "wide", core_flip)]
    moved = [lax.ppermute(far0, "narrow", narrow_flip)]
    late = lax.ppermute(after(side, far0), "wide", across(1))
    owns = chunks + [side]
    twins = [None] + [soon[:, :, i : i + chunk] for i in range(0, share - chunk, chunk)] + [late]
    nears = [mine, lax.ppermute(after(mine, crossed[0]), "wide", core_flip)]
    nears += [around, lax.ppermute(after(around, crossed[0]), "wide", core_flip)]
    nears = [one.reshape(rows0 * rows1, share + chunk, len3) for one in nears]

    def contract(kron, views, routes, out_rows, inputs):
        return pl.pallas_call(
            functools.partial(short_dims_kernel, views, routes),
            out_shape=tuple(
                jax.ShapeDtypeStruct((per_group, rows, chunk, len3), F32) for rows in out_rows
            ),
            in_specs=[whole_block()] * (3 + len(inputs)),
            out_specs=(whole_block(),) * len(out_rows),
            compiler_params=params(12),
            cost_estimate=pl.CostEstimate(flops=10**6, bytes_accessed=10**4, transcendentals=0),
            name="short_dims",
        )(*kron, right3, *inputs)

    block_rows = rows0 * rows1
    far_rows = (n_outer - 1) * block_rows
    def halved(one):
        return [one[i : i + rows0] for i in range(0, n_narrow * rows0, rows0)]

    side_early = [lax.ppermute(half, "wide", core_flip) for half in halved(late)]
    fars = [far0]
    kept, sent = [], []
    for index in range(n_chunks):
        far = fars[index]
        if index:
            if index == 1:
                far = after(far, late)
            crossed.append(lax.ppermute(far, "wide", core_flip))
            moved.append(lax.ppermute(after(far, moved[-1]), "narrow", narrow_flip))
        spread = by_line if index + 1 == n_chunks and n_outer == 4 else doubled
        done = [fars[index]] + ([], moved[:1], kept[:1] + moved[1:2])[min(index, 2)]
        blocks = spread(owns[index + 1], twins[index + 1], *done)
        fars.append(jnp.concatenate(blocks, axis=0))
        ready = ([left2, util23], side_early, ())[min(index, 2)]
        handed = lax.ppermute(after(moved[index], *ready), "wide", core_flip)
        pieces = [far, crossed[index], moved[index], handed]
        inputs = nears + [one.reshape(far_rows, chunk, len3) for one in pieces]
        views = [(i, 0, block_rows, index * chunk) for i in range(len(nears))]
        views += [(len(nears) + i, 0, far_rows, 0) for i in range(len(pieces))]
        cuts = rows0 if index == n_chunks - 1 else 1
        routes = [[(0, slot)] for slot in range(per_group)]
        routes += [[(1 + cut, slot) for cut in range(cuts)] for slot in range(per_group)]
        out_rows = [block_rows] + [block_rows // cuts] * cuts
        keep, *for_act = contract((kron_hi, kron_lo), views, routes, out_rows, inputs)
        kept.append(keep)
        sent.append([])
        for one in for_act:
            before = [one for ones in sent for one in ones][-1:]
            sent[-1].append(lax.ppermute(after(one, *before), "act", act_flip))

    turned = side_early + [
        lax.ppermute(half, "wide", core_flip) for one in blocks[1:] for half in halved(one)
    ]
    inputs = nears + [one.reshape(-1, chunk, len3) for one in blocks + turned]
    views = [(i, 0, block_rows, share) for i in range(len(nears))]
    for ahead in range(n_narrow):
        views += [(len(nears) + i, ahead * block_rows, block_rows, 0) for i in range(len(blocks))]
        first = len(nears) + len(blocks) + ahead
        views += [(first + n_narrow * i, 0, block_rows, 0) for i in range(len(blocks))]
    routes = [[(0, slot), (1, slot)] for slot in range(per_group)]
    count = side_hi.shape[0] // rows0
    ready = sent[-1][:1]
    side_keep, side_got = [], []
    for row in range(rows0):
        kron = [one[row * count : (row + 1) * count] for one in (side_hi, side_lo)]
        kron[0] = after(kron[0], *ready)
        keep, give = contract(kron, views, routes, [rows1, rows1], inputs)
        side_keep.append(keep)
        side_got.append(lax.ppermute(after(give, *side_got[-1:]), "narrow", narrow_flip))
        ready = [give]

    parts = [(keep, None) for keep in kept] + [(ones[0], None) for ones in sent[:-1]]
    parts += [(sent[-1][0], sent[-1]), (side_keep[0], side_keep), (side_got[0], side_got)]
    by_row = []
    for row in range(rows0):
        arrays = [cut[row] if cut else one for one, cut in parts]
        specs = [
            pl.BlockSpec(
                (per_group, rows1) + one.shape[2:],
                lambda i, block=0 if cut else row: (0, block, 0, 0),
            )
            for one, (_, cut) in zip(arrays, parts)
        ]
        scores, local = pl.pallas_call(
            functools.partial(third_dim_kernel, len(parts), rows0, row),
            grid=(1,),
            out_shape=(
                jax.ShapeDtypeStruct((per_group, rows1, len2, len3), F32),
                jax.ShapeDtypeStruct((rows1, len2, len3), F32),
            ),
            in_specs=[smem] * 3 + [whole_block()] * 2 + specs,
            out_specs=(whole_block(),) * 2,
            compiler_params=params(20),
            cost_estimate=pl.CostEstimate(
                flops=10**9, bytes_accessed=5 * 10**6, transcendentals=10**6
            ),
            name="third_dim",
        )(meta, cost_first, cost_second, left2, util23, *arrays)
        by_row.append((scores, local, lax.ppermute(local, "act", act_flip)))

    results = ()
    for row, operands in enumerate(by_row):
        results = pl.pallas_call(
            choice_kernel,
            grid=(1,),
            out_shape=(
                jax.ShapeDtypeStruct(value_now.shape, F32),
                jax.ShapeDtypeStruct((per_group,) + value_now.shape, BF16),
            ),
            in_specs=[whole_block()] * 3 + [pl.BlockSpec(memory_space=pl.ANY)] * len(results),
            out_specs=(
                pl.BlockSpec((1, rows1, len2, len3), lambda i, row=row: (row, 0, 0, 0)),
                pl.BlockSpec(
                    (per_group, 1, rows1, len2, len3), lambda i, row=row: (0, row, 0, 0, 0)
                ),
            ),
            input_output_aliases={3: 0, 4: 1} if results else {},
            compiler_params=params(16),
            cost_estimate=pl.CostEstimate(
                flops=10**7, bytes_accessed=5 * 10**6, transcendentals=10**6
            ),
            name="choice",
        )(*operands, *results)
    return tuple(results)


def gather_fits(mesh, value_shape, actions, offset_reach):
    n_wide, n_narrow, n_act = (mesh.shape[name] for name in ("wide", "narrow", "act"))
    len0, len1, len2, len3 = value_shape
    if n_act != 2 or n_wide < 4 or n_wide & (n_wide - 1) or actions % n_act:
        return False
    if n_narrow != 2 or len2 % (n_act * CHUNK_ROWS) or len2 < 4 * n_act * CHUNK_ROWS:
        return False
    if len2 != LANES or len3 != LANES:
        return False
    if (len1 // n_narrow) % SUBLANES or len0 * len1 // (n_wide * n_narrow) % 16 or len0 % n_wide:
        return False
    if max(len0, len1) > LANES or len1 % n_narrow:
        return False
    raw = len0 * len1 * len2 * len3 // (2 * n_act)
    exchanged = 2 * (actions // n_act) * len0 * len1 * len2 * len3 // (n_wide * n_narrow)
    return raw <= exchanged


def solution(mesh):
    def run(value_now, *rest):
        actions = rest[-1].shape[0]
        small = gather_fits(mesh, value_now.shape, actions, rest[4].shape[-1])
        return jax.shard_map(
            gather_body if small else exchange_body,
            mesh=mesh,
            in_specs=(P("wide", "narrow", None, None), P(), P(), P(), P(), P(), P(), P()),
            out_specs=(P("wide", "narrow", None, None), P("act", "wide", "narrow", None, None)),
            check_vma=False,
        )(value_now, *rest)

    return run
```

```python
import functools

import jax
import jax.numpy as jnp
from jax import lax
from jax.experimental import pallas as pl
from jax.experimental.pallas import tpu as pltpu
from jax.sharding import PartitionSpec as P

DISCOUNT = 0.95
HIGHEST = lax.Precision.HIGHEST
F32 = jnp.float32
BF16 = jnp.bfloat16
LANES = 128
SUBLANES = 8
PLACE = 4
CHUNK_ROWS = 16
MIB = 1024 * 1024


def merged(value, axis, join):
    pieces = lax.all_gather(value, axis)
    head = pieces[0]
    tail = pieces[1:]
    subtotal, _ = lax.scan(lambda subtotal, slab: (join(subtotal, slab), None), head, tail)
    return subtotal


def transition(weights, offset, length):
    band_len = weights.shape[0]
    half_band = (band_len - 1) // 2
    normed = weights / jnp.sum(weights)
    row_ids = jnp.arange(length, dtype=jnp.int32)
    tap_ids = jnp.arange(band_len, dtype=jnp.int32)
    target = jnp.clip(row_ids[:, None] + offset + tap_ids[None, :] - half_band, 0, length - 1)
    matched = (target[:, :, None] == row_ids[None, None, :]).astype(normed.dtype)
    return jnp.einsum("ijk,j->ik", matched, normed, precision=HIGHEST)


def exchange_body(
    value_now,
    cost_first,
    cost_second,
    cost_third,
    cost_fourth,
    trans_weights,
    trans_offsets,
    action_order,
):
    size_act = lax.axis_size("act")
    per_group = action_order.shape[0] // size_act
    group_id = lax.axis_index("act")
    my_actions = lax.dynamic_slice_in_dim(action_order, group_id * per_group, per_group)
    rows_first, rows_second, len_third, len_fourth = value_now.shape
    len_first = rows_first * lax.axis_size("wide")
    len_second = rows_second * lax.axis_size("narrow")
    my_weights = jnp.take(trans_weights, my_actions, axis=0)
    my_offsets = jnp.take(trans_offsets, my_actions, axis=0)

    def build(axis_id, length):
        return jax.vmap(lambda weight_row, offset_one: transition(weight_row, offset_one, length))(
            my_weights[:, axis_id], my_offsets[:, axis_id]
        )

    mat_first = build(0, len_first)
    mat_second = build(1, len_second)
    mat_third = build(2, len_third)
    mat_fourth = build(3, len_fourth)
    spread = lax.all_to_all(value_now, "narrow", split_axis=2, concat_axis=1, tiled=True)
    field = jnp.einsum("gij,ajcd->gaicd", mat_second, spread, precision=HIGHEST)
    field = jnp.einsum("gij,gabcj->gabci", mat_fourth, field, precision=HIGHEST)
    field = lax.all_to_all(field, "narrow", split_axis=2, concat_axis=3, tiled=True)
    field = lax.all_to_all(field, "wide", split_axis=3, concat_axis=1, tiled=True)
    field = jnp.einsum("gij,gjbcd->gibcd", mat_first, field, precision=HIGHEST)
    field = lax.all_to_all(field, "wide", split_axis=1, concat_axis=3, tiled=True)
    expected = jnp.einsum("gij,gabjd->gabid", mat_third, field, precision=HIGHEST)
    start_first = lax.axis_index("wide") * rows_first
    start_second = lax.axis_index("narrow") * rows_second
    util_first = lax.dynamic_slice_in_dim(
        jnp.take(cost_first, my_actions, axis=0), start_first, rows_first, 1
    )
    util_second = lax.dynamic_slice_in_dim(
        jnp.take(cost_second, my_actions, axis=0), start_second, rows_second, 1
    )
    util_third = jnp.take(cost_third, my_actions, axis=0)
    util_fourth = jnp.take(cost_fourth, my_actions, axis=0)
    utility = (
        util_first[:, :, None, None, None]
        + util_second[:, None, :, None, None]
        + util_third[:, None, None, :, None]
        + util_fourth[:, None, None, None, :]
    )
    scores = utility + DISCOUNT * expected
    local_max = jnp.max(scores, axis=0)
    local_sum = jnp.sum(jnp.exp(scores - local_max), axis=0)
    log_total = merged(local_max + jnp.log(local_sum), "act", jnp.logaddexp)
    choice_prob = jnp.exp(scores - log_total).astype(jnp.bfloat16)
    return (log_total, choice_prob)


def halves(x):
    high = x.astype(BF16)
    return high, (x - high.astype(F32)).astype(BF16)


def dot32(a, b):
    return jnp.dot(a, b, preferred_element_type=F32, precision=HIGHEST)


def banded(weights, offset, length, taps):
    half_band = (taps - 1) // 2
    width = weights.shape[1]
    normed = weights / jnp.sum(weights, axis=1, keepdims=True)
    tile = jnp.broadcast_to(normed, (SUBLANES, width))
    tile = pltpu.roll(tile, lax.rem(offset + (width - half_band), width), 1)
    rows = jnp.concatenate([tile] * (length // SUBLANES), axis=0)
    rows = pltpu.roll(rows, 0, 1, stride=1, stride_axis=0)
    lane = lax.broadcasted_iota(jnp.int32, (length, width), 1)
    under = lane >= width - 2 * half_band
    over = (lane >= length) & (lane < length + 2 * half_band)
    under_sum = jnp.sum(jnp.where(under, rows, 0.0), axis=1, keepdims=True)
    over_sum = jnp.sum(jnp.where(over, rows, 0.0), axis=1, keepdims=True)
    span = -(-length // LANES) * LANES
    kept = lane[:, :span]
    body = jnp.where(kept < length, rows[:, :span], 0.0)
    body = body + jnp.where(kept == 0, under_sum, 0.0)
    return body + jnp.where(kept == length - 1, over_sum, 0.0)


def prepare_kernel(
    lengths, taps, sizes, rows0, rows1, arrivals, meta, weights,
    kron_hi, kron_lo, side_hi, side_lo, right3, wide0, wide1,
):
    n_act, n_narrow, n_outer = sizes
    len0, len1, len2, len3 = lengths
    act, narrow, outer, core = (meta[i] for i in range(PLACE))
    actions = weights.shape[0]
    per_group = actions // n_act
    columns = len0 * len1

    def wrapped(index, size):
        return lax.rem(index + size, size)

    lane = lax.broadcasted_iota(jnp.int32, (1, columns), 1)
    ids0 = jnp.zeros((1, columns), jnp.int32)
    ids1 = jnp.zeros((1, columns), jnp.int32)
    for block, (far, part, ahead) in enumerate(arrivals):
        from_outer, from_core = outer ^ far, wrapped(core + part, 2)
        for row in range(rows0):
            start = (block * rows0 + row) * rows1
            inside = (lane >= start) & (lane < start + rows1)
            first = (from_outer * 2 + from_core) * rows0 + row
            second = wrapped(narrow - ahead, n_narrow) * rows1 - start
            ids0 = jnp.where(inside, first, ids0)
            ids1 = jnp.where(inside, second + lane, ids1)
    spread0 = (lax.broadcasted_iota(jnp.int32, (LANES, columns), 0) == ids0).astype(F32)
    spread1 = (lax.broadcasted_iota(jnp.int32, (LANES, columns), 0) == ids1).astype(F32)

    for action in range(actions):
        group, slot = divmod(action, per_group)
        which = meta[PLACE + wrapped(act + group, n_act) * per_group + slot]
        rows = weights[which]
        mats = [
            banded(
                rows[axis : axis + 1, :],
                meta[PLACE + (1 + axis) * actions + which],
                lengths[axis],
                taps,
            )
            for axis in (0, 1, 3)
        ]
        wide0[...] = dot32(mats[0], spread0)
        wide1[...] = dot32(mats[1], spread1)
        base = (outer * 2 + core) * rows0
        products = []
        for ahead in range(n_narrow if group == 0 else 1):
            begin = wrapped(narrow + ahead, n_narrow) * rows1
            second = wide1[pl.ds(pl.multiple_of(begin, SUBLANES), rows1), :]
            blocks = [wide0[pl.ds(base + row, 1), :] * second for row in range(rows0)]
            high, low = halves(jnp.concatenate(blocks, axis=0))
            if ahead == 0:
                start = action * rows0 * rows1
                kron_hi[start : start + rows0 * rows1, :] = high
                kron_lo[start : start + rows0 * rows1, :] = low
            products.append(blocks)
        for row in range(rows0 if group == 0 else 0):
            high, low = halves(jnp.concatenate([blocks[row] for blocks in products], axis=0))
            start = (row * per_group + slot) * n_narrow * rows1
            side_hi[start : start + n_narrow * rows1, :] = high
            side_lo[start : start + n_narrow * rows1, :] = low
        high, low = halves(mats[2].T)
        row_pair = jnp.concatenate([high, low], axis=1)
        right3[action] = jnp.concatenate([row_pair, row_pair], axis=0)


def prepare_third_kernel(taps, segments, meta, weights, third, fourth, left2, util23):
    act, actions, per_group = meta[0], weights.shape[0], left2.shape[0]
    len2, len3 = util23.shape[1:]
    lane2 = lax.broadcasted_iota(jnp.int32, (1, len2), 1)
    ids2 = jnp.zeros((1, len2), jnp.int32)
    filled = 0
    for begin, size, axis, ahead, count in segments:
        source = begin + lax.rem(meta[axis] + ahead, count) * size
        inside = (lane2 >= filled) & (lane2 < filled + size)
        ids2 = jnp.where(inside, source - filled + lane2, ids2)
        filled += size
    order2 = (lax.broadcasted_iota(jnp.int32, (len2, len2), 0) == ids2).astype(F32)

    for slot in range(per_group):
        which = meta[PLACE + act * per_group + slot]
        offset = meta[PLACE + 3 * actions + which]
        matrix = banded(weights[which][2:3, :], offset, len2, taps)
        high, low = halves(dot32(matrix, order2))
        left2[slot] = jnp.concatenate(
            [jnp.concatenate([high, high], axis=1), jnp.concatenate([low, low], axis=1)], axis=0
        )
        column = jnp.broadcast_to(third[pl.ds(which, 1), :], (len3, len2)).T
        util23[slot] = column + fourth[pl.ds(which, 1), :]


def short_dims_kernel(views, routes, kron_hi, kron_lo, right3, *refs):
    n_inputs = 1 + max(view[0] for view in views)
    inputs, outs = refs[:n_inputs], refs[n_inputs:]
    rows, depth = outs[0].shape[2:]
    per_action = kron_hi.shape[0] // len(routes)
    q_hi, q_lo = kron_hi[...], kron_lo[...]
    mixed = []
    for row in range(0, rows, 2):
        cols = [
            jnp.concatenate(
                [
                    inputs[which][lead : lead + count, start + row + extra, :]
                    for which, lead, count, start in views
                ],
                axis=0,
            )
            for extra in range(2)
        ]
        x_hi, x_lo = halves(jnp.concatenate(cols, axis=1))
        out = (
            jnp.dot(q_hi, x_hi, preferred_element_type=F32)
            + jnp.dot(q_hi, x_lo, preferred_element_type=F32)
            + jnp.dot(q_lo, x_hi, preferred_element_type=F32)
        )
        mixed += [out[:, :depth], out[:, depth:]]
    for action, route in enumerate(routes):
        start = action * per_action
        block = jnp.concatenate([one[start : start + per_action] for one in mixed], axis=0)
        t_hi, t_lo = halves(block)
        both = jnp.dot(
            jnp.concatenate([t_hi, t_lo], axis=1), right3[action], preferred_element_type=F32
        )
        done = both[:, :depth] + both[:, depth:]
        for row in range(rows):
            first = row * per_action
            for which, slot in route:
                count = outs[which].shape[1]
                outs[which][slot, :, row, :] = done[first : first + count]
                first += count


def third_dim_kernel(n_pieces, rows0, row, pieces1, piece1, meta, costs0, costs1, left2, util23, *refs):
    pieces, scores, local = refs[:n_pieces], refs[n_pieces], refs[n_pieces + 1]
    per_group, rows1 = scores.shape[:2]
    length = util23.shape[1]
    depth = util23.shape[2]
    which = [meta[PLACE + meta[0] * per_group + slot] for slot in range(per_group)]
    first = (meta[2] * 2 + meta[3]) * rows0 + row
    start1 = (meta[1] * pieces1 + piece1) * rows1
    for second in range(0, rows1, 2):
        for slot in range(per_group):
            cols = [
                jnp.concatenate([piece[slot, second + extra] for piece in pieces], axis=0)
                for extra in range(2)
            ]
            g_hi, g_lo = halves(jnp.concatenate(cols, axis=1))
            both = jnp.dot(
                left2[slot], jnp.concatenate([g_hi, g_lo], axis=0), preferred_element_type=F32
            )
            expected = both[:length] + both[length:]
            for extra in range(2):
                flat = costs0[which[slot], first] + costs1[which[slot], start1 + second + extra]
                scores[slot, second + extra] = (util23[slot] + flat) + DISCOUNT * expected[
                    :, extra * depth : (extra + 1) * depth
                ]
        for extra in range(2):
            found = [scores[slot, second + extra] for slot in range(per_group)]
            top = functools.reduce(jnp.maximum, found)
            total = functools.reduce(jnp.add, [jnp.exp(one - top) for one in found])
            local[second + extra] = top + jnp.log(total)


def choice_kernel(scores, mine, other, *refs):
    new_value, choice_prob = refs[-2:]
    a, b = mine[...], other[...]
    top, low = jnp.maximum(a, b), jnp.minimum(a, b)
    total = top + jnp.log(1.0 + jnp.exp(low - top))
    new_value[0] = total
    for slot in range(scores.shape[0]):
        choice_prob[slot, 0] = jnp.exp(scores[slot] - total).astype(choice_prob.dtype)


def after(value, *done):
    return lax.optimization_barrier((value, *done))[0] if done else value


def whole_block():
    return pl.BlockSpec(memory_space=pltpu.VMEM)


def params(mebibytes):
    return pltpu.CompilerParams(vmem_limit_bytes=mebibytes * MIB)


def gather_body(
    value_now,
    cost_first,
    cost_second,
    cost_third,
    cost_fourth,
    trans_weights,
    trans_offsets,
    action_order,
):
    n_act, n_narrow, n_wide = (lax.axis_size(name) for name in ("act", "narrow", "wide"))
    n_outer = n_wide // 2
    act, narrow, wide = (lax.axis_index(name) for name in ("act", "narrow", "wide"))
    outer, core = wide // 2, wide % 2
    actions, _, taps = trans_weights.shape
    per_group = actions // n_act
    rows0, rows1, len2, len3 = value_now.shape
    len0, len1 = rows0 * n_wide, rows1 * n_narrow
    lengths = (len0, len1, len2, len3)
    chunk = CHUNK_ROWS
    share = (len2 - n_narrow * chunk) // n_act
    n_chunks = share // chunk
    core_flip = [(i, i ^ 1) for i in range(n_wide)]
    act_flip = [(i, (i + 1) % n_act) for i in range(n_act)]
    narrow_flip = [(i, (i + 1) % n_narrow) for i in range(n_narrow)]

    def across(bit):
        return [(i, i ^ (2 * bit)) for i in range(n_wide)]

    def part(begin, size):
        return lax.dynamic_slice_in_dim(value_now, begin, size, 2)

    near = [(0, other, ahead) for ahead in range(n_narrow) for other in range(2)]
    arrivals = near + [
        (far, other, ahead)
        for ahead in range(n_narrow)
        for other in range(2)
        for far in range(1, n_outer)
    ]

    half_band = (taps - 1) // 2
    width = -(-(max(lengths) + 4 * half_band) // LANES) * LANES
    weights = jnp.pad(trans_weights, ((0, 0), (0, 0), (0, width - taps)))
    place = jnp.stack([act, narrow, outer, core]).astype(jnp.int32)
    meta = jnp.concatenate([place, action_order, trans_offsets.T.reshape(-1)])
    smem = pl.BlockSpec(memory_space=pltpu.SMEM)
    q_rows = actions * rows0 * rows1
    kron_hi, kron_lo, side_hi, side_lo, right3 = pl.pallas_call(
        functools.partial(
            prepare_kernel, lengths, taps, (n_act, n_narrow, n_outer), rows0, rows1, arrivals
        ),
        out_shape=(
            jax.ShapeDtypeStruct((q_rows, len0 * len1), BF16),
            jax.ShapeDtypeStruct((q_rows, len0 * len1), BF16),
            jax.ShapeDtypeStruct((q_rows * n_narrow // n_act, len0 * len1), BF16),
            jax.ShapeDtypeStruct((q_rows * n_narrow // n_act, len0 * len1), BF16),
            jax.ShapeDtypeStruct((actions, 2 * len3, 2 * len3), BF16),
        ),
        in_specs=[smem, whole_block()],
        out_specs=(whole_block(),) * 5,
        scratch_shapes=[pltpu.VMEM((len0, len0 * len1), F32), pltpu.VMEM((len1, len0 * len1), F32)],
        compiler_params=params(16),
        cost_estimate=pl.CostEstimate(flops=10**9, bytes_accessed=4 * 10**6, transcendentals=0),
        name="prepare",
    )(meta, weights)
    segments = [(0, share, 0, ahead, n_act) for ahead in range(n_act)]
    segments += [(n_act * share, chunk, 1, ahead, n_narrow) for ahead in range(n_narrow)]
    left2, util23 = pl.pallas_call(
        functools.partial(prepare_third_kernel, taps, segments),
        out_shape=(
            jax.ShapeDtypeStruct((per_group, 2 * len2, 2 * len2), BF16),
            jax.ShapeDtypeStruct((per_group, len2, len3), F32),
        ),
        in_specs=[smem] + [whole_block()] * 3,
        out_specs=(whole_block(),) * 2,
        compiler_params=params(12),
        cost_estimate=pl.CostEstimate(flops=10**9, bytes_accessed=4 * 10**6, transcendentals=0),
        name="prepare_third",
    )(meta, weights, cost_third, cost_fourth)

    side_begin = n_act * share
    inner = (outer == 1) | (outer == 2)
    value_now, inner, place, act_begin, own_begin, other_begin = lax.optimization_barrier(
        (
            value_now,
            inner,
            place,
            act * share,
            side_begin + narrow * chunk,
            side_begin + (n_narrow - 1 - narrow) * chunk,
        )
    )
    chunks = [part(act_begin + index * chunk, chunk) for index in range(n_chunks)]
    to_narrow = jnp.concatenate([part(act_begin, share), part(other_begin, chunk)], axis=2)
    own_side = part(own_begin, chunk)
    mine = jnp.concatenate([part(act_begin, share), own_side], axis=2)
    direct = [lax.ppermute(chunks[0], "wide", across(far)) for far in range(1, n_outer)]
    around = lax.ppermute(to_narrow, "narrow", narrow_flip)
    soon = lax.ppermute(part(act_begin + chunk, share - chunk), "wide", across(1))
    direct, *_ = lax.optimization_barrier((direct, kron_hi, right3))
    side = jnp.concatenate([own_side, around[:, :, share:]], axis=0)

    bits = [1 << bit for bit in range(1, n_outer.bit_length() - 1)]

    def doubled(own, twin, *done):
        size = own.shape[0]
        blocks = [own, twin]
        for bit in bits:
            grown = after(jnp.concatenate(blocks, axis=0), *done)
            more = lax.ppermute(grown, "wide", across(bit))
            blocks += [more[i : i + size] for i in range(0, more.shape[0], size)]
        return blocks[1:]

    inner_swap = [(2 * a + c, 2 * b + c) for a, b in ((1, 2), (2, 1)) for c in range(2)]
    outward = [(2 * a + c, 2 * b + c) for a, b in ((1, 0), (2, 3)) for c in range(2)]

    def by_line(own, twin, *done):
        size = own.shape[0]
        grown = after(jnp.concatenate([own, twin], axis=0), *done)
        came = lax.ppermute(grown, "wide", inner_swap)
        passed = lax.ppermute(after(came, moved[-1]), "wide", outward)
        return [
            twin,
            jnp.where(inner, came[size:], passed[:size]),
            jnp.where(inner, came[:size], passed[size:]),
        ]

    far0 = jnp.concatenate(direct, axis=0)
    crossed = [lax.ppermute(far0, "wide", core_flip)]
    moved = [lax.ppermute(far0, "narrow", narrow_flip)]
    late = lax.ppermute(after(side, far0), "wide", across(1))
    owns = chunks + [side]
    twins = [None] + [soon[:, :, i : i + chunk] for i in range(0, share - chunk, chunk)] + [late]
    nears = [mine, lax.ppermute(after(mine, crossed[0]), "wide", core_flip)]
    nears += [around, lax.ppermute(after(around, crossed[0]), "wide", core_flip)]
    nears = [one.reshape(rows0 * rows1, share + chunk, len3) for one in nears]

    def contract(kron, views, routes, out_rows, inputs):
        return pl.pallas_call(
            functools.partial(short_dims_kernel, views, routes),
            out_shape=tuple(
                jax.ShapeDtypeStruct((per_group, rows, chunk, len3), F32) for rows in out_rows
            ),
            in_specs=[whole_block()] * (3 + len(inputs)),
            out_specs=(whole_block(),) * len(out_rows),
            compiler_params=params(12),
            cost_estimate=pl.CostEstimate(flops=10**6, bytes_accessed=10**4, transcendentals=0),
            name="short_dims",
        )(*kron, right3, *inputs)

    block_rows = rows0 * rows1
    far_rows = (n_outer - 1) * block_rows
    def halved(one):
        return [one[i : i + rows0] for i in range(0, n_narrow * rows0, rows0)]

    side_early = [lax.ppermute(half, "wide", core_flip) for half in halved(late)]
    fars = [far0]
    kept, sent = [], []
    for index in range(n_chunks):
        far = fars[index]
        if index:
            if index == 1:
                far = after(far, late)
            crossed.append(lax.ppermute(far, "wide", core_flip))
            moved.append(lax.ppermute(after(far, moved[-1]), "narrow", narrow_flip))
        spread = by_line if index + 1 == n_chunks and n_outer == 4 else doubled
        done = [fars[index]] + ([], moved[:1], kept[:1] + moved[1:2])[min(index, 2)]
        blocks = spread(owns[index + 1], twins[index + 1], *done)
        fars.append(jnp.concatenate(blocks, axis=0))
        ready = ([left2, util23], side_early, ())[min(index, 2)]
        handed = lax.ppermute(after(moved[index], *ready), "wide", core_flip)
        pieces = [far, crossed[index], moved[index], handed]
        inputs = nears + [one.reshape(far_rows, chunk, len3) for one in pieces]
        views = [(i, 0, block_rows, index * chunk) for i in range(len(nears))]
        views += [(len(nears) + i, 0, far_rows, 0) for i in range(len(pieces))]
        cuts = rows0 if index == n_chunks - 1 else 1
        routes = [[(0, slot)] for slot in range(per_group)]
        routes += [[(1 + cut, slot) for cut in range(cuts)] for slot in range(per_group)]
        out_rows = [block_rows] + [block_rows // cuts] * cuts
        keep, *for_act = contract((kron_hi, kron_lo), views, routes, out_rows, inputs)
        kept.append(keep)
        sent.append([])
        for one in for_act:
            before = [one for ones in sent for one in ones][-1:]
            sent[-1].append(lax.ppermute(after(one, *before), "act", act_flip))

    turned = side_early + [
        lax.ppermute(half, "wide", core_flip) for one in blocks[1:] for half in halved(one)
    ]
    inputs = nears + [one.reshape(-1, chunk, len3) for one in blocks + turned]
    views = [(i, 0, block_rows, share) for i in range(len(nears))]
    for ahead in range(n_narrow):
        views += [(len(nears) + i, ahead * block_rows, block_rows, 0) for i in range(len(blocks))]
        first = len(nears) + len(blocks) + ahead
        views += [(first + n_narrow * i, 0, block_rows, 0) for i in range(len(blocks))]
    routes = [[(0, slot), (1, slot)] for slot in range(per_group)]
    count = side_hi.shape[0] // rows0
    ready = sent[-1][:1]
    side_keep, side_got = [], []
    for row in range(rows0):
        kron = [one[row * count : (row + 1) * count] for one in (side_hi, side_lo)]
        kron[0] = after(kron[0], *ready)
        keep, give = contract(kron, views, routes, [rows1, rows1], inputs)
        side_keep.append(keep)
        side_got.append(lax.ppermute(after(give, *side_got[-1:]), "narrow", narrow_flip))
        ready = [give]

    parts = [(keep, None) for keep in kept] + [(ones[0], None) for ones in sent[:-1]]
    parts += [(sent[-1][0], sent[-1]), (side_keep[0], side_keep), (side_got[0], side_got)]
    by_row = []
    units = [(row, piece) for row in range(rows0) for piece in range(2)]
    unit1 = rows1 // 2
    for row, piece in units:
        arrays = [cut[row] if cut else one for one, cut in parts]
        specs = [
            pl.BlockSpec(
                (per_group, unit1) + one.shape[2:],
                lambda i, block=piece if cut else 2 * row + piece: (0, block, 0, 0),
            )
            for one, (_, cut) in zip(arrays, parts)
        ]
        scores, local = pl.pallas_call(
            functools.partial(third_dim_kernel, len(parts), rows0, row, 2, piece),
            grid=(1,),
            out_shape=(
                jax.ShapeDtypeStruct((per_group, unit1, len2, len3), F32),
                jax.ShapeDtypeStruct((unit1, len2, len3), F32),
            ),
            in_specs=[smem] * 3 + [whole_block()] * 2 + specs,
            out_specs=(whole_block(),) * 2,
            compiler_params=params(20),
            cost_estimate=pl.CostEstimate(
                flops=10**9, bytes_accessed=5 * 10**6, transcendentals=10**6
            ),
            name="third_dim",
        )(meta, cost_first, cost_second, left2, util23, *arrays)
        by_row.append((scores, local, lax.ppermute(local, "act", act_flip)))

    results = ()
    for (row, piece), operands in zip(units, by_row):
        results = pl.pallas_call(
            choice_kernel,
            grid=(1,),
            out_shape=(
                jax.ShapeDtypeStruct(value_now.shape, F32),
                jax.ShapeDtypeStruct((per_group,) + value_now.shape, BF16),
            ),
            in_specs=[whole_block()] * 3 + [pl.BlockSpec(memory_space=pl.ANY)] * len(results),
            out_specs=(
                pl.BlockSpec((1, unit1, len2, len3), lambda i, at=(row, piece): at + (0, 0)),
                pl.BlockSpec(
                    (per_group, 1, unit1, len2, len3), lambda i, at=(row, piece): (0,) + at + (0, 0)
                ),
            ),
            input_output_aliases={3: 0, 4: 1} if results else {},
            compiler_params=params(16),
            cost_estimate=pl.CostEstimate(
                flops=10**7, bytes_accessed=5 * 10**6, transcendentals=10**6
            ),
            name="choice",
        )(*operands, *results)
    return tuple(results)


def gather_fits(mesh, value_shape, actions, offset_reach):
    n_wide, n_narrow, n_act = (mesh.shape[name] for name in ("wide", "narrow", "act"))
    len0, len1, len2, len3 = value_shape
    if n_act != 2 or n_wide < 4 or n_wide & (n_wide - 1) or actions % n_act:
        return False
    if n_narrow != 2 or len2 % (n_act * CHUNK_ROWS) or len2 < 4 * n_act * CHUNK_ROWS:
        return False
    if len2 != LANES or len3 != LANES:
        return False
    if (len1 // n_narrow) % SUBLANES or len0 * len1 // (n_wide * n_narrow) % 16 or len0 % n_wide:
        return False
    if max(len0, len1) > LANES or len1 % n_narrow:
        return False
    raw = len0 * len1 * len2 * len3 // (2 * n_act)
    exchanged = 2 * (actions // n_act) * len0 * len1 * len2 * len3 // (n_wide * n_narrow)
    return raw <= exchanged


def solution(mesh):
    def run(value_now, *rest):
        actions = rest[-1].shape[0]
        small = gather_fits(mesh, value_now.shape, actions, rest[4].shape[-1])
        return jax.shard_map(
            gather_body if small else exchange_body,
            mesh=mesh,
            in_specs=(P("wide", "narrow", None, None), P(), P(), P(), P(), P(), P(), P()),
            out_specs=(P("wide", "narrow", None, None), P("act", "wide", "narrow", None, None)),
            check_vma=False,
        )(value_now, *rest)

    return run
```

```python
import functools

import jax
import jax.numpy as jnp
from jax import lax
from jax.experimental import pallas as pl
from jax.experimental.pallas import tpu as pltpu
from jax.sharding import PartitionSpec as P

DISCOUNT = 0.95
HIGHEST = lax.Precision.HIGHEST
F32 = jnp.float32
BF16 = jnp.bfloat16
LANES = 128
SUBLANES = 8
PLACE = 4
CHUNK_ROWS = 16
MIB = 1024 * 1024


def merged(value, axis, join):
    pieces = lax.all_gather(value, axis)
    head = pieces[0]
    tail = pieces[1:]
    subtotal, _ = lax.scan(lambda subtotal, slab: (join(subtotal, slab), None), head, tail)
    return subtotal


def transition(weights, offset, length):
    band_len = weights.shape[0]
    half_band = (band_len - 1) // 2
    normed = weights / jnp.sum(weights)
    row_ids = jnp.arange(length, dtype=jnp.int32)
    tap_ids = jnp.arange(band_len, dtype=jnp.int32)
    target = jnp.clip(row_ids[:, None] + offset + tap_ids[None, :] - half_band, 0, length - 1)
    matched = (target[:, :, None] == row_ids[None, None, :]).astype(normed.dtype)
    return jnp.einsum("ijk,j->ik", matched, normed, precision=HIGHEST)


def exchange_body(
    value_now,
    cost_first,
    cost_second,
    cost_third,
    cost_fourth,
    trans_weights,
    trans_offsets,
    action_order,
):
    size_act = lax.axis_size("act")
    per_group = action_order.shape[0] // size_act
    group_id = lax.axis_index("act")
    my_actions = lax.dynamic_slice_in_dim(action_order, group_id * per_group, per_group)
    rows_first, rows_second, len_third, len_fourth = value_now.shape
    len_first = rows_first * lax.axis_size("wide")
    len_second = rows_second * lax.axis_size("narrow")
    my_weights = jnp.take(trans_weights, my_actions, axis=0)
    my_offsets = jnp.take(trans_offsets, my_actions, axis=0)

    def build(axis_id, length):
        return jax.vmap(lambda weight_row, offset_one: transition(weight_row, offset_one, length))(
            my_weights[:, axis_id], my_offsets[:, axis_id]
        )

    mat_first = build(0, len_first)
    mat_second = build(1, len_second)
    mat_third = build(2, len_third)
    mat_fourth = build(3, len_fourth)
    spread = lax.all_to_all(value_now, "narrow", split_axis=2, concat_axis=1, tiled=True)
    field = jnp.einsum("gij,ajcd->gaicd", mat_second, spread, precision=HIGHEST)
    field = jnp.einsum("gij,gabcj->gabci", mat_fourth, field, precision=HIGHEST)
    field = lax.all_to_all(field, "narrow", split_axis=2, concat_axis=3, tiled=True)
    field = lax.all_to_all(field, "wide", split_axis=3, concat_axis=1, tiled=True)
    field = jnp.einsum("gij,gjbcd->gibcd", mat_first, field, precision=HIGHEST)
    field = lax.all_to_all(field, "wide", split_axis=1, concat_axis=3, tiled=True)
    expected = jnp.einsum("gij,gabjd->gabid", mat_third, field, precision=HIGHEST)
    start_first = lax.axis_index("wide") * rows_first
    start_second = lax.axis_index("narrow") * rows_second
    util_first = lax.dynamic_slice_in_dim(
        jnp.take(cost_first, my_actions, axis=0), start_first, rows_first, 1
    )
    util_second = lax.dynamic_slice_in_dim(
        jnp.take(cost_second, my_actions, axis=0), start_second, rows_second, 1
    )
    util_third = jnp.take(cost_third, my_actions, axis=0)
    util_fourth = jnp.take(cost_fourth, my_actions, axis=0)
    utility = (
        util_first[:, :, None, None, None]
        + util_second[:, None, :, None, None]
        + util_third[:, None, None, :, None]
        + util_fourth[:, None, None, None, :]
    )
    scores = utility + DISCOUNT * expected
    local_max = jnp.max(scores, axis=0)
    local_sum = jnp.sum(jnp.exp(scores - local_max), axis=0)
    log_total = merged(local_max + jnp.log(local_sum), "act", jnp.logaddexp)
    choice_prob = jnp.exp(scores - log_total).astype(jnp.bfloat16)
    return (log_total, choice_prob)


def halves(x):
    high = x.astype(BF16)
    return high, (x - high.astype(F32)).astype(BF16)


def dot32(a, b):
    return jnp.dot(a, b, preferred_element_type=F32, precision=HIGHEST)


def banded(weights, offset, length, taps):
    half_band = (taps - 1) // 2
    width = weights.shape[1]
    normed = weights / jnp.sum(weights, axis=1, keepdims=True)
    tile = jnp.broadcast_to(normed, (SUBLANES, width))
    tile = pltpu.roll(tile, lax.rem(offset + (width - half_band), width), 1)
    rows = jnp.concatenate([tile] * (length // SUBLANES), axis=0)
    rows = pltpu.roll(rows, 0, 1, stride=1, stride_axis=0)
    lane = lax.broadcasted_iota(jnp.int32, (length, width), 1)
    under = lane >= width - 2 * half_band
    over = (lane >= length) & (lane < length + 2 * half_band)
    under_sum = jnp.sum(jnp.where(under, rows, 0.0), axis=1, keepdims=True)
    over_sum = jnp.sum(jnp.where(over, rows, 0.0), axis=1, keepdims=True)
    span = -(-length // LANES) * LANES
    kept = lane[:, :span]
    body = jnp.where(kept < length, rows[:, :span], 0.0)
    body = body + jnp.where(kept == 0, under_sum, 0.0)
    return body + jnp.where(kept == length - 1, over_sum, 0.0)


def prepare_kernel(
    lengths, taps, sizes, rows0, rows1, arrivals, meta, weights,
    kron_hi, kron_lo, side_hi, side_lo, right3, wide0, wide1,
):
    n_act, n_narrow, n_outer = sizes
    len0, len1, len2, len3 = lengths
    act, narrow, outer, core = (meta[i] for i in range(PLACE))
    actions = weights.shape[0]
    per_group = actions // n_act
    columns = len0 * len1

    def wrapped(index, size):
        return lax.rem(index + size, size)

    lane = lax.broadcasted_iota(jnp.int32, (1, columns), 1)
    ids0 = jnp.zeros((1, columns), jnp.int32)
    ids1 = jnp.zeros((1, columns), jnp.int32)
    for block, (far, part, ahead) in enumerate(arrivals):
        from_outer, from_core = outer ^ far, wrapped(core + part, 2)
        for row in range(rows0):
            start = (block * rows0 + row) * rows1
            inside = (lane >= start) & (lane < start + rows1)
            first = (from_outer * 2 + from_core) * rows0 + row
            second = wrapped(narrow - ahead, n_narrow) * rows1 - start
            ids0 = jnp.where(inside, first, ids0)
            ids1 = jnp.where(inside, second + lane, ids1)
    spread0 = (lax.broadcasted_iota(jnp.int32, (LANES, columns), 0) == ids0).astype(F32)
    spread1 = (lax.broadcasted_iota(jnp.int32, (LANES, columns), 0) == ids1).astype(F32)

    for action in range(actions):
        group, slot = divmod(action, per_group)
        which = meta[PLACE + wrapped(act + group, n_act) * per_group + slot]
        rows = weights[which]
        mats = [
            banded(
                rows[axis : axis + 1, :],
                meta[PLACE + (1 + axis) * actions + which],
                lengths[axis],
                taps,
            )
            for axis in (0, 1, 3)
        ]
        wide0[...] = dot32(mats[0], spread0)
        wide1[...] = dot32(mats[1], spread1)
        base = (outer * 2 + core) * rows0
        products = []
        for ahead in range(n_narrow if group == 0 else 1):
            begin = wrapped(narrow + ahead, n_narrow) * rows1
            second = wide1[pl.ds(pl.multiple_of(begin, SUBLANES), rows1), :]
            blocks = [wide0[pl.ds(base + row, 1), :] * second for row in range(rows0)]
            high, low = halves(jnp.concatenate(blocks, axis=0))
            if ahead == 0:
                start = action * rows0 * rows1
                kron_hi[start : start + rows0 * rows1, :] = high
                kron_lo[start : start + rows0 * rows1, :] = low
            products.append(blocks)
        for row in range(rows0 if group == 0 else 0):
            high, low = halves(jnp.concatenate([blocks[row] for blocks in products], axis=0))
            start = (row * per_group + slot) * n_narrow * rows1
            side_hi[start : start + n_narrow * rows1, :] = high
            side_lo[start : start + n_narrow * rows1, :] = low
        high, low = halves(mats[2].T)
        row_pair = jnp.concatenate([high, low], axis=1)
        right3[action] = jnp.concatenate([row_pair, row_pair], axis=0)


def prepare_third_kernel(taps, segments, meta, weights, third, fourth, left2, util23):
    act, actions, per_group = meta[0], weights.shape[0], left2.shape[0]
    len2, len3 = util23.shape[1:]
    lane2 = lax.broadcasted_iota(jnp.int32, (1, len2), 1)
    ids2 = jnp.zeros((1, len2), jnp.int32)
    filled = 0
    for begin, size, axis, ahead, count in segments:
        source = begin + lax.rem(meta[axis] + ahead, count) * size
        inside = (lane2 >= filled) & (lane2 < filled + size)
        ids2 = jnp.where(inside, source - filled + lane2, ids2)
        filled += size
    order2 = (lax.broadcasted_iota(jnp.int32, (len2, len2), 0) == ids2).astype(F32)

    for slot in range(per_group):
        which = meta[PLACE + act * per_group + slot]
        offset = meta[PLACE + 3 * actions + which]
        matrix = banded(weights[which][2:3, :], offset, len2, taps)
        high, low = halves(dot32(matrix, order2))
        left2[slot] = jnp.concatenate(
            [jnp.concatenate([high, high], axis=1), jnp.concatenate([low, low], axis=1)], axis=0
        )
        column = jnp.broadcast_to(third[pl.ds(which, 1), :], (len3, len2)).T
        util23[slot] = column + fourth[pl.ds(which, 1), :]


def short_dims_kernel(views, routes, kron_hi, kron_lo, right3, *refs):
    n_inputs = 1 + max(view[0] for view in views)
    inputs, outs = refs[:n_inputs], refs[n_inputs:]
    rows, depth = outs[0].shape[2:]
    per_action = kron_hi.shape[0] // len(routes)
    q_hi, q_lo = kron_hi[...], kron_lo[...]
    mixed = []
    for row in range(0, rows, 2):
        cols = [
            jnp.concatenate(
                [
                    inputs[which][lead : lead + count, start + row + extra, :]
                    for which, lead, count, start in views
                ],
                axis=0,
            )
            for extra in range(2)
        ]
        x_hi, x_lo = halves(jnp.concatenate(cols, axis=1))
        out = (
            jnp.dot(q_hi, x_hi, preferred_element_type=F32)
            + jnp.dot(q_hi, x_lo, preferred_element_type=F32)
            + jnp.dot(q_lo, x_hi, preferred_element_type=F32)
        )
        mixed += [out[:, :depth], out[:, depth:]]
    for action, route in enumerate(routes):
        start = action * per_action
        block = jnp.concatenate([one[start : start + per_action] for one in mixed], axis=0)
        t_hi, t_lo = halves(block)
        both = jnp.dot(
            jnp.concatenate([t_hi, t_lo], axis=1), right3[action], preferred_element_type=F32
        )
        done = both[:, :depth] + both[:, depth:]
        for row in range(rows):
            first = row * per_action
            for which, slot in route:
                count = outs[which].shape[1]
                outs[which][slot, :, row, :] = done[first : first + count]
                first += count


def third_dim_kernel(n_pieces, rows0, row, pieces1, piece1, meta, costs0, costs1, left2, util23, *refs):
    pieces, scores, local = refs[:n_pieces], refs[n_pieces], refs[n_pieces + 1]
    per_group, rows1 = scores.shape[:2]
    length = util23.shape[1]
    depth = util23.shape[2]
    which = [meta[PLACE + meta[0] * per_group + slot] for slot in range(per_group)]
    first = (meta[2] * 2 + meta[3]) * rows0 + row
    start1 = (meta[1] * pieces1 + piece1) * rows1
    for second in range(0, rows1, 2):
        for slot in range(per_group):
            cols = [
                jnp.concatenate([piece[slot, second + extra] for piece in pieces], axis=0)
                for extra in range(2)
            ]
            g_hi, g_lo = halves(jnp.concatenate(cols, axis=1))
            both = jnp.dot(
                left2[slot], jnp.concatenate([g_hi, g_lo], axis=0), preferred_element_type=F32
            )
            expected = both[:length] + both[length:]
            for extra in range(2):
                flat = costs0[which[slot], first] + costs1[which[slot], start1 + second + extra]
                scores[slot, second + extra] = (util23[slot] + flat) + DISCOUNT * expected[
                    :, extra * depth : (extra + 1) * depth
                ]
        for extra in range(2):
            found = [scores[slot, second + extra] for slot in range(per_group)]
            top = functools.reduce(jnp.maximum, found)
            total = functools.reduce(jnp.add, [jnp.exp(one - top) for one in found])
            local[second + extra] = top + jnp.log(total)


def choice_kernel(scores, mine, other, *refs):
    new_value, choice_prob = refs[-2:]
    a, b = mine[...], other[...]
    top, low = jnp.maximum(a, b), jnp.minimum(a, b)
    total = top + jnp.log(1.0 + jnp.exp(low - top))
    new_value[0] = total
    for slot in range(scores.shape[0]):
        choice_prob[slot, 0] = jnp.exp(scores[slot] - total).astype(choice_prob.dtype)


def after(value, *done):
    return lax.optimization_barrier((value, *done))[0] if done else value


def whole_block():
    return pl.BlockSpec(memory_space=pltpu.VMEM)


def params(mebibytes):
    return pltpu.CompilerParams(vmem_limit_bytes=mebibytes * MIB)


def gather_body(
    value_now,
    cost_first,
    cost_second,
    cost_third,
    cost_fourth,
    trans_weights,
    trans_offsets,
    action_order,
):
    n_act, n_narrow, n_wide = (lax.axis_size(name) for name in ("act", "narrow", "wide"))
    n_outer = n_wide // 2
    act, narrow, wide = (lax.axis_index(name) for name in ("act", "narrow", "wide"))
    outer, core = wide // 2, wide % 2
    actions, _, taps = trans_weights.shape
    per_group = actions // n_act
    rows0, rows1, len2, len3 = value_now.shape
    len0, len1 = rows0 * n_wide, rows1 * n_narrow
    lengths = (len0, len1, len2, len3)
    chunk = CHUNK_ROWS
    share = (len2 - n_narrow * chunk) // n_act
    n_chunks = share // chunk
    core_flip = [(i, i ^ 1) for i in range(n_wide)]
    act_flip = [(i, (i + 1) % n_act) for i in range(n_act)]
    narrow_flip = [(i, (i + 1) % n_narrow) for i in range(n_narrow)]

    def across(bit):
        return [(i, i ^ (2 * bit)) for i in range(n_wide)]

    def part(begin, size):
        return lax.dynamic_slice_in_dim(value_now, begin, size, 2)

    near = [(0, other, ahead) for ahead in range(n_narrow) for other in range(2)]
    arrivals = near + [
        (far, other, ahead)
        for ahead in range(n_narrow)
        for other in range(2)
        for far in range(1, n_outer)
    ]

    half_band = (taps - 1) // 2
    width = -(-(max(lengths) + 4 * half_band) // LANES) * LANES
    weights = jnp.pad(trans_weights, ((0, 0), (0, 0), (0, width - taps)))
    place = jnp.stack([act, narrow, outer, core]).astype(jnp.int32)
    meta = jnp.concatenate([place, action_order, trans_offsets.T.reshape(-1)])
    smem = pl.BlockSpec(memory_space=pltpu.SMEM)
    q_rows = actions * rows0 * rows1
    kron_hi, kron_lo, side_hi, side_lo, right3 = pl.pallas_call(
        functools.partial(
            prepare_kernel, lengths, taps, (n_act, n_narrow, n_outer), rows0, rows1, arrivals
        ),
        out_shape=(
            jax.ShapeDtypeStruct((q_rows, len0 * len1), BF16),
            jax.ShapeDtypeStruct((q_rows, len0 * len1), BF16),
            jax.ShapeDtypeStruct((q_rows * n_narrow // n_act, len0 * len1), BF16),
            jax.ShapeDtypeStruct((q_rows * n_narrow // n_act, len0 * len1), BF16),
            jax.ShapeDtypeStruct((actions, 2 * len3, 2 * len3), BF16),
        ),
        in_specs=[smem, whole_block()],
        out_specs=(whole_block(),) * 5,
        scratch_shapes=[pltpu.VMEM((len0, len0 * len1), F32), pltpu.VMEM((len1, len0 * len1), F32)],
        compiler_params=params(16),
        cost_estimate=pl.CostEstimate(flops=10**9, bytes_accessed=4 * 10**6, transcendentals=0),
        name="prepare",
    )(meta, weights)
    segments = [(0, share, 0, ahead, n_act) for ahead in range(n_act)]
    segments += [(n_act * share, chunk, 1, ahead, n_narrow) for ahead in range(n_narrow)]
    left2, util23 = pl.pallas_call(
        functools.partial(prepare_third_kernel, taps, segments),
        out_shape=(
            jax.ShapeDtypeStruct((per_group, 2 * len2, 2 * len2), BF16),
            jax.ShapeDtypeStruct((per_group, len2, len3), F32),
        ),
        in_specs=[smem] + [whole_block()] * 3,
        out_specs=(whole_block(),) * 2,
        compiler_params=params(12),
        cost_estimate=pl.CostEstimate(flops=10**9, bytes_accessed=4 * 10**6, transcendentals=0),
        name="prepare_third",
    )(meta, weights, cost_third, cost_fourth)

    side_begin = n_act * share
    inner = (outer == 1) | (outer == 2)
    value_now, inner, place, act_begin, own_begin, other_begin = lax.optimization_barrier(
        (
            value_now,
            inner,
            place,
            act * share,
            side_begin + narrow * chunk,
            side_begin + (n_narrow - 1 - narrow) * chunk,
        )
    )
    chunks = [part(act_begin + index * chunk, chunk) for index in range(n_chunks)]
    to_narrow = jnp.concatenate([part(act_begin, share), part(other_begin, chunk)], axis=2)
    own_side = part(own_begin, chunk)
    mine = jnp.concatenate([part(act_begin, share), own_side], axis=2)
    direct = [lax.ppermute(chunks[0], "wide", across(far)) for far in range(1, n_outer)]
    around = lax.ppermute(to_narrow, "narrow", narrow_flip)
    soon = lax.ppermute(part(act_begin + chunk, share - chunk), "wide", across(1))
    direct, *_ = lax.optimization_barrier((direct, kron_hi, right3))
    side = jnp.concatenate([own_side, around[:, :, share:]], axis=0)

    bits = [1 << bit for bit in range(1, n_outer.bit_length() - 1)]

    def doubled(own, twin, *done):
        size = own.shape[0]
        blocks = [own, twin]
        for bit in bits:
            grown = after(jnp.concatenate(blocks, axis=0), *done)
            more = lax.ppermute(grown, "wide", across(bit))
            blocks += [more[i : i + size] for i in range(0, more.shape[0], size)]
        return blocks[1:]

    inner_swap = [(2 * a + c, 2 * b + c) for a, b in ((1, 2), (2, 1)) for c in range(2)]
    outward = [(2 * a + c, 2 * b + c) for a, b in ((1, 0), (2, 3)) for c in range(2)]

    def by_line(own, twin, *done):
        size = own.shape[0]
        grown = after(jnp.concatenate([own, twin], axis=0), *done)
        came = lax.ppermute(grown, "wide", inner_swap)
        passed = lax.ppermute(after(came, moved[-1]), "wide", outward)
        return [
            twin,
            jnp.where(inner, came[size:], passed[:size]),
            jnp.where(inner, came[:size], passed[size:]),
        ]

    far0 = jnp.concatenate(direct, axis=0)
    crossed = [lax.ppermute(far0, "wide", core_flip)]
    moved = [lax.ppermute(far0, "narrow", narrow_flip)]
    late = lax.ppermute(after(side, far0), "wide", across(1))
    owns = chunks + [side]
    twins = [None] + [soon[:, :, i : i + chunk] for i in range(0, share - chunk, chunk)] + [late]
    nears = [mine, lax.ppermute(after(mine, crossed[0]), "wide", core_flip)]
    nears += [around, lax.ppermute(after(around, crossed[0]), "wide", core_flip)]
    nears = [one.reshape(rows0 * rows1, share + chunk, len3) for one in nears]

    def contract(kron, views, routes, out_rows, inputs):
        return pl.pallas_call(
            functools.partial(short_dims_kernel, views, routes),
            out_shape=tuple(
                jax.ShapeDtypeStruct((per_group, rows, chunk, len3), F32) for rows in out_rows
            ),
            in_specs=[whole_block()] * (3 + len(inputs)),
            out_specs=(whole_block(),) * len(out_rows),
            compiler_params=params(12),
            cost_estimate=pl.CostEstimate(flops=10**6, bytes_accessed=10**4, transcendentals=0),
            name="short_dims",
        )(*kron, right3, *inputs)

    block_rows = rows0 * rows1
    far_rows = (n_outer - 1) * block_rows
    def halved(one):
        return [one[i : i + rows0] for i in range(0, n_narrow * rows0, rows0)]

    side_early = [lax.ppermute(half, "wide", core_flip) for half in halved(late)]
    fars = [far0]
    kept, sent = [], []
    for index in range(n_chunks):
        far = fars[index]
        if index:
            if index == 1:
                far = after(far, late)
            crossed.append(lax.ppermute(far, "wide", core_flip))
            moved.append(lax.ppermute(after(far, moved[-1]), "narrow", narrow_flip))
        spread = by_line if index + 1 == n_chunks and n_outer == 4 else doubled
        done = [fars[index]] + ([], moved[:1], kept[:1] + moved[1:2])[min(index, 2)]
        blocks = spread(owns[index + 1], twins[index + 1], *done)
        fars.append(jnp.concatenate(blocks, axis=0))
        ready = ([left2, util23], side_early, ())[min(index, 2)]
        handed = lax.ppermute(after(moved[index], *ready), "wide", core_flip)
        pieces = [far, crossed[index], moved[index], handed]
        inputs = nears + [one.reshape(far_rows, chunk, len3) for one in pieces]
        views = [(i, 0, block_rows, index * chunk) for i in range(len(nears))]
        views += [(len(nears) + i, 0, far_rows, 0) for i in range(len(pieces))]
        cuts = rows0 if index == n_chunks - 1 else 1
        routes = [[(0, slot)] for slot in range(per_group)]
        routes += [[(1 + cut, slot) for cut in range(cuts)] for slot in range(per_group)]
        out_rows = [block_rows] + [block_rows // cuts] * cuts
        keep, *for_act = contract((kron_hi, kron_lo), views, routes, out_rows, inputs)
        kept.append(keep)
        sent.append([])
        for one in for_act:
            before = [one for ones in sent for one in ones][-1:]
            sent[-1].append(lax.ppermute(after(one, *before), "act", act_flip))

    turned = side_early + [
        lax.ppermute(half, "wide", core_flip) for one in blocks[1:] for half in halved(one)
    ]
    inputs = nears + [one.reshape(-1, chunk, len3) for one in blocks + turned]
    views = [(i, 0, block_rows, share) for i in range(len(nears))]
    for ahead in range(n_narrow):
        views += [(len(nears) + i, ahead * block_rows, block_rows, 0) for i in range(len(blocks))]
        first = len(nears) + len(blocks) + ahead
        views += [(first + n_narrow * i, 0, block_rows, 0) for i in range(len(blocks))]
    routes = [[(0, slot), (1, slot)] for slot in range(per_group)]
    count = side_hi.shape[0] // rows0
    ready = sent[-1][:1]
    side_keep, side_got = [], []
    for row in range(rows0):
        kron = [one[row * count : (row + 1) * count] for one in (side_hi, side_lo)]
        kron[0] = after(kron[0], *ready)
        keep, give = contract(kron, views, routes, [rows1, rows1], inputs)
        side_keep.append(keep)
        side_got.append(lax.ppermute(after(give, *side_got[-1:]), "narrow", narrow_flip))
        ready = [give]

    parts = [(keep, None) for keep in kept] + [(ones[0], None) for ones in sent[:-1]]
    parts += [(sent[-1][0], sent[-1]), (side_keep[0], side_keep), (side_got[0], side_got)]
    by_row = []
    units = [(row, piece) for row in range(rows0) for piece in range(4)]
    unit1 = rows1 // 4
    for row, piece in units:
        arrays = [cut[row] if cut else one for one, cut in parts]
        specs = [
            pl.BlockSpec(
                (per_group, unit1) + one.shape[2:],
                lambda i, block=piece if cut else 4 * row + piece: (0, block, 0, 0),
            )
            for one, (_, cut) in zip(arrays, parts)
        ]
        scores, local = pl.pallas_call(
            functools.partial(third_dim_kernel, len(parts), rows0, row, 4, piece),
            grid=(1,),
            out_shape=(
                jax.ShapeDtypeStruct((per_group, unit1, len2, len3), F32),
                jax.ShapeDtypeStruct((unit1, len2, len3), F32),
            ),
            in_specs=[smem] * 3 + [whole_block()] * 2 + specs,
            out_specs=(whole_block(),) * 2,
            compiler_params=params(20),
            cost_estimate=pl.CostEstimate(
                flops=10**9, bytes_accessed=5 * 10**6, transcendentals=10**6
            ),
            name="third_dim",
        )(meta, cost_first, cost_second, left2, util23, *arrays)
        by_row.append((scores, local, lax.ppermute(local, "act", act_flip)))

    results = ()
    for (row, piece), operands in zip(units, by_row):
        results = pl.pallas_call(
            choice_kernel,
            grid=(1,),
            out_shape=(
                jax.ShapeDtypeStruct(value_now.shape, F32),
                jax.ShapeDtypeStruct((per_group,) + value_now.shape, BF16),
            ),
            in_specs=[whole_block()] * 3 + [pl.BlockSpec(memory_space=pl.ANY)] * len(results),
            out_specs=(
                pl.BlockSpec((1, unit1, len2, len3), lambda i, at=(row, piece): at + (0, 0)),
                pl.BlockSpec(
                    (per_group, 1, unit1, len2, len3), lambda i, at=(row, piece): (0,) + at + (0, 0)
                ),
            ),
            input_output_aliases={3: 0, 4: 1} if results else {},
            compiler_params=params(16),
            cost_estimate=pl.CostEstimate(
                flops=10**7, bytes_accessed=5 * 10**6, transcendentals=10**6
            ),
            name="choice",
        )(*operands, *results)
    return tuple(results)


def gather_fits(mesh, value_shape, actions, offset_reach):
    n_wide, n_narrow, n_act = (mesh.shape[name] for name in ("wide", "narrow", "act"))
    len0, len1, len2, len3 = value_shape
    if n_act != 2 or n_wide < 4 or n_wide & (n_wide - 1) or actions % n_act:
        return False
    if n_narrow != 2 or len2 % (n_act * CHUNK_ROWS) or len2 < 4 * n_act * CHUNK_ROWS:
        return False
    if len2 != LANES or len3 != LANES:
        return False
    if (len1 // n_narrow) % SUBLANES or len0 * len1 // (n_wide * n_narrow) % 16 or len0 % n_wide:
        return False
    if max(len0, len1) > LANES or len1 % n_narrow:
        return False
    raw = len0 * len1 * len2 * len3 // (2 * n_act)
    exchanged = 2 * (actions // n_act) * len0 * len1 * len2 * len3 // (n_wide * n_narrow)
    return raw <= exchanged


def solution(mesh):
    def run(value_now, *rest):
        actions = rest[-1].shape[0]
        small = gather_fits(mesh, value_now.shape, actions, rest[4].shape[-1])
        return jax.shard_map(
            gather_body if small else exchange_body,
            mesh=mesh,
            in_specs=(P("wide", "narrow", None, None), P(), P(), P(), P(), P(), P(), P()),
            out_specs=(P("wide", "narrow", None, None), P("act", "wide", "narrow", None, None)),
            check_vma=False,
        )(value_now, *rest)

    return run
```
